32 devices in a mesh: dp: 8 (over z, y), tensor: 4 (over x, core).
Axes of the slice: x: 2, y: 2, z: 4, core: 2. Of those that a mesh axis runs over, the one named last changes fastest.
Arguments:
- picture_averaged_encodings: bfloat16 [1536, 1152], P('dp'), may hold values from -6 to 6
- caption_averaged_encodings: bfloat16 [1536, 1152], P('dp'), may hold values from -6 to 6
- picture_mapping_matrix: bfloat16 [1152, 1152], P(None, 'tensor'), may hold values from -0.1875 to 0.1875
- caption_mapping_matrix: bfloat16 [1152, 1152], P(None, 'tensor'), may hold values from -0.1875 to 0.1875
- picture_weight_perturbation: bfloat16 [1152, 1152], P(None, 'tensor'), may hold values from -0.1875 to 0.1875
- caption_weight_perturbation: bfloat16 [1152, 1152], P(None, 'tensor'), may hold values from -0.1875 to 0.1875
- sharpness_multiplier: float32 [1], replicated, may hold values from 6 to 14
- offset_additive: float32 [1], replicated, may hold values from -8 to -4
Outputs:
- image_hvp: float32 [1152, 1152], P('dp', 'tensor')
- text_hvp: float32 [1152, 1152], P('dp', 'tensor')
The draws below stay inside these ranges and needn't reach their ends.
All inputs are finite; a program needn't handle non-finite values.
Results may differ from the reference program's by a relative error of at most 0.0025.
Values may be sent and summed in bfloat16 or wider, within the bound.
No kernel may reach another device: no remote copies, remote signals or barrier semaphores. Data moves between devices by JAX's collectives and lax.ppermute only.
A program may use at most 128 MiB of HBM per device.

```python
import jax
import jax.numpy as jnp
from jax import lax

D = 1152
PAIRS = 1536
N_DP = 8


def levels(rng, shape, shards, low, top_value):
    def one(position, parts):
        heights = jax.random.uniform(jax.random.fold_in(jax.random.fold_in(rng, 6), position), (parts,), jnp.float32, low / len(shards), top_value / len(shards))
        return jnp.repeat(jnp.exp(heights), shape[position] // parts).reshape((-1,) + (1,) * (len(shape) - position - 1))

    factor_of = one(*shards[0])
    for cut in shards[1:]:
        factor_of = factor_of * one(*cut)
    return factor_of


def normal_values(own_key, extent, scale, bound, pieces=(), held_as=jnp.bfloat16):
    array = jax.random.normal(own_key, extent, jnp.float32) * scale
    if len(pieces) > 0:
        array = levels(own_key, extent, pieces, -0.22, 0.18) * array
    return jnp.clip(array, min=-bound, max=bound).astype(held_as)


def setup_inputs(seed: int = 0) -> dict:
    key_list = jax.random.split(jax.random.key(seed), 9)
    return {
        "picture_averaged_encodings": normal_values(key_list[0], (PAIRS, D), 1.0, 6.0, ((0, 8),)),
        "caption_averaged_encodings": normal_values(key_list[1], (PAIRS, D), 1.0, 6.0, ((0, 8),)),
        "picture_mapping_matrix": normal_values(key_list[2], (D, D), D ** -0.5, 0.1875, ((1, 4),)),
        "caption_mapping_matrix": normal_values(key_list[3], (D, D), D ** -0.5, 0.1875, ((1, 4),)),
        "picture_weight_perturbation": normal_values(key_list[4], (D, D), D ** -0.5, 0.1875, ((1, 4),)),
        "caption_weight_perturbation": normal_values(key_list[5], (D, D), D ** -0.5, 0.1875, ((1, 4),)),
        "sharpness_multiplier": jnp.clip(jax.random.uniform(key_list[6], (1,), jnp.float32, 6.0, 14.0), 6.0, 14.0),
        "offset_additive": jnp.clip(jax.random.uniform(key_list[7], (1,), jnp.float32, -8.0, -4.0), -8.0, -4.0),
    }


EPS = 1e-06

def matmul(left, right):
    return jnp.dot(left, right, preferred_element_type=jnp.float32)

def matmul_nt(left, right):
    return lax.dot_general(left, right, (((1,), (1,)), ((), ())), preferred_element_type=jnp.float32)

def matmul_tn(left, right):
    return lax.dot_general(left, right, (((0,), (0,)), ((), ())), preferred_element_type=jnp.float32)

def unit_parts(raw, raw_rate):
    values = raw.astype(jnp.float32)
    tangent = raw_rate.astype(jnp.float32)
    radius = jnp.sqrt(lax.optimization_barrier(jnp.sum(values * values, axis=1, keepdims=True)) + EPS)
    unit = values / radius
    rate = lax.optimization_barrier(jnp.sum(unit * tangent, axis=1, keepdims=True))
    unit_tangent = (tangent - unit * rate) / radius
    return (unit, unit_tangent, radius, rate)

def unit_backward(unit, unit_tangent, radius, rate, grad, grad_rate):
    inner = lax.optimization_barrier(jnp.sum(unit * grad, axis=1, keepdims=True))
    inner_rate = lax.optimization_barrier(jnp.sum(unit_tangent * grad + unit * grad_rate, axis=1, keepdims=True))
    first = (grad - unit * inner) / radius
    return (grad_rate - unit_tangent * inner - unit * inner_rate - first * rate) / radius

def reference(picture_averaged_encodings, caption_averaged_encodings, picture_mapping_matrix, caption_mapping_matrix, picture_weight_perturbation, caption_weight_perturbation, sharpness_multiplier, offset_additive):
    similarity_multiplier = sharpness_multiplier[0]
    logit_bias = offset_additive[0]
    image_raw = matmul(picture_averaged_encodings, picture_mapping_matrix).astype(jnp.bfloat16)
    image_raw_rate = matmul(picture_averaged_encodings, picture_weight_perturbation).astype(jnp.bfloat16)
    text_raw = matmul(caption_averaged_encodings, caption_mapping_matrix).astype(jnp.bfloat16)
    text_raw_rate = matmul(caption_averaged_encodings, caption_weight_perturbation).astype(jnp.bfloat16)
    image_unit, image_tangent, image_radius, image_rate = unit_parts(image_raw, image_raw_rate)
    text_unit, text_tangent, text_radius, text_rate = unit_parts(text_raw, text_raw_rate)
    image_half = image_unit.astype(jnp.bfloat16)
    image_tangent_half = image_tangent.astype(jnp.bfloat16)
    text_half = text_unit.astype(jnp.bfloat16)
    text_tangent_half = text_tangent.astype(jnp.bfloat16)
    total = picture_averaged_encodings.shape[0]
    block_rows = total // N_DP

    def visit(carry, block_index):
        text_grad, text_grad_rate = carry
        start = (block_index * block_rows).astype(jnp.int32)
        rows_unit = lax.dynamic_slice_in_dim(image_half, start, block_rows, 0)
        rows_tangent = lax.dynamic_slice_in_dim(image_tangent_half, start, block_rows, 0)
        logits = similarity_multiplier * matmul_nt(rows_unit, text_half) + logit_bias
        logit_rate = similarity_multiplier * (matmul_nt(rows_tangent, text_half) + matmul_nt(rows_unit, text_tangent_half))
        probability = jax.nn.sigmoid(logits)
        row_ids = lax.broadcasted_iota(jnp.int32, (block_rows, 1), 0) + start
        col_ids = lax.broadcasted_iota(jnp.int32, (1, total), 1)
        positive = (row_ids == col_ids).astype(jnp.float32)
        weight = (probability - positive).astype(jnp.bfloat16)
        weight_rate = (probability * (1.0 - probability) * logit_rate).astype(jnp.bfloat16)
        image_grad = similarity_multiplier * matmul(weight, text_half)
        image_grad_rate = similarity_multiplier * (matmul(weight_rate, text_half) + matmul(weight, text_tangent_half))
        text_grad = text_grad + similarity_multiplier * matmul_tn(weight, rows_unit)
        text_grad_rate = text_grad_rate + similarity_multiplier * (matmul_tn(weight_rate, rows_unit) + matmul_tn(weight, rows_tangent))
        return ((text_grad, text_grad_rate), (image_grad, image_grad_rate))
    empty_rows = jnp.zeros((total, picture_mapping_matrix.shape[1]), jnp.float32)
    carried, stacked = lax.scan(visit, (empty_rows, empty_rows), jnp.arange(N_DP, dtype=jnp.int32))
    text_grad, text_grad_rate = carried
    image_grad = stacked[0].reshape(total, -1)
    image_grad_rate = stacked[1].reshape(total, -1)
    image_back = unit_backward(image_unit, image_tangent, image_radius, image_rate, image_grad, image_grad_rate).astype(jnp.bfloat16)
    text_back = unit_backward(text_unit, text_tangent, text_radius, text_rate, text_grad, text_grad_rate).astype(jnp.bfloat16)
    image_hvp = matmul_tn(picture_averaged_encodings, image_back)
    text_hvp = matmul_tn(caption_averaged_encodings, text_back)
    return (image_hvp, text_hvp)
```

```python
import jax
import jax.numpy as jnp
from jax import lax
from jax.sharding import PartitionSpec as P

EPS = 1e-06


def swapped(value, axis, mask):
    count = lax.axis_size(axis)
    return lax.ppermute(value, axis, [(source, source ^ mask) for source in range(count)])


def matmul(left, right):
    return jnp.dot(left, right, preferred_element_type=jnp.float32)


def matmul_nt(left, right):
    return lax.dot_general(
        left, right, (((1,), (1,)), ((), ())), preferred_element_type=jnp.float32
    )


def matmul_tn(left, right):
    return lax.dot_general(
        left, right, (((0,), (0,)), ((), ())), preferred_element_type=jnp.float32
    )


def unit_parts(raw, raw_rate):
    values = raw.astype(jnp.float32)
    tangent = raw_rate.astype(jnp.float32)
    radius = jnp.sqrt(jnp.sum(values * values, axis=1, keepdims=True) + EPS)
    unit = values / radius
    rate = jnp.sum(unit * tangent, axis=1, keepdims=True)
    unit_tangent = (tangent - unit * rate) / radius
    return (unit, unit_tangent, radius, rate)


def unit_backward(unit, unit_tangent, radius, rate, grad, grad_rate):
    inner = jnp.sum(unit * grad, axis=1, keepdims=True)
    inner_rate = jnp.sum(unit_tangent * grad + unit * grad_rate, axis=1, keepdims=True)
    first = (grad - unit * inner) / radius
    return (grad_rate - unit_tangent * inner - unit * inner_rate - first * rate) / radius


def local(
    picture_averaged_encodings,
    caption_averaged_encodings,
    picture_mapping_matrix,
    caption_mapping_matrix,
    picture_weight_perturbation,
    caption_weight_perturbation,
    sharpness_multiplier,
    offset_additive,
):
    similarity_multiplier = sharpness_multiplier[0]
    logit_bias = offset_additive[0]
    tensor_rank = lax.axis_index("tensor")
    data_rank = lax.axis_index("dp")
    tensor_count = lax.axis_size("tensor")
    data_count = lax.axis_size("dp")
    planes = data_count // 2
    rows, width = picture_averaged_encodings.shape
    cols = picture_mapping_matrix.shape[1]
    share = rows // tensor_count
    out_rows = width // data_count
    half = jnp.bfloat16

    text = jnp.stack(
        [
            matmul(caption_averaged_encodings, caption_mapping_matrix).astype(half),
            matmul(caption_averaged_encodings, caption_weight_perturbation).astype(half),
        ]
    )
    image = jnp.stack(
        [
            matmul(picture_averaged_encodings, picture_mapping_matrix).astype(half),
            matmul(picture_averaged_encodings, picture_weight_perturbation).astype(half),
        ]
    )

    def share_of(value, axis, mask):
        start = (tensor_rank ^ mask) * share
        return lax.dynamic_slice_in_dim(value, start, share, axis)

    parts = [share_of(text, 1, 0)]
    for mask in range(1, tensor_count):
        parts.append(swapped(share_of(text, 1, mask), "tensor", mask))
    text = jnp.concatenate(parts, axis=2)
    slots = [text] + [swapped(text, "dp", 2 * mask) for mask in range(1, planes)]

    image = jnp.concatenate([image, swapped(image, "dp", 1)], axis=1)
    blocks = [image]
    mask = tensor_count // 2
    image_blocks = {0: image}
    while mask >= 1:
        held = sorted(image_blocks)
        sent = jnp.concatenate([image_blocks[k] for k in held], axis=2)
        got = swapped(sent, "tensor", mask)
        for place, k in enumerate(held):
            image_blocks[k ^ mask] = got[:, :, place * cols : (place + 1) * cols]
        mask //= 2
    image = jnp.concatenate([image_blocks[k] for k in range(tensor_count)], axis=2)
    text = jnp.concatenate(slots, axis=1)

    def out_columns(value, rank):
        taken = [
            lax.dynamic_slice_in_dim(value, (rank ^ (2 * mask)) * out_rows, out_rows, 1)
            for mask in range(planes)
        ]
        return jnp.concatenate(taken, axis=1)

    def plane_encodings(value):
        other = swapped(out_columns(value, data_rank ^ 1), "dp", 1)
        return jnp.concatenate([out_columns(value, data_rank), other], axis=0)

    picture_plane = plane_encodings(picture_averaged_encodings)
    ordered = jnp.concatenate(
        [share_of(caption_averaged_encodings, 0, mask) for mask in range(tensor_count)], axis=0
    )
    caption_plane = plane_encodings(ordered)

    image_unit, image_tangent, image_radius, image_rate = unit_parts(image[0], image[1])
    text_unit, text_tangent, text_radius, text_rate = unit_parts(text[0], text[1])
    image_half = image_unit.astype(half)
    image_tangent_half = image_tangent.astype(half)
    text_half = text_unit.astype(half)
    text_tangent_half = text_tangent.astype(half)

    logits = similarity_multiplier * matmul_nt(text_half, image_half) + logit_bias
    logit_rate = similarity_multiplier * (
        matmul_nt(text_half, image_tangent_half) + matmul_nt(text_tangent_half, image_half)
    )
    probability = jax.nn.sigmoid(logits)
    text_ids = lax.broadcasted_iota(jnp.int32, (logits.shape[0], 1), 0)
    image_ids = lax.broadcasted_iota(jnp.int32, (1, logits.shape[1]), 1)
    positive = ((text_ids < share) & (text_ids + tensor_rank * share == image_ids)).astype(
        jnp.float32
    )
    weight = (probability - positive).astype(half)
    weight_rate = (probability * (1.0 - probability) * logit_rate).astype(half)
    text_grad = similarity_multiplier * matmul(weight, image_half)
    text_grad_rate = similarity_multiplier * (
        matmul(weight_rate, image_half) + matmul(weight, image_tangent_half)
    )
    image_grad = similarity_multiplier * matmul_tn(weight, text_half)
    image_grad_rate = similarity_multiplier * (
        matmul_tn(weight_rate, text_half) + matmul_tn(weight, text_tangent_half)
    )

    text_back = unit_backward(
        text_unit, text_tangent, text_radius, text_rate, text_grad, text_grad_rate
    )
    image_back = unit_backward(
        image_unit, image_tangent, image_radius, image_rate, image_grad, image_grad_rate
    )

    total = text_back[:share]
    for mask in range(1, planes):
        sent = text_back[mask * share : (mask + 1) * share].astype(half)
        total = total + swapped(sent, "dp", 2 * mask).astype(jnp.float32)
    text_back = total.astype(half)
    parts = [text_back[:, :cols]]
    for mask in range(1, tensor_count):
        sent = text_back[:, mask * cols : (mask + 1) * cols]
        parts.append(swapped(sent, "tensor", mask))
    text_back = jnp.concatenate(parts, axis=0)
    text_back = jnp.concatenate([text_back, swapped(text_back, "dp", 1)], axis=0)

    image_blocks = {k: image_back[:, k * cols : (k + 1) * cols] for k in range(tensor_count)}
    mask = 1
    while mask < tensor_count:
        kept = [k for k in sorted(image_blocks) if not k & mask]
        sent = jnp.concatenate([image_blocks[k ^ mask] for k in kept], axis=1)
        got = swapped(sent, "tensor", mask).astype(jnp.float32)
        image_blocks = {
            k: image_blocks[k] + got[:, place * cols : (place + 1) * cols]
            for place, k in enumerate(kept)
        }
        mask *= 2
    image_back = image_blocks[0]
    got = swapped(image_back, "dp", 1)
    image_back = (
        image_back + jnp.concatenate([got[rows:], got[:rows]], axis=0)
    ).astype(half)

    def head(encodings, back):
        product = matmul_tn(encodings, back)
        total = product[:out_rows]
        for mask in range(1, planes):
            sent = product[mask * out_rows : (mask + 1) * out_rows].astype(half)
            total = total + swapped(sent, "dp", 2 * mask).astype(jnp.float32)
        return total

    return (head(picture_plane, image_back), head(caption_plane, text_back))


def solution(mesh):
    in_specs = (
        P("dp", None),
        P("dp", None),
        P(None, "tensor"),
        P(None, "tensor"),
        P(None, "tensor"),
        P(None, "tensor"),
        P(),
        P(),
    )
    out_specs = (P("dp", "tensor"), P("dp", "tensor"))
    return jax.shard_map(local, mesh=mesh, in_specs=in_specs, out_specs=out_specs, check_vma=False)
```

```python
import functools

import jax
import jax.numpy as jnp
from jax import lax
from jax.experimental import pallas as pl
from jax.experimental.pallas import tpu as pltpu
from jax.sharding import PartitionSpec as P

EPS = 1e-06


def swapped(value, axis, mask):
    count = lax.axis_size(axis)
    return lax.ppermute(value, axis, [(source, source ^ mask) for source in range(count)])


def matmul(left, right):
    return jnp.dot(left, right, preferred_element_type=jnp.float32)


def matmul_nt(left, right):
    return lax.dot_general(
        left, right, (((1,), (1,)), ((), ())), preferred_element_type=jnp.float32
    )


def matmul_tn(left, right):
    return lax.dot_general(
        left, right, (((0,), (0,)), ((), ())), preferred_element_type=jnp.float32
    )


def unit_parts(raw, raw_rate):
    values = raw.astype(jnp.float32)
    tangent = raw_rate.astype(jnp.float32)
    radius = jnp.sqrt(jnp.sum(values * values, axis=1, keepdims=True) + EPS)
    unit = values / radius
    rate = jnp.sum(unit * tangent, axis=1, keepdims=True)
    unit_tangent = (tangent - unit * rate) / radius
    return (unit, unit_tangent, radius, rate)


def unit_backward(unit, unit_tangent, radius, rate, grad, grad_rate):
    inner = jnp.sum(unit * grad, axis=1, keepdims=True)
    inner_rate = jnp.sum(unit_tangent * grad + unit * grad_rate, axis=1, keepdims=True)
    first = (grad - unit * inner) / radius
    return (grad_rate - unit_tangent * inner - unit * inner_rate - first * rate) / radius


def general(
    picture_averaged_encodings,
    caption_averaged_encodings,
    picture_mapping_matrix,
    caption_mapping_matrix,
    picture_weight_perturbation,
    caption_weight_perturbation,
    sharpness_multiplier,
    offset_additive,
):
    similarity_multiplier = sharpness_multiplier[0]
    logit_bias = offset_additive[0]
    tensor_rank = lax.axis_index("tensor")
    data_rank = lax.axis_index("dp")
    tensor_count = lax.axis_size("tensor")
    data_count = lax.axis_size("dp")
    planes = data_count // 2
    rows, width = picture_averaged_encodings.shape
    cols = picture_mapping_matrix.shape[1]
    share = rows // tensor_count
    out_rows = width // data_count
    half = jnp.bfloat16

    text = jnp.stack(
        [
            matmul(caption_averaged_encodings, caption_mapping_matrix).astype(half),
            matmul(caption_averaged_encodings, caption_weight_perturbation).astype(half),
        ]
    )
    image = jnp.stack(
        [
            matmul(picture_averaged_encodings, picture_mapping_matrix).astype(half),
            matmul(picture_averaged_encodings, picture_weight_perturbation).astype(half),
        ]
    )

    def share_of(value, axis, mask):
        start = (tensor_rank ^ mask) * share
        return lax.dynamic_slice_in_dim(value, start, share, axis)

    parts = [share_of(text, 1, 0)]
    for mask in range(1, tensor_count):
        parts.append(swapped(share_of(text, 1, mask), "tensor", mask))
    text = jnp.concatenate(parts, axis=2)
    slots = [text] + [swapped(text, "dp", 2 * mask) for mask in range(1, planes)]

    image = jnp.concatenate([image, swapped(image, "dp", 1)], axis=1)
    blocks = [image]
    mask = tensor_count // 2
    image_blocks = {0: image}
    while mask >= 1:
        held = sorted(image_blocks)
        sent = jnp.concatenate([image_blocks[k] for k in held], axis=2)
        got = swapped(sent, "tensor", mask)
        for place, k in enumerate(held):
            image_blocks[k ^ mask] = got[:, :, place * cols : (place + 1) * cols]
        mask //= 2
    image = jnp.concatenate([image_blocks[k] for k in range(tensor_count)], axis=2)
    text = jnp.concatenate(slots, axis=1)

    def out_columns(value, rank):
        taken = [
            lax.dynamic_slice_in_dim(value, (rank ^ (2 * mask)) * out_rows, out_rows, 1)
            for mask in range(planes)
        ]
        return jnp.concatenate(taken, axis=1)

    def plane_encodings(value):
        other = swapped(out_columns(value, data_rank ^ 1), "dp", 1)
        return jnp.concatenate([out_columns(value, data_rank), other], axis=0)

    picture_plane = plane_encodings(picture_averaged_encodings)
    ordered = jnp.concatenate(
        [share_of(caption_averaged_encodings, 0, mask) for mask in range(tensor_count)], axis=0
    )
    caption_plane = plane_encodings(ordered)

    image_unit, image_tangent, image_radius, image_rate = unit_parts(image[0], image[1])
    text_unit, text_tangent, text_radius, text_rate = unit_parts(text[0], text[1])
    image_half = image_unit.astype(half)
    image_tangent_half = image_tangent.astype(half)
    text_half = text_unit.astype(half)
    text_tangent_half = text_tangent.astype(half)

    logits = similarity_multiplier * matmul_nt(text_half, image_half) + logit_bias
    logit_rate = similarity_multiplier * (
        matmul_nt(text_half, image_tangent_half) + matmul_nt(text_tangent_half, image_half)
    )
    probability = jax.nn.sigmoid(logits)
    text_ids = lax.broadcasted_iota(jnp.int32, (logits.shape[0], 1), 0)
    image_ids = lax.broadcasted_iota(jnp.int32, (1, logits.shape[1]), 1)
    positive = ((text_ids < share) & (text_ids + tensor_rank * share == image_ids)).astype(
        jnp.float32
    )
    weight = (probability - positive).astype(half)
    weight_rate = (probability * (1.0 - probability) * logit_rate).astype(half)
    text_grad = similarity_multiplier * matmul(weight, image_half)
    text_grad_rate = similarity_multiplier * (
        matmul(weight_rate, image_half) + matmul(weight, image_tangent_half)
    )
    image_grad = similarity_multiplier * matmul_tn(weight, text_half)
    image_grad_rate = similarity_multiplier * (
        matmul_tn(weight_rate, text_half) + matmul_tn(weight, text_tangent_half)
    )

    text_back = unit_backward(
        text_unit, text_tangent, text_radius, text_rate, text_grad, text_grad_rate
    )
    image_back = unit_backward(
        image_unit, image_tangent, image_radius, image_rate, image_grad, image_grad_rate
    )

    total = text_back[:share]
    for mask in range(1, planes):
        sent = text_back[mask * share : (mask + 1) * share].astype(half)
        total = total + swapped(sent, "dp", 2 * mask).astype(jnp.float32)
    text_back = total.astype(half)
    parts = [text_back[:, :cols]]
    for mask in range(1, tensor_count):
        sent = text_back[:, mask * cols : (mask + 1) * cols]
        parts.append(swapped(sent, "tensor", mask))
    text_back = jnp.concatenate(parts, axis=0)
    text_back = jnp.concatenate([text_back, swapped(text_back, "dp", 1)], axis=0)

    image_blocks = {k: image_back[:, k * cols : (k + 1) * cols] for k in range(tensor_count)}
    mask = 1
    while mask < tensor_count:
        kept = [k for k in sorted(image_blocks) if not k & mask]
        sent = jnp.concatenate([image_blocks[k ^ mask] for k in kept], axis=1)
        got = swapped(sent, "tensor", mask).astype(jnp.float32)
        image_blocks = {
            k: image_blocks[k] + got[:, place * cols : (place + 1) * cols]
            for place, k in enumerate(kept)
        }
        mask *= 2
    image_back = image_blocks[0]
    got = swapped(image_back, "dp", 1)
    image_back = (
        image_back + jnp.concatenate([got[rows:], got[:rows]], axis=0)
    ).astype(half)

    def head(encodings, back):
        product = matmul_tn(encodings, back)
        total = product[:out_rows]
        for mask in range(1, planes):
            sent = product[mask * out_rows : (mask + 1) * out_rows].astype(half)
            total = total + swapped(sent, "dp", 2 * mask).astype(jnp.float32)
        return total

    return (head(picture_plane, image_back), head(caption_plane, text_back))


def call(kernel, outs, *args):
    def place(value):
        scalar = value.ndim == 1
        return pl.BlockSpec(memory_space=pltpu.SMEM if scalar else pltpu.VMEM)

    return pl.pallas_call(
        kernel,
        out_shape=[jax.ShapeDtypeStruct(shape, dtype) for shape, dtype in outs],
        in_specs=[place(value) for value in args],
        out_specs=[pl.BlockSpec(memory_space=pltpu.VMEM) for _ in outs],
        compiler_params=pltpu.CompilerParams(vmem_limit_bytes=48 * 1024 * 1024),
    )(*args)


def project_kernel(share, starts, encodings, weight, direction, *outs):
    main = weight.shape[1] // 128 * 128
    left = jnp.concatenate(
        [
            encodings[pl.ds(pl.multiple_of(starts[k], 16), share), :]
            for k in range(starts.shape[0])
        ],
        axis=0,
    )
    tails = jnp.concatenate([weight[:, main:], direction[:, main:]], axis=1)
    tail = 2 * (weight.shape[1] - main)
    rows = outs[0].shape[0]
    for right, first in ((weight[:, :main], 0), (direction[:, :main], main), (tails, 2 * main)):
        product = matmul(left, right).astype(jnp.bfloat16)
        for place, out in enumerate(outs):
            out[:, first : first + right.shape[1]] = product[place * rows : (place + 1) * rows]


def gathered(blocks, main, tail, which):
    first = 2 * main + which * tail
    mains = [block[:, which * main : (which + 1) * main] for block in blocks]
    tails = [block[:, first : first + tail] for block in blocks]
    return jnp.concatenate(mains + tails, axis=1)


def text_rows_kernel(main, tail, *refs):
    blocks, out = [ref[...].astype(jnp.float32) for ref in refs[:-1]], refs[-1]
    width = out.shape[1] // 2
    out[:, :width] = gathered(blocks, main, tail, 0).astype(jnp.bfloat16)
    out[:, width:] = gathered(blocks, main, tail, 1).astype(jnp.bfloat16)


def row_factors(values, tangent):
    squares = jnp.sum(values * values, axis=1, keepdims=True)
    cross = jnp.sum(values * tangent, axis=1, keepdims=True)
    inverse = 1.0 / jnp.sqrt(squares + EPS)
    return inverse, cross * inverse


def unit_rows(values, tangent, inverse, rate):
    unit = values * inverse
    return unit, (tangent - unit * rate) * inverse


def back_rows(unit, tangent, inverse, rate, grad, grad_rate):
    inner = jnp.sum(unit * grad, axis=1, keepdims=True)
    inner_rate = jnp.sum(tangent * grad + unit * grad_rate, axis=1, keepdims=True)
    scaled = rate * inverse
    return (
        grad_rate - tangent * inner - grad * scaled + unit * (inner * scaled - inner_rate)
    ) * inverse


STEP = 48


def image_rows_kernel(main, tail, *refs):
    blocks, (unit, tangent, half, tangent_half, factors) = refs[:-5], refs[-5:]
    count = len(blocks) // 2
    rows = blocks[0].shape[0]
    for shard in range(2):
        held = blocks[shard * count : (shard + 1) * count]

        @pl.loop(0, rows // STEP)
        def _(step):
            here = pl.ds(pl.multiple_of(step * STEP, STEP), STEP)
            there = pl.ds(pl.multiple_of(shard * rows + step * STEP, STEP), STEP)
            parts = [block[here, :].astype(jnp.float32) for block in held]
            values = gathered(parts, main, tail, 0)
            rates = gathered(parts, main, tail, 1)
            inverse, rate = row_factors(values, rates)
            one, two = unit_rows(values, rates, inverse, rate)
            unit[there, :] = one
            tangent[there, :] = two
            half[there, :] = one.astype(jnp.bfloat16)
            tangent_half[there, :] = two.astype(jnp.bfloat16)
            factors[0, there, :] = jnp.broadcast_to(inverse, (STEP, 128))
            factors[1, there, :] = jnp.broadcast_to(rate, (STEP, 128))


def block_kernel(
    main, tail, slots, start, scalars, unit, tangent, half, tangent_half, factors, *refs
):
    texts, refs = refs[:slots], refs[slots:]
    own, sent, packed = refs[0], refs[1:slots], refs[slots:]
    f32, bf16 = jnp.float32, jnp.bfloat16
    share, width = texts[0].shape[0], texts[0].shape[1] // 2
    rows = unit.shape[0] // 2
    multiplier, bias = scalars[0], scalars[1]

    text_parts = []
    for text in texts:
        values, rates = text[:, :width].astype(f32), text[:, width:].astype(f32)
        inverse, rate = row_factors(values, rates)
        text_parts.append(unit_rows(values, rates, inverse, rate) + (inverse, rate))
    text_half = jnp.concatenate([part[0].astype(bf16) for part in text_parts], axis=0)
    text_tangent_half = jnp.concatenate([part[1].astype(bf16) for part in text_parts], axis=0)

    logits = multiplier * matmul_nt(text_half, half[...]) + bias
    logit_rate = multiplier * (
        matmul_nt(text_half, tangent_half[...]) + matmul_nt(text_tangent_half, half[...])
    )
    probability = jax.nn.sigmoid(logits)
    text_ids = lax.broadcasted_iota(jnp.int32, logits.shape, 0)
    image_ids = lax.broadcasted_iota(jnp.int32, logits.shape, 1)
    positive = jnp.where((text_ids < share) & (text_ids + start[0] == image_ids), 1.0, 0.0)
    weight = probability - positive
    weight_rate = probability * (1.0 - probability) * logit_rate
    weight_half, weight_rate_half = weight.astype(bf16), weight_rate.astype(bf16)

    text_grad = multiplier * matmul(weight_half, half[...])
    text_grad_rate = multiplier * (
        matmul(weight_rate_half, half[...]) + matmul(weight_half, tangent_half[...])
    )
    for slot, (one, two, inverse, rate) in enumerate(text_parts):
        here = slice(slot * share, (slot + 1) * share)
        back = back_rows(one, two, inverse, rate, text_grad[here], text_grad_rate[here])
        if slot == 0:
            own[...] = back
        else:
            sent[slot - 1][...] = back.astype(bf16)

    weight_turned = weight.T.astype(bf16)
    weight_rate_turned = weight_rate.T.astype(bf16)
    image_grad = multiplier * matmul(weight_turned, text_half)
    image_grad_rate = multiplier * (
        matmul(weight_rate_turned, text_half) + matmul(weight_turned, text_tangent_half)
    )
    count = len(packed)
    for shard in range(2):
        here = slice(shard * rows, (shard + 1) * rows)
        back = back_rows(
            unit[here, :],
            tangent[here, :],
            factors[0, here, :1],
            factors[1, here, :1],
            image_grad[here],
            image_grad_rate[here],
        )
        for k, out in enumerate(packed):
            out[:, shard * main : (shard + 1) * main] = back[:, k * main : (k + 1) * main]
            first = 2 * main + shard * tail
            taken = count * main + k * tail
            out[:, first : first + tail] = back[:, taken : taken + tail]


def text_sum_kernel(main, tail, own, *refs):
    count = own.shape[1] // (main + tail)
    got, outs = refs[:-count], refs[-count:]
    total = own[...]
    for ref in got:
        total = total + ref[...].astype(jnp.float32)
    for k, out in enumerate(outs):
        first = count * main + k * tail
        out[:, :main] = total[:, k * main : (k + 1) * main].astype(jnp.bfloat16)
        out[:, main:] = total[:, first : first + tail].astype(jnp.bfloat16)


def stack_kernel(*refs):
    rows = refs[0].shape[0]
    for k, ref in enumerate(refs[:-1]):
        refs[-1][k * rows : (k + 1) * rows, :] = ref[...]


def turn_kernel(share, starts, places, encodings, mine, other):
    ordered = jnp.concatenate(
        [
            encodings[pl.ds(pl.multiple_of(starts[k], 16), share), :].astype(jnp.float32)
            for k in range(starts.shape[0])
        ],
        axis=0,
    )
    turned = ordered.T.astype(jnp.bfloat16)
    size = turned.shape[0] // places.shape[0]
    blocks = places.shape[0] // 2
    for block in range(places.shape[0]):
        taken = turned[block * size : (block + 1) * size, :]
        slot = places[block]

        @pl.when(slot < blocks)
        def _():
            mine[pl.ds(pl.multiple_of(slot * size, 16), size), :] = taken

        @pl.when(slot >= blocks)
        def _():
            other[pl.ds(pl.multiple_of((slot - blocks) * size, 16), size), :] = taken


def image_sum_kernel(main, tail, first, second, third, keep, sent):
    total = first[...] + second[...] + third[...]
    keep[:, :main] = total[:, :main]
    keep[:, main:] = total[:, 2 * main : 2 * main + tail]
    sent[:, :main] = total[:, main : 2 * main].astype(jnp.bfloat16)
    sent[:, main:] = total[:, 2 * main + tail :].astype(jnp.bfloat16)


def add_half_kernel(one, two, out):
    out[...] = (one[...] + two[...].astype(jnp.float32)).astype(jnp.bfloat16)


def head_kernel(main, tail, picture, picture_other, caption, caption_other, *refs):
    image, image_other, text, text_other = refs[:4]
    own, sent = refs[4], refs[5:]
    size = own.shape[0]
    products = (
        matmul(picture[...], image[...]) + matmul(picture_other[...], image_other[...]),
        matmul(caption[...], text[...]) + matmul(caption_other[...], text_other[...]),
    )
    for slot, out in enumerate((own,) + tuple(sent)):
        here = slice(slot * size, (slot + 1) * size)
        for head, product in enumerate(products):
            out[:, head * main : (head + 1) * main] = product[here, :main].astype(out.dtype)
            first = 2 * main + head * tail
            out[:, first : first + tail] = product[here, main:].astype(out.dtype)


def final_kernel(main, tail, own, *refs):
    got, outs = refs[:-2], refs[-2:]
    total = own[...]
    for ref in got:
        total = total + ref[...].astype(jnp.float32)
    for head, out in enumerate(outs):
        out[:, :main] = total[:, head * main : (head + 1) * main]
        first = 2 * main + head * tail
        out[:, main:] = total[:, first : first + tail]


def packed(
    picture_averaged_encodings,
    caption_averaged_encodings,
    picture_mapping_matrix,
    caption_mapping_matrix,
    picture_weight_perturbation,
    caption_weight_perturbation,
    sharpness_multiplier,
    offset_additive,
):
    tensor_rank = lax.axis_index("tensor")
    data_rank = lax.axis_index("dp")
    count = lax.axis_size("tensor")
    data_count = lax.axis_size("dp")
    planes = data_count // 2
    rows, width = picture_averaged_encodings.shape
    cols = picture_mapping_matrix.shape[1]
    main = cols // 128 * 128
    tail = cols - main
    share = rows // count
    size = width // data_count
    f32, bf16 = jnp.float32, jnp.bfloat16
    ranks = jnp.arange(count, dtype=jnp.int32)
    starts = (ranks ^ tensor_rank) * share
    plain = ranks * share

    blocks = call(
        functools.partial(project_kernel, share),
        [((share, 2 * cols), bf16)] * count,
        starts,
        caption_averaged_encodings,
        caption_mapping_matrix,
        caption_weight_perturbation,
    )
    got = [blocks[0]] + [swapped(blocks[k], "tensor", k) for k in range(1, count)]
    (text,) = call(
        functools.partial(text_rows_kernel, main, tail), [((share, 2 * width), bf16)], *got
    )
    texts = [text] + [swapped(text, "dp", 2 * k) for k in range(1, planes)]

    (image,) = call(
        functools.partial(project_kernel, share),
        [((rows, 2 * cols), bf16)],
        plain,
        picture_averaged_encodings,
        picture_mapping_matrix,
        picture_weight_perturbation,
    )
    shards = [[image], [swapped(image, "dp", 1)]]
    mask = count // 2
    order = [0]
    while mask >= 1:
        if mask > 1:
            got = [[swapped(one, "tensor", mask) for one in held] for held in shards]
        else:
            flat = jnp.stack([one for held in shards for one in held])
            flat = swapped(flat, "tensor", mask)
            step = len(order)
            got = [[flat[shard * step + k] for k in range(step)] for shard in range(2)]
        shards = [held + more for held, more in zip(shards, got)]
        order = order + [k ^ mask for k in order]
        mask //= 2
    places = [order.index(k) for k in range(count)]
    image_blocks = [held[place] for held in shards for place in places]
    unit, tangent, half, tangent_half, factors = call(
        functools.partial(image_rows_kernel, main, tail),
        [
            ((2 * rows, width), f32),
            ((2 * rows, width), f32),
            ((2 * rows, width), bf16),
            ((2 * rows, width), bf16),
            ((2, 2 * rows, 128), f32),
        ],
        *image_blocks,
    )

    block_ids = jnp.arange(data_count, dtype=jnp.int32)
    slots = ((block_ids ^ data_rank) >> 1) + planes * ((block_ids ^ data_rank) & 1)

    def turned(encodings, order):
        mine, other = call(
            functools.partial(turn_kernel, share),
            [((planes * size, rows), bf16)] * 2,
            order,
            slots,
            encodings,
        )
        return mine, swapped(other, "dp", 1)

    picture_pair = turned(picture_averaged_encodings, plain)
    caption_pair = turned(caption_averaged_encodings, starts)

    outs = call(
        functools.partial(block_kernel, main, tail, planes),
        [((share, width), f32)]
        + [((share, width), bf16)] * (planes - 1)
        + [((rows, 2 * cols), f32)] * count,
        (tensor_rank * share).astype(jnp.int32).reshape(1),
        jnp.concatenate([sharpness_multiplier, offset_additive]),
        unit,
        tangent,
        half,
        tangent_half,
        factors,
        *texts,
    )
    text_partial, image_partial = outs[:planes], outs[planes:]

    got = [swapped(text_partial[k], "dp", 2 * k) for k in range(1, planes)]
    blocks = call(
        functools.partial(text_sum_kernel, main, tail),
        [((share, cols), bf16)] * count,
        text_partial[0],
        *got,
    )
    got = [blocks[0]] + [swapped(blocks[k], "tensor", k) for k in range(1, count)]
    (text_back,) = call(stack_kernel, [((rows, cols), bf16)], *got)
    text_back_other = swapped(text_back, "dp", 1)

    third = image_partial[2] + swapped(image_partial[3], "tensor", 1)
    second = swapped(image_partial[1], "tensor", 1)
    keep, sent = call(
        functools.partial(image_sum_kernel, main, tail),
        [((rows, cols), f32), ((rows, cols), bf16)],
        image_partial[0],
        second,
        swapped(third, "tensor", 2),
    )
    (image_back,) = call(add_half_kernel, [((rows, cols), bf16)], keep, swapped(sent, "dp", 1))
    image_back_other = swapped(image_back, "dp", 1)

    products = call(
        functools.partial(head_kernel, main, tail),
        [((size, 2 * cols), f32)] + [((size, 2 * cols), bf16)] * (planes - 1),
        *picture_pair,
        *caption_pair,
        image_back,
        image_back_other,
        text_back,
        text_back_other,
    )
    got = [swapped(products[k], "dp", 2 * k) for k in range(1, planes)]
    return tuple(
        call(
            functools.partial(final_kernel, main, tail),
            [((size, cols), f32)] * 2,
            products[0],
            *got,
        )
    )


def fits(mesh):
    data_count = mesh.shape["dp"]
    return mesh.shape["tensor"] == 4 and data_count % 2 == 0 and data_count & (data_count - 1) == 0


def solution(mesh):
    in_specs = (
        P("dp", None),
        P("dp", None),
        P(None, "tensor"),
        P(None, "tensor"),
        P(None, "tensor"),
        P(None, "tensor"),
        P(),
        P(),
    )
    out_specs = (P("dp", "tensor"), P("dp", "tensor"))
    local = packed if fits(mesh) else general
    return jax.shard_map(local, mesh=mesh, in_specs=in_specs, out_specs=out_specs, check_vma=False)
```

```python
import functools

import jax
import jax.numpy as jnp
from jax import lax
from jax.experimental import pallas as pl
from jax.experimental.pallas import tpu as pltpu
from jax.sharding import PartitionSpec as P

EPS = 1e-06


def swapped(value, axis, mask):
    count = lax.axis_size(axis)
    return lax.ppermute(value, axis, [(source, source ^ mask) for source in range(count)])


def matmul(left, right):
    return jnp.dot(left, right, preferred_element_type=jnp.float32)


def matmul_nt(left, right):
    return lax.dot_general(
        left, right, (((1,), (1,)), ((), ())), preferred_element_type=jnp.float32
    )


def matmul_tn(left, right):
    return lax.dot_general(
        left, right, (((0,), (0,)), ((), ())), preferred_element_type=jnp.float32
    )


def unit_parts(raw, raw_rate):
    values = raw.astype(jnp.float32)
    tangent = raw_rate.astype(jnp.float32)
    radius = jnp.sqrt(jnp.sum(values * values, axis=1, keepdims=True) + EPS)
    unit = values / radius
    rate = jnp.sum(unit * tangent, axis=1, keepdims=True)
    unit_tangent = (tangent - unit * rate) / radius
    return (unit, unit_tangent, radius, rate)


def unit_backward(unit, unit_tangent, radius, rate, grad, grad_rate):
    inner = jnp.sum(unit * grad, axis=1, keepdims=True)
    inner_rate = jnp.sum(unit_tangent * grad + unit * grad_rate, axis=1, keepdims=True)
    first = (grad - unit * inner) / radius
    return (grad_rate - unit_tangent * inner - unit * inner_rate - first * rate) / radius


def general(
    picture_averaged_encodings,
    caption_averaged_encodings,
    picture_mapping_matrix,
    caption_mapping_matrix,
    picture_weight_perturbation,
    caption_weight_perturbation,
    sharpness_multiplier,
    offset_additive,
):
    similarity_multiplier = sharpness_multiplier[0]
    logit_bias = offset_additive[0]
    tensor_rank = lax.axis_index("tensor")
    data_rank = lax.axis_index("dp")
    tensor_count = lax.axis_size("tensor")
    data_count = lax.axis_size("dp")
    planes = data_count // 2
    rows, width = picture_averaged_encodings.shape
    cols = picture_mapping_matrix.shape[1]
    share = rows // tensor_count
    out_rows = width // data_count
    half = jnp.bfloat16

    text = jnp.stack(
        [
            matmul(caption_averaged_encodings, caption_mapping_matrix).astype(half),
            matmul(caption_averaged_encodings, caption_weight_perturbation).astype(half),
        ]
    )
    image = jnp.stack(
        [
            matmul(picture_averaged_encodings, picture_mapping_matrix).astype(half),
            matmul(picture_averaged_encodings, picture_weight_perturbation).astype(half),
        ]
    )

    def share_of(value, axis, mask):
        start = (tensor_rank ^ mask) * share
        return lax.dynamic_slice_in_dim(value, start, share, axis)

    parts = [share_of(text, 1, 0)]
    for mask in range(1, tensor_count):
        parts.append(swapped(share_of(text, 1, mask), "tensor", mask))
    text = jnp.concatenate(parts, axis=2)
    slots = [text] + [swapped(text, "dp", 2 * mask) for mask in range(1, planes)]

    image = jnp.concatenate([image, swapped(image, "dp", 1)], axis=1)
    blocks = [image]
    mask = tensor_count // 2
    image_blocks = {0: image}
    while mask >= 1:
        held = sorted(image_blocks)
        sent = jnp.concatenate([image_blocks[k] for k in held], axis=2)
        got = swapped(sent, "tensor", mask)
        for place, k in enumerate(held):
            image_blocks[k ^ mask] = got[:, :, place * cols : (place + 1) * cols]
        mask //= 2
    image = jnp.concatenate([image_blocks[k] for k in range(tensor_count)], axis=2)
    text = jnp.concatenate(slots, axis=1)

    def out_columns(value, rank):
        taken = [
            lax.dynamic_slice_in_dim(value, (rank ^ (2 * mask)) * out_rows, out_rows, 1)
            for mask in range(planes)
        ]
        return jnp.concatenate(taken, axis=1)

    def plane_encodings(value):
        other = swapped(out_columns(value, data_rank ^ 1), "dp", 1)
        return jnp.concatenate([out_columns(value, data_rank), other], axis=0)

    picture_plane = plane_encodings(picture_averaged_encodings)
    ordered = jnp.concatenate(
        [share_of(caption_averaged_encodings, 0, mask) for mask in range(tensor_count)], axis=0
    )
    caption_plane = plane_encodings(ordered)

    image_unit, image_tangent, image_radius, image_rate = unit_parts(image[0], image[1])
    text_unit, text_tangent, text_radius, text_rate = unit_parts(text[0], text[1])
    image_half = image_unit.astype(half)
    image_tangent_half = image_tangent.astype(half)
    text_half = text_unit.astype(half)
    text_tangent_half = text_tangent.astype(half)

    logits = similarity_multiplier * matmul_nt(text_half, image_half) + logit_bias
    logit_rate = similarity_multiplier * (
        matmul_nt(text_half, image_tangent_half) + matmul_nt(text_tangent_half, image_half)
    )
    probability = jax.nn.sigmoid(logits)
    text_ids = lax.broadcasted_iota(jnp.int32, (logits.shape[0], 1), 0)
    image_ids = lax.broadcasted_iota(jnp.int32, (1, logits.shape[1]), 1)
    positive = ((text_ids < share) & (text_ids + tensor_rank * share == image_ids)).astype(
        jnp.float32
    )
    weight = (probability - positive).astype(half)
    weight_rate = (probability * (1.0 - probability) * logit_rate).astype(half)
    text_grad = similarity_multiplier * matmul(weight, image_half)
    text_grad_rate = similarity_multiplier * (
        matmul(weight_rate, image_half) + matmul(weight, image_tangent_half)
    )
    image_grad = similarity_multiplier * matmul_tn(weight, text_half)
    image_grad_rate = similarity_multiplier * (
        matmul_tn(weight_rate, text_half) + matmul_tn(weight, text_tangent_half)
    )

    text_back = unit_backward(
        text_unit, text_tangent, text_radius, text_rate, text_grad, text_grad_rate
    )
    image_back = unit_backward(
        image_unit, image_tangent, image_radius, image_rate, image_grad, image_grad_rate
    )

    total = text_back[:share]
    for mask in range(1, planes):
        sent = text_back[mask * share : (mask + 1) * share].astype(half)
        total = total + swapped(sent, "dp", 2 * mask).astype(jnp.float32)
    text_back = total.astype(half)
    parts = [text_back[:, :cols]]
    for mask in range(1, tensor_count):
        sent = text_back[:, mask * cols : (mask + 1) * cols]
        parts.append(swapped(sent, "tensor", mask))
    text_back = jnp.concatenate(parts, axis=0)
    text_back = jnp.concatenate([text_back, swapped(text_back, "dp", 1)], axis=0)

    image_blocks = {k: image_back[:, k * cols : (k + 1) * cols] for k in range(tensor_count)}
    mask = 1
    while mask < tensor_count:
        kept = [k for k in sorted(image_blocks) if not k & mask]
        sent = jnp.concatenate([image_blocks[k ^ mask] for k in kept], axis=1)
        got = swapped(sent, "tensor", mask).astype(jnp.float32)
        image_blocks = {
            k: image_blocks[k] + got[:, place * cols : (place + 1) * cols]
            for place, k in enumerate(kept)
        }
        mask *= 2
    image_back = image_blocks[0]
    got = swapped(image_back, "dp", 1)
    image_back = (
        image_back + jnp.concatenate([got[rows:], got[:rows]], axis=0)
    ).astype(half)

    def head(encodings, back):
        product = matmul_tn(encodings, back)
        total = product[:out_rows]
        for mask in range(1, planes):
            sent = product[mask * out_rows : (mask + 1) * out_rows].astype(half)
            total = total + swapped(sent, "dp", 2 * mask).astype(jnp.float32)
        return total

    return (head(picture_plane, image_back), head(caption_plane, text_back))


def call(kernel, outs, *args, after=()):
    count = len(args)

    def body(*refs):
        kernel(*refs[:count], *refs[count + len(after) :])

    def place(value):
        scalar = value.ndim == 1
        return pl.BlockSpec(memory_space=pltpu.SMEM if scalar else pltpu.VMEM)

    return pl.pallas_call(
        body,
        out_shape=[jax.ShapeDtypeStruct(shape, dtype) for shape, dtype in outs],
        in_specs=[place(value) for value in args]
        + [pl.BlockSpec(memory_space=pl.ANY) for _ in after],
        out_specs=[pl.BlockSpec(memory_space=pltpu.VMEM) for _ in outs],
        compiler_params=pltpu.CompilerParams(vmem_limit_bytes=48 * 1024 * 1024),
    )(*args, *after)


def tied(value, after):
    return pl.pallas_call(
        lambda value_ref, after_ref, out_ref: None,
        out_shape=jax.ShapeDtypeStruct(value.shape, value.dtype),
        in_specs=[pl.BlockSpec(memory_space=pl.ANY)] * 2,
        out_specs=pl.BlockSpec(memory_space=pl.ANY),
        input_output_aliases={0: 0},
    )(value, after)


def project_kernel(share, starts, encodings, weight, direction, *outs):
    main = weight.shape[0] // 128 * 128
    left = jnp.concatenate(
        [
            encodings[pl.ds(pl.multiple_of(starts[k], 16), share), :]
            for k in range(starts.shape[0])
        ],
        axis=0,
    )
    tails = jnp.concatenate([weight[main:, :], direction[main:, :]], axis=0)
    rows = outs[0].shape[0]
    for right, first in ((weight[:main, :], 0), (direction[:main, :], main), (tails, 2 * main)):
        product = matmul_nt(left, right).astype(jnp.bfloat16)
        for place, out in enumerate(outs):
            out[:, first : first + right.shape[0]] = product[place * rows : (place + 1) * rows]


def gathered(blocks, main, tail, which):
    first = 2 * main + which * tail
    mains = [block[:, which * main : (which + 1) * main] for block in blocks]
    tails = [block[:, first : first + tail] for block in blocks]
    return jnp.concatenate(mains + tails, axis=1)


def text_rows_kernel(main, tail, *refs):
    blocks, out = [ref[...].astype(jnp.float32) for ref in refs[:-1]], refs[-1]
    width = out.shape[1] // 2
    out[:, :width] = gathered(blocks, main, tail, 0).astype(jnp.bfloat16)
    out[:, width:] = gathered(blocks, main, tail, 1).astype(jnp.bfloat16)


def row_factors(values, tangent):
    squares = jnp.sum(values * values, axis=1, keepdims=True)
    cross = jnp.sum(values * tangent, axis=1, keepdims=True)
    inverse = 1.0 / jnp.sqrt(squares + EPS)
    return inverse, cross * inverse


def unit_rows(values, tangent, inverse, rate):
    unit = values * inverse
    return unit, (tangent - unit * rate) * inverse


def back_rows(unit, tangent, inverse, rate, grad, grad_rate):
    inner = jnp.sum(unit * grad, axis=1, keepdims=True)
    inner_rate = jnp.sum(tangent * grad + unit * grad_rate, axis=1, keepdims=True)
    scaled = rate * inverse
    return (
        grad_rate - tangent * inner - grad * scaled + unit * (inner * scaled - inner_rate)
    ) * inverse


STEP = 48


def image_rows_kernel(main, tail, *refs):
    blocks, (unit, tangent, half, tangent_half, factors) = refs[:-5], refs[-5:]
    count = len(blocks) // 2
    rows = blocks[0].shape[0]
    for shard in range(2):
        held = blocks[shard * count : (shard + 1) * count]

        @pl.loop(0, rows // STEP)
        def _(step):
            here = pl.ds(pl.multiple_of(step * STEP, STEP), STEP)
            there = pl.ds(pl.multiple_of(shard * rows + step * STEP, STEP), STEP)
            parts = [block[here, :].astype(jnp.float32) for block in held]
            values = gathered(parts, main, tail, 0)
            rates = gathered(parts, main, tail, 1)
            inverse, rate = row_factors(values, rates)
            one, two = unit_rows(values, rates, inverse, rate)
            unit[there, :] = one
            tangent[there, :] = two
            half[there, :] = one.astype(jnp.bfloat16)
            tangent_half[there, :] = two.astype(jnp.bfloat16)
            factors[0, there, :] = jnp.broadcast_to(inverse, (STEP, 128))
            factors[1, there, :] = jnp.broadcast_to(rate, (STEP, 128))


def text_block_kernel(slots, start, scalars, half, tangent_half, *refs):
    texts, refs = refs[:slots], refs[slots:]
    own, sent = refs[0], refs[1:slots]
    text_half, text_tangent_half, weight_turned, weight_rate_turned = refs[slots:]
    f32, bf16 = jnp.float32, jnp.bfloat16
    share, width = texts[0].shape[0], texts[0].shape[1] // 2
    multiplier, bias = scalars[0], scalars[1]

    text_parts = []
    for slot, text in enumerate(texts):
        here = slice(slot * share, (slot + 1) * share)
        values, rates = text[:, :width].astype(f32), text[:, width:].astype(f32)
        inverse, rate = row_factors(values, rates)
        unit, tangent = unit_rows(values, rates, inverse, rate)
        text_parts.append((unit, tangent, inverse, rate))
        text_half[here, :] = unit.astype(bf16)
        text_tangent_half[here, :] = tangent.astype(bf16)

    logits = multiplier * matmul_nt(text_half[...], half[...]) + bias
    logit_rate = multiplier * (
        matmul_nt(text_half[...], tangent_half[...])
        + matmul_nt(text_tangent_half[...], half[...])
    )
    probability = jax.nn.sigmoid(logits)
    text_ids = lax.broadcasted_iota(jnp.int32, logits.shape, 0)
    image_ids = lax.broadcasted_iota(jnp.int32, logits.shape, 1)
    positive = jnp.where((text_ids < share) & (text_ids + start[0] == image_ids), 1.0, 0.0)
    weight = probability - positive
    weight_rate = probability * (1.0 - probability) * logit_rate
    weight_half, weight_rate_half = weight.astype(bf16), weight_rate.astype(bf16)

    text_grad = multiplier * matmul(weight_half, half[...])
    text_grad_rate = multiplier * (
        matmul(weight_rate_half, half[...]) + matmul(weight_half, tangent_half[...])
    )
    for slot, (unit, tangent, inverse, rate) in enumerate(text_parts):
        here = slice(slot * share, (slot + 1) * share)
        back = back_rows(unit, tangent, inverse, rate, text_grad[here], text_grad_rate[here])
        if slot == 0:
            own[...] = back
        else:
            sent[slot - 1][...] = back.astype(bf16)
    weight_turned[...] = weight.T.astype(bf16)
    weight_rate_turned[...] = weight_rate.T.astype(bf16)


def image_block_kernel(
    main,
    tail,
    scalars,
    unit,
    tangent,
    factors,
    text_half,
    text_tangent_half,
    weight,
    weight_rate,
    *packed,
):
    rows = unit.shape[0] // 2
    count = len(packed)
    multiplier = scalars[0]
    for shard in range(2):
        here = slice(shard * rows, (shard + 1) * rows)
        grad = multiplier * matmul(weight[here, :], text_half[...])
        grad_rate = multiplier * (
            matmul(weight_rate[here, :], text_half[...])
            + matmul(weight[here, :], text_tangent_half[...])
        )
        back = back_rows(
            unit[here, :],
            tangent[here, :],
            factors[0, here, :1],
            factors[1, here, :1],
            grad,
            grad_rate,
        )
        for k, out in enumerate(packed):
            out[:, shard * main : (shard + 1) * main] = back[:, k * main : (k + 1) * main]
            first = 2 * main + shard * tail
            taken = count * main + k * tail
            out[:, first : first + tail] = back[:, taken : taken + tail]


def text_sum_kernel(main, tail, own, *refs):
    count = own.shape[1] // (main + tail)
    got, outs = refs[:-count], refs[-count:]
    total = own[...]
    for ref in got:
        total = total + ref[...].astype(jnp.float32)
    for k, out in enumerate(outs):
        first = count * main + k * tail
        out[:, :main] = total[:, k * main : (k + 1) * main].astype(jnp.bfloat16)
        out[:, main:] = total[:, first : first + tail].astype(jnp.bfloat16)


def stack_kernel(*refs):
    rows = refs[0].shape[0]
    for k, ref in enumerate(refs[:-1]):
        refs[-1][k * rows : (k + 1) * rows, :] = ref[...]


def turn_kernel(share, starts, places, encodings, mine, other):
    ordered = jnp.concatenate(
        [
            encodings[pl.ds(pl.multiple_of(starts[k], 16), share), :].astype(jnp.float32)
            for k in range(starts.shape[0])
        ],
        axis=0,
    )
    turned = ordered.T.astype(jnp.bfloat16)
    size = turned.shape[0] // places.shape[0]
    blocks = places.shape[0] // 2
    for block in range(places.shape[0]):
        taken = turned[block * size : (block + 1) * size, :]
        slot = places[block]

        @pl.when(slot < blocks)
        def _():
            mine[pl.ds(pl.multiple_of(slot * size, 16), size), :] = taken

        @pl.when(slot >= blocks)
        def _():
            other[pl.ds(pl.multiple_of((slot - blocks) * size, 16), size), :] = taken


def image_pair_kernel(main, tail, near, mine, got, out):
    total = mine[...] + got[...]
    rows = mine.shape[0]
    size = out.shape[0] - rows
    rounded = total.astype(jnp.bfloat16)
    out[:rows, :] = rounded
    start = pl.multiple_of(near[0], 16)
    for fold in range(2):
        here = pl.ds(start + fold * size, size)
        left = mine[here, :] + got[here, :] - out[here, :].astype(jnp.float32)
        out[rows:, fold * main : (fold + 1) * main] = left[:, :main].astype(jnp.bfloat16)
        first = 2 * main + fold * tail
        out[rows:, first : first + tail] = left[:, 2 * main : 2 * main + tail].astype(
            jnp.bfloat16
        )


def image_sum_kernel(main, tail, far, first, second, third, keep, sent):
    rows = first.shape[0]
    size = third.shape[0] - rows
    total = first[...] + second[...] + third[:rows, :].astype(jnp.float32)
    keep[:, :main] = total[:, :main]
    keep[:, main:] = total[:, 2 * main : 2 * main + tail]
    sent[:, :main] = total[:, main : 2 * main].astype(jnp.bfloat16)
    sent[:, main:] = total[:, 2 * main + tail :].astype(jnp.bfloat16)
    left = third[rows:, :].astype(jnp.float32)
    start = pl.multiple_of(far[0], 16)
    for fold in range(2):
        here = pl.ds(start + fold * size, size)
        keep[here, :main] += left[:, fold * main : (fold + 1) * main]
        at = 2 * main + fold * tail
        keep[here, main:] += left[:, at : at + tail]


def add_half_kernel(one, two, out):
    out[...] = (one[...] + two[...].astype(jnp.float32)).astype(jnp.bfloat16)


def head_kernel(main, tail, picture, picture_other, caption, caption_other, *refs):
    image, image_other, text, text_other = refs[:4]
    own, sent = refs[4], refs[5:]
    size = own.shape[0]
    products = (
        matmul(picture[...], image[...]) + matmul(picture_other[...], image_other[...]),
        matmul(caption[...], text[...]) + matmul(caption_other[...], text_other[...]),
    )
    for slot, out in enumerate((own,) + tuple(sent)):
        here = slice(slot * size, (slot + 1) * size)
        for head, product in enumerate(products):
            out[:, head * main : (head + 1) * main] = product[here, :main].astype(out.dtype)
            first = 2 * main + head * tail
            out[:, first : first + tail] = product[here, main:].astype(out.dtype)


def final_kernel(main, tail, own, *refs):
    got, outs = refs[:-2], refs[-2:]
    total = own[...]
    for ref in got:
        total = total + ref[...].astype(jnp.float32)
    for head, out in enumerate(outs):
        out[:, :main] = total[:, head * main : (head + 1) * main]
        first = 2 * main + head * tail
        out[:, main:] = total[:, first : first + tail]


def packed(
    picture_averaged_encodings,
    caption_averaged_encodings,
    picture_mapping_matrix,
    caption_mapping_matrix,
    picture_weight_perturbation,
    caption_weight_perturbation,
    sharpness_multiplier,
    offset_additive,
):
    tensor_rank = lax.axis_index("tensor")
    data_rank = lax.axis_index("dp")
    count = lax.axis_size("tensor")
    data_count = lax.axis_size("dp")
    planes = data_count // 2
    rows, width = picture_averaged_encodings.shape
    cols = picture_mapping_matrix.shape[1]
    main = cols // 128 * 128
    tail = cols - main
    share = rows // count
    size = width // data_count
    f32, bf16 = jnp.float32, jnp.bfloat16
    ranks = jnp.arange(count, dtype=jnp.int32)
    starts = (ranks ^ tensor_rank) * share
    plain = ranks * share

    blocks = call(
        functools.partial(project_kernel, share),
        [((share, 2 * cols), bf16)] * count,
        starts,
        caption_averaged_encodings,
        caption_mapping_matrix.T,
        caption_weight_perturbation.T,
    )
    got = [blocks[0]] + [swapped(blocks[k], "tensor", k) for k in range(1, count)]
    (text,) = call(
        functools.partial(text_rows_kernel, main, tail), [((share, 2 * width), bf16)], *got
    )
    texts = [text] + [swapped(text, "dp", 2 * k) for k in range(1, planes)]

    (image,) = call(
        functools.partial(project_kernel, share),
        [((rows, 2 * cols), bf16)],
        plain,
        picture_averaged_encodings,
        picture_mapping_matrix.T,
        picture_weight_perturbation.T,
        after=(blocks[0],),
    )
    image_other = swapped(image, "dp", 1)
    shards = [[tied(image, text)], [tied(image_other, text)]]
    mask = count // 2
    order = [0]
    while mask >= 1:
        shards = [held + [swapped(one, "tensor", mask) for one in held] for held in shards]
        order = order + [k ^ mask for k in order]
        mask //= 2
    places = [order.index(k) for k in range(count)]
    image_blocks = [held[place] for held in shards for place in places]
    unit, tangent, half, tangent_half, factors = call(
        functools.partial(image_rows_kernel, main, tail),
        [
            ((2 * rows, width), f32),
            ((2 * rows, width), f32),
            ((2 * rows, width), bf16),
            ((2 * rows, width), bf16),
            ((2, 2 * rows, 128), f32),
        ],
        *image_blocks,
    )

    block_ids = jnp.arange(data_count, dtype=jnp.int32)
    slots = ((block_ids ^ data_rank) >> 1) + planes * ((block_ids ^ data_rank) & 1)

    def turned(encodings, order):
        mine, other = call(
            functools.partial(turn_kernel, share),
            [((planes * size, rows), bf16)] * 2,
            order,
            slots,
            encodings,
            after=(shards[1][0],),
        )
        return mine, swapped(other, "dp", 1)

    picture_pair = turned(picture_averaged_encodings, plain)
    caption_pair = turned(caption_averaged_encodings, starts)

    scalars = jnp.concatenate([sharpness_multiplier, offset_additive])
    outs = call(
        functools.partial(text_block_kernel, planes),
        [((share, width), f32)]
        + [((share, width), bf16)] * (planes - 1)
        + [((planes * share, width), bf16)] * 2
        + [((2 * rows, planes * share), bf16)] * 2,
        (tensor_rank * share).astype(jnp.int32).reshape(1),
        scalars,
        half,
        tangent_half,
        *texts,
        after=(picture_pair[1], caption_pair[1]),
    )
    text_partial = outs[:planes]
    image_partial = call(
        functools.partial(image_block_kernel, main, tail),
        [((rows, 2 * cols), f32)] * count,
        scalars,
        unit,
        tangent,
        factors,
        *outs[planes:],
    )

    got = [swapped(text_partial[k], "dp", 2 * k) for k in range(1, planes)]
    blocks = call(
        functools.partial(text_sum_kernel, main, tail),
        [((share, cols), bf16)] * count,
        text_partial[0],
        *got,
    )
    got = [blocks[0]] + [swapped(blocks[k], "tensor", k) for k in range(1, count)]
    (text_back,) = call(stack_kernel, [((rows, cols), bf16)], *got)
    text_back_other = swapped(text_back, "dp", 1)

    near = (tensor_rank // 2 * (2 * share)).astype(jnp.int32).reshape(1)
    far = ((tensor_rank // 2 ^ 1) * (2 * share)).astype(jnp.int32).reshape(1)
    (third,) = call(
        functools.partial(image_pair_kernel, main, tail),
        [((rows + share, 2 * cols), bf16)],
        near,
        image_partial[2],
        swapped(image_partial[3], "tensor", 1),
    )
    second = swapped(image_partial[1], "tensor", 1)
    keep, sent = call(
        functools.partial(image_sum_kernel, main, tail),
        [((rows, cols), f32), ((rows, cols), bf16)],
        far,
        image_partial[0],
        second,
        swapped(third, "tensor", 2),
    )
    (image_back,) = call(add_half_kernel, [((rows, cols), bf16)], keep, swapped(sent, "dp", 1))
    image_back_other = swapped(image_back, "dp", 1)

    products = call(
        functools.partial(head_kernel, main, tail),
        [((size, 2 * cols), f32)] + [((size, 2 * cols), bf16)] * (planes - 1),
        *picture_pair,
        *caption_pair,
        image_back,
        image_back_other,
        text_back,
        text_back_other,
    )
    got = [swapped(products[k], "dp", 2 * k) for k in range(1, planes)]
    return tuple(
        call(
            functools.partial(final_kernel, main, tail),
            [((size, cols), f32)] * 2,
            products[0],
            *got,
        )
    )


def fits(mesh):
    data_count = mesh.shape["dp"]
    return mesh.shape["tensor"] == 4 and data_count % 2 == 0 and data_count & (data_count - 1) == 0


def solution(mesh):
    in_specs = (
        P("dp", None),
        P("dp", None),
        P(None, "tensor"),
        P(None, "tensor"),
        P(None, "tensor"),
        P(None, "tensor"),
        P(),
        P(),
    )
    out_specs = (P("dp", "tensor"), P("dp", "tensor"))
    local = packed if fits(mesh) else general
    return jax.shard_map(local, mesh=mesh, in_specs=in_specs, out_specs=out_specs, check_vma=False)
```

```python
import functools

import jax
import jax.numpy as jnp
from jax import lax
from jax.experimental import pallas as pl
from jax.experimental.pallas import tpu as pltpu
from jax.sharding import PartitionSpec as P

EPS = 1e-06


def swapped(value, axis, mask):
    count = lax.axis_size(axis)
    return lax.ppermute(value, axis, [(source, source ^ mask) for source in range(count)])


def matmul(left, right):
    return jnp.dot(left, right, preferred_element_type=jnp.float32)


def matmul_nt(left, right):
    return lax.dot_general(
        left, right, (((1,), (1,)), ((), ())), preferred_element_type=jnp.float32
    )


def matmul_tn(left, right):
    return lax.dot_general(
        left, right, (((0,), (0,)), ((), ())), preferred_element_type=jnp.float32
    )


def unit_parts(raw, raw_rate):
    values = raw.astype(jnp.float32)
    tangent = raw_rate.astype(jnp.float32)
    radius = jnp.sqrt(jnp.sum(values * values, axis=1, keepdims=True) + EPS)
    unit = values / radius
    rate = jnp.sum(unit * tangent, axis=1, keepdims=True)
    unit_tangent = (tangent - unit * rate) / radius
    return (unit, unit_tangent, radius, rate)


def unit_backward(unit, unit_tangent, radius, rate, grad, grad_rate):
    inner = jnp.sum(unit * grad, axis=1, keepdims=True)
    inner_rate = jnp.sum(unit_tangent * grad + unit * grad_rate, axis=1, keepdims=True)
    first = (grad - unit * inner) / radius
    return (grad_rate - unit_tangent * inner - unit * inner_rate - first * rate) / radius


def general(
    picture_averaged_encodings,
    caption_averaged_encodings,
    picture_mapping_matrix,
    caption_mapping_matrix,
    picture_weight_perturbation,
    caption_weight_perturbation,
    sharpness_multiplier,
    offset_additive,
):
    similarity_multiplier = sharpness_multiplier[0]
    logit_bias = offset_additive[0]
    tensor_rank = lax.axis_index("tensor")
    data_rank = lax.axis_index("dp")
    tensor_count = lax.axis_size("tensor")
    data_count = lax.axis_size("dp")
    planes = data_count // 2
    rows, width = picture_averaged_encodings.shape
    cols = picture_mapping_matrix.shape[1]
    share = rows // tensor_count
    out_rows = width // data_count
    half = jnp.bfloat16

    text = jnp.stack(
        [
            matmul(caption_averaged_encodings, caption_mapping_matrix).astype(half),
            matmul(caption_averaged_encodings, caption_weight_perturbation).astype(half),
        ]
    )
    image = jnp.stack(
        [
            matmul(picture_averaged_encodings, picture_mapping_matrix).astype(half),
            matmul(picture_averaged_encodings, picture_weight_perturbation).astype(half),
        ]
    )

    def share_of(value, axis, mask):
        start = (tensor_rank ^ mask) * share
        return lax.dynamic_slice_in_dim(value, start, share, axis)

    parts = [share_of(text, 1, 0)]
    for mask in range(1, tensor_count):
        parts.append(swapped(share_of(text, 1, mask), "tensor", mask))
    text = jnp.concatenate(parts, axis=2)
    slots = [text] + [swapped(text, "dp", 2 * mask) for mask in range(1, planes)]

    image = jnp.concatenate([image, swapped(image, "dp", 1)], axis=1)
    blocks = [image]
    mask = tensor_count // 2
    image_blocks = {0: image}
    while mask >= 1:
        held = sorted(image_blocks)
        sent = jnp.concatenate([image_blocks[k] for k in held], axis=2)
        got = swapped(sent, "tensor", mask)
        for place, k in enumerate(held):
            image_blocks[k ^ mask] = got[:, :, place * cols : (place + 1) * cols]
        mask //= 2
    image = jnp.concatenate([image_blocks[k] for k in range(tensor_count)], axis=2)
    text = jnp.concatenate(slots, axis=1)

    def out_columns(value, rank):
        taken = [
            lax.dynamic_slice_in_dim(value, (rank ^ (2 * mask)) * out_rows, out_rows, 1)
            for mask in range(planes)
        ]
        return jnp.concatenate(taken, axis=1)

    def plane_encodings(value):
        other = swapped(out_columns(value, data_rank ^ 1), "dp", 1)
        return jnp.concatenate([out_columns(value, data_rank), other], axis=0)

    picture_plane = plane_encodings(picture_averaged_encodings)
    ordered = jnp.concatenate(
        [share_of(caption_averaged_encodings, 0, mask) for mask in range(tensor_count)], axis=0
    )
    caption_plane = plane_encodings(ordered)

    image_unit, image_tangent, image_radius, image_rate = unit_parts(image[0], image[1])
    text_unit, text_tangent, text_radius, text_rate = unit_parts(text[0], text[1])
    image_half = image_unit.astype(half)
    image_tangent_half = image_tangent.astype(half)
    text_half = text_unit.astype(half)
    text_tangent_half = text_tangent.astype(half)

    logits = similarity_multiplier * matmul_nt(text_half, image_half) + logit_bias
    logit_rate = similarity_multiplier * (
        matmul_nt(text_half, image_tangent_half) + matmul_nt(text_tangent_half, image_half)
    )
    probability = jax.nn.sigmoid(logits)
    text_ids = lax.broadcasted_iota(jnp.int32, (logits.shape[0], 1), 0)
    image_ids = lax.broadcasted_iota(jnp.int32, (1, logits.shape[1]), 1)
    positive = ((text_ids < share) & (text_ids + tensor_rank * share == image_ids)).astype(
        jnp.float32
    )
    weight = (probability - positive).astype(half)
    weight_rate = (probability * (1.0 - probability) * logit_rate).astype(half)
    text_grad = similarity_multiplier * matmul(weight, image_half)
    text_grad_rate = similarity_multiplier * (
        matmul(weight_rate, image_half) + matmul(weight, image_tangent_half)
    )
    image_grad = similarity_multiplier * matmul_tn(weight, text_half)
    image_grad_rate = similarity_multiplier * (
        matmul_tn(weight_rate, text_half) + matmul_tn(weight, text_tangent_half)
    )

    text_back = unit_backward(
        text_unit, text_tangent, text_radius, text_rate, text_grad, text_grad_rate
    )
    image_back = unit_backward(
        image_unit, image_tangent, image_radius, image_rate, image_grad, image_grad_rate
    )

    total = text_back[:share]
    for mask in range(1, planes):
        sent = text_back[mask * share : (mask + 1) * share].astype(half)
        total = total + swapped(sent, "dp", 2 * mask).astype(jnp.float32)
    text_back = total.astype(half)
    parts = [text_back[:, :cols]]
    for mask in range(1, tensor_count):
        sent = text_back[:, mask * cols : (mask + 1) * cols]
        parts.append(swapped(sent, "tensor", mask))
    text_back = jnp.concatenate(parts, axis=0)
    text_back = jnp.concatenate([text_back, swapped(text_back, "dp", 1)], axis=0)

    image_blocks = {k: image_back[:, k * cols : (k + 1) * cols] for k in range(tensor_count)}
    mask = 1
    while mask < tensor_count:
        kept = [k for k in sorted(image_blocks) if not k & mask]
        sent = jnp.concatenate([image_blocks[k ^ mask] for k in kept], axis=1)
        got = swapped(sent, "tensor", mask).astype(jnp.float32)
        image_blocks = {
            k: image_blocks[k] + got[:, place * cols : (place + 1) * cols]
            for place, k in enumerate(kept)
        }
        mask *= 2
    image_back = image_blocks[0]
    got = swapped(image_back, "dp", 1)
    image_back = (
        image_back + jnp.concatenate([got[rows:], got[:rows]], axis=0)
    ).astype(half)

    def head(encodings, back):
        product = matmul_tn(encodings, back)
        total = product[:out_rows]
        for mask in range(1, planes):
            sent = product[mask * out_rows : (mask + 1) * out_rows].astype(half)
            total = total + swapped(sent, "dp", 2 * mask).astype(jnp.float32)
        return total

    return (head(picture_plane, image_back), head(caption_plane, text_back))


def call(kernel, outs, *args, after=()):
    count = len(args)

    def body(*refs):
        kernel(*refs[:count], *refs[count + len(after) :])

    def place(value):
        scalar = value.ndim == 1
        return pl.BlockSpec(memory_space=pltpu.SMEM if scalar else pltpu.VMEM)

    return pl.pallas_call(
        body,
        out_shape=[jax.ShapeDtypeStruct(shape, dtype) for shape, dtype in outs],
        in_specs=[place(value) for value in args]
        + [pl.BlockSpec(memory_space=pl.ANY) for _ in after],
        out_specs=[pl.BlockSpec(memory_space=pltpu.VMEM) for _ in outs],
        compiler_params=pltpu.CompilerParams(vmem_limit_bytes=48 * 1024 * 1024),
    )(*args, *after)


def project_kernel(share, starts, encodings, weight, direction, *outs):
    main = weight.shape[0] // 128 * 128
    left = jnp.concatenate(
        [
            encodings[pl.ds(pl.multiple_of(starts[k], 16), share), :]
            for k in range(starts.shape[0])
        ],
        axis=0,
    )
    tails = jnp.concatenate([weight[main:, :], direction[main:, :]], axis=0)
    rows = outs[0].shape[0]
    for right, first in ((weight[:main, :], 0), (direction[:main, :], main), (tails, 2 * main)):
        product = matmul_nt(left, right).astype(jnp.bfloat16)
        for place, out in enumerate(outs):
            out[:, first : first + right.shape[0]] = product[place * rows : (place + 1) * rows]


def gathered(blocks, main, tail, which):
    first = 2 * main + which * tail
    mains = [block[:, which * main : (which + 1) * main] for block in blocks]
    tails = [block[:, first : first + tail] for block in blocks]
    return jnp.concatenate(mains + tails, axis=1)


def text_rows_kernel(main, tail, *refs):
    blocks, out = [ref[...].astype(jnp.float32) for ref in refs[:-1]], refs[-1]
    width = out.shape[1] // 2
    out[:, :width] = gathered(blocks, main, tail, 0).astype(jnp.bfloat16)
    out[:, width:] = gathered(blocks, main, tail, 1).astype(jnp.bfloat16)


def row_factors(values, tangent):
    squares = jnp.sum(values * values, axis=1, keepdims=True)
    cross = jnp.sum(values * tangent, axis=1, keepdims=True)
    inverse = 1.0 / jnp.sqrt(squares + EPS)
    return inverse, cross * inverse


def unit_rows(values, tangent, inverse, rate):
    unit = values * inverse
    return unit, (tangent - unit * rate) * inverse


def back_rows(unit, tangent, inverse, rate, grad, grad_rate):
    inner = jnp.sum(unit * grad, axis=1, keepdims=True)
    inner_rate = jnp.sum(tangent * grad + unit * grad_rate, axis=1, keepdims=True)
    scaled = rate * inverse
    return (
        grad_rate - tangent * inner - grad * scaled + unit * (inner * scaled - inner_rate)
    ) * inverse


STEP = 48


def image_rows_kernel(main, tail, count, near, far, unit, tangent, half, tangent_half, factors):
    rows = unit.shape[0] // 2
    for shard in range(2):
        held = [
            (near, far)[k % 2].at[pl.ds((k - k % 2 + shard) * rows, rows), :] for k in range(count)
        ]

        @pl.loop(0, rows // STEP)
        def _(step):
            here = pl.ds(pl.multiple_of(step * STEP, STEP), STEP)
            there = pl.ds(pl.multiple_of(shard * rows + step * STEP, STEP), STEP)
            parts = [block[here, :].astype(jnp.float32) for block in held]
            values = gathered(parts, main, tail, 0)
            rates = gathered(parts, main, tail, 1)
            inverse, rate = row_factors(values, rates)
            one, two = unit_rows(values, rates, inverse, rate)
            unit[there, :] = one
            tangent[there, :] = two
            half[there, :] = one.astype(jnp.bfloat16)
            tangent_half[there, :] = two.astype(jnp.bfloat16)
            factors[0, there, :] = jnp.broadcast_to(inverse, (STEP, 128))
            factors[1, there, :] = jnp.broadcast_to(rate, (STEP, 128))


def text_block_kernel(slots, start, scalars, half, tangent_half, *refs):
    texts, refs = refs[:slots], refs[slots:]
    own, middle, sent, text_half, text_tangent_half, weight_turned, weight_rate_turned = refs
    f32, bf16 = jnp.float32, jnp.bfloat16
    share, width = texts[0].shape[0], texts[0].shape[1] // 2
    multiplier, bias = scalars[0], scalars[1]

    text_parts = []
    for slot, text in enumerate(texts):
        here = slice(slot * share, (slot + 1) * share)
        values, rates = text[:, :width].astype(f32), text[:, width:].astype(f32)
        inverse, rate = row_factors(values, rates)
        unit, tangent = unit_rows(values, rates, inverse, rate)
        text_parts.append((unit, tangent, inverse, rate))
        text_half[here, :] = unit.astype(bf16)
        text_tangent_half[here, :] = tangent.astype(bf16)

    logits = multiplier * matmul_nt(text_half[...], half[...]) + bias
    logit_rate = multiplier * (
        matmul_nt(text_half[...], tangent_half[...])
        + matmul_nt(text_tangent_half[...], half[...])
    )
    probability = jax.nn.sigmoid(logits)
    text_ids = lax.broadcasted_iota(jnp.int32, logits.shape, 0)
    image_ids = lax.broadcasted_iota(jnp.int32, logits.shape, 1)
    positive = jnp.where((text_ids < share) & (text_ids + start[0] == image_ids), 1.0, 0.0)
    weight = probability - positive
    weight_rate = probability * (1.0 - probability) * logit_rate
    weight_half, weight_rate_half = weight.astype(bf16), weight_rate.astype(bf16)

    text_grad = multiplier * matmul(weight_half, half[...])
    text_grad_rate = multiplier * (
        matmul(weight_rate_half, half[...]) + matmul(weight_half, tangent_half[...])
    )
    for slot, (unit, tangent, inverse, rate) in enumerate(text_parts):
        here = slice(slot * share, (slot + 1) * share)
        back = back_rows(unit, tangent, inverse, rate, text_grad[here], text_grad_rate[here])
        if slot == 0:
            own[...] = back
        elif slot == 2:
            middle[...] = back
        else:
            place = slot // 2 * share
            sent[place : place + share, :] = back.astype(bf16)
    weight_turned[...] = weight.T.astype(bf16)
    weight_rate_turned[...] = weight_rate.T.astype(bf16)


def image_block_kernel(
    main,
    tail,
    scalars,
    unit,
    tangent,
    factors,
    text_half,
    text_tangent_half,
    weight,
    weight_rate,
    *packed,
):
    rows = unit.shape[0] // 2
    count = len(packed)
    multiplier = scalars[0]
    for shard in range(2):
        here = slice(shard * rows, (shard + 1) * rows)
        grad = multiplier * matmul(weight[here, :], text_half[...])
        grad_rate = multiplier * (
            matmul(weight_rate[here, :], text_half[...])
            + matmul(weight[here, :], text_tangent_half[...])
        )
        back = back_rows(
            unit[here, :],
            tangent[here, :],
            factors[0, here, :1],
            factors[1, here, :1],
            grad,
            grad_rate,
        )
        for k, out in enumerate(packed):
            out[:, shard * main : (shard + 1) * main] = back[:, k * main : (k + 1) * main]
            first = 2 * main + shard * tail
            taken = count * main + k * tail
            out[:, first : first + tail] = back[:, taken : taken + tail]


def text_sum_kernel(main, tail, own, *refs):
    count = own.shape[1] // (main + tail)
    got, outs = refs[:-count], refs[-count:]
    total = own[...]
    for ref in got:
        total = total + ref[...].astype(jnp.float32)
    for k, out in enumerate(outs):
        first = count * main + k * tail
        out[:, :main] = total[:, k * main : (k + 1) * main].astype(jnp.bfloat16)
        out[:, main:] = total[:, first : first + tail].astype(jnp.bfloat16)


def stack_kernel(*refs):
    rows = refs[0].shape[0]
    for k, ref in enumerate(refs[:-1]):
        refs[-1][k * rows : (k + 1) * rows, :] = ref[...]


def turn_kernel(share, plain, starts, places, picture, caption, *outs):
    for which, (encodings, order) in enumerate(((picture, plain), (caption, starts))):
        ordered = jnp.concatenate(
            [
                encodings[pl.ds(pl.multiple_of(order[k], 16), share), :].astype(jnp.float32)
                for k in range(order.shape[0])
            ],
            axis=0,
        )
        turned = ordered.T.astype(jnp.bfloat16)
        count = places.shape[0]
        size, rows = turned.shape[0] // count, turned.shape[1]
        fold = count // 4
        for block in range(count):
            taken = turned[block * size : (block + 1) * size, :]
            slot = places[block]
            at = pl.multiple_of(which * fold * size + slot % fold * size, 16)
            for side in range(2):
                for half in range(2):

                    @pl.when(slot // fold == 2 * side + half)
                    def _():
                        outs[side][pl.ds(at, size), half * rows : (half + 1) * rows] = taken


def image_pair_kernel(main, tail, near, mine, got, out):
    total = mine[...] + got[...]
    rows = mine.shape[0]
    size = out.shape[0] - rows
    rounded = total.astype(jnp.bfloat16)
    out[:rows, :] = rounded
    start = pl.multiple_of(near[0], 16)
    for fold in range(2):
        here = pl.ds(start + fold * size, size)
        left = mine[here, :] + got[here, :] - out[here, :].astype(jnp.float32)
        out[rows:, fold * main : (fold + 1) * main] = left[:, :main].astype(jnp.bfloat16)
        first = 2 * main + fold * tail
        out[rows:, first : first + tail] = left[:, 2 * main : 2 * main + tail].astype(
            jnp.bfloat16
        )


def image_sum_kernel(main, tail, far, first, second, third, keep, sent):
    rows = first.shape[0]
    size = third.shape[0] - rows
    total = first[...] + second[...] + third[:rows, :].astype(jnp.float32)
    keep[:, :main] = total[:, :main]
    keep[:, main:] = total[:, 2 * main : 2 * main + tail]
    sent[:, :main] = total[:, main : 2 * main].astype(jnp.bfloat16)
    sent[:, main:] = total[:, 2 * main + tail :].astype(jnp.bfloat16)
    left = third[rows:, :].astype(jnp.float32)
    start = pl.multiple_of(far[0], 16)
    for fold in range(2):
        here = pl.ds(start + fold * size, size)
        keep[here, :main] += left[:, fold * main : (fold + 1) * main]
        at = 2 * main + fold * tail
        keep[here, main:] += left[:, at : at + tail]


def forward_kernel(own, middle, got, total, sent):
    share = own.shape[0]
    total[...] = own[...] + got[:share, :].astype(jnp.float32)
    sent[...] = (middle[...] + got[share:, :].astype(jnp.float32)).astype(jnp.bfloat16)


def add_half_kernel(one, two, out):
    out[...] = (one[...] + two[...].astype(jnp.float32)).astype(jnp.bfloat16)


def head_kernel(main, tail, mine, other, *refs):
    backs, own, sent = refs[:4], refs[4], refs[5:]
    size = own.shape[0]
    rows = backs[0].shape[0]
    outs = (own,) + tuple(sent)
    fold = len(outs) // 2
    for head in range(2):
        near, far = backs[2 * head], backs[2 * head + 1]
        for half in range(2):
            here = slice(head * fold * size, (head + 1) * fold * size)
            lanes = slice(half * rows, (half + 1) * rows)
            product = matmul(mine[here, lanes], near[...]) + matmul(other[here, lanes], far[...])
            for place in range(fold):
                out = outs[half * fold + place]
                part = product[place * size : (place + 1) * size]
                out[:, head * main : (head + 1) * main] = part[:, :main].astype(out.dtype)
                first = 2 * main + head * tail
                out[:, first : first + tail] = part[:, main:].astype(out.dtype)


def final_kernel(main, tail, own, *refs):
    got, outs = refs[:-2], refs[-2:]
    total = own[...]
    for ref in got:
        total = total + ref[...].astype(jnp.float32)
    for head, out in enumerate(outs):
        out[:, :main] = total[:, head * main : (head + 1) * main]
        first = 2 * main + head * tail
        out[:, main:] = total[:, first : first + tail]


def packed(
    picture_averaged_encodings,
    caption_averaged_encodings,
    picture_mapping_matrix,
    caption_mapping_matrix,
    picture_weight_perturbation,
    caption_weight_perturbation,
    sharpness_multiplier,
    offset_additive,
):
    tensor_rank = lax.axis_index("tensor")
    data_rank = lax.axis_index("dp")
    count = lax.axis_size("tensor")
    data_count = lax.axis_size("dp")
    planes = data_count // 2
    rows, width = picture_averaged_encodings.shape
    cols = picture_mapping_matrix.shape[1]
    main = cols // 128 * 128
    tail = cols - main
    share = rows // count
    size = width // data_count
    f32, bf16 = jnp.float32, jnp.bfloat16
    ranks = jnp.arange(count, dtype=jnp.int32)
    starts = (ranks ^ tensor_rank) * share
    plain = ranks * share

    blocks = call(
        functools.partial(project_kernel, share),
        [((share, 2 * cols), bf16)] * count,
        starts,
        caption_averaged_encodings,
        caption_mapping_matrix.T,
        caption_weight_perturbation.T,
    )
    (image,) = call(
        functools.partial(project_kernel, share),
        [((rows, 2 * cols), bf16)],
        plain,
        picture_averaged_encodings,
        picture_mapping_matrix.T,
        picture_weight_perturbation.T,
        after=(blocks[0],),
    )
    image_other = swapped(image, "dp", 1)
    image_far = swapped(image, "tensor", 2)
    image_far_other = swapped(image_other, "tensor", 2)

    block_ids = jnp.arange(data_count, dtype=jnp.int32)
    slots = ((block_ids ^ data_rank) >> 1) + planes * ((block_ids ^ data_rank) & 1)
    mine, other = call(
        functools.partial(turn_kernel, share),
        [((planes * size, 2 * rows), bf16)] * 2,
        plain,
        starts,
        slots,
        picture_averaged_encodings,
        caption_averaged_encodings,
        after=(image,),
    )
    other = swapped(other, "dp", 1)

    got = [blocks[0]] + [swapped(blocks[k], "tensor", k) for k in range(1, count)]
    (text,) = call(
        functools.partial(text_rows_kernel, main, tail),
        [((share, 2 * width), bf16)],
        *got,
        after=(mine,),
    )
    text_two = swapped(text, "dp", 4)
    text_one = swapped(text, "dp", 2)
    text_three = swapped(text_two, "dp", 2)
    texts = [text, text_one, text_two, text_three]

    (near,) = call(
        stack_kernel,
        [((4 * rows, 2 * cols), bf16)],
        image,
        image_other,
        image_far,
        image_far_other,
        after=(text_one, text_two, other),
    )
    far = swapped(near, "tensor", 1)
    unit, tangent, half, tangent_half, factors = call(
        functools.partial(image_rows_kernel, main, tail, count),
        [
            ((2 * rows, width), f32),
            ((2 * rows, width), f32),
            ((2 * rows, width), bf16),
            ((2 * rows, width), bf16),
            ((2, 2 * rows, 128), f32),
        ],
        near,
        far,
    )

    scalars = jnp.concatenate([sharpness_multiplier, offset_additive])
    outs = call(
        functools.partial(text_block_kernel, planes),
        [((share, width), f32)] * 2
        + [((2 * share, width), bf16)]
        + [((planes * share, width), bf16)] * 2
        + [((2 * rows, planes * share), bf16)] * 2,
        (tensor_rank * share).astype(jnp.int32).reshape(1),
        scalars,
        half,
        tangent_half,
        *texts,
    )
    image_partial = call(
        functools.partial(image_block_kernel, main, tail),
        [((rows, 2 * cols), f32)] * count,
        scalars,
        unit,
        tangent,
        factors,
        *outs[3:],
    )

    total, sent = call(
        forward_kernel,
        [((share, width), f32), ((share, width), bf16)],
        outs[0],
        outs[1],
        swapped(outs[2], "dp", 2),
    )
    blocks = call(
        functools.partial(text_sum_kernel, main, tail),
        [((share, cols), bf16)] * count,
        total,
        swapped(sent, "dp", 4),
    )
    got = [blocks[0]] + [swapped(blocks[k], "tensor", k) for k in range(1, count)]
    (text_back,) = call(stack_kernel, [((rows, cols), bf16)], *got)
    text_back_other = swapped(text_back, "dp", 1)

    near = (tensor_rank // 2 * (2 * share)).astype(jnp.int32).reshape(1)
    far = ((tensor_rank // 2 ^ 1) * (2 * share)).astype(jnp.int32).reshape(1)
    (third,) = call(
        functools.partial(image_pair_kernel, main, tail),
        [((rows + share, 2 * cols), bf16)],
        near,
        image_partial[2],
        swapped(image_partial[3], "tensor", 1),
    )
    second = swapped(image_partial[1], "tensor", 1)
    keep, sent = call(
        functools.partial(image_sum_kernel, main, tail),
        [((rows, cols), f32), ((rows, cols), bf16)],
        far,
        image_partial[0],
        second,
        swapped(third, "tensor", 2),
    )
    (image_back,) = call(add_half_kernel, [((rows, cols), bf16)], keep, swapped(sent, "dp", 1))
    image_back_other = swapped(image_back, "dp", 1)

    products = call(
        functools.partial(head_kernel, main, tail),
        [((size, 2 * cols), f32)] + [((size, 2 * cols), bf16)] * (planes - 1),
        mine,
        other,
        image_back,
        image_back_other,
        text_back,
        text_back_other,
    )
    got = [swapped(products[k], "dp", 2 * k) for k in range(1, planes)]
    return tuple(
        call(
            functools.partial(final_kernel, main, tail),
            [((size, cols), f32)] * 2,
            products[0],
            *got,
        )
    )


def fits(mesh):
    return mesh.shape["tensor"] == 4 and mesh.shape["dp"] == 8


def solution(mesh):
    in_specs = (
        P("dp", None),
        P("dp", None),
        P(None, "tensor"),
        P(None, "tensor"),
        P(None, "tensor"),
        P(None, "tensor"),
        P(),
        P(),
    )
    out_specs = (P("dp", "tensor"), P("dp", "tensor"))
    local = packed if fits(mesh) else general
    return jax.shard_map(local, mesh=mesh, in_specs=in_specs, out_specs=out_specs, check_vma=False)
```

```python
import functools

import jax
import jax.numpy as jnp
from jax import lax
from jax.experimental import pallas as pl
from jax.experimental.pallas import tpu as pltpu
from jax.sharding import PartitionSpec as P

EPS = 1e-06


def swapped(value, axis, mask):
    count = lax.axis_size(axis)
    return lax.ppermute(value, axis, [(source, source ^ mask) for source in range(count)])


def matmul(left, right):
    return jnp.dot(left, right, preferred_element_type=jnp.float32)


def matmul_nt(left, right):
    return lax.dot_general(
        left, right, (((1,), (1,)), ((), ())), preferred_element_type=jnp.float32
    )


def matmul_tn(left, right):
    return lax.dot_general(
        left, right, (((0,), (0,)), ((), ())), preferred_element_type=jnp.float32
    )


def unit_parts(raw, raw_rate):
    values = raw.astype(jnp.float32)
    tangent = raw_rate.astype(jnp.float32)
    radius = jnp.sqrt(jnp.sum(values * values, axis=1, keepdims=True) + EPS)
    unit = values / radius
    rate = jnp.sum(unit * tangent, axis=1, keepdims=True)
    unit_tangent = (tangent - unit * rate) / radius
    return (unit, unit_tangent, radius, rate)


def unit_backward(unit, unit_tangent, radius, rate, grad, grad_rate):
    inner = jnp.sum(unit * grad, axis=1, keepdims=True)
    inner_rate = jnp.sum(unit_tangent * grad + unit * grad_rate, axis=1, keepdims=True)
    first = (grad - unit * inner) / radius
    return (grad_rate - unit_tangent * inner - unit * inner_rate - first * rate) / radius


def general(
    picture_averaged_encodings,
    caption_averaged_encodings,
    picture_mapping_matrix,
    caption_mapping_matrix,
    picture_weight_perturbation,
    caption_weight_perturbation,
    sharpness_multiplier,
    offset_additive,
):
    similarity_multiplier = sharpness_multiplier[0]
    logit_bias = offset_additive[0]
    tensor_rank = lax.axis_index("tensor")
    data_rank = lax.axis_index("dp")
    tensor_count = lax.axis_size("tensor")
    data_count = lax.axis_size("dp")
    planes = data_count // 2
    rows, width = picture_averaged_encodings.shape
    cols = picture_mapping_matrix.shape[1]
    share = rows // tensor_count
    out_rows = width // data_count
    half = jnp.bfloat16

    text = jnp.stack(
        [
            matmul(caption_averaged_encodings, caption_mapping_matrix).astype(half),
            matmul(caption_averaged_encodings, caption_weight_perturbation).astype(half),
        ]
    )
    image = jnp.stack(
        [
            matmul(picture_averaged_encodings, picture_mapping_matrix).astype(half),
            matmul(picture_averaged_encodings, picture_weight_perturbation).astype(half),
        ]
    )

    def share_of(value, axis, mask):
        start = (tensor_rank ^ mask) * share
        return lax.dynamic_slice_in_dim(value, start, share, axis)

    parts = [share_of(text, 1, 0)]
    for mask in range(1, tensor_count):
        parts.append(swapped(share_of(text, 1, mask), "tensor", mask))
    text = jnp.concatenate(parts, axis=2)
    slots = [text] + [swapped(text, "dp", 2 * mask) for mask in range(1, planes)]

    image = jnp.concatenate([image, swapped(image, "dp", 1)], axis=1)
    blocks = [image]
    mask = tensor_count // 2
    image_blocks = {0: image}
    while mask >= 1:
        held = sorted(image_blocks)
        sent = jnp.concatenate([image_blocks[k] for k in held], axis=2)
        got = swapped(sent, "tensor", mask)
        for place, k in enumerate(held):
            image_blocks[k ^ mask] = got[:, :, place * cols : (place + 1) * cols]
        mask //= 2
    image = jnp.concatenate([image_blocks[k] for k in range(tensor_count)], axis=2)
    text = jnp.concatenate(slots, axis=1)

    def out_columns(value, rank):
        taken = [
            lax.dynamic_slice_in_dim(value, (rank ^ (2 * mask)) * out_rows, out_rows, 1)
            for mask in range(planes)
        ]
        return jnp.concatenate(taken, axis=1)

    def plane_encodings(value):
        other = swapped(out_columns(value, data_rank ^ 1), "dp", 1)
        return jnp.concatenate([out_columns(value, data_rank), other], axis=0)

    picture_plane = plane_encodings(picture_averaged_encodings)
    ordered = jnp.concatenate(
        [share_of(caption_averaged_encodings, 0, mask) for mask in range(tensor_count)], axis=0
    )
    caption_plane = plane_encodings(ordered)

    image_unit, image_tangent, image_radius, image_rate = unit_parts(image[0], image[1])
    text_unit, text_tangent, text_radius, text_rate = unit_parts(text[0], text[1])
    image_half = image_unit.astype(half)
    image_tangent_half = image_tangent.astype(half)
    text_half = text_unit.astype(half)
    text_tangent_half = text_tangent.astype(half)

    logits = similarity_multiplier * matmul_nt(text_half, image_half) + logit_bias
    logit_rate = similarity_multiplier * (
        matmul_nt(text_half, image_tangent_half) + matmul_nt(text_tangent_half, image_half)
    )
    probability = jax.nn.sigmoid(logits)
    text_ids = lax.broadcasted_iota(jnp.int32, (logits.shape[0], 1), 0)
    image_ids = lax.broadcasted_iota(jnp.int32, (1, logits.shape[1]), 1)
    positive = ((text_ids < share) & (text_ids + tensor_rank * share == image_ids)).astype(
        jnp.float32
    )
    weight = (probability - positive).astype(half)
    weight_rate = (probability * (1.0 - probability) * logit_rate).astype(half)
    text_grad = similarity_multiplier * matmul(weight, image_half)
    text_grad_rate = similarity_multiplier * (
        matmul(weight_rate, image_half) + matmul(weight, image_tangent_half)
    )
    image_grad = similarity_multiplier * matmul_tn(weight, text_half)
    image_grad_rate = similarity_multiplier * (
        matmul_tn(weight_rate, text_half) + matmul_tn(weight, text_tangent_half)
    )

    text_back = unit_backward(
        text_unit, text_tangent, text_radius, text_rate, text_grad, text_grad_rate
    )
    image_back = unit_backward(
        image_unit, image_tangent, image_radius, image_rate, image_grad, image_grad_rate
    )

    total = text_back[:share]
    for mask in range(1, planes):
        sent = text_back[mask * share : (mask + 1) * share].astype(half)
        total = total + swapped(sent, "dp", 2 * mask).astype(jnp.float32)
    text_back = total.astype(half)
    parts = [text_back[:, :cols]]
    for mask in range(1, tensor_count):
        sent = text_back[:, mask * cols : (mask + 1) * cols]
        parts.append(swapped(sent, "tensor", mask))
    text_back = jnp.concatenate(parts, axis=0)
    text_back = jnp.concatenate([text_back, swapped(text_back, "dp", 1)], axis=0)

    image_blocks = {k: image_back[:, k * cols : (k + 1) * cols] for k in range(tensor_count)}
    mask = 1
    while mask < tensor_count:
        kept = [k for k in sorted(image_blocks) if not k & mask]
        sent = jnp.concatenate([image_blocks[k ^ mask] for k in kept], axis=1)
        got = swapped(sent, "tensor", mask).astype(jnp.float32)
        image_blocks = {
            k: image_blocks[k] + got[:, place * cols : (place + 1) * cols]
            for place, k in enumerate(kept)
        }
        mask *= 2
    image_back = image_blocks[0]
    got = swapped(image_back, "dp", 1)
    image_back = (
        image_back + jnp.concatenate([got[rows:], got[:rows]], axis=0)
    ).astype(half)

    def head(encodings, back):
        product = matmul_tn(encodings, back)
        total = product[:out_rows]
        for mask in range(1, planes):
            sent = product[mask * out_rows : (mask + 1) * out_rows].astype(half)
            total = total + swapped(sent, "dp", 2 * mask).astype(jnp.float32)
        return total

    return (head(picture_plane, image_back), head(caption_plane, text_back))


def call(kernel, outs, *args, after=()):
    count = len(args)

    def body(*refs):
        kernel(*refs[:count], *refs[count + len(after) :])

    def place(value):
        scalar = value.ndim == 1
        return pl.BlockSpec(memory_space=pltpu.SMEM if scalar else pltpu.VMEM)

    return pl.pallas_call(
        body,
        out_shape=[jax.ShapeDtypeStruct(shape, dtype) for shape, dtype in outs],
        in_specs=[place(value) for value in args]
        + [pl.BlockSpec(memory_space=pl.ANY) for _ in after],
        out_specs=[pl.BlockSpec(memory_space=pltpu.VMEM) for _ in outs],
        compiler_params=pltpu.CompilerParams(vmem_limit_bytes=48 * 1024 * 1024),
    )(*args, *after)


def project_kernel(share, starts, encodings, weight, direction, *outs):
    main = weight.shape[0] // 128 * 128
    left = jnp.concatenate(
        [
            encodings[pl.ds(pl.multiple_of(starts[k], 16), share), :]
            for k in range(starts.shape[0])
        ],
        axis=0,
    )
    tails = jnp.concatenate([weight[main:, :], direction[main:, :]], axis=0)
    rows = outs[0].shape[0]
    for right, first in ((weight[:main, :], 0), (direction[:main, :], main), (tails, 2 * main)):
        product = matmul_nt(left, right).astype(jnp.bfloat16)
        for place, out in enumerate(outs):
            out[:, first : first + right.shape[0]] = product[place * rows : (place + 1) * rows]


def gathered(blocks, main, tail, which):
    first = 2 * main + which * tail
    mains = [block[:, which * main : (which + 1) * main] for block in blocks]
    tails = [block[:, first : first + tail] for block in blocks]
    return jnp.concatenate(mains + tails, axis=1)


def text_rows_kernel(main, tail, *refs):
    blocks, out = [ref[...].astype(jnp.float32) for ref in refs[:-1]], refs[-1]
    width = out.shape[1] // 2
    out[:, :width] = gathered(blocks, main, tail, 0).astype(jnp.bfloat16)
    out[:, width:] = gathered(blocks, main, tail, 1).astype(jnp.bfloat16)


def row_factors(values, tangent):
    squares = jnp.sum(values * values, axis=1, keepdims=True)
    cross = jnp.sum(values * tangent, axis=1, keepdims=True)
    inverse = 1.0 / jnp.sqrt(squares + EPS)
    return inverse, cross * inverse


def unit_rows(values, tangent, inverse, rate):
    unit = values * inverse
    return unit, (tangent - unit * rate) * inverse


def back_rows(unit, tangent, inverse, rate, grad, grad_rate):
    inner = jnp.sum(unit * grad, axis=1, keepdims=True)
    inner_rate = jnp.sum(tangent * grad + unit * grad_rate, axis=1, keepdims=True)
    scaled = rate * inverse
    return (
        grad_rate - tangent * inner - grad * scaled + unit * (inner * scaled - inner_rate)
    ) * inverse


STEP = 48


def image_rows_kernel(main, tail, count, near, far, unit, tangent, half, tangent_half, factors):
    rows = unit.shape[0] // 2
    for shard in range(2):
        held = [
            (near, far)[k % 2].at[pl.ds((k - k % 2 + shard) * rows, rows), :] for k in range(count)
        ]

        @pl.loop(0, rows // STEP)
        def _(step):
            here = pl.ds(pl.multiple_of(step * STEP, STEP), STEP)
            there = pl.ds(pl.multiple_of(shard * rows + step * STEP, STEP), STEP)
            parts = [block[here, :].astype(jnp.float32) for block in held]
            values = gathered(parts, main, tail, 0)
            rates = gathered(parts, main, tail, 1)
            inverse, rate = row_factors(values, rates)
            one, two = unit_rows(values, rates, inverse, rate)
            unit[there, :] = one
            tangent[there, :] = two
            half[there, :] = one.astype(jnp.bfloat16)
            tangent_half[there, :] = two.astype(jnp.bfloat16)
            factors[0, there, :] = jnp.broadcast_to(inverse, (STEP, 128))
            factors[1, there, :] = jnp.broadcast_to(rate, (STEP, 128))


def text_block_kernel(slots, start, scalars, half, tangent_half, *refs):
    texts, refs = refs[:slots], refs[slots:]
    sums, refs = refs[:slots], refs[slots:]
    text_half, text_tangent_half, weight_turned, weight_rate_turned = refs
    f32, bf16 = jnp.float32, jnp.bfloat16
    share, width = texts[0].shape[0], texts[0].shape[1] // 2
    multiplier, bias = scalars[0], scalars[1]

    text_parts = []
    for slot, text in enumerate(texts):
        here = slice(slot * share, (slot + 1) * share)
        values, rates = text[:, :width].astype(f32), text[:, width:].astype(f32)
        inverse, rate = row_factors(values, rates)
        unit, tangent = unit_rows(values, rates, inverse, rate)
        text_parts.append((unit, tangent, inverse, rate))
        text_half[here, :] = unit.astype(bf16)
        text_tangent_half[here, :] = tangent.astype(bf16)

    logits = multiplier * matmul_nt(text_half[...], half[...]) + bias
    logit_rate = multiplier * (
        matmul_nt(text_half[...], tangent_half[...])
        + matmul_nt(text_tangent_half[...], half[...])
    )
    probability = jax.nn.sigmoid(logits)
    text_ids = lax.broadcasted_iota(jnp.int32, logits.shape, 0)
    image_ids = lax.broadcasted_iota(jnp.int32, logits.shape, 1)
    positive = jnp.where((text_ids < share) & (text_ids + start[0] == image_ids), 1.0, 0.0)
    weight = probability - positive
    weight_rate = probability * (1.0 - probability) * logit_rate
    weight_half, weight_rate_half = weight.astype(bf16), weight_rate.astype(bf16)

    text_grad = multiplier * matmul(weight_half, half[...])
    text_grad_rate = multiplier * (
        matmul(weight_rate_half, half[...]) + matmul(weight_half, tangent_half[...])
    )
    for slot, (unit, tangent, inverse, rate) in enumerate(text_parts):
        here = slice(slot * share, (slot + 1) * share)
        back = back_rows(unit, tangent, inverse, rate, text_grad[here], text_grad_rate[here])
        sums[slot][...] = back.astype(sums[slot].dtype)
    weight_turned[...] = weight.T.astype(bf16)
    weight_rate_turned[...] = weight_rate.T.astype(bf16)


def image_block_kernel(
    main,
    tail,
    scalars,
    unit,
    tangent,
    factors,
    text_half,
    text_tangent_half,
    weight,
    weight_rate,
    kept,
    sent,
):
    rows = unit.shape[0] // 2
    count = 4
    multiplier = scalars[0]
    for shard in range(2):
        here = slice(shard * rows, (shard + 1) * rows)
        grad = multiplier * matmul(weight[here, :], text_half[...])
        grad_rate = multiplier * (
            matmul(weight_rate[here, :], text_half[...])
            + matmul(weight[here, :], text_tangent_half[...])
        )
        back = back_rows(
            unit[here, :],
            tangent[here, :],
            factors[0, here, :1],
            factors[1, here, :1],
            grad,
            grad_rate,
        )
        for k in range(count):
            out = (kept, sent)[k % 2]
            to = slice(k // 2 * rows, (k // 2 + 1) * rows)
            out[to, shard * main : (shard + 1) * main] = back[:, k * main : (k + 1) * main]
            first = 2 * main + shard * tail
            taken = count * main + k * tail
            out[to, first : first + tail] = back[:, taken : taken + tail]


def text_sum_kernel(main, tail, own, *refs):
    count = own.shape[1] // (main + tail)
    got, outs = refs[:-count], refs[-count:]
    total = own[...]
    for ref in got:
        total = total + ref[...].astype(jnp.float32)
    for k, out in enumerate(outs):
        first = count * main + k * tail
        out[:, :main] = total[:, k * main : (k + 1) * main].astype(jnp.bfloat16)
        out[:, main:] = total[:, first : first + tail].astype(jnp.bfloat16)


def stack_kernel(*refs):
    rows = refs[0].shape[0]
    for k, ref in enumerate(refs[:-1]):
        refs[-1][k * rows : (k + 1) * rows, :] = ref[...]


def turn_kernel(share, plain, starts, places, picture, caption, *outs):
    for which, (encodings, order) in enumerate(((picture, plain), (caption, starts))):
        ordered = jnp.concatenate(
            [
                encodings[pl.ds(pl.multiple_of(order[k], 16), share), :].astype(jnp.float32)
                for k in range(order.shape[0])
            ],
            axis=0,
        )
        turned = ordered.T.astype(jnp.bfloat16)
        count = places.shape[0]
        size, rows = turned.shape[0] // count, turned.shape[1]
        fold = count // 4
        for block in range(count):
            taken = turned[block * size : (block + 1) * size, :]
            slot = places[block]
            at = pl.multiple_of(which * fold * size + slot % fold * size, 16)
            for side in range(2):
                for half in range(2):

                    @pl.when(slot // fold == 2 * side + half)
                    def _():
                        outs[side][pl.ds(at, size), half * rows : (half + 1) * rows] = taken


def image_pair_kernel(main, tail, near, kept, got, total, *outs):
    rows = total.shape[0]
    size = outs[0].shape[0] - rows
    start = pl.multiple_of(near[0], 16)
    total[...] = kept[:rows, :] + got[:rows, :]
    for which, out in enumerate(outs):
        here = slice(which * rows, (which + 1) * rows)
        out[:rows, :] = (kept[here, :] + got[here, :]).astype(jnp.bfloat16)
        for fold in range(2):
            at = pl.ds(pl.multiple_of(which * rows + start + fold * size, 16), size)
            there = pl.ds(pl.multiple_of(start + fold * size, 16), size)
            left = kept[at, :] + got[at, :] - out[there, :].astype(jnp.float32)
            out[rows:, fold * main : (fold + 1) * main] = left[:, :main].astype(jnp.bfloat16)
            first = 2 * main + fold * tail
            out[rows:, first : first + tail] = left[:, 2 * main : 2 * main + tail].astype(
                jnp.bfloat16
            )


def image_sum_kernel(main, tail, near, far, total, over_x, over_y, over_both, *outs):
    rows = total.shape[0]
    size = over_x.shape[0] - rows
    for shard, out in enumerate(outs):
        for first, step, at, width in ((0, main, 0, main), (2 * main, tail, main, tail)):
            same = slice(first + shard * step, first + shard * step + step)
            other = slice(first + (1 - shard) * step, first + (1 - shard) * step + step)
            for part in range(rows // size):
                here = slice(part * size, (part + 1) * size)
                value = total[here, same] + over_x[here, same].astype(jnp.float32)
                value += over_y[here, other].astype(jnp.float32)
                value += over_both[here, other].astype(jnp.float32)
                sources = ((over_x, far),) if shard == 0 else ((over_y, near), (over_both, far))
                for source, start in sources:
                    for fold in range(2):
                        lanes = slice(first + fold * step, first + fold * step + step)
                        left = source[rows:, lanes].astype(jnp.float32)
                        mine = start[0] + fold * size == part * size
                        value += jnp.where(mine, left, 0.0)
                out[here, at : at + width] = value.astype(jnp.bfloat16)


def head_kernel(main, tail, mine, other, *refs):
    backs, own, sent = refs[:4], refs[4], refs[5:]
    size = own.shape[0]
    rows = backs[0].shape[0]
    outs = (own,) + tuple(sent)
    fold = len(outs) // 2
    for head in range(2):
        near, far = backs[2 * head], backs[2 * head + 1]
        for half in range(2):
            here = slice(head * fold * size, (head + 1) * fold * size)
            lanes = slice(half * rows, (half + 1) * rows)
            product = matmul(mine[here, lanes], near[...]) + matmul(other[here, lanes], far[...])
            for place in range(fold):
                out = outs[half * fold + place]
                part = product[place * size : (place + 1) * size]
                out[:, head * main : (head + 1) * main] = part[:, :main].astype(out.dtype)
                first = 2 * main + head * tail
                out[:, first : first + tail] = part[:, main:].astype(out.dtype)


def final_kernel(main, tail, own, *refs):
    got, outs = refs[:-2], refs[-2:]
    total = own[...]
    for ref in got:
        total = total + ref[...].astype(jnp.float32)
    for head, out in enumerate(outs):
        out[:, :main] = total[:, head * main : (head + 1) * main]
        first = 2 * main + head * tail
        out[:, main:] = total[:, first : first + tail]


def packed(
    picture_averaged_encodings,
    caption_averaged_encodings,
    picture_mapping_matrix,
    caption_mapping_matrix,
    picture_weight_perturbation,
    caption_weight_perturbation,
    sharpness_multiplier,
    offset_additive,
):
    tensor_rank = lax.axis_index("tensor")
    data_rank = lax.axis_index("dp")
    count = lax.axis_size("tensor")
    data_count = lax.axis_size("dp")
    planes = data_count // 2
    rows, width = picture_averaged_encodings.shape
    cols = picture_mapping_matrix.shape[1]
    main = cols // 128 * 128
    tail = cols - main
    share = rows // count
    size = width // data_count
    f32, bf16 = jnp.float32, jnp.bfloat16
    ranks = jnp.arange(count, dtype=jnp.int32)
    starts = (ranks ^ tensor_rank) * share
    plain = ranks * share

    blocks = call(
        functools.partial(project_kernel, share),
        [((share, 2 * cols), bf16)] * count,
        starts,
        caption_averaged_encodings,
        caption_mapping_matrix.T,
        caption_weight_perturbation.T,
    )
    got = [blocks[0]] + [swapped(blocks[k], "tensor", k) for k in range(1, count)]

    (image,) = call(
        functools.partial(project_kernel, share),
        [((rows, 2 * cols), bf16)],
        plain,
        picture_averaged_encodings,
        picture_mapping_matrix.T,
        picture_weight_perturbation.T,
        after=(got[1],),
    )
    image_other = swapped(image, "dp", 1)
    image_far = swapped(image, "tensor", 2)
    image_far_other = swapped(image_other, "tensor", 2)

    (text,) = call(
        functools.partial(text_rows_kernel, main, tail),
        [((share, 2 * width), bf16)],
        *got,
    )
    text_two = swapped(text, "dp", 4)
    text_one = swapped(text, "dp", 2)
    text_three = swapped(text_two, "dp", 2)
    texts = [text, text_one, text_two, text_three]

    block_ids = jnp.arange(data_count, dtype=jnp.int32)
    slots = ((block_ids ^ data_rank) >> 1) + planes * ((block_ids ^ data_rank) & 1)
    mine, other = call(
        functools.partial(turn_kernel, share),
        [((planes * size, 2 * rows), bf16)] * 2,
        plain,
        starts,
        slots,
        picture_averaged_encodings,
        caption_averaged_encodings,
        after=(text,),
    )
    other = swapped(other, "dp", 1)

    (near,) = call(
        stack_kernel,
        [((4 * rows, 2 * cols), bf16)],
        image,
        image_other,
        image_far,
        image_far_other,
        after=(text_one, text_two, other),
    )
    far = swapped(near, "tensor", 1)
    unit, tangent, half, tangent_half, factors = call(
        functools.partial(image_rows_kernel, main, tail, count),
        [
            ((2 * rows, width), f32),
            ((2 * rows, width), f32),
            ((2 * rows, width), bf16),
            ((2 * rows, width), bf16),
            ((2, 2 * rows, 128), f32),
        ],
        near,
        far,
    )

    scalars = jnp.concatenate([sharpness_multiplier, offset_additive])
    outs = call(
        functools.partial(text_block_kernel, planes),
        [((share, width), f32)]
        + [((share, width), bf16)] * (planes - 1)
        + [((planes * share, width), bf16)] * 2
        + [((2 * rows, planes * share), bf16)] * 2,
        (tensor_rank * share).astype(jnp.int32).reshape(1),
        scalars,
        half,
        tangent_half,
        *texts,
    )
    kept, sent = call(
        functools.partial(image_block_kernel, main, tail),
        [((2 * rows, 2 * cols), f32)] * 2,
        scalars,
        unit,
        tangent,
        factors,
        *outs[planes:],
    )

    got = [swapped(outs[k], "dp", 2 * k) for k in range(1, planes)]
    blocks = call(
        functools.partial(text_sum_kernel, main, tail),
        [((share, cols), bf16)] * count,
        outs[0],
        *got,
    )
    got = [blocks[0]] + [swapped(blocks[k], "tensor", k) for k in range(1, count)]
    (text_back,) = call(stack_kernel, [((rows, cols), bf16)], *got)
    text_back_other = swapped(text_back, "dp", 1)

    near = (tensor_rank // 2 * (2 * share)).astype(jnp.int32).reshape(1)
    far = ((tensor_rank // 2 ^ 1) * (2 * share)).astype(jnp.int32).reshape(1)
    total, to_y, to_x = call(
        functools.partial(image_pair_kernel, main, tail),
        [((rows, 2 * cols), f32)] + [((rows + share, 2 * cols), bf16)] * 2,
        near,
        kept,
        swapped(sent, "tensor", 1),
    )
    flat = [(source, source ^ (count + 2)) for source in range(data_count * count)]
    image_back, image_back_other = call(
        functools.partial(image_sum_kernel, main, tail),
        [((rows, cols), bf16)] * 2,
        near,
        far,
        total,
        swapped(to_x, "tensor", 2),
        swapped(to_y, "dp", 1),
        lax.ppermute(to_x, ("dp", "tensor"), flat),
    )

    products = call(
        functools.partial(head_kernel, main, tail),
        [((size, 2 * cols), f32)] + [((size, 2 * cols), bf16)] * (planes - 1),
        mine,
        other,
        image_back,
        image_back_other,
        text_back,
        text_back_other,
    )
    got = [swapped(products[k], "dp", 2 * k) for k in range(1, planes)]
    return tuple(
        call(
            functools.partial(final_kernel, main, tail),
            [((size, cols), f32)] * 2,
            products[0],
            *got,
        )
    )


def fits(mesh):
    return mesh.shape["tensor"] == 4 and mesh.shape["dp"] == 8


def solution(mesh):
    in_specs = (
        P("dp", None),
        P("dp", None),
        P(None, "tensor"),
        P(None, "tensor"),
        P(None, "tensor"),
        P(None, "tensor"),
        P(),
        P(),
    )
    out_specs = (P("dp", "tensor"), P("dp", "tensor"))
    local = packed if fits(mesh) else general
    return jax.shard_map(local, mesh=mesh, in_specs=in_specs, out_specs=out_specs, check_vma=False)
```

```python
import functools

import jax
import jax.numpy as jnp
from jax import lax
from jax.experimental import pallas as pl
from jax.experimental.pallas import tpu as pltpu
from jax.sharding import PartitionSpec as P

EPS = 1e-06


def swapped(value, axis, mask):
    count = lax.axis_size(axis)
    return lax.ppermute(value, axis, [(source, source ^ mask) for source in range(count)])


def matmul(left, right):
    return jnp.dot(left, right, preferred_element_type=jnp.float32)


def matmul_nt(left, right):
    return lax.dot_general(
        left, right, (((1,), (1,)), ((), ())), preferred_element_type=jnp.float32
    )


def matmul_tn(left, right):
    return lax.dot_general(
        left, right, (((0,), (0,)), ((), ())), preferred_element_type=jnp.float32
    )


def unit_parts(raw, raw_rate):
    values = raw.astype(jnp.float32)
    tangent = raw_rate.astype(jnp.float32)
    radius = jnp.sqrt(jnp.sum(values * values, axis=1, keepdims=True) + EPS)
    unit = values / radius
    rate = jnp.sum(unit * tangent, axis=1, keepdims=True)
    unit_tangent = (tangent - unit * rate) / radius
    return (unit, unit_tangent, radius, rate)


def unit_backward(unit, unit_tangent, radius, rate, grad, grad_rate):
    inner = jnp.sum(unit * grad, axis=1, keepdims=True)
    inner_rate = jnp.sum(unit_tangent * grad + unit * grad_rate, axis=1, keepdims=True)
    first = (grad - unit * inner) / radius
    return (grad_rate - unit_tangent * inner - unit * inner_rate - first * rate) / radius


def general(
    picture_averaged_encodings,
    caption_averaged_encodings,
    picture_mapping_matrix,
    caption_mapping_matrix,
    picture_weight_perturbation,
    caption_weight_perturbation,
    sharpness_multiplier,
    offset_additive,
):
    similarity_multiplier = sharpness_multiplier[0]
    logit_bias = offset_additive[0]
    tensor_rank = lax.axis_index("tensor")
    data_rank = lax.axis_index("dp")
    tensor_count = lax.axis_size("tensor")
    data_count = lax.axis_size("dp")
    planes = data_count // 2
    rows, width = picture_averaged_encodings.shape
    cols = picture_mapping_matrix.shape[1]
    share = rows // tensor_count
    out_rows = width // data_count
    half = jnp.bfloat16

    text = jnp.stack(
        [
            matmul(caption_averaged_encodings, caption_mapping_matrix).astype(half),
            matmul(caption_averaged_encodings, caption_weight_perturbation).astype(half),
        ]
    )
    image = jnp.stack(
        [
            matmul(picture_averaged_encodings, picture_mapping_matrix).astype(half),
            matmul(picture_averaged_encodings, picture_weight_perturbation).astype(half),
        ]
    )

    def share_of(value, axis, mask):
        start = (tensor_rank ^ mask) * share
        return lax.dynamic_slice_in_dim(value, start, share, axis)

    parts = [share_of(text, 1, 0)]
    for mask in range(1, tensor_count):
        parts.append(swapped(share_of(text, 1, mask), "tensor", mask))
    text = jnp.concatenate(parts, axis=2)
    slots = [text] + [swapped(text, "dp", 2 * mask) for mask in range(1, planes)]

    image = jnp.concatenate([image, swapped(image, "dp", 1)], axis=1)
    blocks = [image]
    mask = tensor_count // 2
    image_blocks = {0: image}
    while mask >= 1:
        held = sorted(image_blocks)
        sent = jnp.concatenate([image_blocks[k] for k in held], axis=2)
        got = swapped(sent, "tensor", mask)
        for place, k in enumerate(held):
            image_blocks[k ^ mask] = got[:, :, place * cols : (place + 1) * cols]
        mask //= 2
    image = jnp.concatenate([image_blocks[k] for k in range(tensor_count)], axis=2)
    text = jnp.concatenate(slots, axis=1)

    def out_columns(value, rank):
        taken = [
            lax.dynamic_slice_in_dim(value, (rank ^ (2 * mask)) * out_rows, out_rows, 1)
            for mask in range(planes)
        ]
        return jnp.concatenate(taken, axis=1)

    def plane_encodings(value):
        other = swapped(out_columns(value, data_rank ^ 1), "dp", 1)
        return jnp.concatenate([out_columns(value, data_rank), other], axis=0)

    picture_plane = plane_encodings(picture_averaged_encodings)
    ordered = jnp.concatenate(
        [share_of(caption_averaged_encodings, 0, mask) for mask in range(tensor_count)], axis=0
    )
    caption_plane = plane_encodings(ordered)

    image_unit, image_tangent, image_radius, image_rate = unit_parts(image[0], image[1])
    text_unit, text_tangent, text_radius, text_rate = unit_parts(text[0], text[1])
    image_half = image_unit.astype(half)
    image_tangent_half = image_tangent.astype(half)
    text_half = text_unit.astype(half)
    text_tangent_half = text_tangent.astype(half)

    logits = similarity_multiplier * matmul_nt(text_half, image_half) + logit_bias
    logit_rate = similarity_multiplier * (
        matmul_nt(text_half, image_tangent_half) + matmul_nt(text_tangent_half, image_half)
    )
    probability = jax.nn.sigmoid(logits)
    text_ids = lax.broadcasted_iota(jnp.int32, (logits.shape[0], 1), 0)
    image_ids = lax.broadcasted_iota(jnp.int32, (1, logits.shape[1]), 1)
    positive = ((text_ids < share) & (text_ids + tensor_rank * share == image_ids)).astype(
        jnp.float32
    )
    weight = (probability - positive).astype(half)
    weight_rate = (probability * (1.0 - probability) * logit_rate).astype(half)
    text_grad = similarity_multiplier * matmul(weight, image_half)
    text_grad_rate = similarity_multiplier * (
        matmul(weight_rate, image_half) + matmul(weight, image_tangent_half)
    )
    image_grad = similarity_multiplier * matmul_tn(weight, text_half)
    image_grad_rate = similarity_multiplier * (
        matmul_tn(weight_rate, text_half) + matmul_tn(weight, text_tangent_half)
    )

    text_back = unit_backward(
        text_unit, text_tangent, text_radius, text_rate, text_grad, text_grad_rate
    )
    image_back = unit_backward(
        image_unit, image_tangent, image_radius, image_rate, image_grad, image_grad_rate
    )

    total = text_back[:share]
    for mask in range(1, planes):
        sent = text_back[mask * share : (mask + 1) * share].astype(half)
        total = total + swapped(sent, "dp", 2 * mask).astype(jnp.float32)
    text_back = total.astype(half)
    parts = [text_back[:, :cols]]
    for mask in range(1, tensor_count):
        sent = text_back[:, mask * cols : (mask + 1) * cols]
        parts.append(swapped(sent, "tensor", mask))
    text_back = jnp.concatenate(parts, axis=0)
    text_back = jnp.concatenate([text_back, swapped(text_back, "dp", 1)], axis=0)

    image_blocks = {k: image_back[:, k * cols : (k + 1) * cols] for k in range(tensor_count)}
    mask = 1
    while mask < tensor_count:
        kept = [k for k in sorted(image_blocks) if not k & mask]
        sent = jnp.concatenate([image_blocks[k ^ mask] for k in kept], axis=1)
        got = swapped(sent, "tensor", mask).astype(jnp.float32)
        image_blocks = {
            k: image_blocks[k] + got[:, place * cols : (place + 1) * cols]
            for place, k in enumerate(kept)
        }
        mask *= 2
    image_back = image_blocks[0]
    got = swapped(image_back, "dp", 1)
    image_back = (
        image_back + jnp.concatenate([got[rows:], got[:rows]], axis=0)
    ).astype(half)

    def head(encodings, back):
        product = matmul_tn(encodings, back)
        total = product[:out_rows]
        for mask in range(1, planes):
            sent = product[mask * out_rows : (mask + 1) * out_rows].astype(half)
            total = total + swapped(sent, "dp", 2 * mask).astype(jnp.float32)
        return total

    return (head(picture_plane, image_back), head(caption_plane, text_back))


def call(kernel, outs, *args, after=()):
    count = len(args)

    def body(*refs):
        kernel(*refs[:count], *refs[count + len(after) :])

    def place(value):
        scalar = value.ndim == 1
        return pl.BlockSpec(memory_space=pltpu.SMEM if scalar else pltpu.VMEM)

    return pl.pallas_call(
        body,
        out_shape=[jax.ShapeDtypeStruct(shape, dtype) for shape, dtype in outs],
        in_specs=[place(value) for value in args]
        + [pl.BlockSpec(memory_space=pl.ANY) for _ in after],
        out_specs=[pl.BlockSpec(memory_space=pltpu.VMEM) for _ in outs],
        compiler_params=pltpu.CompilerParams(vmem_limit_bytes=48 * 1024 * 1024),
    )(*args, *after)


def project_kernel(share, starts, encodings, weight, direction, *outs):
    main = weight.shape[0] // 128 * 128
    left = jnp.concatenate(
        [
            encodings[pl.ds(pl.multiple_of(starts[k], 16), share), :]
            for k in range(starts.shape[0])
        ],
        axis=0,
    )
    tails = jnp.concatenate([weight[main:, :], direction[main:, :]], axis=0)
    rows = outs[0].shape[0]
    for right, first in ((weight[:main, :], 0), (direction[:main, :], main), (tails, 2 * main)):
        product = matmul_nt(left, right).astype(jnp.bfloat16)
        for place, out in enumerate(outs):
            out[:, first : first + right.shape[0]] = product[place * rows : (place + 1) * rows]


def gathered(blocks, main, tail, which):
    first = 2 * main + which * tail
    mains = [block[:, which * main : (which + 1) * main] for block in blocks]
    tails = [block[:, first : first + tail] for block in blocks]
    return jnp.concatenate(mains + tails, axis=1)


def text_rows_kernel(main, tail, *refs):
    blocks, out = [ref[...].astype(jnp.float32) for ref in refs[:-1]], refs[-1]
    width = out.shape[1] // 2
    out[:, :width] = gathered(blocks, main, tail, 0).astype(jnp.bfloat16)
    out[:, width:] = gathered(blocks, main, tail, 1).astype(jnp.bfloat16)


def row_factors(values, tangent):
    squares = jnp.sum(values * values, axis=1, keepdims=True)
    cross = jnp.sum(values * tangent, axis=1, keepdims=True)
    inverse = 1.0 / jnp.sqrt(squares + EPS)
    return inverse, cross * inverse


def unit_rows(values, tangent, inverse, rate):
    unit = values * inverse
    return unit, (tangent - unit * rate) * inverse


def back_rows(unit, tangent, inverse, rate, grad, grad_rate):
    inner = jnp.sum(unit * grad, axis=1, keepdims=True)
    inner_rate = jnp.sum(tangent * grad + unit * grad_rate, axis=1, keepdims=True)
    scaled = rate * inverse
    return (
        grad_rate - tangent * inner - grad * scaled + unit * (inner * scaled - inner_rate)
    ) * inverse


STEP = 48


def image_rows_kernel(main, tail, count, near, far, unit, tangent, half, tangent_half, factors):
    rows = unit.shape[0] // 2
    for shard in range(2):
        held = [
            (near, far)[k % 2].at[pl.ds((k - k % 2 + shard) * rows, rows), :] for k in range(count)
        ]

        @pl.loop(0, rows // STEP)
        def _(step):
            here = pl.ds(pl.multiple_of(step * STEP, STEP), STEP)
            there = pl.ds(pl.multiple_of(shard * rows + step * STEP, STEP), STEP)
            parts = [block[here, :].astype(jnp.float32) for block in held]
            values = gathered(parts, main, tail, 0)
            rates = gathered(parts, main, tail, 1)
            inverse, rate = row_factors(values, rates)
            one, two = unit_rows(values, rates, inverse, rate)
            unit[there, :] = one
            tangent[there, :] = two
            half[there, :] = one.astype(jnp.bfloat16)
            tangent_half[there, :] = two.astype(jnp.bfloat16)
            factors[0, there, :] = jnp.broadcast_to(inverse, (STEP, 128))
            factors[1, there, :] = jnp.broadcast_to(rate, (STEP, 128))


def text_block_kernel(slots, start, scalars, half, tangent_half, *refs):
    texts, refs = refs[:slots], refs[slots:]
    sums, refs = refs[:slots], refs[slots:]
    text_half, text_tangent_half, weight_turned, weight_rate_turned = refs
    f32, bf16 = jnp.float32, jnp.bfloat16
    share, width = texts[0].shape[0], texts[0].shape[1] // 2
    multiplier, bias = scalars[0], scalars[1]

    text_parts = []
    for slot, text in enumerate(texts):
        here = slice(slot * share, (slot + 1) * share)
        values, rates = text[:, :width].astype(f32), text[:, width:].astype(f32)
        inverse, rate = row_factors(values, rates)
        unit, tangent = unit_rows(values, rates, inverse, rate)
        text_parts.append((unit, tangent, inverse, rate))
        text_half[here, :] = unit.astype(bf16)
        text_tangent_half[here, :] = tangent.astype(bf16)

    logits = multiplier * matmul_nt(text_half[...], half[...]) + bias
    logit_rate = multiplier * (
        matmul_nt(text_half[...], tangent_half[...])
        + matmul_nt(text_tangent_half[...], half[...])
    )
    probability = jax.nn.sigmoid(logits)
    text_ids = lax.broadcasted_iota(jnp.int32, logits.shape, 0)
    image_ids = lax.broadcasted_iota(jnp.int32, logits.shape, 1)
    positive = jnp.where((text_ids < share) & (text_ids + start[0] == image_ids), 1.0, 0.0)
    weight = probability - positive
    weight_rate = probability * (1.0 - probability) * logit_rate
    weight_half, weight_rate_half = weight.astype(bf16), weight_rate.astype(bf16)

    text_grad = multiplier * matmul(weight_half, half[...])
    text_grad_rate = multiplier * (
        matmul(weight_rate_half, half[...]) + matmul(weight_half, tangent_half[...])
    )
    for slot, (unit, tangent, inverse, rate) in enumerate(text_parts):
        here = slice(slot * share, (slot + 1) * share)
        back = back_rows(unit, tangent, inverse, rate, text_grad[here], text_grad_rate[here])
        sums[slot][...] = back.astype(sums[slot].dtype)
    weight_turned[...] = weight.T.astype(bf16)
    weight_rate_turned[...] = weight_rate.T.astype(bf16)


def image_block_kernel(
    main,
    tail,
    scalars,
    unit,
    tangent,
    factors,
    text_half,
    text_tangent_half,
    weight,
    weight_rate,
    kept,
    sent,
):
    rows = unit.shape[0] // 2
    count = 4
    multiplier = scalars[0]
    for shard in range(2):
        here = slice(shard * rows, (shard + 1) * rows)
        grad = multiplier * matmul(weight[here, :], text_half[...])
        grad_rate = multiplier * (
            matmul(weight_rate[here, :], text_half[...])
            + matmul(weight[here, :], text_tangent_half[...])
        )
        back = back_rows(
            unit[here, :],
            tangent[here, :],
            factors[0, here, :1],
            factors[1, here, :1],
            grad,
            grad_rate,
        )
        for k in range(count):
            out = (kept, sent)[k % 2]
            to = slice(k // 2 * rows, (k // 2 + 1) * rows)
            out[to, shard * main : (shard + 1) * main] = back[:, k * main : (k + 1) * main]
            first = 2 * main + shard * tail
            taken = count * main + k * tail
            out[to, first : first + tail] = back[:, taken : taken + tail]


def text_sum_kernel(main, tail, own, *refs):
    count = own.shape[1] // (main + tail)
    got, outs = refs[:-count], refs[-count:]
    total = own[...]
    for ref in got:
        total = total + ref[...].astype(jnp.float32)
    for k, out in enumerate(outs):
        first = count * main + k * tail
        out[:, :main] = total[:, k * main : (k + 1) * main].astype(jnp.bfloat16)
        out[:, main:] = total[:, first : first + tail].astype(jnp.bfloat16)


def stack_kernel(*refs):
    rows = refs[0].shape[0]
    for k, ref in enumerate(refs[:-1]):
        refs[-1][k * rows : (k + 1) * rows, : ref.shape[1]] = ref[...]


def turn_kernel(share, plain, starts, places, picture, caption, *outs):
    for which, (encodings, order) in enumerate(((picture, plain), (caption, starts))):
        ordered = jnp.concatenate(
            [
                encodings[pl.ds(pl.multiple_of(order[k], 16), share), :].astype(jnp.float32)
                for k in range(order.shape[0])
            ],
            axis=0,
        )
        turned = ordered.T.astype(jnp.bfloat16)
        count = places.shape[0]
        size, rows = turned.shape[0] // count, turned.shape[1]
        fold = count // 4
        for block in range(count):
            taken = turned[block * size : (block + 1) * size, :]
            slot = places[block]
            at = pl.multiple_of(which * fold * size + slot % fold * size, 16)
            for side in range(2):
                for half in range(2):

                    @pl.when(slot // fold == 2 * side + half)
                    def _():
                        outs[side][pl.ds(at, size), half * rows : (half + 1) * rows] = taken


def image_pair_kernel(main, tail, near, kept, got, total, *outs):
    rows, width = total.shape
    size = outs[0].shape[0] - rows
    start = pl.multiple_of(near[0], 16)
    total[...] = kept[:rows, :width] + got[:rows, :width]
    for which, out in enumerate(outs):
        here = slice(which * rows, (which + 1) * rows)
        out[:rows, :] = (kept[here, :width] + got[here, :width]).astype(jnp.bfloat16)
        for fold in range(2):
            at = pl.ds(pl.multiple_of(which * rows + start + fold * size, 16), size)
            there = pl.ds(pl.multiple_of(start + fold * size, 16), size)
            left = kept[at, :width] + got[at, :width] - out[there, :].astype(jnp.float32)
            out[rows:, fold * main : (fold + 1) * main] = left[:, :main].astype(jnp.bfloat16)
            first = 2 * main + fold * tail
            out[rows:, first : first + tail] = left[:, 2 * main : 2 * main + tail].astype(
                jnp.bfloat16
            )


def image_sum_kernel(main, tail, near, far, total, over_x, over_y, over_both, *outs):
    rows = total.shape[0]
    size = over_x.shape[0] - rows
    for shard, out in enumerate(outs):
        for first, step, at, width in ((0, main, 0, main), (2 * main, tail, main, tail)):
            same = slice(first + shard * step, first + shard * step + step)
            other = slice(first + (1 - shard) * step, first + (1 - shard) * step + step)
            for part in range(rows // size):
                here = slice(part * size, (part + 1) * size)
                value = total[here, same] + over_x[here, same].astype(jnp.float32)
                value += over_y[here, other].astype(jnp.float32)
                value += over_both[here, other].astype(jnp.float32)
                sources = ((over_x, far),) if shard == 0 else ((over_y, near), (over_both, far))
                for source, start in sources:
                    for fold in range(2):
                        lanes = slice(first + fold * step, first + fold * step + step)
                        left = source[rows:, lanes].astype(jnp.float32)
                        mine = start[0] + fold * size == part * size
                        value += jnp.where(mine, left, 0.0)
                out[here, at : at + width] = value.astype(jnp.bfloat16)


def head_kernel(main, tail, mine, other, *refs):
    backs, own, sent = refs[:4], refs[4], refs[5:]
    size = own.shape[0]
    rows = backs[0].shape[0]
    outs = (own,) + tuple(sent)
    fold = len(outs) // 2
    for head in range(2):
        near, far = backs[2 * head], backs[2 * head + 1]
        for half in range(2):
            here = slice(head * fold * size, (head + 1) * fold * size)
            lanes = slice(half * rows, (half + 1) * rows)
            product = matmul(mine[here, lanes], near[...]) + matmul(other[here, lanes], far[...])
            for place in range(fold):
                out = outs[half * fold + place]
                part = product[place * size : (place + 1) * size]
                out[:, head * main : (head + 1) * main] = part[:, :main].astype(out.dtype)
                first = 2 * main + head * tail
                out[:, first : first + tail] = part[:, main:].astype(out.dtype)


def final_kernel(main, tail, own, *refs):
    got, outs = refs[:-2], refs[-2:]
    total = own[...]
    for ref in got:
        total = total + ref[...].astype(jnp.float32)
    for head, out in enumerate(outs):
        out[:, :main] = total[:, head * main : (head + 1) * main]
        first = 2 * main + head * tail
        out[:, main:] = total[:, first : first + tail]


def packed(
    picture_averaged_encodings,
    caption_averaged_encodings,
    picture_mapping_matrix,
    caption_mapping_matrix,
    picture_weight_perturbation,
    caption_weight_perturbation,
    sharpness_multiplier,
    offset_additive,
):
    tensor_rank = lax.axis_index("tensor")
    data_rank = lax.axis_index("dp")
    count = lax.axis_size("tensor")
    data_count = lax.axis_size("dp")
    planes = data_count // 2
    rows, width = picture_averaged_encodings.shape
    cols = picture_mapping_matrix.shape[1]
    main = cols // 128 * 128
    tail = cols - main
    share = rows // count
    size = width // data_count
    wide = -(-2 * cols // 128) * 128
    f32, bf16 = jnp.float32, jnp.bfloat16
    ranks = jnp.arange(count, dtype=jnp.int32)
    starts = (ranks ^ tensor_rank) * share
    plain = ranks * share

    blocks = call(
        functools.partial(project_kernel, share),
        [((share, 2 * cols), bf16)] * count,
        starts,
        caption_averaged_encodings,
        caption_mapping_matrix.T,
        caption_weight_perturbation.T,
    )
    got = [blocks[0]] + [swapped(blocks[k], "tensor", k) for k in range(1, count)]

    (image,) = call(
        functools.partial(project_kernel, share),
        [((rows, 2 * cols), bf16)],
        plain,
        picture_averaged_encodings,
        picture_mapping_matrix.T,
        picture_weight_perturbation.T,
        after=(got[1],),
    )
    image_other = swapped(image, "dp", 1)
    image_far = swapped(image, "tensor", 2)
    image_far_other = swapped(image_other, "tensor", 2)

    block_ids = jnp.arange(data_count, dtype=jnp.int32)
    slots = ((block_ids ^ data_rank) >> 1) + planes * ((block_ids ^ data_rank) & 1)
    mine, other = call(
        functools.partial(turn_kernel, share),
        [((planes * size, 2 * rows), bf16)] * 2,
        plain,
        starts,
        slots,
        picture_averaged_encodings,
        caption_averaged_encodings,
        after=(image,),
    )
    other = swapped(other, "dp", 1)

    (text,) = call(
        functools.partial(text_rows_kernel, main, tail),
        [((share, 2 * width), bf16)],
        *got,
        after=(image, mine),
    )
    text_two = swapped(text, "dp", 4)
    text_one = swapped(text, "dp", 2)
    text_three = swapped(text_two, "dp", 2)
    texts = [text, text_one, text_two, text_three]

    (near,) = call(
        stack_kernel,
        [((4 * rows, wide), bf16)],
        image,
        image_other,
        image_far,
        image_far_other,
        after=(text_one, text_two, other),
    )
    far = swapped(near, "tensor", 1)
    unit, tangent, half, tangent_half, factors = call(
        functools.partial(image_rows_kernel, main, tail, count),
        [
            ((2 * rows, width), f32),
            ((2 * rows, width), f32),
            ((2 * rows, width), bf16),
            ((2 * rows, width), bf16),
            ((2, 2 * rows, 128), f32),
        ],
        near,
        far,
    )

    scalars = jnp.concatenate([sharpness_multiplier, offset_additive])
    outs = call(
        functools.partial(text_block_kernel, planes),
        [((share, width), f32)]
        + [((share, width), bf16)] * (planes - 1)
        + [((planes * share, width), bf16)] * 2
        + [((2 * rows, planes * share), bf16)] * 2,
        (tensor_rank * share).astype(jnp.int32).reshape(1),
        scalars,
        half,
        tangent_half,
        *texts,
    )
    kept, sent = call(
        functools.partial(image_block_kernel, main, tail),
        [((2 * rows, wide), f32)] * 2,
        scalars,
        unit,
        tangent,
        factors,
        *outs[planes:],
    )

    got = [swapped(outs[k], "dp", 2 * k) for k in range(1, planes)]
    blocks = call(
        functools.partial(text_sum_kernel, main, tail),
        [((share, cols), bf16)] * count,
        outs[0],
        *got,
    )
    got = [blocks[0]] + [swapped(blocks[k], "tensor", k) for k in range(1, count)]
    (text_back,) = call(stack_kernel, [((rows, cols), bf16)], *got)
    text_back_other = swapped(text_back, "dp", 1)

    near = (tensor_rank // 2 * (2 * share)).astype(jnp.int32).reshape(1)
    far = ((tensor_rank // 2 ^ 1) * (2 * share)).astype(jnp.int32).reshape(1)
    total, to_y, to_x = call(
        functools.partial(image_pair_kernel, main, tail),
        [((rows, 2 * cols), f32)] + [((rows + share, 2 * cols), bf16)] * 2,
        near,
        kept,
        swapped(sent, "tensor", 1),
    )
    flat = [(source, source ^ (count + 2)) for source in range(data_count * count)]
    image_back, image_back_other = call(
        functools.partial(image_sum_kernel, main, tail),
        [((rows, cols), bf16)] * 2,
        near,
        far,
        total,
        swapped(to_x, "tensor", 2),
        swapped(to_y, "dp", 1),
        lax.ppermute(to_x, ("dp", "tensor"), flat),
    )

    products = call(
        functools.partial(head_kernel, main, tail),
        [((size, 2 * cols), f32)] + [((size, 2 * cols), bf16)] * (planes - 1),
        mine,
        other,
        image_back,
        image_back_other,
        text_back,
        text_back_other,
    )
    got = [swapped(products[k], "dp", 2 * k) for k in range(1, planes)]
    return tuple(
        call(
            functools.partial(final_kernel, main, tail),
            [((size, cols), f32)] * 2,
            products[0],
            *got,
        )
    )


def fits(mesh):
    return mesh.shape["tensor"] == 4 and mesh.shape["dp"] == 8


def solution(mesh):
    in_specs = (
        P("dp", None),
        P("dp", None),
        P(None, "tensor"),
        P(None, "tensor"),
        P(None, "tensor"),
        P(None, "tensor"),
        P(),
        P(),
    )
    out_specs = (P("dp", "tensor"), P("dp", "tensor"))
    local = packed if fits(mesh) else general
    return jax.shard_map(local, mesh=mesh, in_specs=in_specs, out_specs=out_specs, check_vma=False)
```

```python
import functools

import jax
import jax.numpy as jnp
from jax import lax
from jax.experimental import pallas as pl
from jax.experimental.pallas import tpu as pltpu
from jax.sharding import PartitionSpec as P

EPS = 1e-06


def swapped(value, axis, mask):
    count = lax.axis_size(axis)
    return lax.ppermute(value, axis, [(source, source ^ mask) for source in range(count)])


def matmul(left, right):
    return jnp.dot(left, right, preferred_element_type=jnp.float32)


def matmul_nt(left, right):
    return lax.dot_general(
        left, right, (((1,), (1,)), ((), ())), preferred_element_type=jnp.float32
    )


def matmul_tn(left, right):
    return lax.dot_general(
        left, right, (((0,), (0,)), ((), ())), preferred_element_type=jnp.float32
    )


def unit_parts(raw, raw_rate):
    values = raw.astype(jnp.float32)
    tangent = raw_rate.astype(jnp.float32)
    radius = jnp.sqrt(jnp.sum(values * values, axis=1, keepdims=True) + EPS)
    unit = values / radius
    rate = jnp.sum(unit * tangent, axis=1, keepdims=True)
    unit_tangent = (tangent - unit * rate) / radius
    return (unit, unit_tangent, radius, rate)


def unit_backward(unit, unit_tangent, radius, rate, grad, grad_rate):
    inner = jnp.sum(unit * grad, axis=1, keepdims=True)
    inner_rate = jnp.sum(unit_tangent * grad + unit * grad_rate, axis=1, keepdims=True)
    first = (grad - unit * inner) / radius
    return (grad_rate - unit_tangent * inner - unit * inner_rate - first * rate) / radius


def general(
    picture_averaged_encodings,
    caption_averaged_encodings,
    picture_mapping_matrix,
    caption_mapping_matrix,
    picture_weight_perturbation,
    caption_weight_perturbation,
    sharpness_multiplier,
    offset_additive,
):
    similarity_multiplier = sharpness_multiplier[0]
    logit_bias = offset_additive[0]
    tensor_rank = lax.axis_index("tensor")
    data_rank = lax.axis_index("dp")
    tensor_count = lax.axis_size("tensor")
    data_count = lax.axis_size("dp")
    planes = data_count // 2
    rows, width = picture_averaged_encodings.shape
    cols = picture_mapping_matrix.shape[1]
    share = rows // tensor_count
    out_rows = width // data_count
    half = jnp.bfloat16

    text = jnp.stack(
        [
            matmul(caption_averaged_encodings, caption_mapping_matrix).astype(half),
            matmul(caption_averaged_encodings, caption_weight_perturbation).astype(half),
        ]
    )
    image = jnp.stack(
        [
            matmul(picture_averaged_encodings, picture_mapping_matrix).astype(half),
            matmul(picture_averaged_encodings, picture_weight_perturbation).astype(half),
        ]
    )

    def share_of(value, axis, mask):
        start = (tensor_rank ^ mask) * share
        return lax.dynamic_slice_in_dim(value, start, share, axis)

    parts = [share_of(text, 1, 0)]
    for mask in range(1, tensor_count):
        parts.append(swapped(share_of(text, 1, mask), "tensor", mask))
    text = jnp.concatenate(parts, axis=2)
    slots = [text] + [swapped(text, "dp", 2 * mask) for mask in range(1, planes)]

    image = jnp.concatenate([image, swapped(image, "dp", 1)], axis=1)
    blocks = [image]
    mask = tensor_count // 2
    image_blocks = {0: image}
    while mask >= 1:
        held = sorted(image_blocks)
        sent = jnp.concatenate([image_blocks[k] for k in held], axis=2)
        got = swapped(sent, "tensor", mask)
        for place, k in enumerate(held):
            image_blocks[k ^ mask] = got[:, :, place * cols : (place + 1) * cols]
        mask //= 2
    image = jnp.concatenate([image_blocks[k] for k in range(tensor_count)], axis=2)
    text = jnp.concatenate(slots, axis=1)

    def out_columns(value, rank):
        taken = [
            lax.dynamic_slice_in_dim(value, (rank ^ (2 * mask)) * out_rows, out_rows, 1)
            for mask in range(planes)
        ]
        return jnp.concatenate(taken, axis=1)

    def plane_encodings(value):
        other = swapped(out_columns(value, data_rank ^ 1), "dp", 1)
        return jnp.concatenate([out_columns(value, data_rank), other], axis=0)

    picture_plane = plane_encodings(picture_averaged_encodings)
    ordered = jnp.concatenate(
        [share_of(caption_averaged_encodings, 0, mask) for mask in range(tensor_count)], axis=0
    )
    caption_plane = plane_encodings(ordered)

    image_unit, image_tangent, image_radius, image_rate = unit_parts(image[0], image[1])
    text_unit, text_tangent, text_radius, text_rate = unit_parts(text[0], text[1])
    image_half = image_unit.astype(half)
    image_tangent_half = image_tangent.astype(half)
    text_half = text_unit.astype(half)
    text_tangent_half = text_tangent.astype(half)

    logits = similarity_multiplier * matmul_nt(text_half, image_half) + logit_bias
    logit_rate = similarity_multiplier * (
        matmul_nt(text_half, image_tangent_half) + matmul_nt(text_tangent_half, image_half)
    )
    probability = jax.nn.sigmoid(logits)
    text_ids = lax.broadcasted_iota(jnp.int32, (logits.shape[0], 1), 0)
    image_ids = lax.broadcasted_iota(jnp.int32, (1, logits.shape[1]), 1)
    positive = ((text_ids < share) & (text_ids + tensor_rank * share == image_ids)).astype(
        jnp.float32
    )
    weight = (probability - positive).astype(half)
    weight_rate = (probability * (1.0 - probability) * logit_rate).astype(half)
    text_grad = similarity_multiplier * matmul(weight, image_half)
    text_grad_rate = similarity_multiplier * (
        matmul(weight_rate, image_half) + matmul(weight, image_tangent_half)
    )
    image_grad = similarity_multiplier * matmul_tn(weight, text_half)
    image_grad_rate = similarity_multiplier * (
        matmul_tn(weight_rate, text_half) + matmul_tn(weight, text_tangent_half)
    )

    text_back = unit_backward(
        text_unit, text_tangent, text_radius, text_rate, text_grad, text_grad_rate
    )
    image_back = unit_backward(
        image_unit, image_tangent, image_radius, image_rate, image_grad, image_grad_rate
    )

    total = text_back[:share]
    for mask in range(1, planes):
        sent = text_back[mask * share : (mask + 1) * share].astype(half)
        total = total + swapped(sent, "dp", 2 * mask).astype(jnp.float32)
    text_back = total.astype(half)
    parts = [text_back[:, :cols]]
    for mask in range(1, tensor_count):
        sent = text_back[:, mask * cols : (mask + 1) * cols]
        parts.append(swapped(sent, "tensor", mask))
    text_back = jnp.concatenate(parts, axis=0)
    text_back = jnp.concatenate([text_back, swapped(text_back, "dp", 1)], axis=0)

    image_blocks = {k: image_back[:, k * cols : (k + 1) * cols] for k in range(tensor_count)}
    mask = 1
    while mask < tensor_count:
        kept = [k for k in sorted(image_blocks) if not k & mask]
        sent = jnp.concatenate([image_blocks[k ^ mask] for k in kept], axis=1)
        got = swapped(sent, "tensor", mask).astype(jnp.float32)
        image_blocks = {
            k: image_blocks[k] + got[:, place * cols : (place + 1) * cols]
            for place, k in enumerate(kept)
        }
        mask *= 2
    image_back = image_blocks[0]
    got = swapped(image_back, "dp", 1)
    image_back = (
        image_back + jnp.concatenate([got[rows:], got[:rows]], axis=0)
    ).astype(half)

    def head(encodings, back):
        product = matmul_tn(encodings, back)
        total = product[:out_rows]
        for mask in range(1, planes):
            sent = product[mask * out_rows : (mask + 1) * out_rows].astype(half)
            total = total + swapped(sent, "dp", 2 * mask).astype(jnp.float32)
        return total

    return (head(picture_plane, image_back), head(caption_plane, text_back))


def call(kernel, outs, *args, after=()):
    count = len(args)

    def body(*refs):
        kernel(*refs[:count], *refs[count + len(after) :])

    def place(value):
        scalar = value.ndim == 1
        return pl.BlockSpec(memory_space=pltpu.SMEM if scalar else pltpu.VMEM)

    return pl.pallas_call(
        body,
        out_shape=[jax.ShapeDtypeStruct(shape, dtype) for shape, dtype in outs],
        in_specs=[place(value) for value in args]
        + [pl.BlockSpec(memory_space=pl.ANY) for _ in after],
        out_specs=[pl.BlockSpec(memory_space=pltpu.VMEM) for _ in outs],
        compiler_params=pltpu.CompilerParams(vmem_limit_bytes=48 * 1024 * 1024),
    )(*args, *after)


def project_kernel(share, starts, encodings, weight, direction, *outs):
    main = weight.shape[0] // 128 * 128
    left = jnp.concatenate(
        [
            encodings[pl.ds(pl.multiple_of(starts[k], 16), share), :]
            for k in range(starts.shape[0])
        ],
        axis=0,
    )
    tails = jnp.concatenate([weight[main:, :], direction[main:, :]], axis=0)
    for right, first in ((weight[:main, :], 0), (direction[:main, :], main), (tails, 2 * main)):
        product = matmul_nt(left, right).astype(jnp.bfloat16)
        place = 0
        for out in outs:
            rows = out.shape[0]
            out[:, first : first + right.shape[0]] = product[place : place + rows]
            place += rows


def gathered(blocks, main, tail, which):
    first = 2 * main + which * tail
    mains = [block[:, which * main : (which + 1) * main] for block in blocks]
    tails = [block[:, first : first + tail] for block in blocks]
    return jnp.concatenate(mains + tails, axis=1)


def relay_kernel(mine, got, out):
    rows = mine.shape[0]
    out[:rows, :] = mine[...]
    out[rows:, :] = got[rows:, :]


def text_rows_kernel(main, tail, own, far, near, out):
    rows, width = own.shape[0], out.shape[1] // 2
    parts = (own[...], near[:rows, :], far[:rows, :], near[rows:, :])
    blocks = [part.astype(jnp.float32) for part in parts]
    out[:, :width] = gathered(blocks, main, tail, 0).astype(jnp.bfloat16)
    out[:, width:] = gathered(blocks, main, tail, 1).astype(jnp.bfloat16)


def row_factors(values, tangent):
    squares = jnp.sum(values * values, axis=1, keepdims=True)
    cross = jnp.sum(values * tangent, axis=1, keepdims=True)
    inverse = 1.0 / jnp.sqrt(squares + EPS)
    return inverse, cross * inverse


def unit_rows(values, tangent, inverse, rate):
    unit = values * inverse
    return unit, (tangent - unit * rate) * inverse


def back_rows(unit, tangent, inverse, rate, grad, grad_rate):
    inner = jnp.sum(unit * grad, axis=1, keepdims=True)
    inner_rate = jnp.sum(tangent * grad + unit * grad_rate, axis=1, keepdims=True)
    scaled = rate * inverse
    return (
        grad_rate - tangent * inner - grad * scaled + unit * (inner * scaled - inner_rate)
    ) * inverse


STEP = 48


def image_rows_kernel(main, tail, count, near, far, unit, tangent, half, tangent_half, factors):
    rows = unit.shape[0] // 2
    for shard in range(2):
        held = [
            (near, far)[k % 2].at[pl.ds((k - k % 2 + shard) * rows, rows), :] for k in range(count)
        ]

        @pl.loop(0, rows // STEP)
        def _(step):
            here = pl.ds(pl.multiple_of(step * STEP, STEP), STEP)
            there = pl.ds(pl.multiple_of(shard * rows + step * STEP, STEP), STEP)
            parts = [block[here, :].astype(jnp.float32) for block in held]
            values = gathered(parts, main, tail, 0)
            rates = gathered(parts, main, tail, 1)
            inverse, rate = row_factors(values, rates)
            one, two = unit_rows(values, rates, inverse, rate)
            unit[there, :] = one
            tangent[there, :] = two
            half[there, :] = one.astype(jnp.bfloat16)
            tangent_half[there, :] = two.astype(jnp.bfloat16)
            factors[0, there, :] = jnp.broadcast_to(inverse, (STEP, 128))
            factors[1, there, :] = jnp.broadcast_to(rate, (STEP, 128))


def text_block_kernel(slots, start, scalars, half, tangent_half, *refs):
    texts, refs = refs[:slots], refs[slots:]
    sums, refs = refs[:slots], refs[slots:]
    text_half, text_tangent_half, weight_turned, weight_rate_turned = refs
    f32, bf16 = jnp.float32, jnp.bfloat16
    share, width = texts[0].shape[0], texts[0].shape[1] // 2
    multiplier, bias = scalars[0], scalars[1]

    text_parts = []
    for slot, text in enumerate(texts):
        here = slice(slot * share, (slot + 1) * share)
        values, rates = text[:, :width].astype(f32), text[:, width:].astype(f32)
        inverse, rate = row_factors(values, rates)
        unit, tangent = unit_rows(values, rates, inverse, rate)
        text_parts.append((unit, tangent, inverse, rate))
        text_half[here, :] = unit.astype(bf16)
        text_tangent_half[here, :] = tangent.astype(bf16)

    logits = multiplier * matmul_nt(text_half[...], half[...]) + bias
    logit_rate = multiplier * (
        matmul_nt(text_half[...], tangent_half[...])
        + matmul_nt(text_tangent_half[...], half[...])
    )
    probability = jax.nn.sigmoid(logits)
    text_ids = lax.broadcasted_iota(jnp.int32, logits.shape, 0)
    image_ids = lax.broadcasted_iota(jnp.int32, logits.shape, 1)
    positive = jnp.where((text_ids < share) & (text_ids + start[0] == image_ids), 1.0, 0.0)
    weight = probability - positive
    weight_rate = probability * (1.0 - probability) * logit_rate
    weight_half, weight_rate_half = weight.astype(bf16), weight_rate.astype(bf16)

    text_grad = multiplier * matmul(weight_half, half[...])
    text_grad_rate = multiplier * (
        matmul(weight_rate_half, half[...]) + matmul(weight_half, tangent_half[...])
    )
    for slot, (unit, tangent, inverse, rate) in enumerate(text_parts):
        here = slice(slot * share, (slot + 1) * share)
        back = back_rows(unit, tangent, inverse, rate, text_grad[here], text_grad_rate[here])
        sums[slot][...] = back.astype(sums[slot].dtype)
    weight_turned[...] = weight.T.astype(bf16)
    weight_rate_turned[...] = weight_rate.T.astype(bf16)


def image_block_kernel(
    main,
    tail,
    scalars,
    unit,
    tangent,
    factors,
    text_half,
    text_tangent_half,
    weight,
    weight_rate,
    kept,
    sent,
):
    rows = unit.shape[0] // 2
    count = 4
    multiplier = scalars[0]
    for shard in range(2):
        here = slice(shard * rows, (shard + 1) * rows)
        grad = multiplier * matmul(weight[here, :], text_half[...])
        grad_rate = multiplier * (
            matmul(weight_rate[here, :], text_half[...])
            + matmul(weight[here, :], text_tangent_half[...])
        )
        back = back_rows(
            unit[here, :],
            tangent[here, :],
            factors[0, here, :1],
            factors[1, here, :1],
            grad,
            grad_rate,
        )
        for k in range(count):
            out = (kept, sent)[k % 2]
            to = slice(k // 2 * rows, (k // 2 + 1) * rows)
            out[to, shard * main : (shard + 1) * main] = back[:, k * main : (k + 1) * main]
            first = 2 * main + shard * tail
            taken = count * main + k * tail
            out[to, first : first + tail] = back[:, taken : taken + tail]


def text_sum_kernel(main, tail, own, *refs):
    count = own.shape[1] // (main + tail)
    got, outs = refs[:-count], refs[-count:]
    total = own[...]
    for ref in got:
        total = total + ref[...].astype(jnp.float32)
    for k, out in enumerate(outs):
        first = count * main + k * tail
        out[:, :main] = total[:, k * main : (k + 1) * main].astype(jnp.bfloat16)
        out[:, main:] = total[:, first : first + tail].astype(jnp.bfloat16)


def stack_kernel(*refs):
    rows = refs[0].shape[0]
    for k, ref in enumerate(refs[:-1]):
        refs[-1][k * rows : (k + 1) * rows, : ref.shape[1]] = ref[...]


def place_kernel(starts, *refs):
    rows = refs[0].shape[0]
    for k, ref in enumerate(refs[:-1]):
        refs[-1][pl.ds(pl.multiple_of(starts[k], 16), rows), :] = ref[...]


def turn_kernel(places, core, picture, caption, mine, other):
    for which, encodings in enumerate((picture, caption)):
        turned = encodings[...].astype(jnp.float32).T.astype(jnp.bfloat16)
        count = places.shape[0]
        size, rows = turned.shape[0] // count, turned.shape[1]
        fold = count // 4
        for block in range(count):
            taken = turned[block * size : (block + 1) * size, :]
            slot = places[block]
            at = pl.multiple_of(slot % fold * size, 16)
            for half in range(2):
                lanes = slice(half * rows, (half + 1) * rows)

                @pl.when(slot // fold == half)
                def _():
                    mine[pl.ds(which * fold * size + at, size), lanes] = taken

                @pl.when((slot // fold == 2 + half) & (core[0] == which))
                def _():
                    other[pl.ds(at, size), lanes] = taken


def image_pair_kernel(main, tail, near, kept, got, total, *outs):
    rows, width = total.shape
    size = outs[0].shape[0] - rows
    start = pl.multiple_of(near[0], 16)
    total[...] = kept[:rows, :width] + got[:rows, :width]
    for which, out in enumerate(outs):
        here = slice(which * rows, (which + 1) * rows)
        out[:rows, :] = (kept[here, :width] + got[here, :width]).astype(jnp.bfloat16)
        for fold in range(2):
            at = pl.ds(pl.multiple_of(which * rows + start + fold * size, 16), size)
            there = pl.ds(pl.multiple_of(start + fold * size, 16), size)
            left = kept[at, :width] + got[at, :width] - out[there, :].astype(jnp.float32)
            out[rows:, fold * main : (fold + 1) * main] = left[:, :main].astype(jnp.bfloat16)
            first = 2 * main + fold * tail
            out[rows:, first : first + tail] = left[:, 2 * main : 2 * main + tail].astype(
                jnp.bfloat16
            )


def image_sum_kernel(main, tail, near, far, total, over_x, over_y, over_both, *outs):
    rows = total.shape[0]
    size = over_x.shape[0] - rows
    for shard, out in enumerate(outs):
        for first, step, at, width in ((0, main, 0, main), (2 * main, tail, main, tail)):
            same = slice(first + shard * step, first + shard * step + step)
            other = slice(first + (1 - shard) * step, first + (1 - shard) * step + step)
            for part in range(rows // size):
                here = slice(part * size, (part + 1) * size)
                value = total[here, same] + over_x[here, same].astype(jnp.float32)
                value += over_y[here, other].astype(jnp.float32)
                value += over_both[here, other].astype(jnp.float32)
                sources = ((over_x, far),) if shard == 0 else ((over_y, near), (over_both, far))
                for source, start in sources:
                    for fold in range(2):
                        lanes = slice(first + fold * step, first + fold * step + step)
                        left = source[rows:, lanes].astype(jnp.float32)
                        mine = start[0] + fold * size == part * size
                        value += jnp.where(mine, left, 0.0)
                out[here, at : at + width] = value.astype(jnp.bfloat16)


def folds(rows, main, tail):
    across = main // tail
    for k in range(rows // 16):
        here = slice(k * 16, (k + 1) * 16)
        at = rows + k // across * 16
        first = k % across * tail
        yield here, slice(at, at + 16), slice(first, first + tail)


def head_kernel(main, tail, head, core, mine, near, far, back, back_other, own, *sent):
    size, rows = own.shape[0], back.shape[0]
    fold = (len(sent) + 1) // 2
    other = jnp.where(core[0] == head, near[...], far[...])
    for half in range(2):
        here = slice(head * fold * size, (head + 1) * fold * size)
        lanes = slice(half * rows, (half + 1) * rows)
        product = matmul(mine[here, lanes], back[...]) + matmul(other[:, lanes], back_other[...])
        for place in range(fold):
            part = product[place * size : (place + 1) * size]
            slot = half * fold + place
            if slot == 0:
                own[...] = part
                continue
            part = part.astype(jnp.bfloat16)
            out = sent[slot - 1]
            out[:size, :] = part[:, :main]
            for rows_in, rows_out, lanes_out in folds(size, main, tail):
                out[rows_out, lanes_out] = part[rows_in, main:]


def final_kernel(main, tail, own, *refs):
    got, out = refs[:-1], refs[-1]
    size = own.shape[0]
    total = own[:, :main]
    for ref in got:
        total = total + ref[:size, :].astype(jnp.float32)
    out[:, :main] = total
    for rows_in, rows_out, lanes_out in folds(size, main, tail):
        total = own[rows_in, main:]
        for ref in got:
            total = total + ref[rows_out, lanes_out].astype(jnp.float32)
        out[rows_in, main:] = total


def packed(
    picture_averaged_encodings,
    caption_averaged_encodings,
    picture_mapping_matrix,
    caption_mapping_matrix,
    picture_weight_perturbation,
    caption_weight_perturbation,
    sharpness_multiplier,
    offset_additive,
):
    tensor_rank = lax.axis_index("tensor")
    data_rank = lax.axis_index("dp")
    count = lax.axis_size("tensor")
    data_count = lax.axis_size("dp")
    planes = data_count // 2
    rows, width = picture_averaged_encodings.shape
    cols = picture_mapping_matrix.shape[1]
    main = cols // 128 * 128
    tail = cols - main
    share = rows // count
    size = width // data_count
    wide = -(-2 * cols // 128) * 128
    f32, bf16 = jnp.float32, jnp.bfloat16
    ranks = jnp.arange(count, dtype=jnp.int32)
    starts = (ranks ^ tensor_rank) * share
    plain = ranks * share

    blocks = call(
        functools.partial(project_kernel, share),
        [((share, 2 * cols), bf16)] * 2 + [((2 * share, 2 * cols), bf16)],
        starts,
        caption_averaged_encodings,
        caption_mapping_matrix.T,
        caption_weight_perturbation.T,
    )
    text_far = swapped(blocks[2], "tensor", 2)
    (relay,) = call(relay_kernel, [((2 * share, 2 * cols), bf16)], blocks[1], text_far)
    text_near = swapped(relay, "tensor", 1)

    (image,) = call(
        functools.partial(project_kernel, share),
        [((rows, 2 * cols), bf16)],
        plain,
        picture_averaged_encodings,
        picture_mapping_matrix.T,
        picture_weight_perturbation.T,
        after=(blocks[0],),
    )
    image_other = swapped(image, "dp", 1)
    image_far = swapped(image, "tensor", 2)
    image_far_other = swapped(image_other, "tensor", 2)

    (text,) = call(
        functools.partial(text_rows_kernel, main, tail),
        [((share, 2 * width), bf16)],
        blocks[0],
        text_far,
        text_near,
    )
    text_two = swapped(text, "dp", 4)
    text_one = swapped(text, "dp", 2)
    text_three = swapped(text_two, "dp", 2)
    texts = [text, text_one, text_two, text_three]

    block_ids = jnp.arange(data_count, dtype=jnp.int32)
    slots = ((block_ids ^ data_rank) >> 1) + planes * ((block_ids ^ data_rank) & 1)
    core = (tensor_rank & 1).astype(jnp.int32).reshape(1)
    mine, other = call(
        turn_kernel,
        [((planes * size, 2 * rows), bf16), ((planes // 2 * size, 2 * rows), bf16)],
        slots,
        core,
        picture_averaged_encodings,
        caption_averaged_encodings,
        after=(image,),
    )
    other = swapped(other, "dp", 1)
    others = (other, swapped(other, "tensor", 1))

    (near,) = call(
        stack_kernel,
        [((4 * rows, wide), bf16)],
        image,
        image_other,
        image_far,
        image_far_other,
        after=(text_one, text_two, others[0]),
    )
    far = swapped(near, "tensor", 1)
    unit, tangent, half, tangent_half, factors = call(
        functools.partial(image_rows_kernel, main, tail, count),
        [
            ((2 * rows, width), f32),
            ((2 * rows, width), f32),
            ((2 * rows, width), bf16),
            ((2 * rows, width), bf16),
            ((2, 2 * rows, 128), f32),
        ],
        near,
        far,
    )

    scalars = jnp.concatenate([sharpness_multiplier, offset_additive])
    outs = call(
        functools.partial(text_block_kernel, planes),
        [((share, width), f32)]
        + [((share, width), bf16)] * (planes - 1)
        + [((planes * share, width), bf16)] * 2
        + [((2 * rows, planes * share), bf16)] * 2,
        (tensor_rank * share).astype(jnp.int32).reshape(1),
        scalars,
        half,
        tangent_half,
        *texts,
    )
    kept, sent = call(
        functools.partial(image_block_kernel, main, tail),
        [((2 * rows, wide), f32)] * 2,
        scalars,
        unit,
        tangent,
        factors,
        *outs[planes:],
    )

    got = [swapped(outs[k], "dp", 2 * k) for k in range(1, planes)]
    blocks = call(
        functools.partial(text_sum_kernel, main, tail),
        [((share, cols), bf16)] * count,
        outs[0],
        *got,
    )
    got = [blocks[0]] + [swapped(blocks[k], "tensor", k) for k in range(1, count)]
    (text_back,) = call(place_kernel, [((rows, cols), bf16)], starts, *got)
    text_back_other = swapped(text_back, "dp", 1)

    near = (tensor_rank // 2 * (2 * share)).astype(jnp.int32).reshape(1)
    far = ((tensor_rank // 2 ^ 1) * (2 * share)).astype(jnp.int32).reshape(1)
    total, to_y, to_x = call(
        functools.partial(image_pair_kernel, main, tail),
        [((rows, 2 * cols), f32)] + [((rows + share, 2 * cols), bf16)] * 2,
        near,
        kept,
        swapped(sent, "tensor", 1),
    )
    flat = [(source, source ^ (count + 2)) for source in range(data_count * count)]
    image_back, image_back_other = call(
        functools.partial(image_sum_kernel, main, tail),
        [((rows, cols), bf16)] * 2,
        near,
        far,
        total,
        swapped(to_x, "tensor", 2),
        swapped(to_y, "dp", 1),
        lax.ppermute(to_x, ("dp", "tensor"), flat),
    )

    tall = size + -(-size // 16 // (main // tail)) * 16

    def head(which, back, back_other):
        products = call(
            functools.partial(head_kernel, main, tail, which),
            [((size, cols), f32)] + [((tall, main), bf16)] * (planes - 1),
            core,
            mine,
            *others,
            back,
            back_other,
        )
        got = [swapped(products[k], "dp", 2 * k) for k in range(1, planes)]
        (out,) = call(
            functools.partial(final_kernel, main, tail), [((size, cols), f32)], products[0], *got
        )
        return out

    return head(0, image_back, image_back_other), head(1, text_back, text_back_other)


def fits(mesh):
    return mesh.shape["tensor"] == 4 and mesh.shape["dp"] == 8


def solution(mesh):
    in_specs = (
        P("dp", None),
        P("dp", None),
        P(None, "tensor"),
        P(None, "tensor"),
        P(None, "tensor"),
        P(None, "tensor"),
        P(),
        P(),
    )
    out_specs = (P("dp", "tensor"), P("dp", "tensor"))
    local = packed if fits(mesh) else general
    return jax.shard_map(local, mesh=mesh, in_specs=in_specs, out_specs=out_specs, check_vma=False)
```

```python
import functools

import jax
import jax.numpy as jnp
from jax import lax
from jax.experimental import pallas as pl
from jax.experimental.pallas import tpu as pltpu
from jax.sharding import PartitionSpec as P

EPS = 1e-06


def swapped(value, axis, mask):
    count = lax.axis_size(axis)
    return lax.ppermute(value, axis, [(source, source ^ mask) for source in range(count)])


def matmul(left, right):
    return jnp.dot(left, right, preferred_element_type=jnp.float32)


def matmul_nt(left, right):
    return lax.dot_general(
        left, right, (((1,), (1,)), ((), ())), preferred_element_type=jnp.float32
    )


def matmul_tn(left, right):
    return lax.dot_general(
        left, right, (((0,), (0,)), ((), ())), preferred_element_type=jnp.float32
    )


def unit_parts(raw, raw_rate):
    values = raw.astype(jnp.float32)
    tangent = raw_rate.astype(jnp.float32)
    radius = jnp.sqrt(jnp.sum(values * values, axis=1, keepdims=True) + EPS)
    unit = values / radius
    rate = jnp.sum(unit * tangent, axis=1, keepdims=True)
    unit_tangent = (tangent - unit * rate) / radius
    return (unit, unit_tangent, radius, rate)


def unit_backward(unit, unit_tangent, radius, rate, grad, grad_rate):
    inner = jnp.sum(unit * grad, axis=1, keepdims=True)
    inner_rate = jnp.sum(unit_tangent * grad + unit * grad_rate, axis=1, keepdims=True)
    first = (grad - unit * inner) / radius
    return (grad_rate - unit_tangent * inner - unit * inner_rate - first * rate) / radius


def general(
    picture_averaged_encodings,
    caption_averaged_encodings,
    picture_mapping_matrix,
    caption_mapping_matrix,
    picture_weight_perturbation,
    caption_weight_perturbation,
    sharpness_multiplier,
    offset_additive,
):
    similarity_multiplier = sharpness_multiplier[0]
    logit_bias = offset_additive[0]
    tensor_rank = lax.axis_index("tensor")
    data_rank = lax.axis_index("dp")
    tensor_count = lax.axis_size("tensor")
    data_count = lax.axis_size("dp")
    planes = data_count // 2
    rows, width = picture_averaged_encodings.shape
    cols = picture_mapping_matrix.shape[1]
    share = rows // tensor_count
    out_rows = width // data_count
    half = jnp.bfloat16

    text = jnp.stack(
        [
            matmul(caption_averaged_encodings, caption_mapping_matrix).astype(half),
            matmul(caption_averaged_encodings, caption_weight_perturbation).astype(half),
        ]
    )
    image = jnp.stack(
        [
            matmul(picture_averaged_encodings, picture_mapping_matrix).astype(half),
            matmul(picture_averaged_encodings, picture_weight_perturbation).astype(half),
        ]
    )

    def share_of(value, axis, mask):
        start = (tensor_rank ^ mask) * share
        return lax.dynamic_slice_in_dim(value, start, share, axis)

    parts = [share_of(text, 1, 0)]
    for mask in range(1, tensor_count):
        parts.append(swapped(share_of(text, 1, mask), "tensor", mask))
    text = jnp.concatenate(parts, axis=2)
    slots = [text] + [swapped(text, "dp", 2 * mask) for mask in range(1, planes)]

    image = jnp.concatenate([image, swapped(image, "dp", 1)], axis=1)
    blocks = [image]
    mask = tensor_count // 2
    image_blocks = {0: image}
    while mask >= 1:
        held = sorted(image_blocks)
        sent = jnp.concatenate([image_blocks[k] for k in held], axis=2)
        got = swapped(sent, "tensor", mask)
        for place, k in enumerate(held):
            image_blocks[k ^ mask] = got[:, :, place * cols : (place + 1) * cols]
        mask //= 2
    image = jnp.concatenate([image_blocks[k] for k in range(tensor_count)], axis=2)
    text = jnp.concatenate(slots, axis=1)

    def out_columns(value, rank):
        taken = [
            lax.dynamic_slice_in_dim(value, (rank ^ (2 * mask)) * out_rows, out_rows, 1)
            for mask in range(planes)
        ]
        return jnp.concatenate(taken, axis=1)

    def plane_encodings(value):
        other = swapped(out_columns(value, data_rank ^ 1), "dp", 1)
        return jnp.concatenate([out_columns(value, data_rank), other], axis=0)

    picture_plane = plane_encodings(picture_averaged_encodings)
    ordered = jnp.concatenate(
        [share_of(caption_averaged_encodings, 0, mask) for mask in range(tensor_count)], axis=0
    )
    caption_plane = plane_encodings(ordered)

    image_unit, image_tangent, image_radius, image_rate = unit_parts(image[0], image[1])
    text_unit, text_tangent, text_radius, text_rate = unit_parts(text[0], text[1])
    image_half = image_unit.astype(half)
    image_tangent_half = image_tangent.astype(half)
    text_half = text_unit.astype(half)
    text_tangent_half = text_tangent.astype(half)

    logits = similarity_multiplier * matmul_nt(text_half, image_half) + logit_bias
    logit_rate = similarity_multiplier * (
        matmul_nt(text_half, image_tangent_half) + matmul_nt(text_tangent_half, image_half)
    )
    probability = jax.nn.sigmoid(logits)
    text_ids = lax.broadcasted_iota(jnp.int32, (logits.shape[0], 1), 0)
    image_ids = lax.broadcasted_iota(jnp.int32, (1, logits.shape[1]), 1)
    positive = ((text_ids < share) & (text_ids + tensor_rank * share == image_ids)).astype(
        jnp.float32
    )
    weight = (probability - positive).astype(half)
    weight_rate = (probability * (1.0 - probability) * logit_rate).astype(half)
    text_grad = similarity_multiplier * matmul(weight, image_half)
    text_grad_rate = similarity_multiplier * (
        matmul(weight_rate, image_half) + matmul(weight, image_tangent_half)
    )
    image_grad = similarity_multiplier * matmul_tn(weight, text_half)
    image_grad_rate = similarity_multiplier * (
        matmul_tn(weight_rate, text_half) + matmul_tn(weight, text_tangent_half)
    )

    text_back = unit_backward(
        text_unit, text_tangent, text_radius, text_rate, text_grad, text_grad_rate
    )
    image_back = unit_backward(
        image_unit, image_tangent, image_radius, image_rate, image_grad, image_grad_rate
    )

    total = text_back[:share]
    for mask in range(1, planes):
        sent = text_back[mask * share : (mask + 1) * share].astype(half)
        total = total + swapped(sent, "dp", 2 * mask).astype(jnp.float32)
    text_back = total.astype(half)
    parts = [text_back[:, :cols]]
    for mask in range(1, tensor_count):
        sent = text_back[:, mask * cols : (mask + 1) * cols]
        parts.append(swapped(sent, "tensor", mask))
    text_back = jnp.concatenate(parts, axis=0)
    text_back = jnp.concatenate([text_back, swapped(text_back, "dp", 1)], axis=0)

    image_blocks = {k: image_back[:, k * cols : (k + 1) * cols] for k in range(tensor_count)}
    mask = 1
    while mask < tensor_count:
        kept = [k for k in sorted(image_blocks) if not k & mask]
        sent = jnp.concatenate([image_blocks[k ^ mask] for k in kept], axis=1)
        got = swapped(sent, "tensor", mask).astype(jnp.float32)
        image_blocks = {
            k: image_blocks[k] + got[:, place * cols : (place + 1) * cols]
            for place, k in enumerate(kept)
        }
        mask *= 2
    image_back = image_blocks[0]
    got = swapped(image_back, "dp", 1)
    image_back = (
        image_back + jnp.concatenate([got[rows:], got[:rows]], axis=0)
    ).astype(half)

    def head(encodings, back):
        product = matmul_tn(encodings, back)
        total = product[:out_rows]
        for mask in range(1, planes):
            sent = product[mask * out_rows : (mask + 1) * out_rows].astype(half)
            total = total + swapped(sent, "dp", 2 * mask).astype(jnp.float32)
        return total

    return (head(picture_plane, image_back), head(caption_plane, text_back))


def call(kernel, outs, *args, after=(), scratch=()):
    count = len(args)

    def body(*refs):
        kernel(*refs[:count], *refs[count + len(after) :])

    def place(value):
        scalar = value.ndim == 1
        return pl.BlockSpec(memory_space=pltpu.SMEM if scalar else pltpu.VMEM)

    return pl.pallas_call(
        body,
        out_shape=[jax.ShapeDtypeStruct(shape, dtype) for shape, dtype in outs],
        in_specs=[place(value) for value in args]
        + [pl.BlockSpec(memory_space=pl.ANY) for _ in after],
        out_specs=[pl.BlockSpec(memory_space=pltpu.VMEM) for _ in outs],
        scratch_shapes=[pltpu.VMEM(shape, dtype) for shape, dtype in scratch],
        compiler_params=pltpu.CompilerParams(vmem_limit_bytes=48 * 1024 * 1024),
    )(*args, *after)


def folds(rows, main, tail):
    across = main // tail
    for k in range(rows // 16):
        here = slice(k * 16, (k + 1) * 16)
        at = rows + k // across * 16
        first = k % across * tail
        yield here, slice(at, at + 16), slice(first, first + tail)


def folded_rows(rows, main, tail):
    return rows + -(-rows // 16 // (main // tail)) * 16


def fold(out, first, value, main):
    rows, cols = value.shape
    out[first : first + rows, :] = value[:, :main].astype(out.dtype)
    for here, there, lanes in folds(rows, main, cols - main):
        there = slice(first + there.start, first + there.stop)
        out[there, lanes] = value[here, main:].astype(out.dtype)


def unfold(ref, first, rows, main, tail):
    tails = [
        ref[first + there.start : first + there.stop, lanes]
        for _, there, lanes in folds(rows, main, tail)
    ]
    return jnp.concatenate([ref[first : first + rows, :], jnp.concatenate(tails, axis=0)], axis=1)


def project_kernel(share, starts, encodings, weight, direction, *outs):
    main = weight.shape[0] // 128 * 128
    left = jnp.concatenate(
        [
            encodings[pl.ds(pl.multiple_of(starts[k], 16), share), :]
            for k in range(starts.shape[0])
        ],
        axis=0,
    )
    tails = jnp.concatenate([weight[main:, :], direction[main:, :]], axis=0)
    for right, first in ((weight[:main, :], 0), (direction[:main, :], main), (tails, 2 * main)):
        product = matmul_nt(left, right).astype(jnp.bfloat16)
        place = 0
        for out in outs:
            rows = out.shape[0]
            out[:, first : first + right.shape[0]] = product[place : place + rows]
            place += rows


def gathered(blocks, main, tail, which):
    first = 2 * main + which * tail
    mains = [block[:, which * main : (which + 1) * main] for block in blocks]
    tails = [block[:, first : first + tail] for block in blocks]
    return jnp.concatenate(mains + tails, axis=1)


def relay_kernel(mine, got, out):
    rows = mine.shape[0]
    out[:rows, :] = mine[...]
    out[rows:, :] = got[rows:, :]


def text_rows_kernel(main, tail, own, far, near, out):
    rows, width = own.shape[0], out.shape[1] // 2
    parts = (own[...], near[:rows, :], far[:rows, :], near[rows:, :])
    blocks = [part.astype(jnp.float32) for part in parts]
    out[:, :width] = gathered(blocks, main, tail, 0).astype(jnp.bfloat16)
    out[:, width:] = gathered(blocks, main, tail, 1).astype(jnp.bfloat16)


def row_factors(values, tangent):
    squares = jnp.sum(values * values, axis=1, keepdims=True)
    cross = jnp.sum(values * tangent, axis=1, keepdims=True)
    inverse = 1.0 / jnp.sqrt(squares + EPS)
    return inverse, cross * inverse


def unit_rows(values, tangent, inverse, rate):
    unit = values * inverse
    return unit, (tangent - unit * rate) * inverse


def back_rows(unit, tangent, inverse, rate, grad, grad_rate):
    inner = jnp.sum(unit * grad, axis=1, keepdims=True)
    inner_rate = jnp.sum(tangent * grad + unit * grad_rate, axis=1, keepdims=True)
    scaled = rate * inverse
    return (
        grad_rate - tangent * inner - grad * scaled + unit * (inner * scaled - inner_rate)
    ) * inverse


STEP = 48


def image_rows_kernel(main, tail, count, near, far, unit, tangent, half, tangent_half, factors):
    rows = unit.shape[0] // 2
    for shard in range(2):
        held = [
            (near, far)[k % 2].at[pl.ds((k - k % 2 + shard) * rows, rows), :] for k in range(count)
        ]

        @pl.loop(0, rows // STEP)
        def _(step):
            here = pl.ds(pl.multiple_of(step * STEP, STEP), STEP)
            there = pl.ds(pl.multiple_of(shard * rows + step * STEP, STEP), STEP)
            parts = [block[here, :].astype(jnp.float32) for block in held]
            values = gathered(parts, main, tail, 0)
            rates = gathered(parts, main, tail, 1)
            inverse, rate = row_factors(values, rates)
            one, two = unit_rows(values, rates, inverse, rate)
            unit[there, :] = one
            tangent[there, :] = two
            half[there, :] = one.astype(jnp.bfloat16)
            tangent_half[there, :] = two.astype(jnp.bfloat16)
            factors[0, there, :] = jnp.broadcast_to(inverse, (STEP, 128))
            factors[1, there, :] = jnp.broadcast_to(rate, (STEP, 128))


def text_block_kernel(slots, start, scalars, half, tangent_half, *refs):
    texts, refs = refs[:slots], refs[slots:]
    sums, refs = refs[:slots], refs[slots:]
    text_half, text_tangent_half, weight_turned, weight_rate_turned = refs
    f32, bf16 = jnp.float32, jnp.bfloat16
    share, width = texts[0].shape[0], texts[0].shape[1] // 2
    multiplier, bias = scalars[0], scalars[1]

    text_parts = []
    for slot, text in enumerate(texts):
        here = slice(slot * share, (slot + 1) * share)
        values, rates = text[:, :width].astype(f32), text[:, width:].astype(f32)
        inverse, rate = row_factors(values, rates)
        unit, tangent = unit_rows(values, rates, inverse, rate)
        text_parts.append((unit, tangent, inverse, rate))
        text_half[here, :] = unit.astype(bf16)
        text_tangent_half[here, :] = tangent.astype(bf16)

    logits = multiplier * matmul_nt(text_half[...], half[...]) + bias
    logit_rate = multiplier * (
        matmul_nt(text_half[...], tangent_half[...])
        + matmul_nt(text_tangent_half[...], half[...])
    )
    probability = jax.nn.sigmoid(logits)
    text_ids = lax.broadcasted_iota(jnp.int32, logits.shape, 0)
    image_ids = lax.broadcasted_iota(jnp.int32, logits.shape, 1)
    positive = jnp.where((text_ids < share) & (text_ids + start[0] == image_ids), 1.0, 0.0)
    weight = probability - positive
    weight_rate = probability * (1.0 - probability) * logit_rate
    weight_half, weight_rate_half = weight.astype(bf16), weight_rate.astype(bf16)

    text_grad = multiplier * matmul(weight_half, half[...])
    text_grad_rate = multiplier * (
        matmul(weight_rate_half, half[...]) + matmul(weight_half, tangent_half[...])
    )
    for slot, (unit, tangent, inverse, rate) in enumerate(text_parts):
        here = slice(slot * share, (slot + 1) * share)
        back = back_rows(unit, tangent, inverse, rate, text_grad[here], text_grad_rate[here])
        sums[slot][...] = back.astype(sums[slot].dtype)
    weight_turned[...] = weight.T.astype(bf16)
    weight_rate_turned[...] = weight_rate.T.astype(bf16)


def image_block_kernel(
    main,
    tail,
    scalars,
    unit,
    tangent,
    factors,
    text_half,
    text_tangent_half,
    weight,
    weight_rate,
    kept,
    sent,
):
    rows = unit.shape[0] // 2
    count = 4
    multiplier = scalars[0]
    for shard in range(2):
        here = slice(shard * rows, (shard + 1) * rows)
        grad = multiplier * matmul(weight[here, :], text_half[...])
        grad_rate = multiplier * (
            matmul(weight_rate[here, :], text_half[...])
            + matmul(weight[here, :], text_tangent_half[...])
        )
        back = back_rows(
            unit[here, :],
            tangent[here, :],
            factors[0, here, :1],
            factors[1, here, :1],
            grad,
            grad_rate,
        )
        for k in range(count):
            out = (kept, sent)[k % 2]
            to = slice(k // 2 * rows, (k // 2 + 1) * rows)
            out[to, shard * main : (shard + 1) * main] = back[:, k * main : (k + 1) * main]
            first = 2 * main + shard * tail
            taken = count * main + k * tail
            out[to, first : first + tail] = back[:, taken : taken + tail]


def text_sum_kernel(main, tail, own, *refs):
    count = own.shape[1] // (main + tail)
    got, outs = refs[:-count], refs[-count:]
    total = own[...]
    for ref in got:
        total = total + ref[...].astype(jnp.float32)
    for k, out in enumerate(outs):
        first = count * main + k * tail
        out[:, :main] = total[:, k * main : (k + 1) * main].astype(jnp.bfloat16)
        out[:, main:] = total[:, first : first + tail].astype(jnp.bfloat16)


def stack_kernel(*refs):
    rows = refs[0].shape[0]
    for k, ref in enumerate(refs[:-1]):
        refs[-1][k * rows : (k + 1) * rows, : ref.shape[1]] = ref[...]


def fold_kernel(*refs):
    value = jnp.concatenate([ref[...] for ref in refs[:-1]], axis=0)
    fold(refs[-1], 0, value, refs[-1].shape[1])


def turn_kernel(places, core, picture, caption, mine, other):
    for which, encodings in enumerate((picture, caption)):
        turned = encodings[...].astype(jnp.float32).T.astype(jnp.bfloat16)
        count = places.shape[0]
        size, rows = turned.shape[0] // count, turned.shape[1]
        fold = count // 4
        for block in range(count):
            taken = turned[block * size : (block + 1) * size, :]
            slot = places[block]
            at = pl.multiple_of(slot % fold * size, 16)
            for half in range(2):
                lanes = slice(half * rows, (half + 1) * rows)

                @pl.when(slot // fold == half)
                def _():
                    mine[pl.ds(which * fold * size + at, size), lanes] = taken

                @pl.when((slot // fold == 2 + half) & (core[0] == which))
                def _():
                    other[pl.ds(at, size), lanes] = taken


def shard_columns(value, main, tail, shard):
    at = 2 * main + shard * tail
    return jnp.concatenate(
        [value[:, shard * main : (shard + 1) * main], value[:, at : at + tail]], axis=1
    )


def image_pair_kernel(main, tail, share, near, kept, got, total, over_x, over_y, over_both):
    rows = total.shape[0]
    ours = kept[:rows, :] + got[:rows, :]
    theirs = kept[rows:, :] + got[rows:, :]
    total[...] = shard_columns(ours, main, tail, 0)
    fold(over_y, 0, shard_columns(ours, main, tail, 1), main)
    fold(over_both, 0, shard_columns(theirs, main, tail, 1), main)
    value = shard_columns(theirs, main, tail, 0)
    rounded = value.astype(jnp.bfloat16)
    fold(over_x, 0, rounded, main)
    left = value - rounded.astype(jnp.float32)
    left = jnp.where(near[0] == 0, left[: 2 * share], left[2 * share : 4 * share])
    fold(over_x, folded_rows(rows, main, tail), left, main)


def image_sum_kernel(main, tail, share, near, total, over_x, over_y, over_both, out):
    rows = total.shape[0]
    value = total[...]
    for source in (over_x, over_y, over_both):
        value = value + unfold(source, 0, rows, main, tail).astype(jnp.float32)
    left = unfold(over_x, folded_rows(rows, main, tail), 2 * share, main, tail)
    left = left.astype(jnp.float32)
    zero = jnp.zeros_like(left)
    far = near[0] == 0
    value = value + jnp.concatenate(
        [jnp.where(far, zero, left), jnp.where(far, left, zero)], axis=0
    )
    fold(out, 0, value.astype(jnp.bfloat16), main)


def head_kernel(main, tail, head, core, starts, mine, near, far, back, back_other, own, *refs):
    sent, (ordered,) = refs[:-1], refs[-1:]
    size, rows = own.shape[0], ordered.shape[1]
    share = rows // starts.shape[0]
    for which, ref in enumerate((back, back_other)):
        value = unfold(ref, 0, rows, main, tail)
        for k in range(starts.shape[0]):
            at = pl.ds(pl.multiple_of(starts[k], 16), share)
            ordered[which, at, :] = value[k * share : (k + 1) * share]
    count = (len(sent) + 1) // 2
    other = jnp.where(core[0] == head, near[...], far[...])
    for half in range(2):
        here = slice(head * count * size, (head + 1) * count * size)
        lanes = slice(half * rows, (half + 1) * rows)
        product = matmul(mine[here, lanes], ordered[0]) + matmul(other[:, lanes], ordered[1])
        for place in range(count):
            part = product[place * size : (place + 1) * size]
            slot = half * count + place
            if slot == 0:
                own[...] = part
            else:
                fold(sent[slot - 1], 0, part, main)


def final_kernel(main, tail, own, *refs):
    got, out = refs[:-1], refs[-1]
    total = own[...]
    for ref in got:
        total = total + unfold(ref, 0, own.shape[0], main, tail).astype(jnp.float32)
    out[...] = total


def final_kernel(main, tail, own, *refs):
    got, out = refs[:-1], refs[-1]
    size = own.shape[0]
    total = own[:, :main]
    for ref in got:
        total = total + ref[:size, :].astype(jnp.float32)
    out[:, :main] = total
    for rows_in, rows_out, lanes_out in folds(size, main, tail):
        total = own[rows_in, main:]
        for ref in got:
            total = total + ref[rows_out, lanes_out].astype(jnp.float32)
        out[rows_in, main:] = total


def packed(
    picture_averaged_encodings,
    caption_averaged_encodings,
    picture_mapping_matrix,
    caption_mapping_matrix,
    picture_weight_perturbation,
    caption_weight_perturbation,
    sharpness_multiplier,
    offset_additive,
):
    tensor_rank = lax.axis_index("tensor")
    data_rank = lax.axis_index("dp")
    count = lax.axis_size("tensor")
    data_count = lax.axis_size("dp")
    planes = data_count // 2
    rows, width = picture_averaged_encodings.shape
    cols = picture_mapping_matrix.shape[1]
    main = cols // 128 * 128
    tail = cols - main
    share = rows // count
    size = width // data_count
    wide = -(-2 * cols // 128) * 128
    f32, bf16 = jnp.float32, jnp.bfloat16
    ranks = jnp.arange(count, dtype=jnp.int32)
    starts = (ranks ^ tensor_rank) * share
    plain = ranks * share

    blocks = call(
        functools.partial(project_kernel, share),
        [((share, 2 * cols), bf16)] * 2 + [((2 * share, 2 * cols), bf16)],
        starts,
        caption_averaged_encodings,
        caption_mapping_matrix.T,
        caption_weight_perturbation.T,
    )
    text_far = swapped(blocks[2], "tensor", 2)
    (relay,) = call(relay_kernel, [((2 * share, 2 * cols), bf16)], blocks[1], text_far)
    text_near = swapped(relay, "tensor", 1)

    (image,) = call(
        functools.partial(project_kernel, share),
        [((rows, 2 * cols), bf16)],
        plain,
        picture_averaged_encodings,
        picture_mapping_matrix.T,
        picture_weight_perturbation.T,
        after=(blocks[0],),
    )
    image_other = swapped(image, "dp", 1)
    image_far = swapped(image, "tensor", 2)
    image_far_other = swapped(image_other, "tensor", 2)

    (text,) = call(
        functools.partial(text_rows_kernel, main, tail),
        [((share, 2 * width), bf16)],
        blocks[0],
        text_far,
        text_near,
    )
    text_two = swapped(text, "dp", 4)
    text_one = swapped(text, "dp", 2)
    text_three = swapped(text_two, "dp", 2)
    texts = [text, text_one, text_two, text_three]

    block_ids = jnp.arange(data_count, dtype=jnp.int32)
    slots = ((block_ids ^ data_rank) >> 1) + planes * ((block_ids ^ data_rank) & 1)
    core = (tensor_rank & 1).astype(jnp.int32).reshape(1)
    mine, other = call(
        turn_kernel,
        [((planes * size, 2 * rows), bf16), ((planes // 2 * size, 2 * rows), bf16)],
        slots,
        core,
        picture_averaged_encodings,
        caption_averaged_encodings,
        after=(image,),
    )
    other = swapped(other, "dp", 1)
    others = (other, swapped(other, "tensor", 1))

    (near,) = call(
        stack_kernel,
        [((4 * rows, wide), bf16)],
        image,
        image_other,
        image_far,
        image_far_other,
        after=(text_one, text_two, others[0]),
    )
    far = swapped(near, "tensor", 1)
    unit, tangent, half, tangent_half, factors = call(
        functools.partial(image_rows_kernel, main, tail, count),
        [
            ((2 * rows, width), f32),
            ((2 * rows, width), f32),
            ((2 * rows, width), bf16),
            ((2 * rows, width), bf16),
            ((2, 2 * rows, 128), f32),
        ],
        near,
        far,
    )

    scalars = jnp.concatenate([sharpness_multiplier, offset_additive])
    outs = call(
        functools.partial(text_block_kernel, planes),
        [((share, width), f32)]
        + [((share, width), bf16)] * (planes - 1)
        + [((planes * share, width), bf16)] * 2
        + [((2 * rows, planes * share), bf16)] * 2,
        (tensor_rank * share).astype(jnp.int32).reshape(1),
        scalars,
        half,
        tangent_half,
        *texts,
    )
    kept, sent = call(
        functools.partial(image_block_kernel, main, tail),
        [((2 * rows, wide), f32)] * 2,
        scalars,
        unit,
        tangent,
        factors,
        *outs[planes:],
    )

    near = (tensor_rank // 2).astype(jnp.int32).reshape(1)
    tall = folded_rows(rows, main, tail)
    more = folded_rows(2 * share, main, tail)
    total, to_x, to_y, to_both = call(
        functools.partial(image_pair_kernel, main, tail, share),
        [((rows, cols), f32), ((tall + more, main), bf16)] + [((tall, main), bf16)] * 2,
        near,
        kept,
        swapped(sent, "tensor", 1),
    )
    flat = [(source, source ^ (count + 2)) for source in range(data_count * count)]
    (image_back,) = call(
        functools.partial(image_sum_kernel, main, tail, share),
        [((tall, main), bf16)],
        near,
        total,
        swapped(to_x, "tensor", 2),
        swapped(to_y, "dp", 1),
        lax.ppermute(to_both, ("dp", "tensor"), flat),
    )
    image_back_other = swapped(image_back, "dp", 1)

    got = [swapped(outs[k], "dp", 2 * k) for k in range(1, planes)]
    blocks = call(
        functools.partial(text_sum_kernel, main, tail),
        [((share, cols), bf16)] * count,
        outs[0],
        *got,
        after=(to_x,),
    )
    got = [blocks[0]] + [swapped(blocks[k], "tensor", k) for k in range(1, count)]
    (text_back,) = call(fold_kernel, [((tall, main), bf16)], *got)
    text_back_other = swapped(text_back, "dp", 1)


    def head(which, order, back, back_other):
        products = call(
            functools.partial(head_kernel, main, tail, which),
            [((size, cols), f32)]
            + [((folded_rows(size, main, tail), main), bf16)] * (planes - 1),
            core,
            order,
            mine,
            *others,
            back,
            back_other,
            scratch=[((2, rows, cols), bf16)],
        )
        got = [swapped(products[k], "dp", 2 * k) for k in range(1, planes)]
        (out,) = call(
            functools.partial(final_kernel, main, tail), [((size, cols), f32)], products[0], *got
        )
        return out

    return (
        head(0, plain, image_back, image_back_other),
        head(1, starts, text_back, text_back_other),
    )


def fits(mesh):
    return mesh.shape["tensor"] == 4 and mesh.shape["dp"] == 8


def solution(mesh):
    in_specs = (
        P("dp", None),
        P("dp", None),
        P(None, "tensor"),
        P(None, "tensor"),
        P(None, "tensor"),
        P(None, "tensor"),
        P(),
        P(),
    )
    out_specs = (P("dp", "tensor"), P("dp", "tensor"))
    local = packed if fits(mesh) else general
    return jax.shard_map(local, mesh=mesh, in_specs=in_specs, out_specs=out_specs, check_vma=False)
```

```python
import functools

import jax
import jax.numpy as jnp
from jax import lax
from jax.experimental import pallas as pl
from jax.experimental.pallas import tpu as pltpu
from jax.sharding import PartitionSpec as P

EPS = 1e-06


def swapped(value, axis, mask):
    count = lax.axis_size(axis)
    return lax.ppermute(value, axis, [(source, source ^ mask) for source in range(count)])


def matmul(left, right):
    return jnp.dot(left, right, preferred_element_type=jnp.float32)


def matmul_nt(left, right):
    return lax.dot_general(
        left, right, (((1,), (1,)), ((), ())), preferred_element_type=jnp.float32
    )


def matmul_tn(left, right):
    return lax.dot_general(
        left, right, (((0,), (0,)), ((), ())), preferred_element_type=jnp.float32
    )


def unit_parts(raw, raw_rate):
    values = raw.astype(jnp.float32)
    tangent = raw_rate.astype(jnp.float32)
    radius = jnp.sqrt(jnp.sum(values * values, axis=1, keepdims=True) + EPS)
    unit = values / radius
    rate = jnp.sum(unit * tangent, axis=1, keepdims=True)
    unit_tangent = (tangent - unit * rate) / radius
    return (unit, unit_tangent, radius, rate)


def unit_backward(unit, unit_tangent, radius, rate, grad, grad_rate):
    inner = jnp.sum(unit * grad, axis=1, keepdims=True)
    inner_rate = jnp.sum(unit_tangent * grad + unit * grad_rate, axis=1, keepdims=True)
    first = (grad - unit * inner) / radius
    return (grad_rate - unit_tangent * inner - unit * inner_rate - first * rate) / radius


def general(
    picture_averaged_encodings,
    caption_averaged_encodings,
    picture_mapping_matrix,
    caption_mapping_matrix,
    picture_weight_perturbation,
    caption_weight_perturbation,
    sharpness_multiplier,
    offset_additive,
):
    similarity_multiplier = sharpness_multiplier[0]
    logit_bias = offset_additive[0]
    tensor_rank = lax.axis_index("tensor")
    data_rank = lax.axis_index("dp")
    tensor_count = lax.axis_size("tensor")
    data_count = lax.axis_size("dp")
    planes = data_count // 2
    rows, width = picture_averaged_encodings.shape
    cols = picture_mapping_matrix.shape[1]
    share = rows // tensor_count
    out_rows = width // data_count
    half = jnp.bfloat16

    text = jnp.stack(
        [
            matmul(caption_averaged_encodings, caption_mapping_matrix).astype(half),
            matmul(caption_averaged_encodings, caption_weight_perturbation).astype(half),
        ]
    )
    image = jnp.stack(
        [
            matmul(picture_averaged_encodings, picture_mapping_matrix).astype(half),
            matmul(picture_averaged_encodings, picture_weight_perturbation).astype(half),
        ]
    )

    def share_of(value, axis, mask):
        start = (tensor_rank ^ mask) * share
        return lax.dynamic_slice_in_dim(value, start, share, axis)

    parts = [share_of(text, 1, 0)]
    for mask in range(1, tensor_count):
        parts.append(swapped(share_of(text, 1, mask), "tensor", mask))
    text = jnp.concatenate(parts, axis=2)
    slots = [text] + [swapped(text, "dp", 2 * mask) for mask in range(1, planes)]

    image = jnp.concatenate([image, swapped(image, "dp", 1)], axis=1)
    blocks = [image]
    mask = tensor_count // 2
    image_blocks = {0: image}
    while mask >= 1:
        held = sorted(image_blocks)
        sent = jnp.concatenate([image_blocks[k] for k in held], axis=2)
        got = swapped(sent, "tensor", mask)
        for place, k in enumerate(held):
            image_blocks[k ^ mask] = got[:, :, place * cols : (place + 1) * cols]
        mask //= 2
    image = jnp.concatenate([image_blocks[k] for k in range(tensor_count)], axis=2)
    text = jnp.concatenate(slots, axis=1)

    def out_columns(value, rank):
        taken = [
            lax.dynamic_slice_in_dim(value, (rank ^ (2 * mask)) * out_rows, out_rows, 1)
            for mask in range(planes)
        ]
        return jnp.concatenate(taken, axis=1)

    def plane_encodings(value):
        other = swapped(out_columns(value, data_rank ^ 1), "dp", 1)
        return jnp.concatenate([out_columns(value, data_rank), other], axis=0)

    picture_plane = plane_encodings(picture_averaged_encodings)
    ordered = jnp.concatenate(
        [share_of(caption_averaged_encodings, 0, mask) for mask in range(tensor_count)], axis=0
    )
    caption_plane = plane_encodings(ordered)

    image_unit, image_tangent, image_radius, image_rate = unit_parts(image[0], image[1])
    text_unit, text_tangent, text_radius, text_rate = unit_parts(text[0], text[1])
    image_half = image_unit.astype(half)
    image_tangent_half = image_tangent.astype(half)
    text_half = text_unit.astype(half)
    text_tangent_half = text_tangent.astype(half)

    logits = similarity_multiplier * matmul_nt(text_half, image_half) + logit_bias
    logit_rate = similarity_multiplier * (
        matmul_nt(text_half, image_tangent_half) + matmul_nt(text_tangent_half, image_half)
    )
    probability = jax.nn.sigmoid(logits)
    text_ids = lax.broadcasted_iota(jnp.int32, (logits.shape[0], 1), 0)
    image_ids = lax.broadcasted_iota(jnp.int32, (1, logits.shape[1]), 1)
    positive = ((text_ids < share) & (text_ids + tensor_rank * share == image_ids)).astype(
        jnp.float32
    )
    weight = (probability - positive).astype(half)
    weight_rate = (probability * (1.0 - probability) * logit_rate).astype(half)
    text_grad = similarity_multiplier * matmul(weight, image_half)
    text_grad_rate = similarity_multiplier * (
        matmul(weight_rate, image_half) + matmul(weight, image_tangent_half)
    )
    image_grad = similarity_multiplier * matmul_tn(weight, text_half)
    image_grad_rate = similarity_multiplier * (
        matmul_tn(weight_rate, text_half) + matmul_tn(weight, text_tangent_half)
    )

    text_back = unit_backward(
        text_unit, text_tangent, text_radius, text_rate, text_grad, text_grad_rate
    )
    image_back = unit_backward(
        image_unit, image_tangent, image_radius, image_rate, image_grad, image_grad_rate
    )

    total = text_back[:share]
    for mask in range(1, planes):
        sent = text_back[mask * share : (mask + 1) * share].astype(half)
        total = total + swapped(sent, "dp", 2 * mask).astype(jnp.float32)
    text_back = total.astype(half)
    parts = [text_back[:, :cols]]
    for mask in range(1, tensor_count):
        sent = text_back[:, mask * cols : (mask + 1) * cols]
        parts.append(swapped(sent, "tensor", mask))
    text_back = jnp.concatenate(parts, axis=0)
    text_back = jnp.concatenate([text_back, swapped(text_back, "dp", 1)], axis=0)

    image_blocks = {k: image_back[:, k * cols : (k + 1) * cols] for k in range(tensor_count)}
    mask = 1
    while mask < tensor_count:
        kept = [k for k in sorted(image_blocks) if not k & mask]
        sent = jnp.concatenate([image_blocks[k ^ mask] for k in kept], axis=1)
        got = swapped(sent, "tensor", mask).astype(jnp.float32)
        image_blocks = {
            k: image_blocks[k] + got[:, place * cols : (place + 1) * cols]
            for place, k in enumerate(kept)
        }
        mask *= 2
    image_back = image_blocks[0]
    got = swapped(image_back, "dp", 1)
    image_back = (
        image_back + jnp.concatenate([got[rows:], got[:rows]], axis=0)
    ).astype(half)

    def head(encodings, back):
        product = matmul_tn(encodings, back)
        total = product[:out_rows]
        for mask in range(1, planes):
            sent = product[mask * out_rows : (mask + 1) * out_rows].astype(half)
            total = total + swapped(sent, "dp", 2 * mask).astype(jnp.float32)
        return total

    return (head(picture_plane, image_back), head(caption_plane, text_back))


def call(kernel, outs, *args, after=(), scratch=()):
    count = len(args)

    def body(*refs):
        kernel(*refs[:count], *refs[count + len(after) :])

    def place(value):
        scalar = value.ndim == 1
        return pl.BlockSpec(memory_space=pltpu.SMEM if scalar else pltpu.VMEM)

    return pl.pallas_call(
        body,
        out_shape=[jax.ShapeDtypeStruct(shape, dtype) for shape, dtype in outs],
        in_specs=[place(value) for value in args]
        + [pl.BlockSpec(memory_space=pl.ANY) for _ in after],
        out_specs=[pl.BlockSpec(memory_space=pltpu.VMEM) for _ in outs],
        scratch_shapes=[pltpu.VMEM(shape, dtype) for shape, dtype in scratch],
        compiler_params=pltpu.CompilerParams(vmem_limit_bytes=48 * 1024 * 1024),
    )(*args, *after)


def folds(rows, main, tail):
    across = main // tail
    for k in range(rows // 16):
        here = slice(k * 16, (k + 1) * 16)
        at = rows + k // across * 16
        first = k % across * tail
        yield here, slice(at, at + 16), slice(first, first + tail)


def folded_rows(rows, main, tail):
    return rows + -(-rows // 16 // (main // tail)) * 16


def fold(out, first, value, main):
    rows, cols = value.shape
    out[first : first + rows, :] = value[:, :main].astype(out.dtype)
    for here, there, lanes in folds(rows, main, cols - main):
        there = slice(first + there.start, first + there.stop)
        out[there, lanes] = value[here, main:].astype(out.dtype)


def unfold(ref, first, rows, main, tail):
    tails = [
        ref[first + there.start : first + there.stop, lanes]
        for _, there, lanes in folds(rows, main, tail)
    ]
    return jnp.concatenate([ref[first : first + rows, :], jnp.concatenate(tails, axis=0)], axis=1)


def project_kernel(share, starts, encodings, weight, direction, *outs):
    main = weight.shape[0] // 128 * 128
    left = jnp.concatenate(
        [
            encodings[pl.ds(pl.multiple_of(starts[k], 16), share), :]
            for k in range(starts.shape[0])
        ],
        axis=0,
    )
    tails = jnp.concatenate([weight[main:, :], direction[main:, :]], axis=0)
    for right, first in ((weight[:main, :], 0), (direction[:main, :], main), (tails, 2 * main)):
        product = matmul_nt(left, right).astype(jnp.bfloat16)
        place = 0
        for out in outs:
            rows = out.shape[0]
            out[:, first : first + right.shape[0]] = product[place : place + rows]
            place += rows


def gathered(blocks, main, tail, which):
    first = 2 * main + which * tail
    mains = [block[:, which * main : (which + 1) * main] for block in blocks]
    tails = [block[:, first : first + tail] for block in blocks]
    return jnp.concatenate(mains + tails, axis=1)


def relay_kernel(mine, got, out):
    rows = out.shape[0] // 2
    out[:rows, :] = mine[mine.shape[0] - rows :, :]
    out[rows:, :] = got[rows:, :]


def text_rows_kernel(main, tail, own, far, near, out):
    rows, width = own.shape[0], out.shape[1] // 2
    parts = (own[...], near[:rows, :], far[:rows, :], near[rows:, :])
    blocks = [part.astype(jnp.float32) for part in parts]
    out[:, :width] = gathered(blocks, main, tail, 0).astype(jnp.bfloat16)
    out[:, width:] = gathered(blocks, main, tail, 1).astype(jnp.bfloat16)


def row_factors(values, tangent):
    squares = jnp.sum(values * values, axis=1, keepdims=True)
    cross = jnp.sum(values * tangent, axis=1, keepdims=True)
    inverse = 1.0 / jnp.sqrt(squares + EPS)
    return inverse, cross * inverse


def unit_rows(values, tangent, inverse, rate):
    unit = values * inverse
    return unit, (tangent - unit * rate) * inverse


def back_rows(unit, tangent, inverse, rate, grad, grad_rate):
    inner = jnp.sum(unit * grad, axis=1, keepdims=True)
    inner_rate = jnp.sum(tangent * grad + unit * grad_rate, axis=1, keepdims=True)
    scaled = rate * inverse
    return (
        grad_rate - tangent * inner - grad * scaled + unit * (inner * scaled - inner_rate)
    ) * inverse


STEP = 48


def image_rows_kernel(main, tail, count, near, far, unit, tangent, half, tangent_half, factors):
    rows = unit.shape[0] // 2
    for shard in range(2):
        held = [
            (near, far)[k % 2].at[pl.ds((k - k % 2 + shard) * rows, rows), :] for k in range(count)
        ]

        @pl.loop(0, rows // STEP)
        def _(step):
            here = pl.ds(pl.multiple_of(step * STEP, STEP), STEP)
            there = pl.ds(pl.multiple_of(shard * rows + step * STEP, STEP), STEP)
            parts = [block[here, :].astype(jnp.float32) for block in held]
            values = gathered(parts, main, tail, 0)
            rates = gathered(parts, main, tail, 1)
            inverse, rate = row_factors(values, rates)
            one, two = unit_rows(values, rates, inverse, rate)
            unit[there, :] = one
            tangent[there, :] = two
            half[there, :] = one.astype(jnp.bfloat16)
            tangent_half[there, :] = two.astype(jnp.bfloat16)
            factors[0, there, :] = jnp.broadcast_to(inverse, (STEP, 128))
            factors[1, there, :] = jnp.broadcast_to(rate, (STEP, 128))


def text_block_kernel(slots, start, scalars, half, tangent_half, *refs):
    texts, refs = refs[:slots], refs[slots:]
    sums, refs = refs[:slots], refs[slots:]
    text_half, text_tangent_half, weight_turned, weight_rate_turned = refs
    f32, bf16 = jnp.float32, jnp.bfloat16
    share, width = texts[0].shape[0], texts[0].shape[1] // 2
    multiplier, bias = scalars[0], scalars[1]

    text_parts = []
    for slot, text in enumerate(texts):
        here = slice(slot * share, (slot + 1) * share)
        values, rates = text[:, :width].astype(f32), text[:, width:].astype(f32)
        inverse, rate = row_factors(values, rates)
        unit, tangent = unit_rows(values, rates, inverse, rate)
        text_parts.append((unit, tangent, inverse, rate))
        text_half[here, :] = unit.astype(bf16)
        text_tangent_half[here, :] = tangent.astype(bf16)

    logits = multiplier * matmul_nt(text_half[...], half[...]) + bias
    logit_rate = multiplier * (
        matmul_nt(text_half[...], tangent_half[...])
        + matmul_nt(text_tangent_half[...], half[...])
    )
    probability = jax.nn.sigmoid(logits)
    text_ids = lax.broadcasted_iota(jnp.int32, logits.shape, 0)
    image_ids = lax.broadcasted_iota(jnp.int32, logits.shape, 1)
    positive = jnp.where((text_ids < share) & (text_ids + start[0] == image_ids), 1.0, 0.0)
    weight = probability - positive
    weight_rate = probability * (1.0 - probability) * logit_rate
    weight_half, weight_rate_half = weight.astype(bf16), weight_rate.astype(bf16)

    text_grad = multiplier * matmul(weight_half, half[...])
    text_grad_rate = multiplier * (
        matmul(weight_rate_half, half[...]) + matmul(weight_half, tangent_half[...])
    )
    for slot, (unit, tangent, inverse, rate) in enumerate(text_parts):
        here = slice(slot * share, (slot + 1) * share)
        back = back_rows(unit, tangent, inverse, rate, text_grad[here], text_grad_rate[here])
        sums[slot][...] = back.astype(sums[slot].dtype)
    weight_turned[...] = weight.T.astype(bf16)
    weight_rate_turned[...] = weight_rate.T.astype(bf16)


def image_block_kernel(
    main,
    tail,
    scalars,
    unit,
    tangent,
    factors,
    text_half,
    text_tangent_half,
    weight,
    weight_rate,
    kept,
    sent,
):
    rows = unit.shape[0] // 2
    count = 4
    multiplier = scalars[0]
    for shard in range(2):
        here = slice(shard * rows, (shard + 1) * rows)
        grad = multiplier * matmul(weight[here, :], text_half[...])
        grad_rate = multiplier * (
            matmul(weight_rate[here, :], text_half[...])
            + matmul(weight[here, :], text_tangent_half[...])
        )
        back = back_rows(
            unit[here, :],
            tangent[here, :],
            factors[0, here, :1],
            factors[1, here, :1],
            grad,
            grad_rate,
        )
        for k in range(count):
            out = (kept, sent)[k % 2]
            to = slice(k // 2 * rows, (k // 2 + 1) * rows)
            out[to, shard * main : (shard + 1) * main] = back[:, k * main : (k + 1) * main]
            first = 2 * main + shard * tail
            taken = count * main + k * tail
            out[to, first : first + tail] = back[:, taken : taken + tail]


def text_sum_kernel(main, tail, own, *refs):
    got, (mine, far) = refs[:-2], refs[-2:]
    rows = own.shape[0]
    total = own[...]
    for ref in got:
        total = total + ref[...].astype(jnp.float32)
    total = total.astype(jnp.bfloat16)
    count = own.shape[1] // (main + tail)
    for k in range(count):
        out = (mine, far)[k // 2]
        here = slice(k % 2 * rows, (k % 2 + 1) * rows)
        first = count * main + k * tail
        out[here, :main] = total[:, k * main : (k + 1) * main]
        out[here, main:] = total[:, first : first + tail]


def stack_kernel(*refs):
    rows = refs[0].shape[0]
    for k, ref in enumerate(refs[:-1]):
        refs[-1][k * rows : (k + 1) * rows, : ref.shape[1]] = ref[...]


def fold_kernel(mine, far, near, out):
    rows = mine.shape[0] // 2
    parts = (mine[:rows, :], near[:rows, :], far[:rows, :], near[rows:, :])
    fold(out, 0, jnp.concatenate(parts, axis=0), out.shape[1])


def turn_kernel(places, core, picture, caption, mine, other):
    for which, encodings in enumerate((picture, caption)):
        turned = encodings[...].astype(jnp.float32).T.astype(jnp.bfloat16)
        count = places.shape[0]
        size, rows = turned.shape[0] // count, turned.shape[1]
        fold = count // 4
        for block in range(count):
            taken = turned[block * size : (block + 1) * size, :]
            slot = places[block]
            at = pl.multiple_of(slot % fold * size, 16)
            for half in range(2):
                lanes = slice(half * rows, (half + 1) * rows)

                @pl.when(slot // fold == half)
                def _():
                    mine[pl.ds(which * fold * size + at, size), lanes] = taken

                @pl.when((slot // fold == 2 + half) & (core[0] == which))
                def _():
                    other[pl.ds(at, size), lanes] = taken


def shard_columns(value, main, tail, shard):
    at = 2 * main + shard * tail
    return jnp.concatenate(
        [value[:, shard * main : (shard + 1) * main], value[:, at : at + tail]], axis=1
    )


def image_pair_kernel(main, tail, share, near, kept, got, total, over_x, over_y, over_both):
    rows = total.shape[0]
    ours = kept[:rows, :] + got[:rows, :]
    theirs = kept[rows:, :] + got[rows:, :]
    total[...] = shard_columns(ours, main, tail, 0)
    fold(over_y, 0, shard_columns(ours, main, tail, 1), main)
    fold(over_both, 0, shard_columns(theirs, main, tail, 1), main)
    value = shard_columns(theirs, main, tail, 0)
    rounded = value.astype(jnp.bfloat16)
    fold(over_x, 0, rounded, main)
    left = value - rounded.astype(jnp.float32)
    left = jnp.where(near[0] == 0, left[: 2 * share], left[2 * share : 4 * share])
    fold(over_x, folded_rows(rows, main, tail), left, main)


def image_sum_kernel(main, tail, share, near, total, over_x, over_y, over_both, out):
    rows = total.shape[0]
    value = total[...]
    for source in (over_x, over_y, over_both):
        value = value + unfold(source, 0, rows, main, tail).astype(jnp.float32)
    left = unfold(over_x, folded_rows(rows, main, tail), 2 * share, main, tail)
    left = left.astype(jnp.float32)
    zero = jnp.zeros_like(left)
    far = near[0] == 0
    value = value + jnp.concatenate(
        [jnp.where(far, zero, left), jnp.where(far, left, zero)], axis=0
    )
    fold(out, 0, value.astype(jnp.bfloat16), main)


def head_kernel(main, tail, head, core, starts, mine, near, far, back, back_other, own, *refs):
    sent, (ordered,) = refs[:-1], refs[-1:]
    size, rows = own.shape[0], ordered.shape[1]
    share = rows // starts.shape[0]
    for which, ref in enumerate((back, back_other)):
        value = unfold(ref, 0, rows, main, tail)
        for k in range(starts.shape[0]):
            at = pl.ds(pl.multiple_of(starts[k], 16), share)
            ordered[which, at, :] = value[k * share : (k + 1) * share]
    count = (len(sent) + 1) // 2
    other = jnp.where(core[0] == head, near[...], far[...])
    for half in range(2):
        here = slice(head * count * size, (head + 1) * count * size)
        lanes = slice(half * rows, (half + 1) * rows)
        product = matmul(mine[here, lanes], ordered[0]) + matmul(other[:, lanes], ordered[1])
        for place in range(count):
            part = product[place * size : (place + 1) * size]
            slot = half * count + place
            if slot == 0:
                own[...] = part
            else:
                fold(sent[slot - 1], 0, part, main)


def final_kernel(main, tail, own, *refs):
    got, out = refs[:-1], refs[-1]
    total = own[...]
    for ref in got:
        total = total + unfold(ref, 0, own.shape[0], main, tail).astype(jnp.float32)
    out[...] = total


def final_kernel(main, tail, own, *refs):
    got, out = refs[:-1], refs[-1]
    size = own.shape[0]
    total = own[:, :main]
    for ref in got:
        total = total + ref[:size, :].astype(jnp.float32)
    out[:, :main] = total
    for rows_in, rows_out, lanes_out in folds(size, main, tail):
        total = own[rows_in, main:]
        for ref in got:
            total = total + ref[rows_out, lanes_out].astype(jnp.float32)
        out[rows_in, main:] = total


def packed(
    picture_averaged_encodings,
    caption_averaged_encodings,
    picture_mapping_matrix,
    caption_mapping_matrix,
    picture_weight_perturbation,
    caption_weight_perturbation,
    sharpness_multiplier,
    offset_additive,
):
    tensor_rank = lax.axis_index("tensor")
    data_rank = lax.axis_index("dp")
    count = lax.axis_size("tensor")
    data_count = lax.axis_size("dp")
    planes = data_count // 2
    rows, width = picture_averaged_encodings.shape
    cols = picture_mapping_matrix.shape[1]
    main = cols // 128 * 128
    tail = cols - main
    share = rows // count
    size = width // data_count
    wide = -(-2 * cols // 128) * 128
    f32, bf16 = jnp.float32, jnp.bfloat16
    ranks = jnp.arange(count, dtype=jnp.int32)
    starts = (ranks ^ tensor_rank) * share
    plain = ranks * share

    blocks = call(
        functools.partial(project_kernel, share),
        [((share, 2 * cols), bf16)] * 2 + [((2 * share, 2 * cols), bf16)],
        starts,
        caption_averaged_encodings,
        caption_mapping_matrix.T,
        caption_weight_perturbation.T,
    )
    text_far = swapped(blocks[2], "tensor", 2)
    (relay,) = call(relay_kernel, [((2 * share, 2 * cols), bf16)], blocks[1], text_far)
    text_near = swapped(relay, "tensor", 1)

    (image,) = call(
        functools.partial(project_kernel, share),
        [((rows, 2 * cols), bf16)],
        plain,
        picture_averaged_encodings,
        picture_mapping_matrix.T,
        picture_weight_perturbation.T,
        after=(blocks[0],),
    )
    image_other = swapped(image, "dp", 1)
    image_far = swapped(image, "tensor", 2)
    image_far_other = swapped(image_other, "tensor", 2)

    (text,) = call(
        functools.partial(text_rows_kernel, main, tail),
        [((share, 2 * width), bf16)],
        blocks[0],
        text_far,
        text_near,
    )
    text_two = swapped(text, "dp", 4)
    text_one = swapped(text, "dp", 2)
    text_three = swapped(text_two, "dp", 2)
    texts = [text, text_one, text_two, text_three]

    block_ids = jnp.arange(data_count, dtype=jnp.int32)
    slots = ((block_ids ^ data_rank) >> 1) + planes * ((block_ids ^ data_rank) & 1)
    core = (tensor_rank & 1).astype(jnp.int32).reshape(1)
    mine, other = call(
        turn_kernel,
        [((planes * size, 2 * rows), bf16), ((planes // 2 * size, 2 * rows), bf16)],
        slots,
        core,
        picture_averaged_encodings,
        caption_averaged_encodings,
        after=(image,),
    )
    other = swapped(other, "dp", 1)
    others = (other, swapped(other, "tensor", 1))

    (near,) = call(
        stack_kernel,
        [((4 * rows, wide), bf16)],
        image,
        image_other,
        image_far,
        image_far_other,
        after=(text_one, text_two, others[0]),
    )
    far = swapped(near, "tensor", 1)
    unit, tangent, half, tangent_half, factors = call(
        functools.partial(image_rows_kernel, main, tail, count),
        [
            ((2 * rows, width), f32),
            ((2 * rows, width), f32),
            ((2 * rows, width), bf16),
            ((2 * rows, width), bf16),
            ((2, 2 * rows, 128), f32),
        ],
        near,
        far,
    )

    scalars = jnp.concatenate([sharpness_multiplier, offset_additive])
    outs = call(
        functools.partial(text_block_kernel, planes),
        [((share, width), f32)]
        + [((share, width), bf16)] * (planes - 1)
        + [((planes * share, width), bf16)] * 2
        + [((2 * rows, planes * share), bf16)] * 2,
        (tensor_rank * share).astype(jnp.int32).reshape(1),
        scalars,
        half,
        tangent_half,
        *texts,
        after=(others[1],),
    )
    kept, sent = call(
        functools.partial(image_block_kernel, main, tail),
        [((2 * rows, wide), f32)] * 2,
        scalars,
        unit,
        tangent,
        factors,
        *outs[planes:],
    )

    near = (tensor_rank // 2).astype(jnp.int32).reshape(1)
    tall = folded_rows(rows, main, tail)
    more = folded_rows(2 * share, main, tail)
    total, to_x, to_y, to_both = call(
        functools.partial(image_pair_kernel, main, tail, share),
        [((rows, cols), f32), ((tall + more, main), bf16)] + [((tall, main), bf16)] * 2,
        near,
        kept,
        swapped(sent, "tensor", 1),
    )
    flat = [(source, source ^ (count + 2)) for source in range(data_count * count)]
    (image_back,) = call(
        functools.partial(image_sum_kernel, main, tail, share),
        [((tall, main), bf16)],
        near,
        total,
        swapped(to_x, "tensor", 2),
        swapped(to_y, "dp", 1),
        lax.ppermute(to_both, ("dp", "tensor"), flat),
    )
    image_back_other = swapped(image_back, "dp", 1)

    got = [swapped(outs[k], "dp", 2 * k) for k in range(1, planes)]
    text_mine, text_far = call(
        functools.partial(text_sum_kernel, main, tail),
        [((2 * share, cols), bf16)] * 2,
        outs[0],
        *got,
        after=(to_x,),
    )
    text_far = swapped(text_far, "tensor", 2)
    (relay,) = call(relay_kernel, [((2 * share, cols), bf16)], text_mine, text_far)
    text_near = swapped(relay, "tensor", 1)
    (text_back,) = call(fold_kernel, [((tall, main), bf16)], text_mine, text_far, text_near)
    text_back_other = swapped(text_back, "dp", 1)


    def head(which, order, back, back_other):
        products = call(
            functools.partial(head_kernel, main, tail, which),
            [((size, cols), f32)]
            + [((folded_rows(size, main, tail), main), bf16)] * (planes - 1),
            core,
            order,
            mine,
            *others,
            back,
            back_other,
            scratch=[((2, rows, cols), bf16)],
        )
        got = [swapped(products[k], "dp", 2 * k) for k in range(1, planes)]
        (out,) = call(
            functools.partial(final_kernel, main, tail), [((size, cols), f32)], products[0], *got
        )
        return out

    return (
        head(0, plain, image_back, image_back_other),
        head(1, starts, text_back, text_back_other),
    )


def fits(mesh):
    return mesh.shape["tensor"] == 4 and mesh.shape["dp"] == 8


def solution(mesh):
    in_specs = (
        P("dp", None),
        P("dp", None),
        P(None, "tensor"),
        P(None, "tensor"),
        P(None, "tensor"),
        P(None, "tensor"),
        P(),
        P(),
    )
    out_specs = (P("dp", "tensor"), P("dp", "tensor"))
    local = packed if fits(mesh) else general
    return jax.shard_map(local, mesh=mesh, in_specs=in_specs, out_specs=out_specs, check_vma=False)
```

```python
import functools

import jax
import jax.numpy as jnp
from jax import lax
from jax.experimental import pallas as pl
from jax.experimental.pallas import tpu as pltpu
from jax.sharding import PartitionSpec as P

EPS = 1e-06


def swapped(value, axis, mask):
    count = lax.axis_size(axis)
    return lax.ppermute(value, axis, [(source, source ^ mask) for source in range(count)])


def matmul(left, right):
    return jnp.dot(left, right, preferred_element_type=jnp.float32)


def matmul_nt(left, right):
    return lax.dot_general(
        left, right, (((1,), (1,)), ((), ())), preferred_element_type=jnp.float32
    )


def matmul_tn(left, right):
    return lax.dot_general(
        left, right, (((0,), (0,)), ((), ())), preferred_element_type=jnp.float32
    )


def unit_parts(raw, raw_rate):
    values = raw.astype(jnp.float32)
    tangent = raw_rate.astype(jnp.float32)
    radius = jnp.sqrt(jnp.sum(values * values, axis=1, keepdims=True) + EPS)
    unit = values / radius
    rate = jnp.sum(unit * tangent, axis=1, keepdims=True)
    unit_tangent = (tangent - unit * rate) / radius
    return (unit, unit_tangent, radius, rate)


def unit_backward(unit, unit_tangent, radius, rate, grad, grad_rate):
    inner = jnp.sum(unit * grad, axis=1, keepdims=True)
    inner_rate = jnp.sum(unit_tangent * grad + unit * grad_rate, axis=1, keepdims=True)
    first = (grad - unit * inner) / radius
    return (grad_rate - unit_tangent * inner - unit * inner_rate - first * rate) / radius


def general(
    picture_averaged_encodings,
    caption_averaged_encodings,
    picture_mapping_matrix,
    caption_mapping_matrix,
    picture_weight_perturbation,
    caption_weight_perturbation,
    sharpness_multiplier,
    offset_additive,
):
    similarity_multiplier = sharpness_multiplier[0]
    logit_bias = offset_additive[0]
    tensor_rank = lax.axis_index("tensor")
    data_rank = lax.axis_index("dp")
    tensor_count = lax.axis_size("tensor")
    data_count = lax.axis_size("dp")
    planes = data_count // 2
    rows, width = picture_averaged_encodings.shape
    cols = picture_mapping_matrix.shape[1]
    share = rows // tensor_count
    out_rows = width // data_count
    half = jnp.bfloat16

    text = jnp.stack(
        [
            matmul(caption_averaged_encodings, caption_mapping_matrix).astype(half),
            matmul(caption_averaged_encodings, caption_weight_perturbation).astype(half),
        ]
    )
    image = jnp.stack(
        [
            matmul(picture_averaged_encodings, picture_mapping_matrix).astype(half),
            matmul(picture_averaged_encodings, picture_weight_perturbation).astype(half),
        ]
    )

    def share_of(value, axis, mask):
        start = (tensor_rank ^ mask) * share
        return lax.dynamic_slice_in_dim(value, start, share, axis)

    parts = [share_of(text, 1, 0)]
    for mask in range(1, tensor_count):
        parts.append(swapped(share_of(text, 1, mask), "tensor", mask))
    text = jnp.concatenate(parts, axis=2)
    slots = [text] + [swapped(text, "dp", 2 * mask) for mask in range(1, planes)]

    image = jnp.concatenate([image, swapped(image, "dp", 1)], axis=1)
    blocks = [image]
    mask = tensor_count // 2
    image_blocks = {0: image}
    while mask >= 1:
        held = sorted(image_blocks)
        sent = jnp.concatenate([image_blocks[k] for k in held], axis=2)
        got = swapped(sent, "tensor", mask)
        for place, k in enumerate(held):
            image_blocks[k ^ mask] = got[:, :, place * cols : (place + 1) * cols]
        mask //= 2
    image = jnp.concatenate([image_blocks[k] for k in range(tensor_count)], axis=2)
    text = jnp.concatenate(slots, axis=1)

    def out_columns(value, rank):
        taken = [
            lax.dynamic_slice_in_dim(value, (rank ^ (2 * mask)) * out_rows, out_rows, 1)
            for mask in range(planes)
        ]
        return jnp.concatenate(taken, axis=1)

    def plane_encodings(value):
        other = swapped(out_columns(value, data_rank ^ 1), "dp", 1)
        return jnp.concatenate([out_columns(value, data_rank), other], axis=0)

    picture_plane = plane_encodings(picture_averaged_encodings)
    ordered = jnp.concatenate(
        [share_of(caption_averaged_encodings, 0, mask) for mask in range(tensor_count)], axis=0
    )
    caption_plane = plane_encodings(ordered)

    image_unit, image_tangent, image_radius, image_rate = unit_parts(image[0], image[1])
    text_unit, text_tangent, text_radius, text_rate = unit_parts(text[0], text[1])
    image_half = image_unit.astype(half)
    image_tangent_half = image_tangent.astype(half)
    text_half = text_unit.astype(half)
    text_tangent_half = text_tangent.astype(half)

    logits = similarity_multiplier * matmul_nt(text_half, image_half) + logit_bias
    logit_rate = similarity_multiplier * (
        matmul_nt(text_half, image_tangent_half) + matmul_nt(text_tangent_half, image_half)
    )
    probability = jax.nn.sigmoid(logits)
    text_ids = lax.broadcasted_iota(jnp.int32, (logits.shape[0], 1), 0)
    image_ids = lax.broadcasted_iota(jnp.int32, (1, logits.shape[1]), 1)
    positive = ((text_ids < share) & (text_ids + tensor_rank * share == image_ids)).astype(
        jnp.float32
    )
    weight = (probability - positive).astype(half)
    weight_rate = (probability * (1.0 - probability) * logit_rate).astype(half)
    text_grad = similarity_multiplier * matmul(weight, image_half)
    text_grad_rate = similarity_multiplier * (
        matmul(weight_rate, image_half) + matmul(weight, image_tangent_half)
    )
    image_grad = similarity_multiplier * matmul_tn(weight, text_half)
    image_grad_rate = similarity_multiplier * (
        matmul_tn(weight_rate, text_half) + matmul_tn(weight, text_tangent_half)
    )

    text_back = unit_backward(
        text_unit, text_tangent, text_radius, text_rate, text_grad, text_grad_rate
    )
    image_back = unit_backward(
        image_unit, image_tangent, image_radius, image_rate, image_grad, image_grad_rate
    )

    total = text_back[:share]
    for mask in range(1, planes):
        sent = text_back[mask * share : (mask + 1) * share].astype(half)
        total = total + swapped(sent, "dp", 2 * mask).astype(jnp.float32)
    text_back = total.astype(half)
    parts = [text_back[:, :cols]]
    for mask in range(1, tensor_count):
        sent = text_back[:, mask * cols : (mask + 1) * cols]
        parts.append(swapped(sent, "tensor", mask))
    text_back = jnp.concatenate(parts, axis=0)
    text_back = jnp.concatenate([text_back, swapped(text_back, "dp", 1)], axis=0)

    image_blocks = {k: image_back[:, k * cols : (k + 1) * cols] for k in range(tensor_count)}
    mask = 1
    while mask < tensor_count:
        kept = [k for k in sorted(image_blocks) if not k & mask]
        sent = jnp.concatenate([image_blocks[k ^ mask] for k in kept], axis=1)
        got = swapped(sent, "tensor", mask).astype(jnp.float32)
        image_blocks = {
            k: image_blocks[k] + got[:, place * cols : (place + 1) * cols]
            for place, k in enumerate(kept)
        }
        mask *= 2
    image_back = image_blocks[0]
    got = swapped(image_back, "dp", 1)
    image_back = (
        image_back + jnp.concatenate([got[rows:], got[:rows]], axis=0)
    ).astype(half)

    def head(encodings, back):
        product = matmul_tn(encodings, back)
        total = product[:out_rows]
        for mask in range(1, planes):
            sent = product[mask * out_rows : (mask + 1) * out_rows].astype(half)
            total = total + swapped(sent, "dp", 2 * mask).astype(jnp.float32)
        return total

    return (head(picture_plane, image_back), head(caption_plane, text_back))


def call(kernel, outs, *args, after=(), scratch=()):
    count = len(args)

    def body(*refs):
        kernel(*refs[:count], *refs[count + len(after) :])

    def place(value):
        scalar = value.ndim == 1
        return pl.BlockSpec(memory_space=pltpu.SMEM if scalar else pltpu.VMEM)

    return pl.pallas_call(
        body,
        out_shape=[jax.ShapeDtypeStruct(shape, dtype) for shape, dtype in outs],
        in_specs=[place(value) for value in args]
        + [pl.BlockSpec(memory_space=pl.ANY) for _ in after],
        out_specs=[pl.BlockSpec(memory_space=pltpu.VMEM) for _ in outs],
        scratch_shapes=[pltpu.VMEM(shape, dtype) for shape, dtype in scratch],
        compiler_params=pltpu.CompilerParams(vmem_limit_bytes=48 * 1024 * 1024),
    )(*args, *after)


def folds(rows, main, tail):
    across = main // tail
    for k in range(rows // 16):
        here = slice(k * 16, (k + 1) * 16)
        at = rows + k // across * 16
        first = k % across * tail
        yield here, slice(at, at + 16), slice(first, first + tail)


def folded_rows(rows, main, tail):
    return rows + -(-rows // 16 // (main // tail)) * 16


def fold(out, first, value, main):
    rows, cols = value.shape
    out[first : first + rows, :] = value[:, :main].astype(out.dtype)
    for here, there, lanes in folds(rows, main, cols - main):
        there = slice(first + there.start, first + there.stop)
        out[there, lanes] = value[here, main:].astype(out.dtype)


def unfold(ref, first, rows, main, tail):
    tails = [
        ref[first + there.start : first + there.stop, lanes]
        for _, there, lanes in folds(rows, main, tail)
    ]
    return jnp.concatenate([ref[first : first + rows, :], jnp.concatenate(tails, axis=0)], axis=1)


def project_kernel(share, starts, encodings, weight, direction, *outs):
    main = weight.shape[0] // 128 * 128
    left = jnp.concatenate(
        [
            encodings[pl.ds(pl.multiple_of(starts[k], 16), share), :]
            for k in range(starts.shape[0])
        ],
        axis=0,
    )
    tails = jnp.concatenate([weight[main:, :], direction[main:, :]], axis=0)
    for right, first in ((weight[:main, :], 0), (direction[:main, :], main), (tails, 2 * main)):
        product = matmul_nt(left, right).astype(jnp.bfloat16)
        place = 0
        for out in outs:
            rows = out.shape[0]
            out[:, first : first + right.shape[0]] = product[place : place + rows]
            place += rows


def gathered(blocks, main, tail, which):
    first = 2 * main + which * tail
    mains = [block[:, which * main : (which + 1) * main] for block in blocks]
    tails = [block[:, first : first + tail] for block in blocks]
    return jnp.concatenate(mains + tails, axis=1)


def relay_kernel(mine, got, out):
    rows = mine.shape[0]
    out[:rows, :] = mine[...]
    out[rows:, :] = got[rows:, :]


def text_rows_kernel(main, tail, own, far, near, out):
    rows, width = own.shape[0], out.shape[1] // 2
    parts = (own[...], near[:rows, :], far[:rows, :], near[rows:, :])
    blocks = [part.astype(jnp.float32) for part in parts]
    out[:, :width] = gathered(blocks, main, tail, 0).astype(jnp.bfloat16)
    out[:, width:] = gathered(blocks, main, tail, 1).astype(jnp.bfloat16)


def row_factors(values, tangent):
    squares = jnp.sum(values * values, axis=1, keepdims=True)
    cross = jnp.sum(values * tangent, axis=1, keepdims=True)
    inverse = 1.0 / jnp.sqrt(squares + EPS)
    return inverse, cross * inverse


def unit_rows(values, tangent, inverse, rate):
    unit = values * inverse
    return unit, (tangent - unit * rate) * inverse


def back_rows(unit, tangent, inverse, rate, grad, grad_rate):
    inner = jnp.sum(unit * grad, axis=1, keepdims=True)
    inner_rate = jnp.sum(tangent * grad + unit * grad_rate, axis=1, keepdims=True)
    scaled = rate * inverse
    return (
        grad_rate - tangent * inner - grad * scaled + unit * (inner * scaled - inner_rate)
    ) * inverse


STEP = 48


def image_rows_kernel(main, tail, count, near, far, unit, tangent, half, tangent_half, factors):
    rows = unit.shape[0] // 2
    for shard in range(2):
        held = [
            (near, far)[k % 2].at[pl.ds((k - k % 2 + shard) * rows, rows), :] for k in range(count)
        ]

        @pl.loop(0, rows // STEP)
        def _(step):
            here = pl.ds(pl.multiple_of(step * STEP, STEP), STEP)
            there = pl.ds(pl.multiple_of(shard * rows + step * STEP, STEP), STEP)
            parts = [block[here, :].astype(jnp.float32) for block in held]
            values = gathered(parts, main, tail, 0)
            rates = gathered(parts, main, tail, 1)
            inverse, rate = row_factors(values, rates)
            one, two = unit_rows(values, rates, inverse, rate)
            unit[there, :] = one
            tangent[there, :] = two
            half[there, :] = one.astype(jnp.bfloat16)
            tangent_half[there, :] = two.astype(jnp.bfloat16)
            factors[0, there, :] = jnp.broadcast_to(inverse, (STEP, 128))
            factors[1, there, :] = jnp.broadcast_to(rate, (STEP, 128))


def text_rows(text):
    width = text.shape[1] // 2
    values, rates = text[:, :width].astype(jnp.float32), text[:, width:].astype(jnp.float32)
    inverse, rate = row_factors(values, rates)
    return unit_rows(values, rates, inverse, rate) + (inverse, rate)


def weight_kernel(slots, start, scalars, half, tangent_half, *refs):
    texts, outs = refs[:slots], refs[slots:]
    text_half, text_tangent_half, weight, weight_rate, weight_turned, weight_rate_turned = outs
    bf16 = jnp.bfloat16
    share = texts[0].shape[0]
    multiplier, bias = scalars[0], scalars[1]
    for slot, text in enumerate(texts):
        here = slice(slot * share, (slot + 1) * share)
        unit, tangent, _, _ = text_rows(text)
        text_half[here, :] = unit.astype(bf16)
        text_tangent_half[here, :] = tangent.astype(bf16)
    logits = multiplier * matmul_nt(text_half[...], half[...]) + bias
    logit_rate = multiplier * (
        matmul_nt(text_half[...], tangent_half[...])
        + matmul_nt(text_tangent_half[...], half[...])
    )
    probability = jax.nn.sigmoid(logits)
    text_ids = lax.broadcasted_iota(jnp.int32, logits.shape, 0)
    image_ids = lax.broadcasted_iota(jnp.int32, logits.shape, 1)
    positive = jnp.where((text_ids < share) & (text_ids + start[0] == image_ids), 1.0, 0.0)
    value = probability - positive
    value_rate = probability * (1.0 - probability) * logit_rate
    weight[...] = value.astype(bf16)
    weight_rate[...] = value_rate.astype(bf16)
    weight_turned[...] = value.T.astype(bf16)
    weight_rate_turned[...] = value_rate.T.astype(bf16)


def text_block_kernel(slots, scalars, half, tangent_half, weight, weight_rate, *refs):
    texts, sums = refs[:slots], refs[slots:]
    share = texts[0].shape[0]
    multiplier = scalars[0]
    grad = multiplier * matmul(weight[...], half[...])
    grad_rate = multiplier * (
        matmul(weight_rate[...], half[...]) + matmul(weight[...], tangent_half[...])
    )
    for slot, text in enumerate(texts):
        here = slice(slot * share, (slot + 1) * share)
        back = back_rows(*text_rows(text), grad[here], grad_rate[here])
        if slot % 2 == 0:
            sums[slot // 2][...] = back
        else:
            at = slice(slot // 2 * share, (slot // 2 + 1) * share)
            sums[2][at, :] = back.astype(jnp.bfloat16)


def forward_kernel(own, middle, got, total, sent):
    share = own.shape[0]
    total[...] = own[...] + got[:share, :].astype(jnp.float32)
    sent[...] = (middle[...] + got[share:, :].astype(jnp.float32)).astype(jnp.bfloat16)


def image_block_kernel(
    main,
    tail,
    scalars,
    unit,
    tangent,
    factors,
    text_half,
    text_tangent_half,
    weight,
    weight_rate,
    kept,
    sent,
):
    rows = unit.shape[0] // 2
    count = 4
    multiplier = scalars[0]
    for shard in range(2):
        here = slice(shard * rows, (shard + 1) * rows)
        grad = multiplier * matmul(weight[here, :], text_half[...])
        grad_rate = multiplier * (
            matmul(weight_rate[here, :], text_half[...])
            + matmul(weight[here, :], text_tangent_half[...])
        )
        back = back_rows(
            unit[here, :],
            tangent[here, :],
            factors[0, here, :1],
            factors[1, here, :1],
            grad,
            grad_rate,
        )
        for k in range(count):
            out = (kept, sent)[k % 2]
            to = slice(k // 2 * rows, (k // 2 + 1) * rows)
            out[to, shard * main : (shard + 1) * main] = back[:, k * main : (k + 1) * main]
            first = 2 * main + shard * tail
            taken = count * main + k * tail
            out[to, first : first + tail] = back[:, taken : taken + tail]


def text_sum_kernel(main, tail, own, *refs):
    count = own.shape[1] // (main + tail)
    got, outs = refs[:-count], refs[-count:]
    total = own[...]
    for ref in got:
        total = total + ref[...].astype(jnp.float32)
    for k, out in enumerate(outs):
        first = count * main + k * tail
        out[:, :main] = total[:, k * main : (k + 1) * main].astype(jnp.bfloat16)
        out[:, main:] = total[:, first : first + tail].astype(jnp.bfloat16)


def stack_kernel(*refs):
    rows = refs[0].shape[0]
    for k, ref in enumerate(refs[:-1]):
        refs[-1][k * rows : (k + 1) * rows, : ref.shape[1]] = ref[...]


def fold_kernel(*refs):
    value = jnp.concatenate([ref[...] for ref in refs[:-1]], axis=0)
    fold(refs[-1], 0, value, refs[-1].shape[1])


def turn_kernel(places, core, picture, caption, mine, other):
    for which, encodings in enumerate((picture, caption)):
        turned = encodings[...].astype(jnp.float32).T.astype(jnp.bfloat16)
        count = places.shape[0]
        size, rows = turned.shape[0] // count, turned.shape[1]
        fold = count // 4
        for block in range(count):
            taken = turned[block * size : (block + 1) * size, :]
            slot = places[block]
            at = pl.multiple_of(slot % fold * size, 16)
            for half in range(2):
                lanes = slice(half * rows, (half + 1) * rows)

                @pl.when(slot // fold == half)
                def _():
                    mine[pl.ds(which * fold * size + at, size), lanes] = taken

                @pl.when((slot // fold == 2 + half) & (core[0] == which))
                def _():
                    other[pl.ds(at, size), lanes] = taken


def shard_columns(value, main, tail, shard):
    at = 2 * main + shard * tail
    return jnp.concatenate(
        [value[:, shard * main : (shard + 1) * main], value[:, at : at + tail]], axis=1
    )


def image_pair_kernel(main, tail, share, near, kept, got, total, over_x, over_y, over_both):
    rows = total.shape[0]
    ours = kept[:rows, :] + got[:rows, :]
    theirs = kept[rows:, :] + got[rows:, :]
    total[...] = shard_columns(ours, main, tail, 0)
    fold(over_y, 0, shard_columns(ours, main, tail, 1), main)
    fold(over_both, 0, shard_columns(theirs, main, tail, 1), main)
    value = shard_columns(theirs, main, tail, 0)
    rounded = value.astype(jnp.bfloat16)
    fold(over_x, 0, rounded, main)
    left = value - rounded.astype(jnp.float32)
    left = jnp.where(near[0] == 0, left[: 2 * share], left[2 * share : 4 * share])
    fold(over_x, folded_rows(rows, main, tail), left, main)


def image_sum_kernel(main, tail, share, near, total, over_x, over_y, over_both, out):
    rows = total.shape[0]
    value = total[...]
    for source in (over_x, over_y, over_both):
        value = value + unfold(source, 0, rows, main, tail).astype(jnp.float32)
    left = unfold(over_x, folded_rows(rows, main, tail), 2 * share, main, tail)
    left = left.astype(jnp.float32)
    zero = jnp.zeros_like(left)
    far = near[0] == 0
    value = value + jnp.concatenate(
        [jnp.where(far, zero, left), jnp.where(far, left, zero)], axis=0
    )
    fold(out, 0, value.astype(jnp.bfloat16), main)


def head_kernel(main, tail, head, core, starts, mine, near, far, back, back_other, own, *refs):
    sent, (ordered,) = refs[:-1], refs[-1:]
    size, rows = own.shape[0], ordered.shape[1]
    share = rows // starts.shape[0]
    for which, ref in enumerate((back, back_other)):
        value = unfold(ref, 0, rows, main, tail)
        for k in range(starts.shape[0]):
            at = pl.ds(pl.multiple_of(starts[k], 16), share)
            ordered[which, at, :] = value[k * share : (k + 1) * share]
    count = (len(sent) + 1) // 2
    other = jnp.where(core[0] == head, near[...], far[...])
    for half in range(2):
        here = slice(head * count * size, (head + 1) * count * size)
        lanes = slice(half * rows, (half + 1) * rows)
        product = matmul(mine[here, lanes], ordered[0]) + matmul(other[:, lanes], ordered[1])
        for place in range(count):
            part = product[place * size : (place + 1) * size]
            slot = half * count + place
            if slot == 0:
                own[...] = part
            else:
                fold(sent[slot - 1], 0, part, main)


def final_kernel(main, tail, own, *refs):
    got, out = refs[:-1], refs[-1]
    total = own[...]
    for ref in got:
        total = total + unfold(ref, 0, own.shape[0], main, tail).astype(jnp.float32)
    out[...] = total


def final_kernel(main, tail, own, *refs):
    got, out = refs[:-1], refs[-1]
    size = own.shape[0]
    total = own[:, :main]
    for ref in got:
        total = total + ref[:size, :].astype(jnp.float32)
    out[:, :main] = total
    for rows_in, rows_out, lanes_out in folds(size, main, tail):
        total = own[rows_in, main:]
        for ref in got:
            total = total + ref[rows_out, lanes_out].astype(jnp.float32)
        out[rows_in, main:] = total


def packed(
    picture_averaged_encodings,
    caption_averaged_encodings,
    picture_mapping_matrix,
    caption_mapping_matrix,
    picture_weight_perturbation,
    caption_weight_perturbation,
    sharpness_multiplier,
    offset_additive,
):
    tensor_rank = lax.axis_index("tensor")
    data_rank = lax.axis_index("dp")
    count = lax.axis_size("tensor")
    data_count = lax.axis_size("dp")
    planes = data_count // 2
    rows, width = picture_averaged_encodings.shape
    cols = picture_mapping_matrix.shape[1]
    main = cols // 128 * 128
    tail = cols - main
    share = rows // count
    size = width // data_count
    wide = -(-2 * cols // 128) * 128
    f32, bf16 = jnp.float32, jnp.bfloat16
    ranks = jnp.arange(count, dtype=jnp.int32)
    starts = (ranks ^ tensor_rank) * share
    plain = ranks * share

    blocks = call(
        functools.partial(project_kernel, share),
        [((share, 2 * cols), bf16)] * 2 + [((2 * share, 2 * cols), bf16)],
        starts,
        caption_averaged_encodings,
        caption_mapping_matrix.T,
        caption_weight_perturbation.T,
    )
    text_far = swapped(blocks[2], "tensor", 2)
    (relay,) = call(relay_kernel, [((2 * share, 2 * cols), bf16)], blocks[1], text_far)
    text_near = swapped(relay, "tensor", 1)

    (image,) = call(
        functools.partial(project_kernel, share),
        [((rows, 2 * cols), bf16)],
        plain,
        picture_averaged_encodings,
        picture_mapping_matrix.T,
        picture_weight_perturbation.T,
        after=(blocks[0],),
    )
    image_other = swapped(image, "dp", 1)
    image_far = swapped(image, "tensor", 2)
    image_far_other = swapped(image_other, "tensor", 2)

    (text,) = call(
        functools.partial(text_rows_kernel, main, tail),
        [((share, 2 * width), bf16)],
        blocks[0],
        text_far,
        text_near,
    )
    text_two = swapped(text, "dp", 4)
    text_one = swapped(text, "dp", 2)
    text_three = swapped(text_two, "dp", 2)
    texts = [text, text_one, text_two, text_three]

    block_ids = jnp.arange(data_count, dtype=jnp.int32)
    slots = ((block_ids ^ data_rank) >> 1) + planes * ((block_ids ^ data_rank) & 1)
    core = (tensor_rank & 1).astype(jnp.int32).reshape(1)
    mine, other = call(
        turn_kernel,
        [((planes * size, 2 * rows), bf16), ((planes // 2 * size, 2 * rows), bf16)],
        slots,
        core,
        picture_averaged_encodings,
        caption_averaged_encodings,
        after=(image,),
    )
    other = swapped(other, "dp", 1)
    others = (other, swapped(other, "tensor", 1))

    (near,) = call(
        stack_kernel,
        [((4 * rows, wide), bf16)],
        image,
        image_other,
        image_far,
        image_far_other,
        after=(text_one, text_two, others[0]),
    )
    far = swapped(near, "tensor", 1)
    unit, tangent, half, tangent_half, factors = call(
        functools.partial(image_rows_kernel, main, tail, count),
        [
            ((2 * rows, width), f32),
            ((2 * rows, width), f32),
            ((2 * rows, width), bf16),
            ((2 * rows, width), bf16),
            ((2, 2 * rows, 128), f32),
        ],
        near,
        far,
    )

    scalars = jnp.concatenate([sharpness_multiplier, offset_additive])
    text_half, text_tangent_half, weight, weight_rate, weight_turned, weight_rate_turned = call(
        functools.partial(weight_kernel, planes),
        [((planes * share, width), bf16)] * 2
        + [((planes * share, 2 * rows), bf16)] * 2
        + [((2 * rows, planes * share), bf16)] * 2,
        (tensor_rank * share).astype(jnp.int32).reshape(1),
        scalars,
        half,
        tangent_half,
        *texts,
        after=(others[1],),
    )
    kept, sent = call(
        functools.partial(image_block_kernel, main, tail),
        [((2 * rows, wide), f32)] * 2,
        scalars,
        unit,
        tangent,
        factors,
        text_half,
        text_tangent_half,
        weight_turned,
        weight_rate_turned,
    )
    outs = call(
        functools.partial(text_block_kernel, planes),
        [((share, width), f32)] * 2 + [((2 * share, width), bf16)],
        scalars,
        half,
        tangent_half,
        weight,
        weight_rate,
        *texts,
        after=(kept,),
    )

    near = (tensor_rank // 2).astype(jnp.int32).reshape(1)
    tall = folded_rows(rows, main, tail)
    more = folded_rows(2 * share, main, tail)
    total, to_x, to_y, to_both = call(
        functools.partial(image_pair_kernel, main, tail, share),
        [((rows, cols), f32), ((tall + more, main), bf16)] + [((tall, main), bf16)] * 2,
        near,
        kept,
        swapped(sent, "tensor", 1),
        after=(outs[0],),
    )
    flat = [(source, source ^ (count + 2)) for source in range(data_count * count)]
    (image_back,) = call(
        functools.partial(image_sum_kernel, main, tail, share),
        [((tall, main), bf16)],
        near,
        total,
        swapped(to_x, "tensor", 2),
        swapped(to_y, "dp", 1),
        lax.ppermute(to_both, ("dp", "tensor"), flat),
    )
    image_back_other = swapped(image_back, "dp", 1)

    text_total, text_sent = call(
        forward_kernel,
        [((share, width), f32), ((share, width), bf16)],
        outs[0],
        outs[1],
        swapped(outs[2], "dp", 2),
    )
    blocks = call(
        functools.partial(text_sum_kernel, main, tail),
        [((share, cols), bf16)] * count,
        text_total,
        swapped(text_sent, "dp", 4),
        after=(image_back,),
    )
    got = [blocks[0]] + [swapped(blocks[k], "tensor", k) for k in range(1, count)]
    (text_back,) = call(fold_kernel, [((tall, main), bf16)], *got)
    text_back_other = swapped(text_back, "dp", 1)


    def head(which, order, back, back_other):
        products = call(
            functools.partial(head_kernel, main, tail, which),
            [((size, cols), f32)]
            + [((folded_rows(size, main, tail), main), bf16)] * (planes - 1),
            core,
            order,
            mine,
            *others,
            back,
            back_other,
            scratch=[((2, rows, cols), bf16)],
        )
        got = [swapped(products[k], "dp", 2 * k) for k in range(1, planes)]
        (out,) = call(
            functools.partial(final_kernel, main, tail), [((size, cols), f32)], products[0], *got
        )
        return out

    return (
        head(0, plain, image_back, image_back_other),
        head(1, starts, text_back, text_back_other),
    )


def fits(mesh):
    return mesh.shape["tensor"] == 4 and mesh.shape["dp"] == 8


def solution(mesh):
    in_specs = (
        P("dp", None),
        P("dp", None),
        P(None, "tensor"),
        P(None, "tensor"),
        P(None, "tensor"),
        P(None, "tensor"),
        P(),
        P(),
    )
    out_specs = (P("dp", "tensor"), P("dp", "tensor"))
    local = packed if fits(mesh) else general
    return jax.shard_map(local, mesh=mesh, in_specs=in_specs, out_specs=out_specs, check_vma=False)
```

```python
import functools

import jax
import jax.numpy as jnp
from jax import lax
from jax.experimental import pallas as pl
from jax.experimental.pallas import tpu as pltpu
from jax.sharding import PartitionSpec as P

EPS = 1e-06


def swapped(value, axis, mask):
    count = lax.axis_size(axis)
    return lax.ppermute(value, axis, [(source, source ^ mask) for source in range(count)])


def matmul(left, right):
    return jnp.dot(left, right, preferred_element_type=jnp.float32)


def matmul_nt(left, right):
    return lax.dot_general(
        left, right, (((1,), (1,)), ((), ())), preferred_element_type=jnp.float32
    )


def matmul_tn(left, right):
    return lax.dot_general(
        left, right, (((0,), (0,)), ((), ())), preferred_element_type=jnp.float32
    )


def unit_parts(raw, raw_rate):
    values = raw.astype(jnp.float32)
    tangent = raw_rate.astype(jnp.float32)
    radius = jnp.sqrt(jnp.sum(values * values, axis=1, keepdims=True) + EPS)
    unit = values / radius
    rate = jnp.sum(unit * tangent, axis=1, keepdims=True)
    unit_tangent = (tangent - unit * rate) / radius
    return (unit, unit_tangent, radius, rate)


def unit_backward(unit, unit_tangent, radius, rate, grad, grad_rate):
    inner = jnp.sum(unit * grad, axis=1, keepdims=True)
    inner_rate = jnp.sum(unit_tangent * grad + unit * grad_rate, axis=1, keepdims=True)
    first = (grad - unit * inner) / radius
    return (grad_rate - unit_tangent * inner - unit * inner_rate - first * rate) / radius


def general(
    picture_averaged_encodings,
    caption_averaged_encodings,
    picture_mapping_matrix,
    caption_mapping_matrix,
    picture_weight_perturbation,
    caption_weight_perturbation,
    sharpness_multiplier,
    offset_additive,
):
    similarity_multiplier = sharpness_multiplier[0]
    logit_bias = offset_additive[0]
    tensor_rank = lax.axis_index("tensor")
    data_rank = lax.axis_index("dp")
    tensor_count = lax.axis_size("tensor")
    data_count = lax.axis_size("dp")
    planes = data_count // 2
    rows, width = picture_averaged_encodings.shape
    cols = picture_mapping_matrix.shape[1]
    share = rows // tensor_count
    out_rows = width // data_count
    half = jnp.bfloat16

    text = jnp.stack(
        [
            matmul(caption_averaged_encodings, caption_mapping_matrix).astype(half),
            matmul(caption_averaged_encodings, caption_weight_perturbation).astype(half),
        ]
    )
    image = jnp.stack(
        [
            matmul(picture_averaged_encodings, picture_mapping_matrix).astype(half),
            matmul(picture_averaged_encodings, picture_weight_perturbation).astype(half),
        ]
    )

    def share_of(value, axis, mask):
        start = (tensor_rank ^ mask) * share
        return lax.dynamic_slice_in_dim(value, start, share, axis)

    parts = [share_of(text, 1, 0)]
    for mask in range(1, tensor_count):
        parts.append(swapped(share_of(text, 1, mask), "tensor", mask))
    text = jnp.concatenate(parts, axis=2)
    slots = [text] + [swapped(text, "dp", 2 * mask) for mask in range(1, planes)]

    image = jnp.concatenate([image, swapped(image, "dp", 1)], axis=1)
    blocks = [image]
    mask = tensor_count // 2
    image_blocks = {0: image}
    while mask >= 1:
        held = sorted(image_blocks)
        sent = jnp.concatenate([image_blocks[k] for k in held], axis=2)
        got = swapped(sent, "tensor", mask)
        for place, k in enumerate(held):
            image_blocks[k ^ mask] = got[:, :, place * cols : (place + 1) * cols]
        mask //= 2
    image = jnp.concatenate([image_blocks[k] for k in range(tensor_count)], axis=2)
    text = jnp.concatenate(slots, axis=1)

    def out_columns(value, rank):
        taken = [
            lax.dynamic_slice_in_dim(value, (rank ^ (2 * mask)) * out_rows, out_rows, 1)
            for mask in range(planes)
        ]
        return jnp.concatenate(taken, axis=1)

    def plane_encodings(value):
        other = swapped(out_columns(value, data_rank ^ 1), "dp", 1)
        return jnp.concatenate([out_columns(value, data_rank), other], axis=0)

    picture_plane = plane_encodings(picture_averaged_encodings)
    ordered = jnp.concatenate(
        [share_of(caption_averaged_encodings, 0, mask) for mask in range(tensor_count)], axis=0
    )
    caption_plane = plane_encodings(ordered)

    image_unit, image_tangent, image_radius, image_rate = unit_parts(image[0], image[1])
    text_unit, text_tangent, text_radius, text_rate = unit_parts(text[0], text[1])
    image_half = image_unit.astype(half)
    image_tangent_half = image_tangent.astype(half)
    text_half = text_unit.astype(half)
    text_tangent_half = text_tangent.astype(half)

    logits = similarity_multiplier * matmul_nt(text_half, image_half) + logit_bias
    logit_rate = similarity_multiplier * (
        matmul_nt(text_half, image_tangent_half) + matmul_nt(text_tangent_half, image_half)
    )
    probability = jax.nn.sigmoid(logits)
    text_ids = lax.broadcasted_iota(jnp.int32, (logits.shape[0], 1), 0)
    image_ids = lax.broadcasted_iota(jnp.int32, (1, logits.shape[1]), 1)
    positive = ((text_ids < share) & (text_ids + tensor_rank * share == image_ids)).astype(
        jnp.float32
    )
    weight = (probability - positive).astype(half)
    weight_rate = (probability * (1.0 - probability) * logit_rate).astype(half)
    text_grad = similarity_multiplier * matmul(weight, image_half)
    text_grad_rate = similarity_multiplier * (
        matmul(weight_rate, image_half) + matmul(weight, image_tangent_half)
    )
    image_grad = similarity_multiplier * matmul_tn(weight, text_half)
    image_grad_rate = similarity_multiplier * (
        matmul_tn(weight_rate, text_half) + matmul_tn(weight, text_tangent_half)
    )

    text_back = unit_backward(
        text_unit, text_tangent, text_radius, text_rate, text_grad, text_grad_rate
    )
    image_back = unit_backward(
        image_unit, image_tangent, image_radius, image_rate, image_grad, image_grad_rate
    )

    total = text_back[:share]
    for mask in range(1, planes):
        sent = text_back[mask * share : (mask + 1) * share].astype(half)
        total = total + swapped(sent, "dp", 2 * mask).astype(jnp.float32)
    text_back = total.astype(half)
    parts = [text_back[:, :cols]]
    for mask in range(1, tensor_count):
        sent = text_back[:, mask * cols : (mask + 1) * cols]
        parts.append(swapped(sent, "tensor", mask))
    text_back = jnp.concatenate(parts, axis=0)
    text_back = jnp.concatenate([text_back, swapped(text_back, "dp", 1)], axis=0)

    image_blocks = {k: image_back[:, k * cols : (k + 1) * cols] for k in range(tensor_count)}
    mask = 1
    while mask < tensor_count:
        kept = [k for k in sorted(image_blocks) if not k & mask]
        sent = jnp.concatenate([image_blocks[k ^ mask] for k in kept], axis=1)
        got = swapped(sent, "tensor", mask).astype(jnp.float32)
        image_blocks = {
            k: image_blocks[k] + got[:, place * cols : (place + 1) * cols]
            for place, k in enumerate(kept)
        }
        mask *= 2
    image_back = image_blocks[0]
    got = swapped(image_back, "dp", 1)
    image_back = (
        image_back + jnp.concatenate([got[rows:], got[:rows]], axis=0)
    ).astype(half)

    def head(encodings, back):
        product = matmul_tn(encodings, back)
        total = product[:out_rows]
        for mask in range(1, planes):
            sent = product[mask * out_rows : (mask + 1) * out_rows].astype(half)
            total = total + swapped(sent, "dp", 2 * mask).astype(jnp.float32)
        return total

    return (head(picture_plane, image_back), head(caption_plane, text_back))


def call(kernel, outs, *args, after=(), scratch=()):
    count = len(args)

    def body(*refs):
        kernel(*refs[:count], *refs[count + len(after) :])

    def place(value):
        scalar = value.ndim == 1
        return pl.BlockSpec(memory_space=pltpu.SMEM if scalar else pltpu.VMEM)

    return pl.pallas_call(
        body,
        out_shape=[jax.ShapeDtypeStruct(shape, dtype) for shape, dtype in outs],
        in_specs=[place(value) for value in args]
        + [pl.BlockSpec(memory_space=pl.ANY) for _ in after],
        out_specs=[pl.BlockSpec(memory_space=pltpu.VMEM) for _ in outs],
        scratch_shapes=[pltpu.VMEM(shape, dtype) for shape, dtype in scratch],
        compiler_params=pltpu.CompilerParams(vmem_limit_bytes=24 * 1024 * 1024),
    )(*args, *after)


def folds(rows, main, tail):
    across = main // tail
    for k in range(rows // 16):
        here = slice(k * 16, (k + 1) * 16)
        at = rows + k // across * 16
        first = k % across * tail
        yield here, slice(at, at + 16), slice(first, first + tail)


def folded_rows(rows, main, tail):
    return rows + -(-rows // 16 // (main // tail)) * 16


def fold(out, first, value, main):
    rows, cols = value.shape
    out[first : first + rows, :] = value[:, :main].astype(out.dtype)
    for here, there, lanes in folds(rows, main, cols - main):
        there = slice(first + there.start, first + there.stop)
        out[there, lanes] = value[here, main:].astype(out.dtype)


def unfold(ref, first, rows, main, tail):
    tails = [
        ref[first + there.start : first + there.stop, lanes]
        for _, there, lanes in folds(rows, main, tail)
    ]
    return jnp.concatenate([ref[first : first + rows, :], jnp.concatenate(tails, axis=0)], axis=1)


def project_kernel(share, starts, encodings, weight, direction, *outs):
    main = weight.shape[0] // 128 * 128
    left = jnp.concatenate(
        [
            encodings[pl.ds(pl.multiple_of(starts[k], 16), share), :]
            for k in range(starts.shape[0])
        ],
        axis=0,
    )
    tails = jnp.concatenate([weight[main:, :], direction[main:, :]], axis=0)
    for right, first in ((weight[:main, :], 0), (direction[:main, :], main), (tails, 2 * main)):
        product = matmul_nt(left, right).astype(jnp.bfloat16)
        place = 0
        for out in outs:
            rows = out.shape[0]
            out[:, first : first + right.shape[0]] = product[place : place + rows]
            place += rows


def gathered(blocks, main, tail, which):
    first = 2 * main + which * tail
    mains = [block[:, which * main : (which + 1) * main] for block in blocks]
    tails = [block[:, first : first + tail] for block in blocks]
    return jnp.concatenate(mains + tails, axis=1)


def relay_kernel(mine, got, out):
    rows = mine.shape[0]
    out[:rows, :] = mine[...]
    out[rows:, :] = got[rows:, :]


def text_rows_kernel(main, tail, own, far, near, out):
    rows, width = own.shape[0], out.shape[1] // 2
    parts = (own[...], near[:rows, :], far[:rows, :], near[rows:, :])
    blocks = [part.astype(jnp.float32) for part in parts]
    out[:, :width] = gathered(blocks, main, tail, 0).astype(jnp.bfloat16)
    out[:, width:] = gathered(blocks, main, tail, 1).astype(jnp.bfloat16)


def row_factors(values, tangent):
    squares = jnp.sum(values * values, axis=1, keepdims=True)
    cross = jnp.sum(values * tangent, axis=1, keepdims=True)
    inverse = 1.0 / jnp.sqrt(squares + EPS)
    return inverse, cross * inverse


def unit_rows(values, tangent, inverse, rate):
    unit = values * inverse
    return unit, (tangent - unit * rate) * inverse


def back_rows(unit, tangent, inverse, rate, grad, grad_rate):
    inner = jnp.sum(unit * grad, axis=1, keepdims=True)
    inner_rate = jnp.sum(tangent * grad + unit * grad_rate, axis=1, keepdims=True)
    scaled = rate * inverse
    return (
        grad_rate - tangent * inner - grad * scaled + unit * (inner * scaled - inner_rate)
    ) * inverse


STEP = 48


def image_rows_kernel(main, tail, count, near, far, unit, tangent, half_both, factors):
    rows = unit.shape[0] // 2
    for shard in range(2):
        held = [
            (near, far)[k % 2].at[pl.ds((k - k % 2 + shard) * rows, rows), :] for k in range(count)
        ]

        @pl.loop(0, rows // STEP)
        def _(step):
            here = pl.ds(pl.multiple_of(step * STEP, STEP), STEP)
            there = pl.ds(pl.multiple_of(shard * rows + step * STEP, STEP), STEP)
            parts = [block[here, :].astype(jnp.float32) for block in held]
            values = gathered(parts, main, tail, 0)
            rates = gathered(parts, main, tail, 1)
            inverse, rate = row_factors(values, rates)
            one, two = unit_rows(values, rates, inverse, rate)
            unit[there, :] = one
            tangent[there, :] = two
            half_both[there, :] = one.astype(jnp.bfloat16)
            below = pl.ds(pl.multiple_of((2 + shard) * rows + step * STEP, STEP), STEP)
            half_both[below, :] = two.astype(jnp.bfloat16)
            factors[0, there, :] = jnp.broadcast_to(inverse, (STEP, 128))
            factors[1, there, :] = jnp.broadcast_to(rate, (STEP, 128))


def text_rows(text):
    width = text.shape[1] // 2
    values, rates = text[:, :width].astype(jnp.float32), text[:, width:].astype(jnp.float32)
    inverse, rate = row_factors(values, rates)
    return unit_rows(values, rates, inverse, rate) + (inverse, rate)


def weight_kernel(slots, start, scalars, half_both, *refs):
    texts, (text_both, weights, weights_turned) = refs[:slots], refs[slots:]
    bf16 = jnp.bfloat16
    share = texts[0].shape[0]
    count, images = slots * share, half_both.shape[0] // 2
    multiplier, bias = scalars[0], scalars[1]
    for slot, text in enumerate(texts):
        unit, tangent, _, _ = text_rows(text)
        text_both[slot * share : (slot + 1) * share, :] = unit.astype(bf16)
        text_both[count + slot * share : count + (slot + 1) * share, :] = tangent.astype(bf16)
    half, tangent_half = half_both[:images, :], half_both[images:, :]
    text_half, text_tangent_half = text_both[:count, :], text_both[count:, :]
    logits = multiplier * matmul_nt(text_half, half) + bias
    logit_rate = multiplier * (
        matmul_nt(text_half, tangent_half) + matmul_nt(text_tangent_half, half)
    )
    probability = jax.nn.sigmoid(logits)
    text_ids = lax.broadcasted_iota(jnp.int32, logits.shape, 0)
    image_ids = lax.broadcasted_iota(jnp.int32, logits.shape, 1)
    positive = jnp.where((text_ids < share) & (text_ids + start[0] == image_ids), 1.0, 0.0)
    value = probability - positive
    value_rate = probability * (1.0 - probability) * logit_rate
    weights[:, :images] = value_rate.astype(bf16)
    weights[:, images:] = value.astype(bf16)
    weights_turned[:, :count] = value_rate.T.astype(bf16)
    weights_turned[:, count:] = value.T.astype(bf16)


def text_block_kernel(slots, scalars, half_both, weights, *refs):
    texts, sums = refs[:slots], refs[slots:]
    share, images = texts[0].shape[0], half_both.shape[0] // 2
    grad = matmul(weights[:, images:], half_both[:images, :])
    grad_rate = matmul(weights[...], half_both[...])
    for slot, text in enumerate(texts):
        here = slice(slot * share, (slot + 1) * share)
        back = scalars[0] * back_rows(*text_rows(text), grad[here], grad_rate[here])
        if slot % 2 == 0:
            sums[slot // 2][...] = back
        else:
            at = slice(slot // 2 * share, (slot // 2 + 1) * share)
            sums[2][at, :] = back.astype(jnp.bfloat16)


def forward_kernel(own, middle, got, total, sent):
    share = own.shape[0]
    total[...] = own[...] + got[:share, :].astype(jnp.float32)
    sent[...] = (middle[...] + got[share:, :].astype(jnp.float32)).astype(jnp.bfloat16)


def image_block_kernel(main, tail, scalars, unit, tangent, factors, text_both, weights, kept, sent):
    rows, width = unit.shape[0] // 2, unit.shape[1]
    count, texts = width // (main + tail), text_both.shape[0] // 2
    grads = matmul(weights[:, texts:], text_both[:texts, :])
    grad_rates = matmul(weights[...], text_both[...])
    for shard in range(2):
        here = slice(shard * rows, (shard + 1) * rows)
        inverse, rate = factors[0, here, :1], factors[1, here, :1]
        back = back_rows(unit[here, :], tangent[here, :], inverse, rate, grads[here], grad_rates[here])
        back = scalars[0] * back
        for k in range(count):
            out = (kept, sent)[k % 2]
            to = slice(k // 2 * rows, (k // 2 + 1) * rows)
            out[to, shard * main : (shard + 1) * main] = back[:, k * main : (k + 1) * main]
            first = 2 * main + shard * tail
            taken = count * main + k * tail
            out[to, first : first + tail] = back[:, taken : taken + tail]


def text_sum_kernel(main, tail, own, *refs):
    count = own.shape[1] // (main + tail)
    got, outs = refs[:-count], refs[-count:]
    total = own[...]
    for ref in got:
        total = total + ref[...].astype(jnp.float32)
    for k, out in enumerate(outs):
        first = count * main + k * tail
        out[:, :main] = total[:, k * main : (k + 1) * main].astype(jnp.bfloat16)
        out[:, main:] = total[:, first : first + tail].astype(jnp.bfloat16)


def stack_kernel(*refs):
    rows = refs[0].shape[0]
    for k, ref in enumerate(refs[:-1]):
        refs[-1][k * rows : (k + 1) * rows, : ref.shape[1]] = ref[...]


def fold_kernel(*refs):
    value = jnp.concatenate([ref[...] for ref in refs[:-1]], axis=0)
    fold(refs[-1], 0, value, refs[-1].shape[1])


def turn_kernel(places, core, picture, caption, mine, other):
    for which, encodings in enumerate((picture, caption)):
        turned = encodings[...].astype(jnp.float32).T.astype(jnp.bfloat16)
        count = places.shape[0]
        size, rows = turned.shape[0] // count, turned.shape[1]
        fold = count // 4
        for block in range(count):
            taken = turned[block * size : (block + 1) * size, :]
            slot = places[block]
            at = pl.multiple_of(slot % fold * size, 16)
            for half in range(2):
                lanes = slice(half * rows, (half + 1) * rows)

                @pl.when(slot // fold == half)
                def _():
                    mine[pl.ds(which * fold * size + at, size), lanes] = taken

                @pl.when((slot // fold == 2 + half) & (core[0] == which))
                def _():
                    other[pl.ds(at, size), lanes] = taken


def shard_columns(value, main, tail, shard):
    at = 2 * main + shard * tail
    return jnp.concatenate(
        [value[:, shard * main : (shard + 1) * main], value[:, at : at + tail]], axis=1
    )


def image_pair_kernel(main, tail, share, near, kept, got, total, over_x, over_y, over_both):
    rows = total.shape[0]
    ours = kept[:rows, :] + got[:rows, :]
    theirs = kept[rows:, :] + got[rows:, :]
    total[...] = shard_columns(ours, main, tail, 0)
    fold(over_y, 0, shard_columns(ours, main, tail, 1), main)
    fold(over_both, 0, shard_columns(theirs, main, tail, 1), main)
    value = shard_columns(theirs, main, tail, 0)
    rounded = value.astype(jnp.bfloat16)
    fold(over_x, 0, rounded, main)
    left = value - rounded.astype(jnp.float32)
    left = jnp.where(near[0] == 0, left[: 2 * share], left[2 * share : 4 * share])
    fold(over_x, folded_rows(rows, main, tail), left, main)


def image_sum_kernel(main, tail, share, near, total, over_x, over_y, over_both, out):
    rows = total.shape[0]
    value = total[...]
    for source in (over_x, over_y, over_both):
        value = value + unfold(source, 0, rows, main, tail).astype(jnp.float32)
    left = unfold(over_x, folded_rows(rows, main, tail), 2 * share, main, tail)
    left = left.astype(jnp.float32)
    zero = jnp.zeros_like(left)
    far = near[0] == 0
    value = value + jnp.concatenate(
        [jnp.where(far, zero, left), jnp.where(far, left, zero)], axis=0
    )
    fold(out, 0, value.astype(jnp.bfloat16), main)


def head_kernel(main, tail, head, core, starts, mine, near, far, back, back_other, own, *refs):
    sent, (ordered,) = refs[:-1], refs[-1:]
    size, rows = own.shape[0], ordered.shape[1]
    share = rows // starts.shape[0]
    for which, ref in enumerate((back, back_other)):
        value = unfold(ref, 0, rows, main, tail)
        for k in range(starts.shape[0]):
            at = pl.ds(pl.multiple_of(starts[k], 16), share)
            ordered[which, at, :] = value[k * share : (k + 1) * share]
    count = (len(sent) + 1) // 2
    other = jnp.where(core[0] == head, near[...], far[...])
    for half in range(2):
        here = slice(head * count * size, (head + 1) * count * size)
        lanes = slice(half * rows, (half + 1) * rows)
        product = matmul(mine[here, lanes], ordered[0]) + matmul(other[:, lanes], ordered[1])
        for place in range(count):
            part = product[place * size : (place + 1) * size]
            slot = half * count + place
            if slot == 0:
                own[...] = part
            else:
                fold(sent[slot - 1], 0, part, main)


def final_kernel(main, tail, own, *refs):
    got, out = refs[:-1], refs[-1]
    total = own[...]
    for ref in got:
        total = total + unfold(ref, 0, own.shape[0], main, tail).astype(jnp.float32)
    out[...] = total


def final_kernel(main, tail, own, *refs):
    got, out = refs[:-1], refs[-1]
    size = own.shape[0]
    total = own[:, :main]
    for ref in got:
        total = total + ref[:size, :].astype(jnp.float32)
    out[:, :main] = total
    for rows_in, rows_out, lanes_out in folds(size, main, tail):
        total = own[rows_in, main:]
        for ref in got:
            total = total + ref[rows_out, lanes_out].astype(jnp.float32)
        out[rows_in, main:] = total


def packed(
    picture_averaged_encodings,
    caption_averaged_encodings,
    picture_mapping_matrix,
    caption_mapping_matrix,
    picture_weight_perturbation,
    caption_weight_perturbation,
    sharpness_multiplier,
    offset_additive,
):
    tensor_rank = lax.axis_index("tensor")
    data_rank = lax.axis_index("dp")
    count = lax.axis_size("tensor")
    data_count = lax.axis_size("dp")
    planes = data_count // 2
    rows, width = picture_averaged_encodings.shape
    cols = picture_mapping_matrix.shape[1]
    main = cols // 128 * 128
    tail = cols - main
    share = rows // count
    size = width // data_count
    wide = -(-2 * cols // 128) * 128
    f32, bf16 = jnp.float32, jnp.bfloat16
    ranks = jnp.arange(count, dtype=jnp.int32)
    starts = (ranks ^ tensor_rank) * share
    plain = ranks * share

    blocks = call(
        functools.partial(project_kernel, share),
        [((share, 2 * cols), bf16)] * 2 + [((2 * share, 2 * cols), bf16)],
        starts,
        caption_averaged_encodings,
        caption_mapping_matrix.T,
        caption_weight_perturbation.T,
    )
    text_far = swapped(blocks[2], "tensor", 2)
    (relay,) = call(relay_kernel, [((2 * share, 2 * cols), bf16)], blocks[1], text_far)
    text_near = swapped(relay, "tensor", 1)

    (image,) = call(
        functools.partial(project_kernel, share),
        [((rows, 2 * cols), bf16)],
        plain,
        picture_averaged_encodings,
        picture_mapping_matrix.T,
        picture_weight_perturbation.T,
        after=(blocks[0],),
    )
    image_other = swapped(image, "dp", 1)
    image_far = swapped(image, "tensor", 2)
    image_far_other = swapped(image_other, "tensor", 2)

    (text,) = call(
        functools.partial(text_rows_kernel, main, tail),
        [((share, 2 * width), bf16)],
        blocks[0],
        text_far,
        text_near,
    )
    text_two = swapped(text, "dp", 4)
    text_one = swapped(text, "dp", 2)
    text_three = swapped(text_two, "dp", 2)
    texts = [text, text_one, text_two, text_three]

    block_ids = jnp.arange(data_count, dtype=jnp.int32)
    slots = ((block_ids ^ data_rank) >> 1) + planes * ((block_ids ^ data_rank) & 1)
    core = (tensor_rank & 1).astype(jnp.int32).reshape(1)
    mine, other = call(
        turn_kernel,
        [((planes * size, 2 * rows), bf16), ((planes // 2 * size, 2 * rows), bf16)],
        slots,
        core,
        picture_averaged_encodings,
        caption_averaged_encodings,
        after=(image,),
    )
    other = swapped(other, "dp", 1)
    others = (other, swapped(other, "tensor", 1))

    (near,) = call(
        stack_kernel,
        [((4 * rows, wide), bf16)],
        image,
        image_other,
        image_far,
        image_far_other,
        after=(text_one, text_two, others[0]),
    )
    far = swapped(near, "tensor", 1)
    unit, tangent, half_both, factors = call(
        functools.partial(image_rows_kernel, main, tail, count),
        [
            ((2 * rows, width), f32),
            ((2 * rows, width), f32),
            ((4 * rows, width), bf16),
            ((2, 2 * rows, 128), f32),
        ],
        near,
        far,
    )

    scalars = jnp.concatenate([sharpness_multiplier, offset_additive])
    text_both, weights, weights_turned = call(
        functools.partial(weight_kernel, planes),
        [
            ((2 * planes * share, width), bf16),
            ((planes * share, 4 * rows), bf16),
            ((2 * rows, 2 * planes * share), bf16),
        ],
        (tensor_rank * share).astype(jnp.int32).reshape(1),
        scalars,
        half_both,
        *texts,
        after=(others[1],),
    )
    kept, sent = call(
        functools.partial(image_block_kernel, main, tail),
        [((2 * rows, wide), f32)] * 2,
        scalars,
        unit,
        tangent,
        factors,
        text_both,
        weights_turned,
    )
    outs = call(
        functools.partial(text_block_kernel, planes),
        [((share, width), f32)] * 2 + [((2 * share, width), bf16)],
        scalars,
        half_both,
        weights,
        *texts,
        after=(kept,),
    )

    near = (tensor_rank // 2).astype(jnp.int32).reshape(1)
    tall = folded_rows(rows, main, tail)
    more = folded_rows(2 * share, main, tail)
    total, to_x, to_y, to_both = call(
        functools.partial(image_pair_kernel, main, tail, share),
        [((rows, cols), f32), ((tall + more, main), bf16)] + [((tall, main), bf16)] * 2,
        near,
        kept,
        swapped(sent, "tensor", 1),
        after=(outs[0],),
    )
    flat = [(source, source ^ (count + 2)) for source in range(data_count * count)]
    (image_back,) = call(
        functools.partial(image_sum_kernel, main, tail, share),
        [((tall, main), bf16)],
        near,
        total,
        swapped(to_x, "tensor", 2),
        swapped(to_y, "dp", 1),
        lax.ppermute(to_both, ("dp", "tensor"), flat),
    )
    image_back_other = swapped(image_back, "dp", 1)

    def head(which, order, back, back_other):
        return call(
            functools.partial(head_kernel, main, tail, which),
            [((size, cols), f32)]
            + [((folded_rows(size, main, tail), main), bf16)] * (planes - 1),
            core,
            order,
            mine,
            *others,
            back,
            back_other,
            scratch=[((2, rows, cols), bf16)],
        )

    def summed(products):
        got = [swapped(products[k], "dp", 2 * k) for k in range(1, planes)]
        return call(
            functools.partial(final_kernel, main, tail), [((size, cols), f32)], products[0], *got
        )[0]

    image_products = head(0, plain, image_back, image_back_other)

    text_total, text_sent = call(
        forward_kernel,
        [((share, width), f32), ((share, width), bf16)],
        outs[0],
        outs[1],
        swapped(outs[2], "dp", 2),
    )
    blocks = call(
        functools.partial(text_sum_kernel, main, tail),
        [((share, cols), bf16)] * count,
        text_total,
        swapped(text_sent, "dp", 4),
        after=(image_back,),
    )
    got = [blocks[0]] + [swapped(blocks[k], "tensor", k) for k in range(1, count)]
    (text_back,) = call(fold_kernel, [((tall, main), bf16)], *got, after=(image_products[0],))
    text_back_other = swapped(text_back, "dp", 1)

    text_products = head(1, starts, text_back, text_back_other)
    return summed(image_products), summed(text_products)


def fits(mesh):
    return mesh.shape["tensor"] == 4 and mesh.shape["dp"] == 8


def solution(mesh):
    in_specs = (
        P("dp", None),
        P("dp", None),
        P(None, "tensor"),
        P(None, "tensor"),
        P(None, "tensor"),
        P(None, "tensor"),
        P(),
        P(),
    )
    out_specs = (P("dp", "tensor"), P("dp", "tensor"))
    local = packed if fits(mesh) else general
    return jax.shard_map(local, mesh=mesh, in_specs=in_specs, out_specs=out_specs, check_vma=False)
```

```python
import functools

import jax
import jax.numpy as jnp
from jax import lax
from jax.experimental import pallas as pl
from jax.experimental.pallas import tpu as pltpu
from jax.sharding import PartitionSpec as P

EPS = 1e-06


def swapped(value, axis, mask):
    count = lax.axis_size(axis)
    return lax.ppermute(value, axis, [(source, source ^ mask) for source in range(count)])


def matmul(left, right):
    return jnp.dot(left, right, preferred_element_type=jnp.float32)


def matmul_nt(left, right):
    return lax.dot_general(
        left, right, (((1,), (1,)), ((), ())), preferred_element_type=jnp.float32
    )


def matmul_tn(left, right):
    return lax.dot_general(
        left, right, (((0,), (0,)), ((), ())), preferred_element_type=jnp.float32
    )


def unit_parts(raw, raw_rate):
    values = raw.astype(jnp.float32)
    tangent = raw_rate.astype(jnp.float32)
    radius = jnp.sqrt(jnp.sum(values * values, axis=1, keepdims=True) + EPS)
    unit = values / radius
    rate = jnp.sum(unit * tangent, axis=1, keepdims=True)
    unit_tangent = (tangent - unit * rate) / radius
    return (unit, unit_tangent, radius, rate)


def unit_backward(unit, unit_tangent, radius, rate, grad, grad_rate):
    inner = jnp.sum(unit * grad, axis=1, keepdims=True)
    inner_rate = jnp.sum(unit_tangent * grad + unit * grad_rate, axis=1, keepdims=True)
    first = (grad - unit * inner) / radius
    return (grad_rate - unit_tangent * inner - unit * inner_rate - first * rate) / radius


def general(
    picture_averaged_encodings,
    caption_averaged_encodings,
    picture_mapping_matrix,
    caption_mapping_matrix,
    picture_weight_perturbation,
    caption_weight_perturbation,
    sharpness_multiplier,
    offset_additive,
):
    similarity_multiplier = sharpness_multiplier[0]
    logit_bias = offset_additive[0]
    tensor_rank = lax.axis_index("tensor")
    data_rank = lax.axis_index("dp")
    tensor_count = lax.axis_size("tensor")
    data_count = lax.axis_size("dp")
    planes = data_count // 2
    rows, width = picture_averaged_encodings.shape
    cols = picture_mapping_matrix.shape[1]
    share = rows // tensor_count
    out_rows = width // data_count
    half = jnp.bfloat16

    text = jnp.stack(
        [
            matmul(caption_averaged_encodings, caption_mapping_matrix).astype(half),
            matmul(caption_averaged_encodings, caption_weight_perturbation).astype(half),
        ]
    )
    image = jnp.stack(
        [
            matmul(picture_averaged_encodings, picture_mapping_matrix).astype(half),
            matmul(picture_averaged_encodings, picture_weight_perturbation).astype(half),
        ]
    )

    def share_of(value, axis, mask):
        start = (tensor_rank ^ mask) * share
        return lax.dynamic_slice_in_dim(value, start, share, axis)

    parts = [share_of(text, 1, 0)]
    for mask in range(1, tensor_count):
        parts.append(swapped(share_of(text, 1, mask), "tensor", mask))
    text = jnp.concatenate(parts, axis=2)
    slots = [text] + [swapped(text, "dp", 2 * mask) for mask in range(1, planes)]

    image = jnp.concatenate([image, swapped(image, "dp", 1)], axis=1)
    blocks = [image]
    mask = tensor_count // 2
    image_blocks = {0: image}
    while mask >= 1:
        held = sorted(image_blocks)
        sent = jnp.concatenate([image_blocks[k] for k in held], axis=2)
        got = swapped(sent, "tensor", mask)
        for place, k in enumerate(held):
            image_blocks[k ^ mask] = got[:, :, place * cols : (place + 1) * cols]
        mask //= 2
    image = jnp.concatenate([image_blocks[k] for k in range(tensor_count)], axis=2)
    text = jnp.concatenate(slots, axis=1)

    def out_columns(value, rank):
        taken = [
            lax.dynamic_slice_in_dim(value, (rank ^ (2 * mask)) * out_rows, out_rows, 1)
            for mask in range(planes)
        ]
        return jnp.concatenate(taken, axis=1)

    def plane_encodings(value):
        other = swapped(out_columns(value, data_rank ^ 1), "dp", 1)
        return jnp.concatenate([out_columns(value, data_rank), other], axis=0)

    picture_plane = plane_encodings(picture_averaged_encodings)
    ordered = jnp.concatenate(
        [share_of(caption_averaged_encodings, 0, mask) for mask in range(tensor_count)], axis=0
    )
    caption_plane = plane_encodings(ordered)

    image_unit, image_tangent, image_radius, image_rate = unit_parts(image[0], image[1])
    text_unit, text_tangent, text_radius, text_rate = unit_parts(text[0], text[1])
    image_half = image_unit.astype(half)
    image_tangent_half = image_tangent.astype(half)
    text_half = text_unit.astype(half)
    text_tangent_half = text_tangent.astype(half)

    logits = similarity_multiplier * matmul_nt(text_half, image_half) + logit_bias
    logit_rate = similarity_multiplier * (
        matmul_nt(text_half, image_tangent_half) + matmul_nt(text_tangent_half, image_half)
    )
    probability = jax.nn.sigmoid(logits)
    text_ids = lax.broadcasted_iota(jnp.int32, (logits.shape[0], 1), 0)
    image_ids = lax.broadcasted_iota(jnp.int32, (1, logits.shape[1]), 1)
    positive = ((text_ids < share) & (text_ids + tensor_rank * share == image_ids)).astype(
        jnp.float32
    )
    weight = (probability - positive).astype(half)
    weight_rate = (probability * (1.0 - probability) * logit_rate).astype(half)
    text_grad = similarity_multiplier * matmul(weight, image_half)
    text_grad_rate = similarity_multiplier * (
        matmul(weight_rate, image_half) + matmul(weight, image_tangent_half)
    )
    image_grad = similarity_multiplier * matmul_tn(weight, text_half)
    image_grad_rate = similarity_multiplier * (
        matmul_tn(weight_rate, text_half) + matmul_tn(weight, text_tangent_half)
    )

    text_back = unit_backward(
        text_unit, text_tangent, text_radius, text_rate, text_grad, text_grad_rate
    )
    image_back = unit_backward(
        image_unit, image_tangent, image_radius, image_rate, image_grad, image_grad_rate
    )

    total = text_back[:share]
    for mask in range(1, planes):
        sent = text_back[mask * share : (mask + 1) * share].astype(half)
        total = total + swapped(sent, "dp", 2 * mask).astype(jnp.float32)
    text_back = total.astype(half)
    parts = [text_back[:, :cols]]
    for mask in range(1, tensor_count):
        sent = text_back[:, mask * cols : (mask + 1) * cols]
        parts.append(swapped(sent, "tensor", mask))
    text_back = jnp.concatenate(parts, axis=0)
    text_back = jnp.concatenate([text_back, swapped(text_back, "dp", 1)], axis=0)

    image_blocks = {k: image_back[:, k * cols : (k + 1) * cols] for k in range(tensor_count)}
    mask = 1
    while mask < tensor_count:
        kept = [k for k in sorted(image_blocks) if not k & mask]
        sent = jnp.concatenate([image_blocks[k ^ mask] for k in kept], axis=1)
        got = swapped(sent, "tensor", mask).astype(jnp.float32)
        image_blocks = {
            k: image_blocks[k] + got[:, place * cols : (place + 1) * cols]
            for place, k in enumerate(kept)
        }
        mask *= 2
    image_back = image_blocks[0]
    got = swapped(image_back, "dp", 1)
    image_back = (
        image_back + jnp.concatenate([got[rows:], got[:rows]], axis=0)
    ).astype(half)

    def head(encodings, back):
        product = matmul_tn(encodings, back)
        total = product[:out_rows]
        for mask in range(1, planes):
            sent = product[mask * out_rows : (mask + 1) * out_rows].astype(half)
            total = total + swapped(sent, "dp", 2 * mask).astype(jnp.float32)
        return total

    return (head(picture_plane, image_back), head(caption_plane, text_back))


def call(kernel, outs, *args, after=(), scratch=()):
    count = len(args)

    def body(*refs):
        kernel(*refs[:count], *refs[count + len(after) :])

    def place(value):
        scalar = value.ndim == 1
        return pl.BlockSpec(memory_space=pltpu.SMEM if scalar else pltpu.VMEM)

    return pl.pallas_call(
        body,
        out_shape=[jax.ShapeDtypeStruct(shape, dtype) for shape, dtype in outs],
        in_specs=[place(value) for value in args]
        + [pl.BlockSpec(memory_space=pl.ANY) for _ in after],
        out_specs=[pl.BlockSpec(memory_space=pltpu.VMEM) for _ in outs],
        scratch_shapes=[pltpu.VMEM(shape, dtype) for shape, dtype in scratch],
        compiler_params=pltpu.CompilerParams(vmem_limit_bytes=24 * 1024 * 1024),
    )(*args, *after)


def folds(rows, main, tail):
    across = main // tail
    for k in range(rows // 16):
        here = slice(k * 16, (k + 1) * 16)
        at = rows + k // across * 16
        first = k % across * tail
        yield here, slice(at, at + 16), slice(first, first + tail)


def folded_rows(rows, main, tail):
    return rows + -(-rows // 16 // (main // tail)) * 16


def fold(out, first, value, main):
    rows, cols = value.shape
    out[first : first + rows, :] = value[:, :main].astype(out.dtype)
    for here, there, lanes in folds(rows, main, cols - main):
        there = slice(first + there.start, first + there.stop)
        out[there, lanes] = value[here, main:].astype(out.dtype)


def unfold(ref, first, rows, main, tail):
    tails = [
        ref[first + there.start : first + there.stop, lanes]
        for _, there, lanes in folds(rows, main, tail)
    ]
    return jnp.concatenate([ref[first : first + rows, :], jnp.concatenate(tails, axis=0)], axis=1)


def project_kernel(share, starts, encodings, weight, direction, *outs):
    main = weight.shape[0] // 128 * 128
    left = jnp.concatenate(
        [
            encodings[pl.ds(pl.multiple_of(starts[k], 16), share), :]
            for k in range(starts.shape[0])
        ],
        axis=0,
    )
    tails = jnp.concatenate([weight[main:, :], direction[main:, :]], axis=0)
    for right, first in ((weight[:main, :], 0), (direction[:main, :], main), (tails, 2 * main)):
        product = matmul_nt(left, right).astype(jnp.bfloat16)
        place = 0
        for out in outs:
            rows = out.shape[0]
            out[:, first : first + right.shape[0]] = product[place : place + rows]
            place += rows


def gathered(blocks, main, tail, which):
    first = 2 * main + which * tail
    mains = [block[:, which * main : (which + 1) * main] for block in blocks]
    tails = [block[:, first : first + tail] for block in blocks]
    return jnp.concatenate(mains + tails, axis=1)


def relay_kernel(mine, got, out):
    rows = mine.shape[0]
    out[:rows, :] = mine[...]
    out[rows:, :] = got[rows:, :]


def text_rows_kernel(main, tail, own, far, near, out):
    rows, width = own.shape[0], out.shape[1] // 2
    parts = (own[...], near[:rows, :], far[:rows, :], near[rows:, :])
    blocks = [part.astype(jnp.float32) for part in parts]
    out[:, :width] = gathered(blocks, main, tail, 0).astype(jnp.bfloat16)
    out[:, width:] = gathered(blocks, main, tail, 1).astype(jnp.bfloat16)


def row_factors(values, tangent):
    squares = jnp.sum(values * values, axis=1, keepdims=True)
    cross = jnp.sum(values * tangent, axis=1, keepdims=True)
    inverse = 1.0 / jnp.sqrt(squares + EPS)
    return inverse, cross * inverse


def unit_rows(values, tangent, inverse, rate):
    unit = values * inverse
    return unit, (tangent - unit * rate) * inverse


def back_rows(unit, tangent, inverse, rate, grad, grad_rate):
    inner = jnp.sum(unit * grad, axis=1, keepdims=True)
    inner_rate = jnp.sum(tangent * grad + unit * grad_rate, axis=1, keepdims=True)
    scaled = rate * inverse
    return (
        grad_rate - tangent * inner - grad * scaled + unit * (inner * scaled - inner_rate)
    ) * inverse


STEP = 48


def image_rows_kernel(main, tail, count, near, far, unit, tangent, half_both, factors):
    rows = unit.shape[0] // 2
    for shard in range(2):
        held = [
            (near, far)[k % 2].at[pl.ds((k - k % 2 + shard) * rows, rows), :] for k in range(count)
        ]

        @pl.loop(0, rows // STEP)
        def _(step):
            here = pl.ds(pl.multiple_of(step * STEP, STEP), STEP)
            there = pl.ds(pl.multiple_of(shard * rows + step * STEP, STEP), STEP)
            parts = [block[here, :].astype(jnp.float32) for block in held]
            values = gathered(parts, main, tail, 0)
            rates = gathered(parts, main, tail, 1)
            inverse, rate = row_factors(values, rates)
            one, two = unit_rows(values, rates, inverse, rate)
            unit[there, :] = one
            tangent[there, :] = two
            half_both[there, :] = one.astype(jnp.bfloat16)
            below = pl.ds(pl.multiple_of((2 + shard) * rows + step * STEP, STEP), STEP)
            half_both[below, :] = two.astype(jnp.bfloat16)
            factors[0, there, :] = jnp.broadcast_to(inverse, (STEP, 128))
            factors[1, there, :] = jnp.broadcast_to(rate, (STEP, 128))


def text_rows(text):
    width = text.shape[1] // 2
    values, rates = text[:, :width].astype(jnp.float32), text[:, width:].astype(jnp.float32)
    inverse, rate = row_factors(values, rates)
    return unit_rows(values, rates, inverse, rate) + (inverse, rate)


def weight_kernel(slots, first, start, scalars, half_both, *refs):
    texts, refs = refs[: slots - first], refs[slots - first :]
    held, (text_both, weights, weights_turned) = refs[:-3], refs[-3:]
    bf16 = jnp.bfloat16
    share = texts[0].shape[0]
    count, images = slots * share, half_both.shape[0] // 2
    done = first * share
    multiplier, bias = scalars[0], scalars[1]
    if held:
        for part in range(2):
            here = slice(part * done, (part + 1) * done)
            there = slice(part * count, part * count + done)
            text_both[there, :] = held[0][here, :]
            weights_turned[:, there] = held[2][:, here]
        weights[:done, :] = held[1][...]
    for slot, text in enumerate(texts):
        unit, tangent, _, _ = text_rows(text)
        at = done + slot * share
        text_both[at : at + share, :] = unit.astype(bf16)
        text_both[count + at : count + at + share, :] = tangent.astype(bf16)
    half, tangent_half = half_both[:images, :], half_both[images:, :]
    text_half, text_tangent_half = text_both[done:count, :], text_both[count + done :, :]
    logits = multiplier * matmul_nt(text_half, half) + bias
    logit_rate = multiplier * (
        matmul_nt(text_half, tangent_half) + matmul_nt(text_tangent_half, half)
    )
    probability = jax.nn.sigmoid(logits)
    text_ids = lax.broadcasted_iota(jnp.int32, logits.shape, 0) + done
    image_ids = lax.broadcasted_iota(jnp.int32, logits.shape, 1)
    positive = jnp.where((text_ids < share) & (text_ids + start[0] == image_ids), 1.0, 0.0)
    value = probability - positive
    value_rate = probability * (1.0 - probability) * logit_rate
    weights[done:, :images] = value_rate.astype(bf16)
    weights[done:, images:] = value.astype(bf16)
    weights_turned[:, done:count] = value_rate.T.astype(bf16)
    weights_turned[:, count + done :] = value.T.astype(bf16)


def text_block_kernel(slots, scalars, half_both, weights, *refs):
    texts, sums = refs[:slots], refs[slots:]
    share, images = texts[0].shape[0], half_both.shape[0] // 2
    grad = matmul(weights[:, images:], half_both[:images, :])
    grad_rate = matmul(weights[...], half_both[...])
    for slot, text in enumerate(texts):
        here = slice(slot * share, (slot + 1) * share)
        back = scalars[0] * back_rows(*text_rows(text), grad[here], grad_rate[here])
        at = slice(slot // 2 * share, (slot // 2 + 1) * share)
        sums[slot % 2][at, :] = back.astype(sums[slot % 2].dtype)


def forward_kernel(mine, got, total, sent):
    share = total.shape[0]
    total[...] = mine[:share, :] + got[:share, :].astype(jnp.float32)
    sent[...] = (mine[share:, :] + got[share:, :].astype(jnp.float32)).astype(jnp.bfloat16)


def image_block_kernel(main, tail, scalars, unit, tangent, factors, text_both, weights, kept, sent):
    rows, width = unit.shape[0] // 2, unit.shape[1]
    count, texts = width // (main + tail), text_both.shape[0] // 2
    grads = matmul(weights[:, texts:], text_both[:texts, :])
    grad_rates = matmul(weights[...], text_both[...])
    for shard in range(2):
        here = slice(shard * rows, (shard + 1) * rows)
        inverse, rate = factors[0, here, :1], factors[1, here, :1]
        back = back_rows(unit[here, :], tangent[here, :], inverse, rate, grads[here], grad_rates[here])
        back = scalars[0] * back
        for k in range(count):
            out = (kept, sent)[k % 2]
            to = slice(k // 2 * rows, (k // 2 + 1) * rows)
            out[to, shard * main : (shard + 1) * main] = back[:, k * main : (k + 1) * main]
            first = 2 * main + shard * tail
            taken = count * main + k * tail
            out[to, first : first + tail] = back[:, taken : taken + tail]


def text_sum_kernel(main, tail, own, *refs):
    count = own.shape[1] // (main + tail)
    got, outs = refs[:-count], refs[-count:]
    total = own[...]
    for ref in got:
        total = total + ref[...].astype(jnp.float32)
    for k, out in enumerate(outs):
        first = count * main + k * tail
        out[:, :main] = total[:, k * main : (k + 1) * main].astype(jnp.bfloat16)
        out[:, main:] = total[:, first : first + tail].astype(jnp.bfloat16)


def stack_kernel(*refs):
    rows = refs[0].shape[0]
    for k, ref in enumerate(refs[:-1]):
        refs[-1][k * rows : (k + 1) * rows, : ref.shape[1]] = ref[...]


def fold_kernel(*refs):
    value = jnp.concatenate([ref[...] for ref in refs[:-1]], axis=0)
    fold(refs[-1], 0, value, refs[-1].shape[1])


def turn_kernel(places, core, picture, caption, mine, other):
    for which, encodings in enumerate((picture, caption)):
        turned = encodings[...].astype(jnp.float32).T.astype(jnp.bfloat16)
        count = places.shape[0]
        size, rows = turned.shape[0] // count, turned.shape[1]
        fold = count // 4
        for block in range(count):
            taken = turned[block * size : (block + 1) * size, :]
            slot = places[block]
            at = pl.multiple_of(slot % fold * size, 16)
            for half in range(2):
                lanes = slice(half * rows, (half + 1) * rows)

                @pl.when(slot // fold == half)
                def _():
                    mine[pl.ds(which * fold * size + at, size), lanes] = taken

                @pl.when((slot // fold == 2 + half) & (core[0] == which))
                def _():
                    other[pl.ds(at, size), lanes] = taken


def shard_columns(value, main, tail, shard):
    at = 2 * main + shard * tail
    return jnp.concatenate(
        [value[:, shard * main : (shard + 1) * main], value[:, at : at + tail]], axis=1
    )


def image_pair_kernel(main, tail, share, near, kept, got, total, over_x, over_y, over_both):
    rows = total.shape[0]
    ours = kept[:rows, :] + got[:rows, :]
    theirs = kept[rows:, :] + got[rows:, :]
    total[...] = shard_columns(ours, main, tail, 0)
    fold(over_y, 0, shard_columns(ours, main, tail, 1), main)
    fold(over_both, 0, shard_columns(theirs, main, tail, 1), main)
    value = shard_columns(theirs, main, tail, 0)
    rounded = value.astype(jnp.bfloat16)
    fold(over_x, 0, rounded, main)
    left = value - rounded.astype(jnp.float32)
    left = jnp.where(near[0] == 0, left[: 2 * share], left[2 * share : 4 * share])
    fold(over_x, folded_rows(rows, main, tail), left, main)


def image_sum_kernel(main, tail, share, near, total, over_x, over_y, over_both, out):
    rows = total.shape[0]
    value = total[...]
    for source in (over_x, over_y, over_both):
        value = value + unfold(source, 0, rows, main, tail).astype(jnp.float32)
    left = unfold(over_x, folded_rows(rows, main, tail), 2 * share, main, tail)
    left = left.astype(jnp.float32)
    zero = jnp.zeros_like(left)
    far = near[0] == 0
    value = value + jnp.concatenate(
        [jnp.where(far, zero, left), jnp.where(far, left, zero)], axis=0
    )
    fold(out, 0, value.astype(jnp.bfloat16), main)


def head_kernel(main, tail, head, core, starts, mine, near, far, back, back_other, own, *refs):
    sent, (ordered,) = refs[:-1], refs[-1:]
    size, rows = own.shape[0], ordered.shape[1]
    share = rows // starts.shape[0]
    for which, ref in enumerate((back, back_other)):
        value = unfold(ref, 0, rows, main, tail)
        for k in range(starts.shape[0]):
            at = pl.ds(pl.multiple_of(starts[k], 16), share)
            ordered[which, at, :] = value[k * share : (k + 1) * share]
    count = (len(sent) + 1) // 2
    other = jnp.where(core[0] == head, near[...], far[...])
    for half in range(2):
        here = slice(head * count * size, (head + 1) * count * size)
        lanes = slice(half * rows, (half + 1) * rows)
        product = matmul(mine[here, lanes], ordered[0]) + matmul(other[:, lanes], ordered[1])
        for place in range(count):
            part = product[place * size : (place + 1) * size]
            slot = half * count + place
            if slot == 0:
                own[...] = part
            else:
                fold(sent[slot - 1], 0, part, main)


def final_kernel(main, tail, own, *refs):
    got, out = refs[:-1], refs[-1]
    total = own[...]
    for ref in got:
        total = total + unfold(ref, 0, own.shape[0], main, tail).astype(jnp.float32)
    out[...] = total


def final_kernel(main, tail, own, *refs):
    got, out = refs[:-1], refs[-1]
    size = own.shape[0]
    total = own[:, :main]
    for ref in got:
        total = total + ref[:size, :].astype(jnp.float32)
    out[:, :main] = total
    for rows_in, rows_out, lanes_out in folds(size, main, tail):
        total = own[rows_in, main:]
        for ref in got:
            total = total + ref[rows_out, lanes_out].astype(jnp.float32)
        out[rows_in, main:] = total


def packed(
    picture_averaged_encodings,
    caption_averaged_encodings,
    picture_mapping_matrix,
    caption_mapping_matrix,
    picture_weight_perturbation,
    caption_weight_perturbation,
    sharpness_multiplier,
    offset_additive,
):
    tensor_rank = lax.axis_index("tensor")
    data_rank = lax.axis_index("dp")
    count = lax.axis_size("tensor")
    data_count = lax.axis_size("dp")
    planes = data_count // 2
    rows, width = picture_averaged_encodings.shape
    cols = picture_mapping_matrix.shape[1]
    main = cols // 128 * 128
    tail = cols - main
    share = rows // count
    size = width // data_count
    wide = -(-2 * cols // 128) * 128
    f32, bf16 = jnp.float32, jnp.bfloat16
    ranks = jnp.arange(count, dtype=jnp.int32)
    starts = (ranks ^ tensor_rank) * share
    plain = ranks * share

    blocks = call(
        functools.partial(project_kernel, share),
        [((share, 2 * cols), bf16)] * 2 + [((2 * share, 2 * cols), bf16)],
        starts,
        caption_averaged_encodings,
        caption_mapping_matrix.T,
        caption_weight_perturbation.T,
    )
    text_far = swapped(blocks[2], "tensor", 2)
    (relay,) = call(relay_kernel, [((2 * share, 2 * cols), bf16)], blocks[1], text_far)
    text_near = swapped(relay, "tensor", 1)

    (image,) = call(
        functools.partial(project_kernel, share),
        [((rows, 2 * cols), bf16)],
        plain,
        picture_averaged_encodings,
        picture_mapping_matrix.T,
        picture_weight_perturbation.T,
        after=(blocks[0],),
    )
    image_other = swapped(image, "dp", 1)
    image_far = swapped(image, "tensor", 2)
    image_far_other = swapped(image_other, "tensor", 2)

    (text,) = call(
        functools.partial(text_rows_kernel, main, tail),
        [((share, 2 * width), bf16)],
        blocks[0],
        text_far,
        text_near,
    )
    text_two = swapped(text, "dp", 4)
    text_one = swapped(text, "dp", 2)
    text_three = swapped(text_two, "dp", 2)
    texts = [text, text_one, text_two, text_three]

    block_ids = jnp.arange(data_count, dtype=jnp.int32)
    slots = ((block_ids ^ data_rank) >> 1) + planes * ((block_ids ^ data_rank) & 1)
    core = (tensor_rank & 1).astype(jnp.int32).reshape(1)
    mine, other = call(
        turn_kernel,
        [((planes * size, 2 * rows), bf16), ((planes // 2 * size, 2 * rows), bf16)],
        slots,
        core,
        picture_averaged_encodings,
        caption_averaged_encodings,
        after=(image_other,),
    )
    other = swapped(other, "dp", 1)
    others = (other, swapped(other, "tensor", 1))

    (near,) = call(
        stack_kernel,
        [((4 * rows, wide), bf16)],
        image,
        image_other,
        image_far,
        image_far_other,
        after=(text_one, text_two, others[0]),
    )
    far = swapped(near, "tensor", 1)
    unit, tangent, half_both, factors = call(
        functools.partial(image_rows_kernel, main, tail, count),
        [
            ((2 * rows, width), f32),
            ((2 * rows, width), f32),
            ((4 * rows, width), bf16),
            ((2, 2 * rows, 128), f32),
        ],
        near,
        far,
    )

    scalars = jnp.concatenate([sharpness_multiplier, offset_additive])
    def block_weights(slots, first, *held, after=()):
        return call(
            functools.partial(weight_kernel, slots, first),
            [
                ((2 * slots * share, width), bf16),
                ((slots * share, 4 * rows), bf16),
                ((2 * rows, 2 * slots * share), bf16),
            ],
            (tensor_rank * share).astype(jnp.int32).reshape(1),
            scalars,
            half_both,
            *texts[first:slots],
            *held,
            after=after,
        )

    held = block_weights(planes - 1, 0, after=(others[1],))
    text_both, weights, weights_turned = block_weights(planes, planes - 1, *held)
    kept, sent = call(
        functools.partial(image_block_kernel, main, tail),
        [((2 * rows, wide), f32)] * 2,
        scalars,
        unit,
        tangent,
        factors,
        text_both,
        weights_turned,
    )
    outs = call(
        functools.partial(text_block_kernel, planes),
        [((2 * share, width), f32), ((2 * share, width), bf16)],
        scalars,
        half_both,
        weights,
        *texts,
        after=(kept,),
    )

    near = (tensor_rank // 2).astype(jnp.int32).reshape(1)
    tall = folded_rows(rows, main, tail)
    more = folded_rows(2 * share, main, tail)
    total, to_x, to_y, to_both = call(
        functools.partial(image_pair_kernel, main, tail, share),
        [((rows, cols), f32), ((tall + more, main), bf16)] + [((tall, main), bf16)] * 2,
        near,
        kept,
        swapped(sent, "tensor", 1),
        after=(outs[1],),
    )
    flat = [(source, source ^ (count + 2)) for source in range(data_count * count)]
    (image_back,) = call(
        functools.partial(image_sum_kernel, main, tail, share),
        [((tall, main), bf16)],
        near,
        total,
        swapped(to_x, "tensor", 2),
        swapped(to_y, "dp", 1),
        lax.ppermute(to_both, ("dp", "tensor"), flat),
    )
    image_back_other = swapped(image_back, "dp", 1)

    def head(which, order, back, back_other):
        return call(
            functools.partial(head_kernel, main, tail, which),
            [((size, cols), f32)]
            + [((folded_rows(size, main, tail), main), bf16)] * (planes - 1),
            core,
            order,
            mine,
            *others,
            back,
            back_other,
            scratch=[((2, rows, cols), bf16)],
        )

    def summed(products):
        got = [swapped(products[k], "dp", 2 * k) for k in range(1, planes)]
        return call(
            functools.partial(final_kernel, main, tail), [((size, cols), f32)], products[0], *got
        )[0]

    image_products = head(0, plain, image_back, image_back_other)

    text_total, text_sent = call(
        forward_kernel,
        [((share, width), f32), ((share, width), bf16)],
        outs[0],
        swapped(outs[1], "dp", 2),
    )
    blocks = call(
        functools.partial(text_sum_kernel, main, tail),
        [((share, cols), bf16)] * count,
        text_total,
        swapped(text_sent, "dp", 4),
        after=(image_back,),
    )
    got = [blocks[0]] + [swapped(blocks[k], "tensor", k) for k in range(1, count)]
    (text_back,) = call(fold_kernel, [((tall, main), bf16)], *got, after=(image_products[0],))
    text_back_other = swapped(text_back, "dp", 1)

    text_products = head(1, starts, text_back, text_back_other)
    return summed(image_products), summed(text_products)


def fits(mesh):
    return mesh.shape["tensor"] == 4 and mesh.shape["dp"] == 8


def solution(mesh):
    in_specs = (
        P("dp", None),
        P("dp", None),
        P(None, "tensor"),
        P(None, "tensor"),
        P(None, "tensor"),
        P(None, "tensor"),
        P(),
        P(),
    )
    out_specs = (P("dp", "tensor"), P("dp", "tensor"))
    local = packed if fits(mesh) else general
    return jax.shard_map(local, mesh=mesh, in_specs=in_specs, out_specs=out_specs, check_vma=False)
```

```python
import functools

import jax
import jax.numpy as jnp
from jax import lax
from jax.experimental import pallas as pl
from jax.experimental.pallas import tpu as pltpu
from jax.sharding import PartitionSpec as P

EPS = 1e-06


def swapped(value, axis, mask):
    count = lax.axis_size(axis)
    return lax.ppermute(value, axis, [(source, source ^ mask) for source in range(count)])


def matmul(left, right):
    return jnp.dot(left, right, preferred_element_type=jnp.float32)


def matmul_nt(left, right):
    return lax.dot_general(
        left, right, (((1,), (1,)), ((), ())), preferred_element_type=jnp.float32
    )


def matmul_tn(left, right):
    return lax.dot_general(
        left, right, (((0,), (0,)), ((), ())), preferred_element_type=jnp.float32
    )


def unit_parts(raw, raw_rate):
    values = raw.astype(jnp.float32)
    tangent = raw_rate.astype(jnp.float32)
    radius = jnp.sqrt(jnp.sum(values * values, axis=1, keepdims=True) + EPS)
    unit = values / radius
    rate = jnp.sum(unit * tangent, axis=1, keepdims=True)
    unit_tangent = (tangent - unit * rate) / radius
    return (unit, unit_tangent, radius, rate)


def unit_backward(unit, unit_tangent, radius, rate, grad, grad_rate):
    inner = jnp.sum(unit * grad, axis=1, keepdims=True)
    inner_rate = jnp.sum(unit_tangent * grad + unit * grad_rate, axis=1, keepdims=True)
    first = (grad - unit * inner) / radius
    return (grad_rate - unit_tangent * inner - unit * inner_rate - first * rate) / radius


def general(
    picture_averaged_encodings,
    caption_averaged_encodings,
    picture_mapping_matrix,
    caption_mapping_matrix,
    picture_weight_perturbation,
    caption_weight_perturbation,
    sharpness_multiplier,
    offset_additive,
):
    similarity_multiplier = sharpness_multiplier[0]
    logit_bias = offset_additive[0]
    tensor_rank = lax.axis_index("tensor")
    data_rank = lax.axis_index("dp")
    tensor_count = lax.axis_size("tensor")
    data_count = lax.axis_size("dp")
    planes = data_count // 2
    rows, width = picture_averaged_encodings.shape
    cols = picture_mapping_matrix.shape[1]
    share = rows // tensor_count
    out_rows = width // data_count
    half = jnp.bfloat16

    text = jnp.stack(
        [
            matmul(caption_averaged_encodings, caption_mapping_matrix).astype(half),
            matmul(caption_averaged_encodings, caption_weight_perturbation).astype(half),
        ]
    )
    image = jnp.stack(
        [
            matmul(picture_averaged_encodings, picture_mapping_matrix).astype(half),
            matmul(picture_averaged_encodings, picture_weight_perturbation).astype(half),
        ]
    )

    def share_of(value, axis, mask):
        start = (tensor_rank ^ mask) * share
        return lax.dynamic_slice_in_dim(value, start, share, axis)

    parts = [share_of(text, 1, 0)]
    for mask in range(1, tensor_count):
        parts.append(swapped(share_of(text, 1, mask), "tensor", mask))
    text = jnp.concatenate(parts, axis=2)
    slots = [text] + [swapped(text, "dp", 2 * mask) for mask in range(1, planes)]

    image = jnp.concatenate([image, swapped(image, "dp", 1)], axis=1)
    blocks = [image]
    mask = tensor_count // 2
    image_blocks = {0: image}
    while mask >= 1:
        held = sorted(image_blocks)
        sent = jnp.concatenate([image_blocks[k] for k in held], axis=2)
        got = swapped(sent, "tensor", mask)
        for place, k in enumerate(held):
            image_blocks[k ^ mask] = got[:, :, place * cols : (place + 1) * cols]
        mask //= 2
    image = jnp.concatenate([image_blocks[k] for k in range(tensor_count)], axis=2)
    text = jnp.concatenate(slots, axis=1)

    def out_columns(value, rank):
        taken = [
            lax.dynamic_slice_in_dim(value, (rank ^ (2 * mask)) * out_rows, out_rows, 1)
            for mask in range(planes)
        ]
        return jnp.concatenate(taken, axis=1)

    def plane_encodings(value):
        other = swapped(out_columns(value, data_rank ^ 1), "dp", 1)
        return jnp.concatenate([out_columns(value, data_rank), other], axis=0)

    picture_plane = plane_encodings(picture_averaged_encodings)
    ordered = jnp.concatenate(
        [share_of(caption_averaged_encodings, 0, mask) for mask in range(tensor_count)], axis=0
    )
    caption_plane = plane_encodings(ordered)

    image_unit, image_tangent, image_radius, image_rate = unit_parts(image[0], image[1])
    text_unit, text_tangent, text_radius, text_rate = unit_parts(text[0], text[1])
    image_half = image_unit.astype(half)
    image_tangent_half = image_tangent.astype(half)
    text_half = text_unit.astype(half)
    text_tangent_half = text_tangent.astype(half)

    logits = similarity_multiplier * matmul_nt(text_half, image_half) + logit_bias
    logit_rate = similarity_multiplier * (
        matmul_nt(text_half, image_tangent_half) + matmul_nt(text_tangent_half, image_half)
    )
    probability = jax.nn.sigmoid(logits)
    text_ids = lax.broadcasted_iota(jnp.int32, (logits.shape[0], 1), 0)
    image_ids = lax.broadcasted_iota(jnp.int32, (1, logits.shape[1]), 1)
    positive = ((text_ids < share) & (text_ids + tensor_rank * share == image_ids)).astype(
        jnp.float32
    )
    weight = (probability - positive).astype(half)
    weight_rate = (probability * (1.0 - probability) * logit_rate).astype(half)
    text_grad = similarity_multiplier * matmul(weight, image_half)
    text_grad_rate = similarity_multiplier * (
        matmul(weight_rate, image_half) + matmul(weight, image_tangent_half)
    )
    image_grad = similarity_multiplier * matmul_tn(weight, text_half)
    image_grad_rate = similarity_multiplier * (
        matmul_tn(weight_rate, text_half) + matmul_tn(weight, text_tangent_half)
    )

    text_back = unit_backward(
        text_unit, text_tangent, text_radius, text_rate, text_grad, text_grad_rate
    )
    image_back = unit_backward(
        image_unit, image_tangent, image_radius, image_rate, image_grad, image_grad_rate
    )

    total = text_back[:share]
    for mask in range(1, planes):
        sent = text_back[mask * share : (mask + 1) * share].astype(half)
        total = total + swapped(sent, "dp", 2 * mask).astype(jnp.float32)
    text_back = total.astype(half)
    parts = [text_back[:, :cols]]
    for mask in range(1, tensor_count):
        sent = text_back[:, mask * cols : (mask + 1) * cols]
        parts.append(swapped(sent, "tensor", mask))
    text_back = jnp.concatenate(parts, axis=0)
    text_back = jnp.concatenate([text_back, swapped(text_back, "dp", 1)], axis=0)

    image_blocks = {k: image_back[:, k * cols : (k + 1) * cols] for k in range(tensor_count)}
    mask = 1
    while mask < tensor_count:
        kept = [k for k in sorted(image_blocks) if not k & mask]
        sent = jnp.concatenate([image_blocks[k ^ mask] for k in kept], axis=1)
        got = swapped(sent, "tensor", mask).astype(jnp.float32)
        image_blocks = {
            k: image_blocks[k] + got[:, place * cols : (place + 1) * cols]
            for place, k in enumerate(kept)
        }
        mask *= 2
    image_back = image_blocks[0]
    got = swapped(image_back, "dp", 1)
    image_back = (
        image_back + jnp.concatenate([got[rows:], got[:rows]], axis=0)
    ).astype(half)

    def head(encodings, back):
        product = matmul_tn(encodings, back)
        total = product[:out_rows]
        for mask in range(1, planes):
            sent = product[mask * out_rows : (mask + 1) * out_rows].astype(half)
            total = total + swapped(sent, "dp", 2 * mask).astype(jnp.float32)
        return total

    return (head(picture_plane, image_back), head(caption_plane, text_back))


def call(kernel, outs, *args, after=(), scratch=(), fetched=False):
    count = len(args)

    def body(*refs):
        kernel(*refs[:count], *refs[count + len(after) :])

    def place(value):
        if value.ndim == 1:
            return pl.BlockSpec(memory_space=pltpu.SMEM)
        return pl.BlockSpec(memory_space=pltpu.HBM if fetched else pltpu.VMEM)

    return pl.pallas_call(
        body,
        out_shape=[jax.ShapeDtypeStruct(shape, dtype) for shape, dtype in outs],
        in_specs=[place(value) for value in args]
        + [pl.BlockSpec(memory_space=pl.ANY) for _ in after],
        out_specs=[pl.BlockSpec(memory_space=pltpu.VMEM) for _ in outs],
        scratch_shapes=list(scratch),
        compiler_params=pltpu.CompilerParams(
            vmem_limit_bytes=(62 if fetched else 14) * 1024 * 1024
        ),
    )(*args, *after)


def folds(rows, main, tail):
    across = main // tail
    for k in range(rows // 16):
        here = slice(k * 16, (k + 1) * 16)
        at = rows + k // across * 16
        first = k % across * tail
        yield here, slice(at, at + 16), slice(first, first + tail)


def folded_rows(rows, main, tail):
    return rows + -(-rows // 16 // (main // tail)) * 16


def fold(out, first, value, main):
    rows, cols = value.shape
    out[first : first + rows, :] = value[:, :main].astype(out.dtype)
    for here, there, lanes in folds(rows, main, cols - main):
        there = slice(first + there.start, first + there.stop)
        out[there, lanes] = value[here, main:].astype(out.dtype)


def unfold(ref, first, rows, main, tail):
    tails = [
        ref[first + there.start : first + there.stop, lanes]
        for _, there, lanes in folds(rows, main, tail)
    ]
    return jnp.concatenate([ref[first : first + rows, :], jnp.concatenate(tails, axis=0)], axis=1)


def fetch_project_kernel(share, parts, starts, encodings, weight, direction, *refs):
    outs, held, done = refs[:-4], refs[-4:-1], refs[-1]
    copies = []
    for which, (source, target) in enumerate(zip((encodings, weight, direction), held)):
        rows = source.shape[0] // parts
        for part in range(parts):
            here = pl.ds(part * rows, rows)
            copies.append(
                pltpu.make_async_copy(source.at[here, :], target.at[here, :], done.at[which, part])
            )
    for copy in copies:
        copy.start()
    for copy in copies:
        copy.wait()
    project_kernel(share, starts, *held, *outs)


def project_kernel(share, starts, encodings, weight, direction, *outs):
    main = weight.shape[0] // 128 * 128
    left = jnp.concatenate(
        [
            encodings[pl.ds(pl.multiple_of(starts[k], 16), share), :]
            for k in range(starts.shape[0])
        ],
        axis=0,
    )
    tails = jnp.concatenate([weight[main:, :], direction[main:, :]], axis=0)
    for right, first in ((weight[:main, :], 0), (direction[:main, :], main), (tails, 2 * main)):
        product = matmul_nt(left, right).astype(jnp.bfloat16)
        place = 0
        for out in outs:
            rows = out.shape[0]
            out[:, first : first + right.shape[0]] = product[place : place + rows]
            place += rows


def gathered(blocks, main, tail, which):
    first = 2 * main + which * tail
    mains = [block[:, which * main : (which + 1) * main] for block in blocks]
    tails = [block[:, first : first + tail] for block in blocks]
    return jnp.concatenate(mains + tails, axis=1)


def relay_kernel(mine, got, out):
    rows = mine.shape[0]
    out[:rows, :] = mine[...]
    out[rows:, :] = got[rows:, :]


def text_rows_kernel(main, tail, own, far, near, out):
    rows, width = own.shape[0], out.shape[1] // 2
    parts = (own[...], near[:rows, :], far[:rows, :], near[rows:, :])
    blocks = [part.astype(jnp.float32) for part in parts]
    out[:, :width] = gathered(blocks, main, tail, 0).astype(jnp.bfloat16)
    out[:, width:] = gathered(blocks, main, tail, 1).astype(jnp.bfloat16)


def row_factors(values, tangent):
    squares = jnp.sum(values * values, axis=1, keepdims=True)
    cross = jnp.sum(values * tangent, axis=1, keepdims=True)
    inverse = 1.0 / jnp.sqrt(squares + EPS)
    return inverse, cross * inverse


def unit_rows(values, tangent, inverse, rate):
    unit = values * inverse
    return unit, (tangent - unit * rate) * inverse


def back_rows(unit, tangent, inverse, rate, grad, grad_rate):
    inner = jnp.sum(unit * grad, axis=1, keepdims=True)
    inner_rate = jnp.sum(tangent * grad + unit * grad_rate, axis=1, keepdims=True)
    scaled = rate * inverse
    return (
        grad_rate - tangent * inner - grad * scaled + unit * (inner * scaled - inner_rate)
    ) * inverse


STEP = 48


def image_rows_kernel(main, tail, count, near, far, unit, tangent, half_both, factors):
    rows = unit.shape[0] // 2
    for shard in range(2):
        held = [
            (near, far)[k % 2].at[pl.ds((k - k % 2 + shard) * rows, rows), :] for k in range(count)
        ]

        @pl.loop(0, rows // STEP)
        def _(step):
            here = pl.ds(pl.multiple_of(step * STEP, STEP), STEP)
            there = pl.ds(pl.multiple_of(shard * rows + step * STEP, STEP), STEP)
            parts = [block[here, :].astype(jnp.float32) for block in held]
            values = gathered(parts, main, tail, 0)
            rates = gathered(parts, main, tail, 1)
            inverse, rate = row_factors(values, rates)
            one, two = unit_rows(values, rates, inverse, rate)
            unit[there, :] = one
            tangent[there, :] = two
            half_both[there, :] = one.astype(jnp.bfloat16)
            below = pl.ds(pl.multiple_of((2 + shard) * rows + step * STEP, STEP), STEP)
            half_both[below, :] = two.astype(jnp.bfloat16)
            factors[0, there, :] = jnp.broadcast_to(inverse, (STEP, 128))
            factors[1, there, :] = jnp.broadcast_to(rate, (STEP, 128))


def text_rows(text):
    width = text.shape[1] // 2
    values, rates = text[:, :width].astype(jnp.float32), text[:, width:].astype(jnp.float32)
    inverse, rate = row_factors(values, rates)
    return unit_rows(values, rates, inverse, rate) + (inverse, rate)


def weight_kernel(slots, first, start, scalars, half_both, *refs):
    texts, refs = refs[: slots - first], refs[slots - first :]
    held, (text_both, weights, weights_turned) = refs[:-3], refs[-3:]
    bf16 = jnp.bfloat16
    share = texts[0].shape[0]
    count, images = slots * share, half_both.shape[0] // 2
    done = first * share
    multiplier, bias = scalars[0], scalars[1]
    if held:
        for part in range(2):
            here = slice(part * done, (part + 1) * done)
            there = slice(part * count, part * count + done)
            text_both[there, :] = held[0][here, :]
            weights_turned[:, there] = held[2][:, here]
        weights[:done, :] = held[1][...]
    for slot, text in enumerate(texts):
        unit, tangent, _, _ = text_rows(text)
        at = done + slot * share
        text_both[at : at + share, :] = unit.astype(bf16)
        text_both[count + at : count + at + share, :] = tangent.astype(bf16)
    half, tangent_half = half_both[:images, :], half_both[images:, :]
    text_half, text_tangent_half = text_both[done:count, :], text_both[count + done :, :]
    logits = multiplier * matmul_nt(text_half, half) + bias
    logit_rate = multiplier * (
        matmul_nt(text_half, tangent_half) + matmul_nt(text_tangent_half, half)
    )
    probability = jax.nn.sigmoid(logits)
    text_ids = lax.broadcasted_iota(jnp.int32, logits.shape, 0) + done
    image_ids = lax.broadcasted_iota(jnp.int32, logits.shape, 1)
    positive = jnp.where((text_ids < share) & (text_ids + start[0] == image_ids), 1.0, 0.0)
    value = probability - positive
    value_rate = probability * (1.0 - probability) * logit_rate
    weights[done:, :images] = value_rate.astype(bf16)
    weights[done:, images:] = value.astype(bf16)
    weights_turned[:, done:count] = value_rate.T.astype(bf16)
    weights_turned[:, count + done :] = value.T.astype(bf16)


def text_block_kernel(slots, scalars, half_both, weights, *refs):
    texts, sums = refs[:slots], refs[slots:]
    share, images = texts[0].shape[0], half_both.shape[0] // 2
    grad = matmul(weights[:, images:], half_both[:images, :])
    grad_rate = matmul(weights[...], half_both[...])
    for slot, text in enumerate(texts):
        here = slice(slot * share, (slot + 1) * share)
        back = scalars[0] * back_rows(*text_rows(text), grad[here], grad_rate[here])
        at = slice(slot // 2 * share, (slot // 2 + 1) * share)
        sums[slot % 2][at, :] = back.astype(sums[slot % 2].dtype)


def forward_kernel(mine, got, total, sent):
    share = total.shape[0]
    total[...] = mine[:share, :] + got[:share, :].astype(jnp.float32)
    sent[...] = (mine[share:, :] + got[share:, :].astype(jnp.float32)).astype(jnp.bfloat16)


def image_block_kernel(main, tail, scalars, unit, tangent, factors, text_both, weights, kept, sent):
    rows, width = unit.shape[0] // 2, unit.shape[1]
    count, texts = width // (main + tail), text_both.shape[0] // 2
    grads = matmul(weights[:, texts:], text_both[:texts, :])
    grad_rates = matmul(weights[...], text_both[...])
    for shard in range(2):
        here = slice(shard * rows, (shard + 1) * rows)
        inverse, rate = factors[0, here, :1], factors[1, here, :1]
        back = back_rows(unit[here, :], tangent[here, :], inverse, rate, grads[here], grad_rates[here])
        back = scalars[0] * back
        for k in range(count):
            out = (kept, sent)[k % 2]
            to = slice(k // 2 * rows, (k // 2 + 1) * rows)
            out[to, shard * main : (shard + 1) * main] = back[:, k * main : (k + 1) * main]
            first = 2 * main + shard * tail
            taken = count * main + k * tail
            out[to, first : first + tail] = back[:, taken : taken + tail]


def text_sum_kernel(main, tail, own, *refs):
    count = own.shape[1] // (main + tail)
    got, outs = refs[:-count], refs[-count:]
    total = own[...]
    for ref in got:
        total = total + ref[...].astype(jnp.float32)
    for k, out in enumerate(outs):
        first = count * main + k * tail
        out[:, :main] = total[:, k * main : (k + 1) * main].astype(jnp.bfloat16)
        out[:, main:] = total[:, first : first + tail].astype(jnp.bfloat16)


def stack_kernel(*refs):
    rows = refs[0].shape[0]
    for k, ref in enumerate(refs[:-1]):
        refs[-1][k * rows : (k + 1) * rows, : ref.shape[1]] = ref[...]


def fold_kernel(*refs):
    value = jnp.concatenate([ref[...] for ref in refs[:-1]], axis=0)
    fold(refs[-1], 0, value, refs[-1].shape[1])


def turn_kernel(places, core, picture, caption, mine, other):
    for which, encodings in enumerate((picture, caption)):
        turned = encodings[...].T
        count = places.shape[0]
        size, rows = turned.shape[0] // count, turned.shape[1]
        fold = count // 4
        for block in range(count):
            taken = turned[block * size : (block + 1) * size, :]
            slot = places[block]
            at = pl.multiple_of(slot % fold * size, 16)
            for half in range(2):
                lanes = slice(half * rows, (half + 1) * rows)

                @pl.when(slot // fold == half)
                def _():
                    mine[pl.ds(which * fold * size + at, size), lanes] = taken

                @pl.when((slot // fold == 2 + half) & (core[0] == which))
                def _():
                    other[pl.ds(at, size), lanes] = taken


def shard_columns(value, main, tail, shard):
    at = 2 * main + shard * tail
    return jnp.concatenate(
        [value[:, shard * main : (shard + 1) * main], value[:, at : at + tail]], axis=1
    )


def image_pair_kernel(main, tail, share, near, kept, got, total, over_x, over_y, over_both):
    rows = total.shape[0]
    ours = kept[:rows, :] + got[:rows, :]
    theirs = kept[rows:, :] + got[rows:, :]
    total[...] = shard_columns(ours, main, tail, 0)
    fold(over_y, 0, shard_columns(ours, main, tail, 1), main)
    fold(over_both, 0, shard_columns(theirs, main, tail, 1), main)
    value = shard_columns(theirs, main, tail, 0)
    rounded = value.astype(jnp.bfloat16)
    fold(over_x, 0, rounded, main)
    left = value - rounded.astype(jnp.float32)
    left = jnp.where(near[0] == 0, left[: 2 * share], left[2 * share : 4 * share])
    fold(over_x, folded_rows(rows, main, tail), left, main)


def image_sum_kernel(main, tail, share, near, total, over_x, over_y, over_both, out):
    rows = total.shape[0]
    value = total[...]
    for source in (over_x, over_y, over_both):
        value = value + unfold(source, 0, rows, main, tail).astype(jnp.float32)
    left = unfold(over_x, folded_rows(rows, main, tail), 2 * share, main, tail)
    left = left.astype(jnp.float32)
    zero = jnp.zeros_like(left)
    far = near[0] == 0
    value = value + jnp.concatenate(
        [jnp.where(far, zero, left), jnp.where(far, left, zero)], axis=0
    )
    fold(out, 0, value.astype(jnp.bfloat16), main)


def head_kernel(main, tail, head, core, starts, mine, near, far, back, back_other, own, *refs):
    sent, (ordered,) = refs[:-1], refs[-1:]
    size, rows = own.shape[0], ordered.shape[1]
    share = rows // starts.shape[0]
    for which, ref in enumerate((back, back_other)):
        value = unfold(ref, 0, rows, main, tail)
        for k in range(starts.shape[0]):
            at = pl.ds(pl.multiple_of(starts[k], 16), share)
            ordered[which, at, :] = value[k * share : (k + 1) * share]
    count = (len(sent) + 1) // 2
    other = jnp.where(core[0] == head, near[...], far[...])
    for half in range(2):
        here = slice(head * count * size, (head + 1) * count * size)
        lanes = slice(half * rows, (half + 1) * rows)
        product = matmul(mine[here, lanes], ordered[0]) + matmul(other[:, lanes], ordered[1])
        for place in range(count):
            part = product[place * size : (place + 1) * size]
            slot = half * count + place
            if slot == 0:
                own[...] = part
            else:
                fold(sent[slot - 1], 0, part, main)


def final_kernel(main, tail, own, *refs):
    got, out = refs[:-1], refs[-1]
    total = own[...]
    for ref in got:
        total = total + unfold(ref, 0, own.shape[0], main, tail).astype(jnp.float32)
    out[...] = total


def final_kernel(main, tail, own, *refs):
    got, out = refs[:-1], refs[-1]
    size = own.shape[0]
    total = own[:, :main]
    for ref in got:
        total = total + ref[:size, :].astype(jnp.float32)
    out[:, :main] = total
    for rows_in, rows_out, lanes_out in folds(size, main, tail):
        total = own[rows_in, main:]
        for ref in got:
            total = total + ref[rows_out, lanes_out].astype(jnp.float32)
        out[rows_in, main:] = total


def packed(
    picture_averaged_encodings,
    caption_averaged_encodings,
    picture_mapping_matrix,
    caption_mapping_matrix,
    picture_weight_perturbation,
    caption_weight_perturbation,
    sharpness_multiplier,
    offset_additive,
):
    tensor_rank = lax.axis_index("tensor")
    data_rank = lax.axis_index("dp")
    count = lax.axis_size("tensor")
    data_count = lax.axis_size("dp")
    planes = data_count // 2
    rows, width = picture_averaged_encodings.shape
    cols = picture_mapping_matrix.shape[1]
    main = cols // 128 * 128
    tail = cols - main
    share = rows // count
    size = width // data_count
    wide = -(-2 * cols // 128) * 128
    f32, bf16 = jnp.float32, jnp.bfloat16
    ranks = jnp.arange(count, dtype=jnp.int32)
    starts = (ranks ^ tensor_rank) * share
    plain = ranks * share

    parts = 3
    blocks = call(
        functools.partial(fetch_project_kernel, share, parts),
        [((share, 2 * cols), bf16)] * 2 + [((2 * share, 2 * cols), bf16)],
        starts,
        caption_averaged_encodings,
        caption_mapping_matrix.T,
        caption_weight_perturbation.T,
        scratch=[
            pltpu.VMEM((rows, width), bf16),
            pltpu.VMEM((cols, width), bf16),
            pltpu.VMEM((cols, width), bf16),
            pltpu.SemaphoreType.DMA((3, parts)),
        ],
        fetched=True,
    )
    text_far = swapped(blocks[2], "tensor", 2)
    (relay,) = call(relay_kernel, [((2 * share, 2 * cols), bf16)], blocks[1], text_far)
    text_near = swapped(relay, "tensor", 1)

    (image,) = call(
        functools.partial(project_kernel, share),
        [((rows, 2 * cols), bf16)],
        plain,
        picture_averaged_encodings,
        picture_mapping_matrix.T,
        picture_weight_perturbation.T,
        after=(blocks[0],),
    )
    image_other = swapped(image, "dp", 1)
    image_far = swapped(image, "tensor", 2)
    image_far_other = swapped(image_other, "tensor", 2)

    (text,) = call(
        functools.partial(text_rows_kernel, main, tail),
        [((share, 2 * width), bf16)],
        blocks[0],
        text_far,
        text_near,
    )
    text_two = swapped(text, "dp", 4)
    text_one = swapped(text, "dp", 2)
    text_three = swapped(text_two, "dp", 2)
    texts = [text, text_one, text_two, text_three]

    block_ids = jnp.arange(data_count, dtype=jnp.int32)
    slots = ((block_ids ^ data_rank) >> 1) + planes * ((block_ids ^ data_rank) & 1)
    core = (tensor_rank & 1).astype(jnp.int32).reshape(1)
    mine, other = call(
        turn_kernel,
        [((planes * size, 2 * rows), bf16), ((planes // 2 * size, 2 * rows), bf16)],
        slots,
        core,
        picture_averaged_encodings,
        caption_averaged_encodings,
        after=(image_other,),
    )
    other = swapped(other, "dp", 1)
    others = (other, swapped(other, "tensor", 1))

    (near,) = call(
        stack_kernel,
        [((4 * rows, wide), bf16)],
        image,
        image_other,
        image_far,
        image_far_other,
        after=(text_one, text_two, others[0]),
    )
    far = swapped(near, "tensor", 1)
    unit, tangent, half_both, factors = call(
        functools.partial(image_rows_kernel, main, tail, count),
        [
            ((2 * rows, width), f32),
            ((2 * rows, width), f32),
            ((4 * rows, width), bf16),
            ((2, 2 * rows, 128), f32),
        ],
        near,
        far,
    )

    scalars = jnp.concatenate([sharpness_multiplier, offset_additive])
    def block_weights(slots, first, *held, after=()):
        return call(
            functools.partial(weight_kernel, slots, first),
            [
                ((2 * slots * share, width), bf16),
                ((slots * share, 4 * rows), bf16),
                ((2 * rows, 2 * slots * share), bf16),
            ],
            (tensor_rank * share).astype(jnp.int32).reshape(1),
            scalars,
            half_both,
            *texts[first:slots],
            *held,
            after=after,
        )

    held = block_weights(planes - 1, 0, after=(others[1],))
    text_both, weights, weights_turned = block_weights(planes, planes - 1, *held)
    kept, sent = call(
        functools.partial(image_block_kernel, main, tail),
        [((2 * rows, wide), f32)] * 2,
        scalars,
        unit,
        tangent,
        factors,
        text_both,
        weights_turned,
    )
    outs = call(
        functools.partial(text_block_kernel, planes),
        [((2 * share, width), f32), ((2 * share, width), bf16)],
        scalars,
        half_both,
        weights,
        *texts,
        after=(kept,),
    )

    near = (tensor_rank // 2).astype(jnp.int32).reshape(1)
    tall = folded_rows(rows, main, tail)
    more = folded_rows(2 * share, main, tail)
    total, to_x, to_y, to_both = call(
        functools.partial(image_pair_kernel, main, tail, share),
        [((rows, cols), f32), ((tall + more, main), bf16)] + [((tall, main), bf16)] * 2,
        near,
        kept,
        swapped(sent, "tensor", 1),
        after=(outs[1],),
    )
    flat = [(source, source ^ (count + 2)) for source in range(data_count * count)]
    (image_back,) = call(
        functools.partial(image_sum_kernel, main, tail, share),
        [((tall, main), bf16)],
        near,
        total,
        swapped(to_x, "tensor", 2),
        swapped(to_y, "dp", 1),
        lax.ppermute(to_both, ("dp", "tensor"), flat),
    )
    image_back_other = swapped(image_back, "dp", 1)

    def head(which, order, back, back_other):
        return call(
            functools.partial(head_kernel, main, tail, which),
            [((size, cols), f32)]
            + [((folded_rows(size, main, tail), main), bf16)] * (planes - 1),
            core,
            order,
            mine,
            *others,
            back,
            back_other,
            scratch=[pltpu.VMEM((2, rows, cols), bf16)],
        )

    def summed(products):
        got = [swapped(products[k], "dp", 2 * k) for k in range(1, planes)]
        return call(
            functools.partial(final_kernel, main, tail), [((size, cols), f32)], products[0], *got
        )[0]

    image_products = head(0, plain, image_back, image_back_other)

    text_total, text_sent = call(
        forward_kernel,
        [((share, width), f32), ((share, width), bf16)],
        outs[0],
        swapped(outs[1], "dp", 2),
    )
    blocks = call(
        functools.partial(text_sum_kernel, main, tail),
        [((share, cols), bf16)] * count,
        text_total,
        swapped(text_sent, "dp", 4),
        after=(image_back,),
    )
    got = [blocks[0]] + [swapped(blocks[k], "tensor", k) for k in range(1, count)]
    (text_back,) = call(fold_kernel, [((tall, main), bf16)], *got, after=(image_products[0],))
    text_back_other = swapped(text_back, "dp", 1)

    text_products = head(1, starts, text_back, text_back_other)
    return summed(image_products), summed(text_products)


def fits(mesh):
    return mesh.shape["tensor"] == 4 and mesh.shape["dp"] == 8


def solution(mesh):
    in_specs = (
        P("dp", None),
        P("dp", None),
        P(None, "tensor"),
        P(None, "tensor"),
        P(None, "tensor"),
        P(None, "tensor"),
        P(),
        P(),
    )
    out_specs = (P("dp", "tensor"), P("dp", "tensor"))
    local = packed if fits(mesh) else general
    return jax.shard_map(local, mesh=mesh, in_specs=in_specs, out_specs=out_specs, check_vma=False)
```

```python
import functools

import jax
import jax.numpy as jnp
from jax import lax
from jax.experimental import pallas as pl
from jax.experimental.pallas import tpu as pltpu
from jax.sharding import PartitionSpec as P

EPS = 1e-06


def swapped(value, axis, mask):
    count = lax.axis_size(axis)
    return lax.ppermute(value, axis, [(source, source ^ mask) for source in range(count)])


def matmul(left, right):
    return jnp.dot(left, right, preferred_element_type=jnp.float32)


def matmul_nt(left, right):
    return lax.dot_general(
        left, right, (((1,), (1,)), ((), ())), preferred_element_type=jnp.float32
    )


def matmul_tn(left, right):
    return lax.dot_general(
        left, right, (((0,), (0,)), ((), ())), preferred_element_type=jnp.float32
    )


def unit_parts(raw, raw_rate):
    values = raw.astype(jnp.float32)
    tangent = raw_rate.astype(jnp.float32)
    radius = jnp.sqrt(jnp.sum(values * values, axis=1, keepdims=True) + EPS)
    unit = values / radius
    rate = jnp.sum(unit * tangent, axis=1, keepdims=True)
    unit_tangent = (tangent - unit * rate) / radius
    return (unit, unit_tangent, radius, rate)


def unit_backward(unit, unit_tangent, radius, rate, grad, grad_rate):
    inner = jnp.sum(unit * grad, axis=1, keepdims=True)
    inner_rate = jnp.sum(unit_tangent * grad + unit * grad_rate, axis=1, keepdims=True)
    first = (grad - unit * inner) / radius
    return (grad_rate - unit_tangent * inner - unit * inner_rate - first * rate) / radius


def general(
    picture_averaged_encodings,
    caption_averaged_encodings,
    picture_mapping_matrix,
    caption_mapping_matrix,
    picture_weight_perturbation,
    caption_weight_perturbation,
    sharpness_multiplier,
    offset_additive,
):
    similarity_multiplier = sharpness_multiplier[0]
    logit_bias = offset_additive[0]
    tensor_rank = lax.axis_index("tensor")
    data_rank = lax.axis_index("dp")
    tensor_count = lax.axis_size("tensor")
    data_count = lax.axis_size("dp")
    planes = data_count // 2
    rows, width = picture_averaged_encodings.shape
    cols = picture_mapping_matrix.shape[1]
    share = rows // tensor_count
    out_rows = width // data_count
    half = jnp.bfloat16

    text = jnp.stack(
        [
            matmul(caption_averaged_encodings, caption_mapping_matrix).astype(half),
            matmul(caption_averaged_encodings, caption_weight_perturbation).astype(half),
        ]
    )
    image = jnp.stack(
        [
            matmul(picture_averaged_encodings, picture_mapping_matrix).astype(half),
            matmul(picture_averaged_encodings, picture_weight_perturbation).astype(half),
        ]
    )

    def share_of(value, axis, mask):
        start = (tensor_rank ^ mask) * share
        return lax.dynamic_slice_in_dim(value, start, share, axis)

    parts = [share_of(text, 1, 0)]
    for mask in range(1, tensor_count):
        parts.append(swapped(share_of(text, 1, mask), "tensor", mask))
    text = jnp.concatenate(parts, axis=2)
    slots = [text] + [swapped(text, "dp", 2 * mask) for mask in range(1, planes)]

    image = jnp.concatenate([image, swapped(image, "dp", 1)], axis=1)
    blocks = [image]
    mask = tensor_count // 2
    image_blocks = {0: image}
    while mask >= 1:
        held = sorted(image_blocks)
        sent = jnp.concatenate([image_blocks[k] for k in held], axis=2)
        got = swapped(sent, "tensor", mask)
        for place, k in enumerate(held):
            image_blocks[k ^ mask] = got[:, :, place * cols : (place + 1) * cols]
        mask //= 2
    image = jnp.concatenate([image_blocks[k] for k in range(tensor_count)], axis=2)
    text = jnp.concatenate(slots, axis=1)

    def out_columns(value, rank):
        taken = [
            lax.dynamic_slice_in_dim(value, (rank ^ (2 * mask)) * out_rows, out_rows, 1)
            for mask in range(planes)
        ]
        return jnp.concatenate(taken, axis=1)

    def plane_encodings(value):
        other = swapped(out_columns(value, data_rank ^ 1), "dp", 1)
        return jnp.concatenate([out_columns(value, data_rank), other], axis=0)

    picture_plane = plane_encodings(picture_averaged_encodings)
    ordered = jnp.concatenate(
        [share_of(caption_averaged_encodings, 0, mask) for mask in range(tensor_count)], axis=0
    )
    caption_plane = plane_encodings(ordered)

    image_unit, image_tangent, image_radius, image_rate = unit_parts(image[0], image[1])
    text_unit, text_tangent, text_radius, text_rate = unit_parts(text[0], text[1])
    image_half = image_unit.astype(half)
    image_tangent_half = image_tangent.astype(half)
    text_half = text_unit.astype(half)
    text_tangent_half = text_tangent.astype(half)

    logits = similarity_multiplier * matmul_nt(text_half, image_half) + logit_bias
    logit_rate = similarity_multiplier * (
        matmul_nt(text_half, image_tangent_half) + matmul_nt(text_tangent_half, image_half)
    )
    probability = jax.nn.sigmoid(logits)
    text_ids = lax.broadcasted_iota(jnp.int32, (logits.shape[0], 1), 0)
    image_ids = lax.broadcasted_iota(jnp.int32, (1, logits.shape[1]), 1)
    positive = ((text_ids < share) & (text_ids + tensor_rank * share == image_ids)).astype(
        jnp.float32
    )
    weight = (probability - positive).astype(half)
    weight_rate = (probability * (1.0 - probability) * logit_rate).astype(half)
    text_grad = similarity_multiplier * matmul(weight, image_half)
    text_grad_rate = similarity_multiplier * (
        matmul(weight_rate, image_half) + matmul(weight, image_tangent_half)
    )
    image_grad = similarity_multiplier * matmul_tn(weight, text_half)
    image_grad_rate = similarity_multiplier * (
        matmul_tn(weight_rate, text_half) + matmul_tn(weight, text_tangent_half)
    )

    text_back = unit_backward(
        text_unit, text_tangent, text_radius, text_rate, text_grad, text_grad_rate
    )
    image_back = unit_backward(
        image_unit, image_tangent, image_radius, image_rate, image_grad, image_grad_rate
    )

    total = text_back[:share]
    for mask in range(1, planes):
        sent = text_back[mask * share : (mask + 1) * share].astype(half)
        total = total + swapped(sent, "dp", 2 * mask).astype(jnp.float32)
    text_back = total.astype(half)
    parts = [text_back[:, :cols]]
    for mask in range(1, tensor_count):
        sent = text_back[:, mask * cols : (mask + 1) * cols]
        parts.append(swapped(sent, "tensor", mask))
    text_back = jnp.concatenate(parts, axis=0)
    text_back = jnp.concatenate([text_back, swapped(text_back, "dp", 1)], axis=0)

    image_blocks = {k: image_back[:, k * cols : (k + 1) * cols] for k in range(tensor_count)}
    mask = 1
    while mask < tensor_count:
        kept = [k for k in sorted(image_blocks) if not k & mask]
        sent = jnp.concatenate([image_blocks[k ^ mask] for k in kept], axis=1)
        got = swapped(sent, "tensor", mask).astype(jnp.float32)
        image_blocks = {
            k: image_blocks[k] + got[:, place * cols : (place + 1) * cols]
            for place, k in enumerate(kept)
        }
        mask *= 2
    image_back = image_blocks[0]
    got = swapped(image_back, "dp", 1)
    image_back = (
        image_back + jnp.concatenate([got[rows:], got[:rows]], axis=0)
    ).astype(half)

    def head(encodings, back):
        product = matmul_tn(encodings, back)
        total = product[:out_rows]
        for mask in range(1, planes):
            sent = product[mask * out_rows : (mask + 1) * out_rows].astype(half)
            total = total + swapped(sent, "dp", 2 * mask).astype(jnp.float32)
        return total

    return (head(picture_plane, image_back), head(caption_plane, text_back))


def call(kernel, outs, *args, after=(), scratch=()):
    count = len(args)

    def body(*refs):
        kernel(*refs[:count], *refs[count + len(after) :])

    def place(value):
        scalar = value.ndim == 1
        return pl.BlockSpec(memory_space=pltpu.SMEM if scalar else pltpu.VMEM)

    return pl.pallas_call(
        body,
        out_shape=[jax.ShapeDtypeStruct(shape, dtype) for shape, dtype in outs],
        in_specs=[place(value) for value in args]
        + [pl.BlockSpec(memory_space=pl.ANY) for _ in after],
        out_specs=[pl.BlockSpec(memory_space=pltpu.VMEM) for _ in outs],
        scratch_shapes=[pltpu.VMEM(shape, dtype) for shape, dtype in scratch],
        compiler_params=pltpu.CompilerParams(vmem_limit_bytes=14 * 1024 * 1024),
    )(*args, *after)


def folds(rows, main, tail):
    across = main // tail
    for k in range(rows // 16):
        here = slice(k * 16, (k + 1) * 16)
        at = rows + k // across * 16
        first = k % across * tail
        yield here, slice(at, at + 16), slice(first, first + tail)


def folded_rows(rows, main, tail):
    return rows + -(-rows // 16 // (main // tail)) * 16


def fold(out, first, value, main):
    rows, cols = value.shape
    out[first : first + rows, :] = value[:, :main].astype(out.dtype)
    for here, there, lanes in folds(rows, main, cols - main):
        there = slice(first + there.start, first + there.stop)
        out[there, lanes] = value[here, main:].astype(out.dtype)


def unfold(ref, first, rows, main, tail):
    tails = [
        ref[first + there.start : first + there.stop, lanes]
        for _, there, lanes in folds(rows, main, tail)
    ]
    return jnp.concatenate([ref[first : first + rows, :], jnp.concatenate(tails, axis=0)], axis=1)


def project_kernel(share, starts, encodings, weight, direction, *outs):
    main = weight.shape[0] // 128 * 128
    left = jnp.concatenate(
        [
            encodings[pl.ds(pl.multiple_of(starts[k], 16), share), :]
            for k in range(starts.shape[0])
        ],
        axis=0,
    )
    tails = jnp.concatenate([weight[main:, :], direction[main:, :]], axis=0)
    for right, first in ((weight[:main, :], 0), (direction[:main, :], main), (tails, 2 * main)):
        product = matmul_nt(left, right).astype(jnp.bfloat16)
        place = 0
        for out in outs:
            rows = out.shape[0]
            out[:, first : first + right.shape[0]] = product[place : place + rows]
            place += rows


def gathered(blocks, main, tail, which):
    first = 2 * main + which * tail
    mains = [block[:, which * main : (which + 1) * main] for block in blocks]
    tails = [block[:, first : first + tail] for block in blocks]
    return jnp.concatenate(mains + tails, axis=1)


def relay_kernel(mine, got, out):
    rows = mine.shape[0]
    out[:rows, :] = mine[...]
    out[rows:, :] = got[rows:, :]


def text_rows_kernel(main, tail, own, far, near, out):
    rows, width = own.shape[0], out.shape[1] // 2
    parts = (own[...], near[:rows, :], far[:rows, :], near[rows:, :])
    blocks = [part.astype(jnp.float32) for part in parts]
    out[:, :width] = gathered(blocks, main, tail, 0).astype(jnp.bfloat16)
    out[:, width:] = gathered(blocks, main, tail, 1).astype(jnp.bfloat16)


def row_factors(values, tangent):
    squares = jnp.sum(values * values, axis=1, keepdims=True)
    cross = jnp.sum(values * tangent, axis=1, keepdims=True)
    inverse = 1.0 / jnp.sqrt(squares + EPS)
    return inverse, cross * inverse


def unit_rows(values, tangent, inverse, rate):
    unit = values * inverse
    return unit, (tangent - unit * rate) * inverse


def back_rows(unit, tangent, inverse, rate, grad, grad_rate):
    inner = jnp.sum(unit * grad, axis=1, keepdims=True)
    inner_rate = jnp.sum(tangent * grad + unit * grad_rate, axis=1, keepdims=True)
    scaled = rate * inverse
    return (
        grad_rate - tangent * inner - grad * scaled + unit * (inner * scaled - inner_rate)
    ) * inverse


STEP = 48


def image_rows_kernel(main, tail, count, near, far, unit, tangent, half_both, factors):
    rows = unit.shape[0] // 2
    for shard in range(2):
        held = [
            (near, far)[k % 2].at[pl.ds((k - k % 2 + shard) * rows, rows), :] for k in range(count)
        ]

        @pl.loop(0, rows // STEP)
        def _(step):
            here = pl.ds(pl.multiple_of(step * STEP, STEP), STEP)
            there = pl.ds(pl.multiple_of(shard * rows + step * STEP, STEP), STEP)
            parts = [block[here, :].astype(jnp.float32) for block in held]
            values = gathered(parts, main, tail, 0)
            rates = gathered(parts, main, tail, 1)
            inverse, rate = row_factors(values, rates)
            one, two = unit_rows(values, rates, inverse, rate)
            unit[there, :] = one
            tangent[there, :] = two
            half_both[there, :] = one.astype(jnp.bfloat16)
            below = pl.ds(pl.multiple_of((2 + shard) * rows + step * STEP, STEP), STEP)
            half_both[below, :] = two.astype(jnp.bfloat16)
            factors[0, there, :] = jnp.broadcast_to(inverse, (STEP, 128))
            factors[1, there, :] = jnp.broadcast_to(rate, (STEP, 128))


def text_rows(text):
    width = text.shape[1] // 2
    values, rates = text[:, :width].astype(jnp.float32), text[:, width:].astype(jnp.float32)
    inverse, rate = row_factors(values, rates)
    return unit_rows(values, rates, inverse, rate) + (inverse, rate)


def weight_kernel(slots, first, start, scalars, half_both, *refs):
    texts, refs = refs[: slots - first], refs[slots - first :]
    held, (text_both, weights, weights_turned) = refs[:-3], refs[-3:]
    bf16 = jnp.bfloat16
    share = texts[0].shape[0]
    count, images = slots * share, half_both.shape[0] // 2
    done = first * share
    multiplier, bias = scalars[0], scalars[1]
    if held:
        for part in range(2):
            here = slice(part * done, (part + 1) * done)
            there = slice(part * count, part * count + done)
            text_both[there, :] = held[0][here, :]
            weights_turned[:, there] = held[2][:, here]
        weights[:done, :] = held[1][...]
    units, tangents = [], []
    for text in texts:
        unit, tangent, _, _ = text_rows(text)
        units.append(unit.astype(bf16))
        tangents.append(tangent.astype(bf16))
    units, both = jnp.concatenate(units, axis=0), jnp.concatenate(units + tangents, axis=0)
    fresh = units.shape[0]
    text_both[done:count, :] = units
    text_both[count + done :, :] = both[fresh:]
    products = matmul_nt(both, half_both[:images, :])
    logits = multiplier * products[:fresh] + bias
    logit_rate = multiplier * (matmul_nt(units, half_both[images:, :]) + products[fresh:])
    probability = jax.nn.sigmoid(logits)
    text_ids = lax.broadcasted_iota(jnp.int32, logits.shape, 0) + done
    image_ids = lax.broadcasted_iota(jnp.int32, logits.shape, 1)
    positive = jnp.where((text_ids < share) & (text_ids + start[0] == image_ids), 1.0, 0.0)
    value = probability - positive
    value_rate = probability * (1.0 - probability) * logit_rate
    weights[done:, :images] = value_rate.astype(bf16)
    weights[done:, images:] = value.astype(bf16)
    weights_turned[:, done:count] = value_rate.T.astype(bf16)
    weights_turned[:, count + done :] = value.T.astype(bf16)


def text_block_kernel(slots, scalars, half_both, weights, *refs):
    texts, sums = refs[:slots], refs[slots:]
    share, images = texts[0].shape[0], half_both.shape[0] // 2
    grad = matmul(weights[:, images:], half_both[:images, :])
    grad_rate = matmul(weights[...], half_both[...])
    for slot, text in enumerate(texts):
        here = slice(slot * share, (slot + 1) * share)
        back = scalars[0] * back_rows(*text_rows(text), grad[here], grad_rate[here])
        at = slice(slot // 2 * share, (slot // 2 + 1) * share)
        sums[slot % 2][at, :] = back.astype(sums[slot % 2].dtype)


def forward_kernel(mine, got, total, sent):
    share = total.shape[0]
    total[...] = mine[:share, :] + got[:share, :].astype(jnp.float32)
    sent[...] = (mine[share:, :] + got[share:, :].astype(jnp.float32)).astype(jnp.bfloat16)


def image_block_kernel(main, tail, scalars, unit, tangent, factors, text_both, weights, kept, sent):
    rows, width = unit.shape[0] // 2, unit.shape[1]
    count, texts = width // (main + tail), text_both.shape[0] // 2
    grads = matmul(weights[:, texts:], text_both[:texts, :])
    grad_rates = matmul(weights[...], text_both[...])
    for shard in range(2):
        here = slice(shard * rows, (shard + 1) * rows)
        inverse, rate = factors[0, here, :1], factors[1, here, :1]
        back = back_rows(unit[here, :], tangent[here, :], inverse, rate, grads[here], grad_rates[here])
        back = scalars[0] * back
        for k in range(count):
            out = (kept, sent)[k % 2]
            to = slice(k // 2 * rows, (k // 2 + 1) * rows)
            out[to, shard * main : (shard + 1) * main] = back[:, k * main : (k + 1) * main]
            first = 2 * main + shard * tail
            taken = count * main + k * tail
            out[to, first : first + tail] = back[:, taken : taken + tail]


def text_sum_kernel(main, tail, own, *refs):
    count = own.shape[1] // (main + tail)
    got, outs = refs[:-count], refs[-count:]
    total = own[...]
    for ref in got:
        total = total + ref[...].astype(jnp.float32)
    for k, out in enumerate(outs):
        first = count * main + k * tail
        out[:, :main] = total[:, k * main : (k + 1) * main].astype(jnp.bfloat16)
        out[:, main:] = total[:, first : first + tail].astype(jnp.bfloat16)


def stack_kernel(*refs):
    rows = refs[0].shape[0]
    for k, ref in enumerate(refs[:-1]):
        refs[-1][k * rows : (k + 1) * rows, : ref.shape[1]] = ref[...]


def fold_kernel(*refs):
    value = jnp.concatenate([ref[...] for ref in refs[:-1]], axis=0)
    fold(refs[-1], 0, value, refs[-1].shape[1])


def turn_kernel(places, core, picture, caption, mine, other):
    for which, encodings in enumerate((picture, caption)):
        turned = encodings[...].T
        count = places.shape[0]
        size, rows = turned.shape[0] // count, turned.shape[1]
        fold = count // 4
        for block in range(count):
            taken = turned[block * size : (block + 1) * size, :]
            slot = places[block]
            at = pl.multiple_of(slot % fold * size, 16)
            for half in range(2):
                lanes = slice(half * rows, (half + 1) * rows)

                @pl.when(slot // fold == half)
                def _():
                    mine[pl.ds(which * fold * size + at, size), lanes] = taken

                @pl.when((slot // fold == 2 + half) & (core[0] == which))
                def _():
                    other[pl.ds(at, size), lanes] = taken


def shard_columns(value, main, tail, shard):
    at = 2 * main + shard * tail
    return jnp.concatenate(
        [value[:, shard * main : (shard + 1) * main], value[:, at : at + tail]], axis=1
    )


def image_pair_kernel(main, tail, share, near, kept, got, total, over_x, over_y, over_both):
    rows = total.shape[0]
    ours = kept[:rows, :] + got[:rows, :]
    theirs = kept[rows:, :] + got[rows:, :]
    total[...] = shard_columns(ours, main, tail, 0)
    fold(over_y, 0, shard_columns(ours, main, tail, 1), main)
    fold(over_both, 0, shard_columns(theirs, main, tail, 1), main)
    value = shard_columns(theirs, main, tail, 0)
    rounded = value.astype(jnp.bfloat16)
    fold(over_x, 0, rounded, main)
    left = value - rounded.astype(jnp.float32)
    left = jnp.where(near[0] == 0, left[: 2 * share], left[2 * share : 4 * share])
    fold(over_x, folded_rows(rows, main, tail), left, main)


def image_sum_kernel(main, tail, share, near, total, over_x, over_y, over_both, out):
    rows = total.shape[0]
    value = total[...]
    for source in (over_x, over_y, over_both):
        value = value + unfold(source, 0, rows, main, tail).astype(jnp.float32)
    left = unfold(over_x, folded_rows(rows, main, tail), 2 * share, main, tail)
    left = left.astype(jnp.float32)
    zero = jnp.zeros_like(left)
    far = near[0] == 0
    value = value + jnp.concatenate(
        [jnp.where(far, zero, left), jnp.where(far, left, zero)], axis=0
    )
    fold(out, 0, value.astype(jnp.bfloat16), main)


def head_kernel(main, tail, head, core, starts, mine, near, far, back, back_other, own, *refs):
    sent, (ordered,) = refs[:-1], refs[-1:]
    size, rows = own.shape[0], ordered.shape[1]
    share = rows // starts.shape[0]
    for which, ref in enumerate((back, back_other)):
        value = unfold(ref, 0, rows, main, tail)
        for k in range(starts.shape[0]):
            at = pl.ds(pl.multiple_of(starts[k], 16), share)
            ordered[which, at, :] = value[k * share : (k + 1) * share]
    count = (len(sent) + 1) // 2
    other = jnp.where(core[0] == head, near[...], far[...])
    for half in range(2):
        here = slice(head * count * size, (head + 1) * count * size)
        lanes = slice(half * rows, (half + 1) * rows)
        product = matmul(mine[here, lanes], ordered[0]) + matmul(other[:, lanes], ordered[1])
        for place in range(count):
            part = product[place * size : (place + 1) * size]
            slot = half * count + place
            if slot == 0:
                own[...] = part
            else:
                fold(sent[slot - 1], 0, part, main)


def final_kernel(main, tail, own, *refs):
    got, out = refs[:-1], refs[-1]
    total = own[...]
    for ref in got:
        total = total + unfold(ref, 0, own.shape[0], main, tail).astype(jnp.float32)
    out[...] = total


def final_kernel(main, tail, own, *refs):
    got, out = refs[:-1], refs[-1]
    size = own.shape[0]
    total = own[:, :main]
    for ref in got:
        total = total + ref[:size, :].astype(jnp.float32)
    out[:, :main] = total
    for rows_in, rows_out, lanes_out in folds(size, main, tail):
        total = own[rows_in, main:]
        for ref in got:
            total = total + ref[rows_out, lanes_out].astype(jnp.float32)
        out[rows_in, main:] = total


def packed(
    picture_averaged_encodings,
    caption_averaged_encodings,
    picture_mapping_matrix,
    caption_mapping_matrix,
    picture_weight_perturbation,
    caption_weight_perturbation,
    sharpness_multiplier,
    offset_additive,
):
    tensor_rank = lax.axis_index("tensor")
    data_rank = lax.axis_index("dp")
    count = lax.axis_size("tensor")
    data_count = lax.axis_size("dp")
    planes = data_count // 2
    rows, width = picture_averaged_encodings.shape
    cols = picture_mapping_matrix.shape[1]
    main = cols // 128 * 128
    tail = cols - main
    share = rows // count
    size = width // data_count
    wide = -(-2 * cols // 128) * 128
    f32, bf16 = jnp.float32, jnp.bfloat16
    ranks = jnp.arange(count, dtype=jnp.int32)
    starts = (ranks ^ tensor_rank) * share
    plain = ranks * share

    blocks = call(
        functools.partial(project_kernel, share),
        [((share, 2 * cols), bf16)] * 2 + [((2 * share, 2 * cols), bf16)],
        starts,
        caption_averaged_encodings,
        caption_mapping_matrix.T,
        caption_weight_perturbation.T,
    )
    text_far = swapped(blocks[2], "tensor", 2)
    (relay,) = call(relay_kernel, [((2 * share, 2 * cols), bf16)], blocks[1], text_far)
    text_near = swapped(relay, "tensor", 1)

    (image,) = call(
        functools.partial(project_kernel, share),
        [((rows, 2 * cols), bf16)],
        plain,
        picture_averaged_encodings,
        picture_mapping_matrix.T,
        picture_weight_perturbation.T,
        after=(blocks[0],),
    )
    image_other = swapped(image, "dp", 1)
    image_far = swapped(image, "tensor", 2)
    image_far_other = swapped(image_other, "tensor", 2)

    (text,) = call(
        functools.partial(text_rows_kernel, main, tail),
        [((share, 2 * width), bf16)],
        blocks[0],
        text_far,
        text_near,
    )
    text_two = swapped(text, "dp", 4)
    text_one = swapped(text, "dp", 2)
    text_three = swapped(text_two, "dp", 2)
    texts = [text, text_one, text_two, text_three]

    block_ids = jnp.arange(data_count, dtype=jnp.int32)
    slots = ((block_ids ^ data_rank) >> 1) + planes * ((block_ids ^ data_rank) & 1)
    core = (tensor_rank & 1).astype(jnp.int32).reshape(1)
    mine, other = call(
        turn_kernel,
        [((planes * size, 2 * rows), bf16), ((planes // 2 * size, 2 * rows), bf16)],
        slots,
        core,
        picture_averaged_encodings,
        caption_averaged_encodings,
        after=(image_other,),
    )
    other = swapped(other, "dp", 1)
    others = (other, swapped(other, "tensor", 1))

    (near,) = call(
        stack_kernel,
        [((4 * rows, wide), bf16)],
        image,
        image_other,
        image_far,
        image_far_other,
        after=(text_one, text_two, others[0]),
    )
    far = swapped(near, "tensor", 1)
    unit, tangent, half_both, factors = call(
        functools.partial(image_rows_kernel, main, tail, count),
        [
            ((2 * rows, width), f32),
            ((2 * rows, width), f32),
            ((4 * rows, width), bf16),
            ((2, 2 * rows, 128), f32),
        ],
        near,
        far,
    )

    scalars = jnp.concatenate([sharpness_multiplier, offset_additive])
    def block_weights(slots, first, *held, after=()):
        return call(
            functools.partial(weight_kernel, slots, first),
            [
                ((2 * slots * share, width), bf16),
                ((slots * share, 4 * rows), bf16),
                ((2 * rows, 2 * slots * share), bf16),
            ],
            (tensor_rank * share).astype(jnp.int32).reshape(1),
            scalars,
            half_both,
            *texts[first:slots],
            *held,
            after=after,
        )

    held = block_weights(planes - 1, 0, after=(others[1],))
    text_both, weights, weights_turned = block_weights(planes, planes - 1, *held)
    kept, sent = call(
        functools.partial(image_block_kernel, main, tail),
        [((2 * rows, wide), f32)] * 2,
        scalars,
        unit,
        tangent,
        factors,
        text_both,
        weights_turned,
    )
    outs = call(
        functools.partial(text_block_kernel, planes),
        [((2 * share, width), f32), ((2 * share, width), bf16)],
        scalars,
        half_both,
        weights,
        *texts,
        after=(kept,),
    )

    near = (tensor_rank // 2).astype(jnp.int32).reshape(1)
    tall = folded_rows(rows, main, tail)
    more = folded_rows(2 * share, main, tail)
    total, to_x, to_y, to_both = call(
        functools.partial(image_pair_kernel, main, tail, share),
        [((rows, cols), f32), ((tall + more, main), bf16)] + [((tall, main), bf16)] * 2,
        near,
        kept,
        swapped(sent, "tensor", 1),
        after=(outs[1],),
    )
    flat = [(source, source ^ (count + 2)) for source in range(data_count * count)]
    (image_back,) = call(
        functools.partial(image_sum_kernel, main, tail, share),
        [((tall, main), bf16)],
        near,
        total,
        swapped(to_x, "tensor", 2),
        swapped(to_y, "dp", 1),
        lax.ppermute(to_both, ("dp", "tensor"), flat),
    )
    image_back_other = swapped(image_back, "dp", 1)

    def head(which, order, back, back_other):
        return call(
            functools.partial(head_kernel, main, tail, which),
            [((size, cols), f32)]
            + [((folded_rows(size, main, tail), main), bf16)] * (planes - 1),
            core,
            order,
            mine,
            *others,
            back,
            back_other,
            scratch=[((2, rows, cols), bf16)],
        )

    def summed(products):
        got = [swapped(products[k], "dp", 2 * k) for k in range(1, planes)]
        return call(
            functools.partial(final_kernel, main, tail), [((size, cols), f32)], products[0], *got
        )[0]

    image_products = head(0, plain, image_back, image_back_other)

    text_total, text_sent = call(
        forward_kernel,
        [((share, width), f32), ((share, width), bf16)],
        outs[0],
        swapped(outs[1], "dp", 2),
    )
    blocks = call(
        functools.partial(text_sum_kernel, main, tail),
        [((share, cols), bf16)] * count,
        text_total,
        swapped(text_sent, "dp", 4),
        after=(image_back,),
    )
    got = [blocks[0]] + [swapped(blocks[k], "tensor", k) for k in range(1, count)]
    (text_back,) = call(fold_kernel, [((tall, main), bf16)], *got, after=(image_products[0],))
    text_back_other = swapped(text_back, "dp", 1)

    text_products = head(1, starts, text_back, text_back_other)
    return summed(image_products), summed(text_products)


def fits(mesh):
    return mesh.shape["tensor"] == 4 and mesh.shape["dp"] == 8


def solution(mesh):
    in_specs = (
        P("dp", None),
        P("dp", None),
        P(None, "tensor"),
        P(None, "tensor"),
        P(None, "tensor"),
        P(None, "tensor"),
        P(),
        P(),
    )
    out_specs = (P("dp", "tensor"), P("dp", "tensor"))
    local = packed if fits(mesh) else general
    return jax.shard_map(local, mesh=mesh, in_specs=in_specs, out_specs=out_specs, check_vma=False)
```

```python
import functools

import jax
import jax.numpy as jnp
from jax import lax
from jax.experimental import pallas as pl
from jax.experimental.pallas import tpu as pltpu
from jax.sharding import PartitionSpec as P

EPS = 1e-06


def swapped(value, axis, mask):
    count = lax.axis_size(axis)
    return lax.ppermute(value, axis, [(source, source ^ mask) for source in range(count)])


def matmul(left, right):
    return jnp.dot(left, right, preferred_element_type=jnp.float32)


def matmul_nt(left, right):
    return lax.dot_general(
        left, right, (((1,), (1,)), ((), ())), preferred_element_type=jnp.float32
    )


def matmul_tn(left, right):
    return lax.dot_general(
        left, right, (((0,), (0,)), ((), ())), preferred_element_type=jnp.float32
    )


def unit_parts(raw, raw_rate):
    values = raw.astype(jnp.float32)
    tangent = raw_rate.astype(jnp.float32)
    radius = jnp.sqrt(jnp.sum(values * values, axis=1, keepdims=True) + EPS)
    unit = values / radius
    rate = jnp.sum(unit * tangent, axis=1, keepdims=True)
    unit_tangent = (tangent - unit * rate) / radius
    return (unit, unit_tangent, radius, rate)


def unit_backward(unit, unit_tangent, radius, rate, grad, grad_rate):
    inner = jnp.sum(unit * grad, axis=1, keepdims=True)
    inner_rate = jnp.sum(unit_tangent * grad + unit * grad_rate, axis=1, keepdims=True)
    first = (grad - unit * inner) / radius
    return (grad_rate - unit_tangent * inner - unit * inner_rate - first * rate) / radius


def general(
    picture_averaged_encodings,
    caption_averaged_encodings,
    picture_mapping_matrix,
    caption_mapping_matrix,
    picture_weight_perturbation,
    caption_weight_perturbation,
    sharpness_multiplier,
    offset_additive,
):
    similarity_multiplier = sharpness_multiplier[0]
    logit_bias = offset_additive[0]
    tensor_rank = lax.axis_index("tensor")
    data_rank = lax.axis_index("dp")
    tensor_count = lax.axis_size("tensor")
    data_count = lax.axis_size("dp")
    planes = data_count // 2
    rows, width = picture_averaged_encodings.shape
    cols = picture_mapping_matrix.shape[1]
    share = rows // tensor_count
    out_rows = width // data_count
    half = jnp.bfloat16

    text = jnp.stack(
        [
            matmul(caption_averaged_encodings, caption_mapping_matrix).astype(half),
            matmul(caption_averaged_encodings, caption_weight_perturbation).astype(half),
        ]
    )
    image = jnp.stack(
        [
            matmul(picture_averaged_encodings, picture_mapping_matrix).astype(half),
            matmul(picture_averaged_encodings, picture_weight_perturbation).astype(half),
        ]
    )

    def share_of(value, axis, mask):
        start = (tensor_rank ^ mask) * share
        return lax.dynamic_slice_in_dim(value, start, share, axis)

    parts = [share_of(text, 1, 0)]
    for mask in range(1, tensor_count):
        parts.append(swapped(share_of(text, 1, mask), "tensor", mask))
    text = jnp.concatenate(parts, axis=2)
    slots = [text] + [swapped(text, "dp", 2 * mask) for mask in range(1, planes)]

    image = jnp.concatenate([image, swapped(image, "dp", 1)], axis=1)
    blocks = [image]
    mask = tensor_count // 2
    image_blocks = {0: image}
    while mask >= 1:
        held = sorted(image_blocks)
        sent = jnp.concatenate([image_blocks[k] for k in held], axis=2)
        got = swapped(sent, "tensor", mask)
        for place, k in enumerate(held):
            image_blocks[k ^ mask] = got[:, :, place * cols : (place + 1) * cols]
        mask //= 2
    image = jnp.concatenate([image_blocks[k] for k in range(tensor_count)], axis=2)
    text = jnp.concatenate(slots, axis=1)

    def out_columns(value, rank):
        taken = [
            lax.dynamic_slice_in_dim(value, (rank ^ (2 * mask)) * out_rows, out_rows, 1)
            for mask in range(planes)
        ]
        return jnp.concatenate(taken, axis=1)

    def plane_encodings(value):
        other = swapped(out_columns(value, data_rank ^ 1), "dp", 1)
        return jnp.concatenate([out_columns(value, data_rank), other], axis=0)

    picture_plane = plane_encodings(picture_averaged_encodings)
    ordered = jnp.concatenate(
        [share_of(caption_averaged_encodings, 0, mask) for mask in range(tensor_count)], axis=0
    )
    caption_plane = plane_encodings(ordered)

    image_unit, image_tangent, image_radius, image_rate = unit_parts(image[0], image[1])
    text_unit, text_tangent, text_radius, text_rate = unit_parts(text[0], text[1])
    image_half = image_unit.astype(half)
    image_tangent_half = image_tangent.astype(half)
    text_half = text_unit.astype(half)
    text_tangent_half = text_tangent.astype(half)

    logits = similarity_multiplier * matmul_nt(text_half, image_half) + logit_bias
    logit_rate = similarity_multiplier * (
        matmul_nt(text_half, image_tangent_half) + matmul_nt(text_tangent_half, image_half)
    )
    probability = jax.nn.sigmoid(logits)
    text_ids = lax.broadcasted_iota(jnp.int32, (logits.shape[0], 1), 0)
    image_ids = lax.broadcasted_iota(jnp.int32, (1, logits.shape[1]), 1)
    positive = ((text_ids < share) & (text_ids + tensor_rank * share == image_ids)).astype(
        jnp.float32
    )
    weight = (probability - positive).astype(half)
    weight_rate = (probability * (1.0 - probability) * logit_rate).astype(half)
    text_grad = similarity_multiplier * matmul(weight, image_half)
    text_grad_rate = similarity_multiplier * (
        matmul(weight_rate, image_half) + matmul(weight, image_tangent_half)
    )
    image_grad = similarity_multiplier * matmul_tn(weight, text_half)
    image_grad_rate = similarity_multiplier * (
        matmul_tn(weight_rate, text_half) + matmul_tn(weight, text_tangent_half)
    )

    text_back = unit_backward(
        text_unit, text_tangent, text_radius, text_rate, text_grad, text_grad_rate
    )
    image_back = unit_backward(
        image_unit, image_tangent, image_radius, image_rate, image_grad, image_grad_rate
    )

    total = text_back[:share]
    for mask in range(1, planes):
        sent = text_back[mask * share : (mask + 1) * share].astype(half)
        total = total + swapped(sent, "dp", 2 * mask).astype(jnp.float32)
    text_back = total.astype(half)
    parts = [text_back[:, :cols]]
    for mask in range(1, tensor_count):
        sent = text_back[:, mask * cols : (mask + 1) * cols]
        parts.append(swapped(sent, "tensor", mask))
    text_back = jnp.concatenate(parts, axis=0)
    text_back = jnp.concatenate([text_back, swapped(text_back, "dp", 1)], axis=0)

    image_blocks = {k: image_back[:, k * cols : (k + 1) * cols] for k in range(tensor_count)}
    mask = 1
    while mask < tensor_count:
        kept = [k for k in sorted(image_blocks) if not k & mask]
        sent = jnp.concatenate([image_blocks[k ^ mask] for k in kept], axis=1)
        got = swapped(sent, "tensor", mask).astype(jnp.float32)
        image_blocks = {
            k: image_blocks[k] + got[:, place * cols : (place + 1) * cols]
            for place, k in enumerate(kept)
        }
        mask *= 2
    image_back = image_blocks[0]
    got = swapped(image_back, "dp", 1)
    image_back = (
        image_back + jnp.concatenate([got[rows:], got[:rows]], axis=0)
    ).astype(half)

    def head(encodings, back):
        product = matmul_tn(encodings, back)
        total = product[:out_rows]
        for mask in range(1, planes):
            sent = product[mask * out_rows : (mask + 1) * out_rows].astype(half)
            total = total + swapped(sent, "dp", 2 * mask).astype(jnp.float32)
        return total

    return (head(picture_plane, image_back), head(caption_plane, text_back))


def call(kernel, outs, *args, after=(), scratch=()):
    count = len(args)

    def body(*refs):
        kernel(*refs[:count], *refs[count + len(after) :])

    def place(value):
        scalar = value.ndim == 1
        return pl.BlockSpec(memory_space=pltpu.SMEM if scalar else pltpu.VMEM)

    return pl.pallas_call(
        body,
        out_shape=[jax.ShapeDtypeStruct(shape, dtype) for shape, dtype in outs],
        in_specs=[place(value) for value in args]
        + [pl.BlockSpec(memory_space=pl.ANY) for _ in after],
        out_specs=[pl.BlockSpec(memory_space=pltpu.VMEM) for _ in outs],
        scratch_shapes=[pltpu.VMEM(shape, dtype) for shape, dtype in scratch],
        compiler_params=pltpu.CompilerParams(vmem_limit_bytes=14 * 1024 * 1024),
    )(*args, *after)


def folds(rows, main, tail):
    across = main // tail
    for k in range(rows // 16):
        here = slice(k * 16, (k + 1) * 16)
        at = rows + k // across * 16
        first = k % across * tail
        yield here, slice(at, at + 16), slice(first, first + tail)


def folded_rows(rows, main, tail):
    return rows + -(-rows // 16 // (main // tail)) * 16


def fold(out, first, value, main):
    rows, cols = value.shape
    out[first : first + rows, :] = value[:, :main].astype(out.dtype)
    for here, there, lanes in folds(rows, main, cols - main):
        there = slice(first + there.start, first + there.stop)
        out[there, lanes] = value[here, main:].astype(out.dtype)


def unfold(ref, first, rows, main, tail):
    tails = [
        ref[first + there.start : first + there.stop, lanes]
        for _, there, lanes in folds(rows, main, tail)
    ]
    return jnp.concatenate([ref[first : first + rows, :], jnp.concatenate(tails, axis=0)], axis=1)


def project_kernel(share, starts, encodings, weight, direction, *outs):
    main = weight.shape[0] // 128 * 128
    left = jnp.concatenate(
        [
            encodings[pl.ds(pl.multiple_of(starts[k], 16), share), :]
            for k in range(starts.shape[0])
        ],
        axis=0,
    )
    tails = jnp.concatenate([weight[main:, :], direction[main:, :]], axis=0)
    for right, first in ((weight[:main, :], 0), (direction[:main, :], main), (tails, 2 * main)):
        product = matmul_nt(left, right).astype(jnp.bfloat16)
        place = 0
        for out in outs:
            rows = out.shape[0]
            out[:, first : first + right.shape[0]] = product[place : place + rows]
            place += rows


def gathered(blocks, main, tail, which):
    first = 2 * main + which * tail
    mains = [block[:, which * main : (which + 1) * main] for block in blocks]
    tails = [block[:, first : first + tail] for block in blocks]
    return jnp.concatenate(mains + tails, axis=1)


def relay_kernel(mine, got, out):
    rows = mine.shape[0]
    out[:rows, :] = mine[...]
    out[rows:, :] = got[rows:, :]


def text_rows_kernel(main, tail, own, far, near, out):
    rows, width = own.shape[0], out.shape[1] // 2
    parts = (own[...], near[:rows, :], far[:rows, :], near[rows:, :])
    blocks = [part.astype(jnp.float32) for part in parts]
    out[:, :width] = gathered(blocks, main, tail, 0).astype(jnp.bfloat16)
    out[:, width:] = gathered(blocks, main, tail, 1).astype(jnp.bfloat16)


def row_factors(values, tangent):
    squares = jnp.sum(values * values, axis=1, keepdims=True)
    cross = jnp.sum(values * tangent, axis=1, keepdims=True)
    inverse = 1.0 / jnp.sqrt(squares + EPS)
    return inverse, cross * inverse


def unit_rows(values, tangent, inverse, rate):
    unit = values * inverse
    return unit, (tangent - unit * rate) * inverse


def back_rows(unit, tangent, inverse, rate, grad, grad_rate):
    inner = jnp.sum(unit * grad, axis=1, keepdims=True)
    inner_rate = jnp.sum(tangent * grad + unit * grad_rate, axis=1, keepdims=True)
    scaled = rate * inverse
    return (
        grad_rate - tangent * inner - grad * scaled + unit * (inner * scaled - inner_rate)
    ) * inverse


STEP = 48


def image_rows_kernel(main, tail, count, near, far, raw_both, half_both, factors):
    rows = raw_both.shape[0] // 4
    for shard in range(2):
        held = [
            (near, far)[k % 2].at[pl.ds((k - k % 2 + shard) * rows, rows), :] for k in range(count)
        ]

        @pl.loop(0, rows // STEP)
        def _(step):
            here = pl.ds(pl.multiple_of(step * STEP, STEP), STEP)
            there = pl.ds(pl.multiple_of(shard * rows + step * STEP, STEP), STEP)
            parts = [block[here, :].astype(jnp.float32) for block in held]
            values = gathered(parts, main, tail, 0)
            rates = gathered(parts, main, tail, 1)
            inverse, rate = row_factors(values, rates)
            one, two = unit_rows(values, rates, inverse, rate)
            below = pl.ds(pl.multiple_of((2 + shard) * rows + step * STEP, STEP), STEP)
            raw_both[there, :] = values.astype(jnp.bfloat16)
            raw_both[below, :] = rates.astype(jnp.bfloat16)
            half_both[there, :] = one.astype(jnp.bfloat16)
            half_both[below, :] = two.astype(jnp.bfloat16)
            factors[0, there, :] = jnp.broadcast_to(inverse, (STEP, 128))
            factors[1, there, :] = jnp.broadcast_to(rate, (STEP, 128))


def text_rows(text):
    width = text.shape[1] // 2
    values, rates = text[:, :width].astype(jnp.float32), text[:, width:].astype(jnp.float32)
    inverse, rate = row_factors(values, rates)
    return unit_rows(values, rates, inverse, rate) + (inverse, rate)


def weight_kernel(slots, first, start, scalars, half_both, *refs):
    texts, refs = refs[: slots - first], refs[slots - first :]
    held, (text_both, weights, weights_turned) = refs[:-3], refs[-3:]
    bf16 = jnp.bfloat16
    share = texts[0].shape[0]
    count, images = slots * share, half_both.shape[0] // 2
    done = first * share
    multiplier, bias = scalars[0], scalars[1]
    if held:
        for part in range(2):
            here = slice(part * done, (part + 1) * done)
            there = slice(part * count, part * count + done)
            text_both[there, :] = held[0][here, :]
            weights_turned[:, there] = held[2][:, here]
        weights[:done, :] = held[1][...]
    units, tangents = [], []
    for text in texts:
        unit, tangent, _, _ = text_rows(text)
        units.append(unit.astype(bf16))
        tangents.append(tangent.astype(bf16))
    units, both = jnp.concatenate(units, axis=0), jnp.concatenate(units + tangents, axis=0)
    fresh = units.shape[0]
    text_both[done:count, :] = units
    text_both[count + done :, :] = both[fresh:]
    products = matmul_nt(both, half_both[:images, :])
    logits = multiplier * products[:fresh] + bias
    logit_rate = multiplier * (matmul_nt(units, half_both[images:, :]) + products[fresh:])
    probability = jax.nn.sigmoid(logits)
    text_ids = lax.broadcasted_iota(jnp.int32, logits.shape, 0) + done
    image_ids = lax.broadcasted_iota(jnp.int32, logits.shape, 1)
    positive = jnp.where((text_ids < share) & (text_ids + start[0] == image_ids), 1.0, 0.0)
    value = probability - positive
    value_rate = probability * (1.0 - probability) * logit_rate
    weights[done:, :images] = value_rate.astype(bf16)
    weights[done:, images:] = value.astype(bf16)
    weights_turned[:, done:count] = value_rate.T.astype(bf16)
    weights_turned[:, count + done :] = value.T.astype(bf16)


def text_block_kernel(slots, scalars, half_both, weights, *refs):
    texts, sums = refs[:slots], refs[slots:]
    share, images = texts[0].shape[0], half_both.shape[0] // 2
    grad = matmul(weights[:, images:], half_both[:images, :])
    grad_rate = matmul(weights[...], half_both[...])
    for slot, text in enumerate(texts):
        here = slice(slot * share, (slot + 1) * share)
        back = scalars[0] * back_rows(*text_rows(text), grad[here], grad_rate[here])
        at = slice(slot // 2 * share, (slot // 2 + 1) * share)
        sums[slot % 2][at, :] = back.astype(sums[slot % 2].dtype)


def forward_kernel(mine, got, total, sent):
    share = total.shape[0]
    total[...] = mine[:share, :] + got[:share, :].astype(jnp.float32)
    sent[...] = (mine[share:, :] + got[share:, :].astype(jnp.float32)).astype(jnp.bfloat16)


def image_block_kernel(main, tail, scalars, raw_both, factors, text_both, weights, kept, sent):
    rows, width = raw_both.shape[0] // 4, raw_both.shape[1]
    count, texts = width // (main + tail), text_both.shape[0] // 2
    grads = matmul(weights[:, texts:], text_both[:texts, :])
    grad_rates = matmul(weights[...], text_both[...])
    for shard in range(2):
        here = slice(shard * rows, (shard + 1) * rows)
        inverse, rate = factors[0, here, :1], factors[1, here, :1]
        below = slice((2 + shard) * rows, (3 + shard) * rows)
        values, rates = raw_both[here, :], raw_both[below, :]
        unit, tangent = unit_rows(
            values.astype(jnp.float32), rates.astype(jnp.float32), inverse, rate
        )
        back = back_rows(unit, tangent, inverse, rate, grads[here], grad_rates[here])
        back = scalars[0] * back
        for k in range(count):
            out = (kept, sent)[k % 2]
            to = slice(k // 2 * rows, (k // 2 + 1) * rows)
            out[to, shard * main : (shard + 1) * main] = back[:, k * main : (k + 1) * main]
            first = 2 * main + shard * tail
            taken = count * main + k * tail
            out[to, first : first + tail] = back[:, taken : taken + tail]


def text_sum_kernel(main, tail, own, *refs):
    count = own.shape[1] // (main + tail)
    got, outs = refs[:-count], refs[-count:]
    total = own[...]
    for ref in got:
        total = total + ref[...].astype(jnp.float32)
    for k, out in enumerate(outs):
        first = count * main + k * tail
        out[:, :main] = total[:, k * main : (k + 1) * main].astype(jnp.bfloat16)
        out[:, main:] = total[:, first : first + tail].astype(jnp.bfloat16)


def stack_kernel(*refs):
    rows = refs[0].shape[0]
    for k, ref in enumerate(refs[:-1]):
        refs[-1][k * rows : (k + 1) * rows, : ref.shape[1]] = ref[...]


def fold_kernel(*refs):
    value = jnp.concatenate([ref[...] for ref in refs[:-1]], axis=0)
    fold(refs[-1], 0, value, refs[-1].shape[1])


def turn_kernel(places, core, picture, caption, mine, other):
    for which, encodings in enumerate((picture, caption)):
        turned = encodings[...].T
        count = places.shape[0]
        size, rows = turned.shape[0] // count, turned.shape[1]
        fold = count // 4
        for block in range(count):
            taken = turned[block * size : (block + 1) * size, :]
            slot = places[block]
            at = pl.multiple_of(slot % fold * size, 16)
            for half in range(2):
                lanes = slice(half * rows, (half + 1) * rows)

                @pl.when(slot // fold == half)
                def _():
                    mine[pl.ds(which * fold * size + at, size), lanes] = taken

                @pl.when((slot // fold == 2 + half) & (core[0] == which))
                def _():
                    other[pl.ds(at, size), lanes] = taken


def shard_columns(value, main, tail, shard):
    at = 2 * main + shard * tail
    return jnp.concatenate(
        [value[:, shard * main : (shard + 1) * main], value[:, at : at + tail]], axis=1
    )


def image_pair_kernel(main, tail, share, near, kept, got, total, over_x, over_y, over_both):
    rows = total.shape[0]
    ours = kept[:rows, :] + got[:rows, :]
    theirs = kept[rows:, :] + got[rows:, :]
    total[...] = shard_columns(ours, main, tail, 0)
    fold(over_y, 0, shard_columns(ours, main, tail, 1), main)
    fold(over_both, 0, shard_columns(theirs, main, tail, 1), main)
    value = shard_columns(theirs, main, tail, 0)
    rounded = value.astype(jnp.bfloat16)
    fold(over_x, 0, rounded, main)
    left = value - rounded.astype(jnp.float32)
    left = jnp.where(near[0] == 0, left[: 2 * share], left[2 * share : 4 * share])
    fold(over_x, folded_rows(rows, main, tail), left, main)


def image_sum_kernel(main, tail, share, near, total, over_x, over_y, over_both, out):
    rows = total.shape[0]
    value = total[...]
    for source in (over_x, over_y, over_both):
        value = value + unfold(source, 0, rows, main, tail).astype(jnp.float32)
    left = unfold(over_x, folded_rows(rows, main, tail), 2 * share, main, tail)
    left = left.astype(jnp.float32)
    zero = jnp.zeros_like(left)
    far = near[0] == 0
    value = value + jnp.concatenate(
        [jnp.where(far, zero, left), jnp.where(far, left, zero)], axis=0
    )
    fold(out, 0, value.astype(jnp.bfloat16), main)


def head_kernel(main, tail, head, core, starts, mine, near, far, back, back_other, own, *refs):
    sent, (ordered,) = refs[:-1], refs[-1:]
    size, rows = own.shape[0], ordered.shape[1]
    share = rows // starts.shape[0]
    for which, ref in enumerate((back, back_other)):
        value = unfold(ref, 0, rows, main, tail)
        for k in range(starts.shape[0]):
            at = pl.ds(pl.multiple_of(starts[k], 16), share)
            ordered[which, at, :] = value[k * share : (k + 1) * share]
    count = (len(sent) + 1) // 2
    other = jnp.where(core[0] == head, near[...], far[...])
    for half in range(2):
        here = slice(head * count * size, (head + 1) * count * size)
        lanes = slice(half * rows, (half + 1) * rows)
        product = matmul(mine[here, lanes], ordered[0]) + matmul(other[:, lanes], ordered[1])
        for place in range(count):
            part = product[place * size : (place + 1) * size]
            slot = half * count + place
            if slot == 0:
                own[...] = part
            else:
                fold(sent[slot - 1], 0, part, main)


def final_kernel(main, tail, own, *refs):
    got, out = refs[:-1], refs[-1]
    total = own[...]
    for ref in got:
        total = total + unfold(ref, 0, own.shape[0], main, tail).astype(jnp.float32)
    out[...] = total


def final_kernel(main, tail, own, *refs):
    got, out = refs[:-1], refs[-1]
    size = own.shape[0]
    total = own[:, :main]
    for ref in got:
        total = total + ref[:size, :].astype(jnp.float32)
    out[:, :main] = total
    for rows_in, rows_out, lanes_out in folds(size, main, tail):
        total = own[rows_in, main:]
        for ref in got:
            total = total + ref[rows_out, lanes_out].astype(jnp.float32)
        out[rows_in, main:] = total


def packed(
    picture_averaged_encodings,
    caption_averaged_encodings,
    picture_mapping_matrix,
    caption_mapping_matrix,
    picture_weight_perturbation,
    caption_weight_perturbation,
    sharpness_multiplier,
    offset_additive,
):
    tensor_rank = lax.axis_index("tensor")
    data_rank = lax.axis_index("dp")
    count = lax.axis_size("tensor")
    data_count = lax.axis_size("dp")
    planes = data_count // 2
    rows, width = picture_averaged_encodings.shape
    cols = picture_mapping_matrix.shape[1]
    main = cols // 128 * 128
    tail = cols - main
    share = rows // count
    size = width // data_count
    wide = -(-2 * cols // 128) * 128
    f32, bf16 = jnp.float32, jnp.bfloat16
    ranks = jnp.arange(count, dtype=jnp.int32)
    starts = (ranks ^ tensor_rank) * share
    plain = ranks * share

    blocks = call(
        functools.partial(project_kernel, share),
        [((share, 2 * cols), bf16)] * 2 + [((2 * share, 2 * cols), bf16)],
        starts,
        caption_averaged_encodings,
        caption_mapping_matrix.T,
        caption_weight_perturbation.T,
    )
    text_far = swapped(blocks[2], "tensor", 2)
    (relay,) = call(relay_kernel, [((2 * share, 2 * cols), bf16)], blocks[1], text_far)
    text_near = swapped(relay, "tensor", 1)

    (image,) = call(
        functools.partial(project_kernel, share),
        [((rows, 2 * cols), bf16)],
        plain,
        picture_averaged_encodings,
        picture_mapping_matrix.T,
        picture_weight_perturbation.T,
        after=(blocks[0],),
    )
    image_other = swapped(image, "dp", 1)
    image_far = swapped(image, "tensor", 2)
    image_far_other = swapped(image_other, "tensor", 2)

    (text,) = call(
        functools.partial(text_rows_kernel, main, tail),
        [((share, 2 * width), bf16)],
        blocks[0],
        text_far,
        text_near,
    )
    text_two = swapped(text, "dp", 4)
    text_one = swapped(text, "dp", 2)
    text_three = swapped(text_two, "dp", 2)
    texts = [text, text_one, text_two, text_three]

    block_ids = jnp.arange(data_count, dtype=jnp.int32)
    slots = ((block_ids ^ data_rank) >> 1) + planes * ((block_ids ^ data_rank) & 1)
    core = (tensor_rank & 1).astype(jnp.int32).reshape(1)
    mine, other = call(
        turn_kernel,
        [((planes * size, 2 * rows), bf16), ((planes // 2 * size, 2 * rows), bf16)],
        slots,
        core,
        picture_averaged_encodings,
        caption_averaged_encodings,
        after=(image_other,),
    )
    other = swapped(other, "dp", 1)
    others = (other, swapped(other, "tensor", 1))

    (near,) = call(
        stack_kernel,
        [((4 * rows, wide), bf16)],
        image,
        image_other,
        image_far,
        image_far_other,
        after=(text_one, text_two, others[0]),
    )
    far = swapped(near, "tensor", 1)
    raw_both, half_both, factors = call(
        functools.partial(image_rows_kernel, main, tail, count),
        [
            ((4 * rows, width), bf16),
            ((4 * rows, width), bf16),
            ((2, 2 * rows, 128), f32),
        ],
        near,
        far,
    )

    scalars = jnp.concatenate([sharpness_multiplier, offset_additive])
    def block_weights(slots, first, *held, after=()):
        return call(
            functools.partial(weight_kernel, slots, first),
            [
                ((2 * slots * share, width), bf16),
                ((slots * share, 4 * rows), bf16),
                ((2 * rows, 2 * slots * share), bf16),
            ],
            (tensor_rank * share).astype(jnp.int32).reshape(1),
            scalars,
            half_both,
            *texts[first:slots],
            *held,
            after=after,
        )

    held = block_weights(planes - 1, 0, after=(others[1],))
    text_both, weights, weights_turned = block_weights(planes, planes - 1, *held)
    kept, sent = call(
        functools.partial(image_block_kernel, main, tail),
        [((2 * rows, wide), f32)] * 2,
        scalars,
        raw_both,
        factors,
        text_both,
        weights_turned,
    )
    outs = call(
        functools.partial(text_block_kernel, planes),
        [((2 * share, width), f32), ((2 * share, width), bf16)],
        scalars,
        half_both,
        weights,
        *texts,
        after=(kept,),
    )

    near = (tensor_rank // 2).astype(jnp.int32).reshape(1)
    tall = folded_rows(rows, main, tail)
    more = folded_rows(2 * share, main, tail)
    total, to_x, to_y, to_both = call(
        functools.partial(image_pair_kernel, main, tail, share),
        [((rows, cols), f32), ((tall + more, main), bf16)] + [((tall, main), bf16)] * 2,
        near,
        kept,
        swapped(sent, "tensor", 1),
        after=(outs[1],),
    )
    flat = [(source, source ^ (count + 2)) for source in range(data_count * count)]
    (image_back,) = call(
        functools.partial(image_sum_kernel, main, tail, share),
        [((tall, main), bf16)],
        near,
        total,
        swapped(to_x, "tensor", 2),
        swapped(to_y, "dp", 1),
        lax.ppermute(to_both, ("dp", "tensor"), flat),
    )
    image_back_other = swapped(image_back, "dp", 1)

    def head(which, order, back, back_other):
        return call(
            functools.partial(head_kernel, main, tail, which),
            [((size, cols), f32)]
            + [((folded_rows(size, main, tail), main), bf16)] * (planes - 1),
            core,
            order,
            mine,
            *others,
            back,
            back_other,
            scratch=[((2, rows, cols), bf16)],
        )

    def summed(products):
        got = [swapped(products[k], "dp", 2 * k) for k in range(1, planes)]
        return call(
            functools.partial(final_kernel, main, tail), [((size, cols), f32)], products[0], *got
        )[0]

    image_products = head(0, plain, image_back, image_back_other)

    text_total, text_sent = call(
        forward_kernel,
        [((share, width), f32), ((share, width), bf16)],
        outs[0],
        swapped(outs[1], "dp", 2),
    )
    blocks = call(
        functools.partial(text_sum_kernel, main, tail),
        [((share, cols), bf16)] * count,
        text_total,
        swapped(text_sent, "dp", 4),
        after=(image_back,),
    )
    got = [blocks[0]] + [swapped(blocks[k], "tensor", k) for k in range(1, count)]
    (text_back,) = call(fold_kernel, [((tall, main), bf16)], *got, after=(image_products[0],))
    text_back_other = swapped(text_back, "dp", 1)

    text_products = head(1, starts, text_back, text_back_other)
    return summed(image_products), summed(text_products)


def fits(mesh):
    return mesh.shape["tensor"] == 4 and mesh.shape["dp"] == 8


def solution(mesh):
    in_specs = (
        P("dp", None),
        P("dp", None),
        P(None, "tensor"),
        P(None, "tensor"),
        P(None, "tensor"),
        P(None, "tensor"),
        P(),
        P(),
    )
    out_specs = (P("dp", "tensor"), P("dp", "tensor"))
    local = packed if fits(mesh) else general
    return jax.shard_map(local, mesh=mesh, in_specs=in_specs, out_specs=out_specs, check_vma=False)
```

```python
import functools

import jax
import jax.numpy as jnp
from jax import lax
from jax.experimental import pallas as pl
from jax.experimental.pallas import tpu as pltpu
from jax.sharding import PartitionSpec as P

EPS = 1e-06


def swapped(value, axis, mask):
    count = lax.axis_size(axis)
    return lax.ppermute(value, axis, [(source, source ^ mask) for source in range(count)])


def matmul(left, right):
    return jnp.dot(left, right, preferred_element_type=jnp.float32)


def matmul_nt(left, right):
    return lax.dot_general(
        left, right, (((1,), (1,)), ((), ())), preferred_element_type=jnp.float32
    )


def matmul_tn(left, right):
    return lax.dot_general(
        left, right, (((0,), (0,)), ((), ())), preferred_element_type=jnp.float32
    )


def unit_parts(raw, raw_rate):
    values = raw.astype(jnp.float32)
    tangent = raw_rate.astype(jnp.float32)
    radius = jnp.sqrt(jnp.sum(values * values, axis=1, keepdims=True) + EPS)
    unit = values / radius
    rate = jnp.sum(unit * tangent, axis=1, keepdims=True)
    unit_tangent = (tangent - unit * rate) / radius
    return (unit, unit_tangent, radius, rate)


def unit_backward(unit, unit_tangent, radius, rate, grad, grad_rate):
    inner = jnp.sum(unit * grad, axis=1, keepdims=True)
    inner_rate = jnp.sum(unit_tangent * grad + unit * grad_rate, axis=1, keepdims=True)
    first = (grad - unit * inner) / radius
    return (grad_rate - unit_tangent * inner - unit * inner_rate - first * rate) / radius


def general(
    picture_averaged_encodings,
    caption_averaged_encodings,
    picture_mapping_matrix,
    caption_mapping_matrix,
    picture_weight_perturbation,
    caption_weight_perturbation,
    sharpness_multiplier,
    offset_additive,
):
    similarity_multiplier = sharpness_multiplier[0]
    logit_bias = offset_additive[0]
    tensor_rank = lax.axis_index("tensor")
    data_rank = lax.axis_index("dp")
    tensor_count = lax.axis_size("tensor")
    data_count = lax.axis_size("dp")
    planes = data_count // 2
    rows, width = picture_averaged_encodings.shape
    cols = picture_mapping_matrix.shape[1]
    share = rows // tensor_count
    out_rows = width // data_count
    half = jnp.bfloat16

    text = jnp.stack(
        [
            matmul(caption_averaged_encodings, caption_mapping_matrix).astype(half),
            matmul(caption_averaged_encodings, caption_weight_perturbation).astype(half),
        ]
    )
    image = jnp.stack(
        [
            matmul(picture_averaged_encodings, picture_mapping_matrix).astype(half),
            matmul(picture_averaged_encodings, picture_weight_perturbation).astype(half),
        ]
    )

    def share_of(value, axis, mask):
        start = (tensor_rank ^ mask) * share
        return lax.dynamic_slice_in_dim(value, start, share, axis)

    parts = [share_of(text, 1, 0)]
    for mask in range(1, tensor_count):
        parts.append(swapped(share_of(text, 1, mask), "tensor", mask))
    text = jnp.concatenate(parts, axis=2)
    slots = [text] + [swapped(text, "dp", 2 * mask) for mask in range(1, planes)]

    image = jnp.concatenate([image, swapped(image, "dp", 1)], axis=1)
    blocks = [image]
    mask = tensor_count // 2
    image_blocks = {0: image}
    while mask >= 1:
        held = sorted(image_blocks)
        sent = jnp.concatenate([image_blocks[k] for k in held], axis=2)
        got = swapped(sent, "tensor", mask)
        for place, k in enumerate(held):
            image_blocks[k ^ mask] = got[:, :, place * cols : (place + 1) * cols]
        mask //= 2
    image = jnp.concatenate([image_blocks[k] for k in range(tensor_count)], axis=2)
    text = jnp.concatenate(slots, axis=1)

    def out_columns(value, rank):
        taken = [
            lax.dynamic_slice_in_dim(value, (rank ^ (2 * mask)) * out_rows, out_rows, 1)
            for mask in range(planes)
        ]
        return jnp.concatenate(taken, axis=1)

    def plane_encodings(value):
        other = swapped(out_columns(value, data_rank ^ 1), "dp", 1)
        return jnp.concatenate([out_columns(value, data_rank), other], axis=0)

    picture_plane = plane_encodings(picture_averaged_encodings)
    ordered = jnp.concatenate(
        [share_of(caption_averaged_encodings, 0, mask) for mask in range(tensor_count)], axis=0
    )
    caption_plane = plane_encodings(ordered)

    image_unit, image_tangent, image_radius, image_rate = unit_parts(image[0], image[1])
    text_unit, text_tangent, text_radius, text_rate = unit_parts(text[0], text[1])
    image_half = image_unit.astype(half)
    image_tangent_half = image_tangent.astype(half)
    text_half = text_unit.astype(half)
    text_tangent_half = text_tangent.astype(half)

    logits = similarity_multiplier * matmul_nt(text_half, image_half) + logit_bias
    logit_rate = similarity_multiplier * (
        matmul_nt(text_half, image_tangent_half) + matmul_nt(text_tangent_half, image_half)
    )
    probability = jax.nn.sigmoid(logits)
    text_ids = lax.broadcasted_iota(jnp.int32, (logits.shape[0], 1), 0)
    image_ids = lax.broadcasted_iota(jnp.int32, (1, logits.shape[1]), 1)
    positive = ((text_ids < share) & (text_ids + tensor_rank * share == image_ids)).astype(
        jnp.float32
    )
    weight = (probability - positive).astype(half)
    weight_rate = (probability * (1.0 - probability) * logit_rate).astype(half)
    text_grad = similarity_multiplier * matmul(weight, image_half)
    text_grad_rate = similarity_multiplier * (
        matmul(weight_rate, image_half) + matmul(weight, image_tangent_half)
    )
    image_grad = similarity_multiplier * matmul_tn(weight, text_half)
    image_grad_rate = similarity_multiplier * (
        matmul_tn(weight_rate, text_half) + matmul_tn(weight, text_tangent_half)
    )

    text_back = unit_backward(
        text_unit, text_tangent, text_radius, text_rate, text_grad, text_grad_rate
    )
    image_back = unit_backward(
        image_unit, image_tangent, image_radius, image_rate, image_grad, image_grad_rate
    )

    total = text_back[:share]
    for mask in range(1, planes):
        sent = text_back[mask * share : (mask + 1) * share].astype(half)
        total = total + swapped(sent, "dp", 2 * mask).astype(jnp.float32)
    text_back = total.astype(half)
    parts = [text_back[:, :cols]]
    for mask in range(1, tensor_count):
        sent = text_back[:, mask * cols : (mask + 1) * cols]
        parts.append(swapped(sent, "tensor", mask))
    text_back = jnp.concatenate(parts, axis=0)
    text_back = jnp.concatenate([text_back, swapped(text_back, "dp", 1)], axis=0)

    image_blocks = {k: image_back[:, k * cols : (k + 1) * cols] for k in range(tensor_count)}
    mask = 1
    while mask < tensor_count:
        kept = [k for k in sorted(image_blocks) if not k & mask]
        sent = jnp.concatenate([image_blocks[k ^ mask] for k in kept], axis=1)
        got = swapped(sent, "tensor", mask).astype(jnp.float32)
        image_blocks = {
            k: image_blocks[k] + got[:, place * cols : (place + 1) * cols]
            for place, k in enumerate(kept)
        }
        mask *= 2
    image_back = image_blocks[0]
    got = swapped(image_back, "dp", 1)
    image_back = (
        image_back + jnp.concatenate([got[rows:], got[:rows]], axis=0)
    ).astype(half)

    def head(encodings, back):
        product = matmul_tn(encodings, back)
        total = product[:out_rows]
        for mask in range(1, planes):
            sent = product[mask * out_rows : (mask + 1) * out_rows].astype(half)
            total = total + swapped(sent, "dp", 2 * mask).astype(jnp.float32)
        return total

    return (head(picture_plane, image_back), head(caption_plane, text_back))


def call(kernel, outs, *args, after=(), scratch=()):
    count = len(args)

    def body(*refs):
        kernel(*refs[:count], *refs[count + len(after) :])

    def place(value):
        scalar = value.ndim == 1
        return pl.BlockSpec(memory_space=pltpu.SMEM if scalar else pltpu.VMEM)

    return pl.pallas_call(
        body,
        out_shape=[jax.ShapeDtypeStruct(shape, dtype) for shape, dtype in outs],
        in_specs=[place(value) for value in args]
        + [pl.BlockSpec(memory_space=pl.ANY) for _ in after],
        out_specs=[pl.BlockSpec(memory_space=pltpu.VMEM) for _ in outs],
        scratch_shapes=[pltpu.VMEM(shape, dtype) for shape, dtype in scratch],
        compiler_params=pltpu.CompilerParams(vmem_limit_bytes=9 * 1024 * 1024),
    )(*args, *after)


def folds(rows, main, tail):
    across = main // tail
    for k in range(rows // 16):
        here = slice(k * 16, (k + 1) * 16)
        at = rows + k // across * 16
        first = k % across * tail
        yield here, slice(at, at + 16), slice(first, first + tail)


def folded_rows(rows, main, tail):
    return rows + -(-rows // 16 // (main // tail)) * 16


def fold(out, first, value, main):
    rows, cols = value.shape
    out[first : first + rows, :] = value[:, :main].astype(out.dtype)
    for here, there, lanes in folds(rows, main, cols - main):
        there = slice(first + there.start, first + there.stop)
        out[there, lanes] = value[here, main:].astype(out.dtype)


def unfold(ref, first, rows, main, tail):
    tails = [
        ref[first + there.start : first + there.stop, lanes]
        for _, there, lanes in folds(rows, main, tail)
    ]
    return jnp.concatenate([ref[first : first + rows, :], jnp.concatenate(tails, axis=0)], axis=1)


def project_kernel(share, starts, encodings, weight, direction, *outs):
    main = weight.shape[0] // 128 * 128
    left = jnp.concatenate(
        [
            encodings[pl.ds(pl.multiple_of(starts[k], 16), share), :]
            for k in range(starts.shape[0])
        ],
        axis=0,
    )
    tails = jnp.concatenate([weight[main:, :], direction[main:, :]], axis=0)
    for right, first in ((weight[:main, :], 0), (direction[:main, :], main), (tails, 2 * main)):
        product = matmul_nt(left, right).astype(jnp.bfloat16)
        place = 0
        for out in outs:
            rows = out.shape[0]
            out[:, first : first + right.shape[0]] = product[place : place + rows]
            place += rows


def gathered(blocks, main, tail, which):
    first = 2 * main + which * tail
    mains = [block[:, which * main : (which + 1) * main] for block in blocks]
    tails = [block[:, first : first + tail] for block in blocks]
    return jnp.concatenate(mains + tails, axis=1)


def relay_kernel(mine, got, out):
    rows = mine.shape[0]
    out[:rows, :] = mine[...]
    out[rows:, :] = got[rows:, :]


def text_rows_kernel(main, tail, own, far, near, out):
    rows, width = own.shape[0], out.shape[1] // 2
    parts = (own[...], near[:rows, :], far[:rows, :], near[rows:, :])
    blocks = [part.astype(jnp.float32) for part in parts]
    out[:, :width] = gathered(blocks, main, tail, 0).astype(jnp.bfloat16)
    out[:, width:] = gathered(blocks, main, tail, 1).astype(jnp.bfloat16)


def row_factors(values, tangent):
    squares = jnp.sum(values * values, axis=1, keepdims=True)
    cross = jnp.sum(values * tangent, axis=1, keepdims=True)
    inverse = 1.0 / jnp.sqrt(squares + EPS)
    return inverse, cross * inverse


def unit_rows(values, tangent, inverse, rate):
    unit = values * inverse
    return unit, (tangent - unit * rate) * inverse


def back_rows(unit, tangent, inverse, rate, grad, grad_rate):
    inner = jnp.sum(unit * grad, axis=1, keepdims=True)
    inner_rate = jnp.sum(tangent * grad + unit * grad_rate, axis=1, keepdims=True)
    scaled = rate * inverse
    return (
        grad_rate - tangent * inner - grad * scaled + unit * (inner * scaled - inner_rate)
    ) * inverse


STEP = 48


def image_rows_kernel(main, tail, count, near, far, raw_both, half_both, factors):
    rows = raw_both.shape[0] // 4
    for shard in range(2):
        held = [
            (near, far)[k % 2].at[pl.ds((k - k % 2 + shard) * rows, rows), :] for k in range(count)
        ]

        @pl.loop(0, rows // STEP)
        def _(step):
            here = pl.ds(pl.multiple_of(step * STEP, STEP), STEP)
            there = pl.ds(pl.multiple_of(shard * rows + step * STEP, STEP), STEP)
            parts = [block[here, :].astype(jnp.float32) for block in held]
            values = gathered(parts, main, tail, 0)
            rates = gathered(parts, main, tail, 1)
            inverse, rate = row_factors(values, rates)
            one, two = unit_rows(values, rates, inverse, rate)
            below = pl.ds(pl.multiple_of((2 + shard) * rows + step * STEP, STEP), STEP)
            raw_both[there, :] = values.astype(jnp.bfloat16)
            raw_both[below, :] = rates.astype(jnp.bfloat16)
            half_both[there, :] = one.astype(jnp.bfloat16)
            half_both[below, :] = two.astype(jnp.bfloat16)
            factors[0, there, :] = jnp.broadcast_to(inverse, (STEP, 128))
            factors[1, there, :] = jnp.broadcast_to(rate, (STEP, 128))


def text_rows(text):
    width = text.shape[1] // 2
    values, rates = text[:, :width].astype(jnp.float32), text[:, width:].astype(jnp.float32)
    inverse, rate = row_factors(values, rates)
    return unit_rows(values, rates, inverse, rate) + (inverse, rate)


def weight_kernel(slots, first, start, scalars, half_both, *refs):
    texts, refs = refs[: slots - first], refs[slots - first :]
    held, (text_both, weights, weights_turned) = refs[:-3], refs[-3:]
    bf16 = jnp.bfloat16
    share = texts[0].shape[0]
    count, images = slots * share, half_both.shape[0] // 2
    done = first * share
    multiplier, bias = scalars[0], scalars[1]
    if held:
        for part in range(2):
            here = slice(part * done, (part + 1) * done)
            there = slice(part * count, part * count + done)
            text_both[there, :] = held[0][here, :]
            weights_turned[:, there] = held[2][:, here]
        weights[:done, :] = held[1][...]
    units, tangents = [], []
    for text in texts:
        unit, tangent, _, _ = text_rows(text)
        units.append(unit.astype(bf16))
        tangents.append(tangent.astype(bf16))
    units, both = jnp.concatenate(units, axis=0), jnp.concatenate(units + tangents, axis=0)
    fresh = units.shape[0]
    text_both[done:count, :] = units
    text_both[count + done :, :] = both[fresh:]
    products = matmul_nt(both, half_both[:images, :])
    logits = multiplier * products[:fresh] + bias
    logit_rate = multiplier * (matmul_nt(units, half_both[images:, :]) + products[fresh:])
    probability = jax.nn.sigmoid(logits)
    text_ids = lax.broadcasted_iota(jnp.int32, logits.shape, 0) + done
    image_ids = lax.broadcasted_iota(jnp.int32, logits.shape, 1)
    positive = jnp.where((text_ids < share) & (text_ids + start[0] == image_ids), 1.0, 0.0)
    value = probability - positive
    value_rate = probability * (1.0 - probability) * logit_rate
    weights[done:, :images] = value_rate.astype(bf16)
    weights[done:, images:] = value.astype(bf16)
    weights_turned[:, done:count] = value_rate.T.astype(bf16)
    weights_turned[:, count + done :] = value.T.astype(bf16)


def text_block_kernel(slots, scalars, half_both, weights, *refs):
    texts, sums = refs[:slots], refs[slots:]
    share, images = texts[0].shape[0], half_both.shape[0] // 2
    grad = matmul(weights[:, images:], half_both[:images, :])
    grad_rate = matmul(weights[...], half_both[...])
    for slot, text in enumerate(texts):
        here = slice(slot * share, (slot + 1) * share)
        back = scalars[0] * back_rows(*text_rows(text), grad[here], grad_rate[here])
        at = slice(slot // 2 * share, (slot // 2 + 1) * share)
        sums[slot % 2][at, :] = back.astype(sums[slot % 2].dtype)


def forward_kernel(mine, got, total, sent):
    share = total.shape[0]
    total[...] = mine[:share, :] + got[:share, :].astype(jnp.float32)
    sent[...] = (mine[share:, :] + got[share:, :].astype(jnp.float32)).astype(jnp.bfloat16)


def image_block_kernel(main, tail, scalars, raw_both, factors, text_both, weights, kept, sent):
    rows, width = raw_both.shape[0] // 4, raw_both.shape[1]
    count, texts = width // (main + tail), text_both.shape[0] // 2
    grads = matmul(weights[:, texts:], text_both[:texts, :])
    grad_rates = matmul(weights[...], text_both[...])
    for shard in range(2):
        here = slice(shard * rows, (shard + 1) * rows)
        inverse, rate = factors[0, here, :1], factors[1, here, :1]
        below = slice((2 + shard) * rows, (3 + shard) * rows)
        values, rates = raw_both[here, :], raw_both[below, :]
        unit, tangent = unit_rows(
            values.astype(jnp.float32), rates.astype(jnp.float32), inverse, rate
        )
        back = back_rows(unit, tangent, inverse, rate, grads[here], grad_rates[here])
        back = scalars[0] * back
        for k in range(count):
            out = (kept, sent)[k % 2]
            to = slice(k // 2 * rows, (k // 2 + 1) * rows)
            out[to, shard * main : (shard + 1) * main] = back[:, k * main : (k + 1) * main]
            first = 2 * main + shard * tail
            taken = count * main + k * tail
            out[to, first : first + tail] = back[:, taken : taken + tail]


def text_sum_kernel(main, tail, own, *refs):
    count = own.shape[1] // (main + tail)
    got, outs = refs[:-count], refs[-count:]
    total = own[...]
    for ref in got:
        total = total + ref[...].astype(jnp.float32)
    for k, out in enumerate(outs):
        first = count * main + k * tail
        out[:, :main] = total[:, k * main : (k + 1) * main].astype(jnp.bfloat16)
        out[:, main:] = total[:, first : first + tail].astype(jnp.bfloat16)


def stack_kernel(*refs):
    rows = refs[0].shape[0]
    for k, ref in enumerate(refs[:-1]):
        refs[-1][k * rows : (k + 1) * rows, : ref.shape[1]] = ref[...]


def fold_kernel(*refs):
    value = jnp.concatenate([ref[...] for ref in refs[:-1]], axis=0)
    fold(refs[-1], 0, value, refs[-1].shape[1])


def turn_kernel(places, core, picture, caption, mine, other):
    for which, encodings in enumerate((picture, caption)):
        turned = encodings[...].T
        count = places.shape[0]
        size, rows = turned.shape[0] // count, turned.shape[1]
        fold = count // 4
        for block in range(count):
            taken = turned[block * size : (block + 1) * size, :]
            slot = places[block]
            at = pl.multiple_of(slot % fold * size, 16)
            for half in range(2):
                lanes = slice(half * rows, (half + 1) * rows)

                @pl.when(slot // fold == half)
                def _():
                    mine[pl.ds(which * fold * size + at, size), lanes] = taken

                @pl.when((slot // fold == 2 + half) & (core[0] == which))
                def _():
                    other[pl.ds(at, size), lanes] = taken


def shard_columns(value, main, tail, shard):
    at = 2 * main + shard * tail
    return jnp.concatenate(
        [value[:, shard * main : (shard + 1) * main], value[:, at : at + tail]], axis=1
    )


def image_pair_kernel(main, tail, share, near, kept, got, total, over_x, over_y, over_both):
    rows = total.shape[0]
    ours = kept[:rows, :] + got[:rows, :]
    theirs = kept[rows:, :] + got[rows:, :]
    total[...] = shard_columns(ours, main, tail, 0)
    fold(over_y, 0, shard_columns(ours, main, tail, 1), main)
    fold(over_both, 0, shard_columns(theirs, main, tail, 1), main)
    value = shard_columns(theirs, main, tail, 0)
    rounded = value.astype(jnp.bfloat16)
    fold(over_x, 0, rounded, main)
    left = value - rounded.astype(jnp.float32)
    left = jnp.where(near[0] == 0, left[: 2 * share], left[2 * share : 4 * share])
    fold(over_x, folded_rows(rows, main, tail), left, main)


def image_sum_kernel(main, tail, share, near, total, over_x, over_y, over_both, out):
    rows = total.shape[0]
    value = total[...]
    for source in (over_x, over_y, over_both):
        value = value + unfold(source, 0, rows, main, tail).astype(jnp.float32)
    left = unfold(over_x, folded_rows(rows, main, tail), 2 * share, main, tail)
    left = left.astype(jnp.float32)
    zero = jnp.zeros_like(left)
    far = near[0] == 0
    value = value + jnp.concatenate(
        [jnp.where(far, zero, left), jnp.where(far, left, zero)], axis=0
    )
    fold(out, 0, value.astype(jnp.bfloat16), main)


def head_kernel(main, tail, head, core, starts, mine, near, far, back, back_other, own, *refs):
    sent, (ordered,) = refs[:-1], refs[-1:]
    size, rows = own.shape[0], ordered.shape[1]
    share = rows // starts.shape[0]
    for which, ref in enumerate((back, back_other)):
        value = unfold(ref, 0, rows, main, tail)
        for k in range(starts.shape[0]):
            at = pl.ds(pl.multiple_of(starts[k], 16), share)
            ordered[which, at, :] = value[k * share : (k + 1) * share]
    count = (len(sent) + 1) // 2
    other = jnp.where(core[0] == head, near[...], far[...])
    for half in range(2):
        here = slice(head * count * size, (head + 1) * count * size)
        lanes = slice(half * rows, (half + 1) * rows)
        product = matmul(mine[here, lanes], ordered[0]) + matmul(other[:, lanes], ordered[1])
        for place in range(count):
            part = product[place * size : (place + 1) * size]
            slot = half * count + place
            if slot == 0:
                own[...] = part
            else:
                fold(sent[slot - 1], 0, part, main)


def final_kernel(main, tail, own, *refs):
    got, out = refs[:-1], refs[-1]
    total = own[...]
    for ref in got:
        total = total + unfold(ref, 0, own.shape[0], main, tail).astype(jnp.float32)
    out[...] = total


def final_kernel(main, tail, own, *refs):
    got, out = refs[:-1], refs[-1]
    size = own.shape[0]
    total = own[:, :main]
    for ref in got:
        total = total + ref[:size, :].astype(jnp.float32)
    out[:, :main] = total
    for rows_in, rows_out, lanes_out in folds(size, main, tail):
        total = own[rows_in, main:]
        for ref in got:
            total = total + ref[rows_out, lanes_out].astype(jnp.float32)
        out[rows_in, main:] = total


def packed(
    picture_averaged_encodings,
    caption_averaged_encodings,
    picture_mapping_matrix,
    caption_mapping_matrix,
    picture_weight_perturbation,
    caption_weight_perturbation,
    sharpness_multiplier,
    offset_additive,
):
    tensor_rank = lax.axis_index("tensor")
    data_rank = lax.axis_index("dp")
    count = lax.axis_size("tensor")
    data_count = lax.axis_size("dp")
    planes = data_count // 2
    rows, width = picture_averaged_encodings.shape
    cols = picture_mapping_matrix.shape[1]
    main = cols // 128 * 128
    tail = cols - main
    share = rows // count
    size = width // data_count
    wide = -(-2 * cols // 128) * 128
    f32, bf16 = jnp.float32, jnp.bfloat16
    ranks = jnp.arange(count, dtype=jnp.int32)
    starts = (ranks ^ tensor_rank) * share
    plain = ranks * share

    blocks = call(
        functools.partial(project_kernel, share),
        [((share, 2 * cols), bf16)] * 2 + [((2 * share, 2 * cols), bf16)],
        starts,
        caption_averaged_encodings,
        caption_mapping_matrix.T,
        caption_weight_perturbation.T,
    )
    text_far = swapped(blocks[2], "tensor", 2)
    (relay,) = call(relay_kernel, [((2 * share, 2 * cols), bf16)], blocks[1], text_far)
    text_near = swapped(relay, "tensor", 1)

    (image,) = call(
        functools.partial(project_kernel, share),
        [((rows, 2 * cols), bf16)],
        plain,
        picture_averaged_encodings,
        picture_mapping_matrix.T,
        picture_weight_perturbation.T,
        after=(blocks[0],),
    )
    image_other = swapped(image, "dp", 1)
    image_far = swapped(image, "tensor", 2)
    image_far_other = swapped(image_other, "tensor", 2)

    (text,) = call(
        functools.partial(text_rows_kernel, main, tail),
        [((share, 2 * width), bf16)],
        blocks[0],
        text_far,
        text_near,
    )
    text_two = swapped(text, "dp", 4)
    text_one = swapped(text, "dp", 2)
    text_three = swapped(text_two, "dp", 2)
    texts = [text, text_one, text_two, text_three]

    block_ids = jnp.arange(data_count, dtype=jnp.int32)
    slots = ((block_ids ^ data_rank) >> 1) + planes * ((block_ids ^ data_rank) & 1)
    core = (tensor_rank & 1).astype(jnp.int32).reshape(1)
    mine, other = call(
        turn_kernel,
        [((planes * size, 2 * rows), bf16), ((planes // 2 * size, 2 * rows), bf16)],
        slots,
        core,
        picture_averaged_encodings,
        caption_averaged_encodings,
        after=(image_other,),
    )
    other = swapped(other, "dp", 1)
    others = (other, swapped(other, "tensor", 1))

    (near,) = call(
        stack_kernel,
        [((4 * rows, wide), bf16)],
        image,
        image_other,
        image_far,
        image_far_other,
        after=(text_one, text_two, others[0]),
    )
    far = swapped(near, "tensor", 1)
    raw_both, half_both, factors = call(
        functools.partial(image_rows_kernel, main, tail, count),
        [
            ((4 * rows, width), bf16),
            ((4 * rows, width), bf16),
            ((2, 2 * rows, 128), f32),
        ],
        near,
        far,
    )

    scalars = jnp.concatenate([sharpness_multiplier, offset_additive])
    def block_weights(slots, first, *held, after=()):
        return call(
            functools.partial(weight_kernel, slots, first),
            [
                ((2 * slots * share, width), bf16),
                ((slots * share, 4 * rows), bf16),
                ((2 * rows, 2 * slots * share), bf16),
            ],
            (tensor_rank * share).astype(jnp.int32).reshape(1),
            scalars,
            half_both,
            *texts[first:slots],
            *held,
            after=after,
        )

    held = block_weights(planes - 1, 0, after=(others[1],))
    text_both, weights, weights_turned = block_weights(planes, planes - 1, *held)
    kept, sent = call(
        functools.partial(image_block_kernel, main, tail),
        [((2 * rows, wide), f32)] * 2,
        scalars,
        raw_both,
        factors,
        text_both,
        weights_turned,
    )
    outs = call(
        functools.partial(text_block_kernel, planes),
        [((2 * share, width), f32), ((2 * share, width), bf16)],
        scalars,
        half_both,
        weights,
        *texts,
        after=(kept,),
    )

    near = (tensor_rank // 2).astype(jnp.int32).reshape(1)
    tall = folded_rows(rows, main, tail)
    more = folded_rows(2 * share, main, tail)
    total, to_x, to_y, to_both = call(
        functools.partial(image_pair_kernel, main, tail, share),
        [((rows, cols), f32), ((tall + more, main), bf16)] + [((tall, main), bf16)] * 2,
        near,
        kept,
        swapped(sent, "tensor", 1),
        after=(outs[1],),
    )
    flat = [(source, source ^ (count + 2)) for source in range(data_count * count)]
    (image_back,) = call(
        functools.partial(image_sum_kernel, main, tail, share),
        [((tall, main), bf16)],
        near,
        total,
        swapped(to_x, "tensor", 2),
        swapped(to_y, "dp", 1),
        lax.ppermute(to_both, ("dp", "tensor"), flat),
    )
    image_back_other = swapped(image_back, "dp", 1)

    def head(which, order, back, back_other):
        return call(
            functools.partial(head_kernel, main, tail, which),
            [((size, cols), f32)]
            + [((folded_rows(size, main, tail), main), bf16)] * (planes - 1),
            core,
            order,
            mine,
            *others,
            back,
            back_other,
            scratch=[((2, rows, cols), bf16)],
        )

    def summed(products):
        got = [swapped(products[k], "dp", 2 * k) for k in range(1, planes)]
        return call(
            functools.partial(final_kernel, main, tail), [((size, cols), f32)], products[0], *got
        )[0]

    image_products = head(0, plain, image_back, image_back_other)

    text_total, text_sent = call(
        forward_kernel,
        [((share, width), f32), ((share, width), bf16)],
        outs[0],
        swapped(outs[1], "dp", 2),
    )
    blocks = call(
        functools.partial(text_sum_kernel, main, tail),
        [((share, cols), bf16)] * count,
        text_total,
        swapped(text_sent, "dp", 4),
        after=(image_back,),
    )
    got = [blocks[0]] + [swapped(blocks[k], "tensor", k) for k in range(1, count)]
    (text_back,) = call(fold_kernel, [((tall, main), bf16)], *got, after=(image_products[0],))
    text_back_other = swapped(text_back, "dp", 1)

    text_products = head(1, starts, text_back, text_back_other)
    return summed(image_products), summed(text_products)


def fits(mesh):
    return mesh.shape["tensor"] == 4 and mesh.shape["dp"] == 8


def solution(mesh):
    in_specs = (
        P("dp", None),
        P("dp", None),
        P(None, "tensor"),
        P(None, "tensor"),
        P(None, "tensor"),
        P(None, "tensor"),
        P(),
        P(),
    )
    out_specs = (P("dp", "tensor"), P("dp", "tensor"))
    local = packed if fits(mesh) else general
    return jax.shard_map(local, mesh=mesh, in_specs=in_specs, out_specs=out_specs, check_vma=False)
```

```python
import functools

import jax
import jax.numpy as jnp
from jax import lax
from jax.experimental import pallas as pl
from jax.experimental.pallas import tpu as pltpu
from jax.sharding import PartitionSpec as P

EPS = 1e-06


def swapped(value, axis, mask):
    count = lax.axis_size(axis)
    return lax.ppermute(value, axis, [(source, source ^ mask) for source in range(count)])


def matmul(left, right):
    return jnp.dot(left, right, preferred_element_type=jnp.float32)


def matmul_nt(left, right):
    return lax.dot_general(
        left, right, (((1,), (1,)), ((), ())), preferred_element_type=jnp.float32
    )


def matmul_tn(left, right):
    return lax.dot_general(
        left, right, (((0,), (0,)), ((), ())), preferred_element_type=jnp.float32
    )


def unit_parts(raw, raw_rate):
    values = raw.astype(jnp.float32)
    tangent = raw_rate.astype(jnp.float32)
    radius = jnp.sqrt(jnp.sum(values * values, axis=1, keepdims=True) + EPS)
    unit = values / radius
    rate = jnp.sum(unit * tangent, axis=1, keepdims=True)
    unit_tangent = (tangent - unit * rate) / radius
    return (unit, unit_tangent, radius, rate)


def unit_backward(unit, unit_tangent, radius, rate, grad, grad_rate):
    inner = jnp.sum(unit * grad, axis=1, keepdims=True)
    inner_rate = jnp.sum(unit_tangent * grad + unit * grad_rate, axis=1, keepdims=True)
    first = (grad - unit * inner) / radius
    return (grad_rate - unit_tangent * inner - unit * inner_rate - first * rate) / radius


def general(
    picture_averaged_encodings,
    caption_averaged_encodings,
    picture_mapping_matrix,
    caption_mapping_matrix,
    picture_weight_perturbation,
    caption_weight_perturbation,
    sharpness_multiplier,
    offset_additive,
):
    similarity_multiplier = sharpness_multiplier[0]
    logit_bias = offset_additive[0]
    tensor_rank = lax.axis_index("tensor")
    data_rank = lax.axis_index("dp")
    tensor_count = lax.axis_size("tensor")
    data_count = lax.axis_size("dp")
    planes = data_count // 2
    rows, width = picture_averaged_encodings.shape
    cols = picture_mapping_matrix.shape[1]
    share = rows // tensor_count
    out_rows = width // data_count
    half = jnp.bfloat16

    text = jnp.stack(
        [
            matmul(caption_averaged_encodings, caption_mapping_matrix).astype(half),
            matmul(caption_averaged_encodings, caption_weight_perturbation).astype(half),
        ]
    )
    image = jnp.stack(
        [
            matmul(picture_averaged_encodings, picture_mapping_matrix).astype(half),
            matmul(picture_averaged_encodings, picture_weight_perturbation).astype(half),
        ]
    )

    def share_of(value, axis, mask):
        start = (tensor_rank ^ mask) * share
        return lax.dynamic_slice_in_dim(value, start, share, axis)

    parts = [share_of(text, 1, 0)]
    for mask in range(1, tensor_count):
        parts.append(swapped(share_of(text, 1, mask), "tensor", mask))
    text = jnp.concatenate(parts, axis=2)
    slots = [text] + [swapped(text, "dp", 2 * mask) for mask in range(1, planes)]

    image = jnp.concatenate([image, swapped(image, "dp", 1)], axis=1)
    blocks = [image]
    mask = tensor_count // 2
    image_blocks = {0: image}
    while mask >= 1:
        held = sorted(image_blocks)
        sent = jnp.concatenate([image_blocks[k] for k in held], axis=2)
        got = swapped(sent, "tensor", mask)
        for place, k in enumerate(held):
            image_blocks[k ^ mask] = got[:, :, place * cols : (place + 1) * cols]
        mask //= 2
    image = jnp.concatenate([image_blocks[k] for k in range(tensor_count)], axis=2)
    text = jnp.concatenate(slots, axis=1)

    def out_columns(value, rank):
        taken = [
            lax.dynamic_slice_in_dim(value, (rank ^ (2 * mask)) * out_rows, out_rows, 1)
            for mask in range(planes)
        ]
        return jnp.concatenate(taken, axis=1)

    def plane_encodings(value):
        other = swapped(out_columns(value, data_rank ^ 1), "dp", 1)
        return jnp.concatenate([out_columns(value, data_rank), other], axis=0)

    picture_plane = plane_encodings(picture_averaged_encodings)
    ordered = jnp.concatenate(
        [share_of(caption_averaged_encodings, 0, mask) for mask in range(tensor_count)], axis=0
    )
    caption_plane = plane_encodings(ordered)

    image_unit, image_tangent, image_radius, image_rate = unit_parts(image[0], image[1])
    text_unit, text_tangent, text_radius, text_rate = unit_parts(text[0], text[1])
    image_half = image_unit.astype(half)
    image_tangent_half = image_tangent.astype(half)
    text_half = text_unit.astype(half)
    text_tangent_half = text_tangent.astype(half)

    logits = similarity_multiplier * matmul_nt(text_half, image_half) + logit_bias
    logit_rate = similarity_multiplier * (
        matmul_nt(text_half, image_tangent_half) + matmul_nt(text_tangent_half, image_half)
    )
    probability = jax.nn.sigmoid(logits)
    text_ids = lax.broadcasted_iota(jnp.int32, (logits.shape[0], 1), 0)
    image_ids = lax.broadcasted_iota(jnp.int32, (1, logits.shape[1]), 1)
    positive = ((text_ids < share) & (text_ids + tensor_rank * share == image_ids)).astype(
        jnp.float32
    )
    weight = (probability - positive).astype(half)
    weight_rate = (probability * (1.0 - probability) * logit_rate).astype(half)
    text_grad = similarity_multiplier * matmul(weight, image_half)
    text_grad_rate = similarity_multiplier * (
        matmul(weight_rate, image_half) + matmul(weight, image_tangent_half)
    )
    image_grad = similarity_multiplier * matmul_tn(weight, text_half)
    image_grad_rate = similarity_multiplier * (
        matmul_tn(weight_rate, text_half) + matmul_tn(weight, text_tangent_half)
    )

    text_back = unit_backward(
        text_unit, text_tangent, text_radius, text_rate, text_grad, text_grad_rate
    )
    image_back = unit_backward(
        image_unit, image_tangent, image_radius, image_rate, image_grad, image_grad_rate
    )

    total = text_back[:share]
    for mask in range(1, planes):
        sent = text_back[mask * share : (mask + 1) * share].astype(half)
        total = total + swapped(sent, "dp", 2 * mask).astype(jnp.float32)
    text_back = total.astype(half)
    parts = [text_back[:, :cols]]
    for mask in range(1, tensor_count):
        sent = text_back[:, mask * cols : (mask + 1) * cols]
        parts.append(swapped(sent, "tensor", mask))
    text_back = jnp.concatenate(parts, axis=0)
    text_back = jnp.concatenate([text_back, swapped(text_back, "dp", 1)], axis=0)

    image_blocks = {k: image_back[:, k * cols : (k + 1) * cols] for k in range(tensor_count)}
    mask = 1
    while mask < tensor_count:
        kept = [k for k in sorted(image_blocks) if not k & mask]
        sent = jnp.concatenate([image_blocks[k ^ mask] for k in kept], axis=1)
        got = swapped(sent, "tensor", mask).astype(jnp.float32)
        image_blocks = {
            k: image_blocks[k] + got[:, place * cols : (place + 1) * cols]
            for place, k in enumerate(kept)
        }
        mask *= 2
    image_back = image_blocks[0]
    got = swapped(image_back, "dp", 1)
    image_back = (
        image_back + jnp.concatenate([got[rows:], got[:rows]], axis=0)
    ).astype(half)

    def head(encodings, back):
        product = matmul_tn(encodings, back)
        total = product[:out_rows]
        for mask in range(1, planes):
            sent = product[mask * out_rows : (mask + 1) * out_rows].astype(half)
            total = total + swapped(sent, "dp", 2 * mask).astype(jnp.float32)
        return total

    return (head(picture_plane, image_back), head(caption_plane, text_back))


def call(kernel, outs, *args, after=(), scratch=(), fetched=False):
    count = len(args)

    def body(*refs):
        kernel(*refs[:count], *refs[count + len(after) :])

    def place(value):
        if value.ndim == 1:
            return pl.BlockSpec(memory_space=pltpu.SMEM)
        return pl.BlockSpec(memory_space=pltpu.HBM if fetched else pltpu.VMEM)

    return pl.pallas_call(
        body,
        out_shape=[jax.ShapeDtypeStruct(shape, dtype) for shape, dtype in outs],
        in_specs=[place(value) for value in args]
        + [pl.BlockSpec(memory_space=pl.ANY) for _ in after],
        out_specs=[pl.BlockSpec(memory_space=pltpu.VMEM) for _ in outs],
        scratch_shapes=list(scratch),
        compiler_params=pltpu.CompilerParams(
            vmem_limit_bytes=(62 if fetched else 14) * 1024 * 1024
        ),
    )(*args, *after)


def folds(rows, main, tail):
    across = main // tail
    for k in range(rows // 16):
        here = slice(k * 16, (k + 1) * 16)
        at = rows + k // across * 16
        first = k % across * tail
        yield here, slice(at, at + 16), slice(first, first + tail)


def folded_rows(rows, main, tail):
    return rows + -(-rows // 16 // (main // tail)) * 16


def fold(out, first, value, main):
    rows, cols = value.shape
    out[first : first + rows, :] = value[:, :main].astype(out.dtype)
    for here, there, lanes in folds(rows, main, cols - main):
        there = slice(first + there.start, first + there.stop)
        out[there, lanes] = value[here, main:].astype(out.dtype)


def unfold(ref, first, rows, main, tail):
    tails = [
        ref[first + there.start : first + there.stop, lanes]
        for _, there, lanes in folds(rows, main, tail)
    ]
    return jnp.concatenate([ref[first : first + rows, :], jnp.concatenate(tails, axis=0)], axis=1)


def fetch_project_kernel(share, parts, starts, encodings, weight, direction, *refs):
    outs, held, done = refs[:-4], refs[-4:-1], refs[-1]
    copies = []
    for which, (source, target) in enumerate(zip((encodings, weight, direction), held)):
        rows = source.shape[0] // parts
        for part in range(parts):
            here = pl.ds(part * rows, rows)
            copies.append(
                pltpu.make_async_copy(source.at[here, :], target.at[here, :], done.at[which, part])
            )
    for copy in copies:
        copy.start()
    for copy in copies:
        copy.wait()
    project_kernel(share, starts, *held, *outs)


def project_kernel(share, starts, encodings, weight, direction, *outs):
    main = weight.shape[0] // 128 * 128
    left = jnp.concatenate(
        [
            encodings[pl.ds(pl.multiple_of(starts[k], 16), share), :]
            for k in range(starts.shape[0])
        ],
        axis=0,
    )
    tails = jnp.concatenate([weight[main:, :], direction[main:, :]], axis=0)
    for right, first in ((weight[:main, :], 0), (direction[:main, :], main), (tails, 2 * main)):
        product = matmul_nt(left, right).astype(jnp.bfloat16)
        place = 0
        for out in outs:
            rows = out.shape[0]
            out[:, first : first + right.shape[0]] = product[place : place + rows]
            place += rows


def gathered(blocks, main, tail, which):
    first = 2 * main + which * tail
    mains = [block[:, which * main : (which + 1) * main] for block in blocks]
    tails = [block[:, first : first + tail] for block in blocks]
    return jnp.concatenate(mains + tails, axis=1)


def relay_kernel(mine, got, out):
    rows = mine.shape[0]
    out[:rows, :] = mine[...]
    out[rows:, :] = got[rows:, :]


def text_rows_kernel(main, tail, own, far, near, out):
    rows, width = own.shape[0], out.shape[1] // 2
    parts = (own[...], near[:rows, :], far[:rows, :], near[rows:, :])
    blocks = [part.astype(jnp.float32) for part in parts]
    out[:, :width] = gathered(blocks, main, tail, 0).astype(jnp.bfloat16)
    out[:, width:] = gathered(blocks, main, tail, 1).astype(jnp.bfloat16)


def row_factors(values, tangent):
    squares = jnp.sum(values * values, axis=1, keepdims=True)
    cross = jnp.sum(values * tangent, axis=1, keepdims=True)
    inverse = 1.0 / jnp.sqrt(squares + EPS)
    return inverse, cross * inverse


def unit_rows(values, tangent, inverse, rate):
    unit = values * inverse
    return unit, (tangent - unit * rate) * inverse


def back_rows(unit, tangent, inverse, rate, grad, grad_rate):
    inner = jnp.sum(unit * grad, axis=1, keepdims=True)
    inner_rate = jnp.sum(tangent * grad + unit * grad_rate, axis=1, keepdims=True)
    scaled = rate * inverse
    return (
        grad_rate - tangent * inner - grad * scaled + unit * (inner * scaled - inner_rate)
    ) * inverse


STEP = 48


def image_rows_kernel(main, tail, count, near, far, raw_both, half_both, factors):
    rows = raw_both.shape[0] // 4
    for shard in range(2):
        held = [
            (near, far)[k % 2].at[pl.ds((k - k % 2 + shard) * rows, rows), :] for k in range(count)
        ]

        @pl.loop(0, rows // STEP)
        def _(step):
            here = pl.ds(pl.multiple_of(step * STEP, STEP), STEP)
            there = pl.ds(pl.multiple_of(shard * rows + step * STEP, STEP), STEP)
            parts = [block[here, :].astype(jnp.float32) for block in held]
            values = gathered(parts, main, tail, 0)
            rates = gathered(parts, main, tail, 1)
            inverse, rate = row_factors(values, rates)
            one, two = unit_rows(values, rates, inverse, rate)
            below = pl.ds(pl.multiple_of((2 + shard) * rows + step * STEP, STEP), STEP)
            raw_both[there, :] = values.astype(jnp.bfloat16)
            raw_both[below, :] = rates.astype(jnp.bfloat16)
            half_both[there, :] = one.astype(jnp.bfloat16)
            half_both[below, :] = two.astype(jnp.bfloat16)
            factors[0, there, :] = jnp.broadcast_to(inverse, (STEP, 128))
            factors[1, there, :] = jnp.broadcast_to(rate, (STEP, 128))


def text_rows(text):
    width = text.shape[1] // 2
    values, rates = text[:, :width].astype(jnp.float32), text[:, width:].astype(jnp.float32)
    inverse, rate = row_factors(values, rates)
    return unit_rows(values, rates, inverse, rate) + (inverse, rate)


def weight_kernel(slots, first, start, scalars, half_both, *refs):
    texts, refs = refs[: slots - first], refs[slots - first :]
    held, (text_both, weights, weights_turned) = refs[:-3], refs[-3:]
    bf16 = jnp.bfloat16
    share = texts[0].shape[0]
    count, images = slots * share, half_both.shape[0] // 2
    done = first * share
    multiplier, bias = scalars[0], scalars[1]
    if held:
        for part in range(2):
            here = slice(part * done, (part + 1) * done)
            there = slice(part * count, part * count + done)
            text_both[there, :] = held[0][here, :]
            weights_turned[:, there] = held[2][:, here]
        weights[:done, :] = held[1][...]
    units, tangents = [], []
    for text in texts:
        unit, tangent, _, _ = text_rows(text)
        units.append(unit.astype(bf16))
        tangents.append(tangent.astype(bf16))
    units, both = jnp.concatenate(units, axis=0), jnp.concatenate(units + tangents, axis=0)
    fresh = units.shape[0]
    text_both[done:count, :] = units
    text_both[count + done :, :] = both[fresh:]
    products = matmul_nt(both, half_both[:images, :])
    logits = multiplier * products[:fresh] + bias
    logit_rate = multiplier * (matmul_nt(units, half_both[images:, :]) + products[fresh:])
    probability = jax.nn.sigmoid(logits)
    text_ids = lax.broadcasted_iota(jnp.int32, logits.shape, 0) + done
    image_ids = lax.broadcasted_iota(jnp.int32, logits.shape, 1)
    positive = jnp.where((text_ids < share) & (text_ids + start[0] == image_ids), 1.0, 0.0)
    value = probability - positive
    value_rate = probability * (1.0 - probability) * logit_rate
    weights[done:, :images] = value_rate.astype(bf16)
    weights[done:, images:] = value.astype(bf16)
    weights_turned[:, done:count] = value_rate.T.astype(bf16)
    weights_turned[:, count + done :] = value.T.astype(bf16)


def text_block_kernel(slots, scalars, half_both, weights, *refs):
    texts, sums = refs[:slots], refs[slots:]
    share, images = texts[0].shape[0], half_both.shape[0] // 2
    grad = matmul(weights[:, images:], half_both[:images, :])
    grad_rate = matmul(weights[...], half_both[...])
    for slot, text in enumerate(texts):
        here = slice(slot * share, (slot + 1) * share)
        back = scalars[0] * back_rows(*text_rows(text), grad[here], grad_rate[here])
        at = slice(slot // 2 * share, (slot // 2 + 1) * share)
        sums[slot % 2][at, :] = back.astype(sums[slot % 2].dtype)


def forward_kernel(mine, got, total, sent):
    share = total.shape[0]
    total[...] = mine[:share, :] + got[:share, :].astype(jnp.float32)
    sent[...] = (mine[share:, :] + got[share:, :].astype(jnp.float32)).astype(jnp.bfloat16)


def image_block_kernel(main, tail, scalars, raw_both, factors, text_both, weights, kept, sent):
    rows, width = raw_both.shape[0] // 4, raw_both.shape[1]
    count, texts = width // (main + tail), text_both.shape[0] // 2
    grads = matmul(weights[:, texts:], text_both[:texts, :])
    grad_rates = matmul(weights[...], text_both[...])
    for shard in range(2):
        here = slice(shard * rows, (shard + 1) * rows)
        inverse, rate = factors[0, here, :1], factors[1, here, :1]
        below = slice((2 + shard) * rows, (3 + shard) * rows)
        values, rates = raw_both[here, :], raw_both[below, :]
        unit, tangent = unit_rows(
            values.astype(jnp.float32), rates.astype(jnp.float32), inverse, rate
        )
        back = back_rows(unit, tangent, inverse, rate, grads[here], grad_rates[here])
        back = scalars[0] * back
        for k in range(count):
            out = (kept, sent)[k % 2]
            to = slice(k // 2 * rows, (k // 2 + 1) * rows)
            out[to, shard * main : (shard + 1) * main] = back[:, k * main : (k + 1) * main]
            first = 2 * main + shard * tail
            taken = count * main + k * tail
            out[to, first : first + tail] = back[:, taken : taken + tail]


def text_sum_kernel(main, tail, own, *refs):
    count = own.shape[1] // (main + tail)
    got, outs = refs[:-count], refs[-count:]
    total = own[...]
    for ref in got:
        total = total + ref[...].astype(jnp.float32)
    for k, out in enumerate(outs):
        first = count * main + k * tail
        out[:, :main] = total[:, k * main : (k + 1) * main].astype(jnp.bfloat16)
        out[:, main:] = total[:, first : first + tail].astype(jnp.bfloat16)


def stack_kernel(*refs):
    rows = refs[0].shape[0]
    for k, ref in enumerate(refs[:-1]):
        refs[-1][k * rows : (k + 1) * rows, : ref.shape[1]] = ref[...]


def fold_kernel(*refs):
    value = jnp.concatenate([ref[...] for ref in refs[:-1]], axis=0)
    fold(refs[-1], 0, value, refs[-1].shape[1])


def turn_kernel(places, core, picture, caption, mine, other):
    for which, encodings in enumerate((picture, caption)):
        turned = encodings[...].T
        count = places.shape[0]
        size, rows = turned.shape[0] // count, turned.shape[1]
        fold = count // 4
        for block in range(count):
            taken = turned[block * size : (block + 1) * size, :]
            slot = places[block]
            at = pl.multiple_of(slot % fold * size, 16)
            for half in range(2):
                lanes = slice(half * rows, (half + 1) * rows)

                @pl.when(slot // fold == half)
                def _():
                    mine[pl.ds(which * fold * size + at, size), lanes] = taken

                @pl.when((slot // fold == 2 + half) & (core[0] == which))
                def _():
                    other[pl.ds(at, size), lanes] = taken


def shard_columns(value, main, tail, shard):
    at = 2 * main + shard * tail
    return jnp.concatenate(
        [value[:, shard * main : (shard + 1) * main], value[:, at : at + tail]], axis=1
    )


def image_pair_kernel(main, tail, share, near, kept, got, total, over_x, over_y, over_both):
    rows = total.shape[0]
    ours = kept[:rows, :] + got[:rows, :]
    theirs = kept[rows:, :] + got[rows:, :]
    total[...] = shard_columns(ours, main, tail, 0)
    fold(over_y, 0, shard_columns(ours, main, tail, 1), main)
    fold(over_both, 0, shard_columns(theirs, main, tail, 1), main)
    value = shard_columns(theirs, main, tail, 0)
    rounded = value.astype(jnp.bfloat16)
    fold(over_x, 0, rounded, main)
    left = value - rounded.astype(jnp.float32)
    left = jnp.where(near[0] == 0, left[: 2 * share], left[2 * share : 4 * share])
    fold(over_x, folded_rows(rows, main, tail), left, main)


def image_sum_kernel(main, tail, share, near, total, over_x, over_y, over_both, out):
    rows = total.shape[0]
    value = total[...]
    for source in (over_x, over_y, over_both):
        value = value + unfold(source, 0, rows, main, tail).astype(jnp.float32)
    left = unfold(over_x, folded_rows(rows, main, tail), 2 * share, main, tail)
    left = left.astype(jnp.float32)
    zero = jnp.zeros_like(left)
    far = near[0] == 0
    value = value + jnp.concatenate(
        [jnp.where(far, zero, left), jnp.where(far, left, zero)], axis=0
    )
    fold(out, 0, value.astype(jnp.bfloat16), main)


def head_kernel(main, tail, head, core, starts, mine, near, far, back, back_other, own, *refs):
    sent, (ordered,) = refs[:-1], refs[-1:]
    size, rows = own.shape[0], ordered.shape[1]
    share = rows // starts.shape[0]
    for which, ref in enumerate((back, back_other)):
        value = unfold(ref, 0, rows, main, tail)
        for k in range(starts.shape[0]):
            at = pl.ds(pl.multiple_of(starts[k], 16), share)
            ordered[which, at, :] = value[k * share : (k + 1) * share]
    count = (len(sent) + 1) // 2
    other = jnp.where(core[0] == head, near[...], far[...])
    for half in range(2):
        here = slice(head * count * size, (head + 1) * count * size)
        lanes = slice(half * rows, (half + 1) * rows)
        product = matmul(mine[here, lanes], ordered[0]) + matmul(other[:, lanes], ordered[1])
        for place in range(count):
            part = product[place * size : (place + 1) * size]
            slot = half * count + place
            if slot == 0:
                own[...] = part
            else:
                fold(sent[slot - 1], 0, part, main)


def final_kernel(main, tail, own, *refs):
    got, out = refs[:-1], refs[-1]
    total = own[...]
    for ref in got:
        total = total + unfold(ref, 0, own.shape[0], main, tail).astype(jnp.float32)
    out[...] = total


def final_kernel(main, tail, own, *refs):
    got, out = refs[:-1], refs[-1]
    size = own.shape[0]
    total = own[:, :main]
    for ref in got:
        total = total + ref[:size, :].astype(jnp.float32)
    out[:, :main] = total
    for rows_in, rows_out, lanes_out in folds(size, main, tail):
        total = own[rows_in, main:]
        for ref in got:
            total = total + ref[rows_out, lanes_out].astype(jnp.float32)
        out[rows_in, main:] = total


def packed(
    picture_averaged_encodings,
    caption_averaged_encodings,
    picture_mapping_matrix,
    caption_mapping_matrix,
    picture_weight_perturbation,
    caption_weight_perturbation,
    sharpness_multiplier,
    offset_additive,
):
    tensor_rank = lax.axis_index("tensor")
    data_rank = lax.axis_index("dp")
    count = lax.axis_size("tensor")
    data_count = lax.axis_size("dp")
    planes = data_count // 2
    rows, width = picture_averaged_encodings.shape
    cols = picture_mapping_matrix.shape[1]
    main = cols // 128 * 128
    tail = cols - main
    share = rows // count
    size = width // data_count
    wide = -(-2 * cols // 128) * 128
    f32, bf16 = jnp.float32, jnp.bfloat16
    ranks = jnp.arange(count, dtype=jnp.int32)
    starts = (ranks ^ tensor_rank) * share
    plain = ranks * share

    parts = 3
    blocks = call(
        functools.partial(fetch_project_kernel, share, parts),
        [((share, 2 * cols), bf16)] * 2 + [((2 * share, 2 * cols), bf16)],
        starts,
        caption_averaged_encodings,
        caption_mapping_matrix.T,
        caption_weight_perturbation.T,
        scratch=[
            pltpu.VMEM((rows, width), bf16),
            pltpu.VMEM((cols, width), bf16),
            pltpu.VMEM((cols, width), bf16),
            pltpu.SemaphoreType.DMA((3, parts)),
        ],
        fetched=True,
    )
    text_far = swapped(blocks[2], "tensor", 2)
    (relay,) = call(relay_kernel, [((2 * share, 2 * cols), bf16)], blocks[1], text_far)
    text_near = swapped(relay, "tensor", 1)

    (image,) = call(
        functools.partial(project_kernel, share),
        [((rows, 2 * cols), bf16)],
        plain,
        picture_averaged_encodings,
        picture_mapping_matrix.T,
        picture_weight_perturbation.T,
    )
    image_other = swapped(image, "dp", 1)
    image_far = swapped(image, "tensor", 2)
    image_far_other = swapped(image_other, "tensor", 2)

    (text,) = call(
        functools.partial(text_rows_kernel, main, tail),
        [((share, 2 * width), bf16)],
        blocks[0],
        text_far,
        text_near,
    )
    text_two = swapped(text, "dp", 4)
    text_one = swapped(text, "dp", 2)
    text_three = swapped(text_two, "dp", 2)
    texts = [text, text_one, text_two, text_three]

    block_ids = jnp.arange(data_count, dtype=jnp.int32)
    slots = ((block_ids ^ data_rank) >> 1) + planes * ((block_ids ^ data_rank) & 1)
    core = (tensor_rank & 1).astype(jnp.int32).reshape(1)
    mine, other = call(
        turn_kernel,
        [((planes * size, 2 * rows), bf16), ((planes // 2 * size, 2 * rows), bf16)],
        slots,
        core,
        picture_averaged_encodings,
        caption_averaged_encodings,
        after=(image_other,),
    )
    other = swapped(other, "dp", 1)
    others = (other, swapped(other, "tensor", 1))

    (near,) = call(
        stack_kernel,
        [((4 * rows, wide), bf16)],
        image,
        image_other,
        image_far,
        image_far_other,
        after=(text_one, text_two, others[0]),
    )
    far = swapped(near, "tensor", 1)
    raw_both, half_both, factors = call(
        functools.partial(image_rows_kernel, main, tail, count),
        [
            ((4 * rows, width), bf16),
            ((4 * rows, width), bf16),
            ((2, 2 * rows, 128), f32),
        ],
        near,
        far,
    )

    scalars = jnp.concatenate([sharpness_multiplier, offset_additive])
    def block_weights(slots, first, *held, after=()):
        return call(
            functools.partial(weight_kernel, slots, first),
            [
                ((2 * slots * share, width), bf16),
                ((slots * share, 4 * rows), bf16),
                ((2 * rows, 2 * slots * share), bf16),
            ],
            (tensor_rank * share).astype(jnp.int32).reshape(1),
            scalars,
            half_both,
            *texts[first:slots],
            *held,
            after=after,
        )

    held = block_weights(planes - 1, 0, after=(others[1],))
    text_both, weights, weights_turned = block_weights(planes, planes - 1, *held)
    kept, sent = call(
        functools.partial(image_block_kernel, main, tail),
        [((2 * rows, wide), f32)] * 2,
        scalars,
        raw_both,
        factors,
        text_both,
        weights_turned,
    )
    outs = call(
        functools.partial(text_block_kernel, planes),
        [((2 * share, width), f32), ((2 * share, width), bf16)],
        scalars,
        half_both,
        weights,
        *texts,
        after=(kept,),
    )

    near = (tensor_rank // 2).astype(jnp.int32).reshape(1)
    tall = folded_rows(rows, main, tail)
    more = folded_rows(2 * share, main, tail)
    total, to_x, to_y, to_both = call(
        functools.partial(image_pair_kernel, main, tail, share),
        [((rows, cols), f32), ((tall + more, main), bf16)] + [((tall, main), bf16)] * 2,
        near,
        kept,
        swapped(sent, "tensor", 1),
        after=(outs[1],),
    )
    flat = [(source, source ^ (count + 2)) for source in range(data_count * count)]
    (image_back,) = call(
        functools.partial(image_sum_kernel, main, tail, share),
        [((tall, main), bf16)],
        near,
        total,
        swapped(to_x, "tensor", 2),
        swapped(to_y, "dp", 1),
        lax.ppermute(to_both, ("dp", "tensor"), flat),
    )
    image_back_other = swapped(image_back, "dp", 1)

    def head(which, order, back, back_other):
        return call(
            functools.partial(head_kernel, main, tail, which),
            [((size, cols), f32)]
            + [((folded_rows(size, main, tail), main), bf16)] * (planes - 1),
            core,
            order,
            mine,
            *others,
            back,
            back_other,
            scratch=[pltpu.VMEM((2, rows, cols), bf16)],
        )

    def summed(products):
        got = [swapped(products[k], "dp", 2 * k) for k in range(1, planes)]
        return call(
            functools.partial(final_kernel, main, tail), [((size, cols), f32)], products[0], *got
        )[0]

    image_products = head(0, plain, image_back, image_back_other)

    text_total, text_sent = call(
        forward_kernel,
        [((share, width), f32), ((share, width), bf16)],
        outs[0],
        swapped(outs[1], "dp", 2),
    )
    blocks = call(
        functools.partial(text_sum_kernel, main, tail),
        [((share, cols), bf16)] * count,
        text_total,
        swapped(text_sent, "dp", 4),
        after=(image_back,),
    )
    got = [blocks[0]] + [swapped(blocks[k], "tensor", k) for k in range(1, count)]
    (text_back,) = call(fold_kernel, [((tall, main), bf16)], *got, after=(image_products[0],))
    text_back_other = swapped(text_back, "dp", 1)

    text_products = head(1, starts, text_back, text_back_other)
    return summed(image_products), summed(text_products)


def fits(mesh):
    return mesh.shape["tensor"] == 4 and mesh.shape["dp"] == 8


def solution(mesh):
    in_specs = (
        P("dp", None),
        P("dp", None),
        P(None, "tensor"),
        P(None, "tensor"),
        P(None, "tensor"),
        P(None, "tensor"),
        P(),
        P(),
    )
    out_specs = (P("dp", "tensor"), P("dp", "tensor"))
    local = packed if fits(mesh) else general
    return jax.shard_map(local, mesh=mesh, in_specs=in_specs, out_specs=out_specs, check_vma=False)
```

```python
import functools

import jax
import jax.numpy as jnp
from jax import lax
from jax.experimental import pallas as pl
from jax.experimental.pallas import tpu as pltpu
from jax.sharding import PartitionSpec as P

EPS = 1e-06


def swapped(value, axis, mask):
    count = lax.axis_size(axis)
    return lax.ppermute(value, axis, [(source, source ^ mask) for source in range(count)])


def matmul(left, right):
    return jnp.dot(left, right, preferred_element_type=jnp.float32)


def matmul_nt(left, right):
    return lax.dot_general(
        left, right, (((1,), (1,)), ((), ())), preferred_element_type=jnp.float32
    )


def matmul_tn(left, right):
    return lax.dot_general(
        left, right, (((0,), (0,)), ((), ())), preferred_element_type=jnp.float32
    )


def unit_parts(raw, raw_rate):
    values = raw.astype(jnp.float32)
    tangent = raw_rate.astype(jnp.float32)
    radius = jnp.sqrt(jnp.sum(values * values, axis=1, keepdims=True) + EPS)
    unit = values / radius
    rate = jnp.sum(unit * tangent, axis=1, keepdims=True)
    unit_tangent = (tangent - unit * rate) / radius
    return (unit, unit_tangent, radius, rate)


def unit_backward(unit, unit_tangent, radius, rate, grad, grad_rate):
    inner = jnp.sum(unit * grad, axis=1, keepdims=True)
    inner_rate = jnp.sum(unit_tangent * grad + unit * grad_rate, axis=1, keepdims=True)
    first = (grad - unit * inner) / radius
    return (grad_rate - unit_tangent * inner - unit * inner_rate - first * rate) / radius


def general(
    picture_averaged_encodings,
    caption_averaged_encodings,
    picture_mapping_matrix,
    caption_mapping_matrix,
    picture_weight_perturbation,
    caption_weight_perturbation,
    sharpness_multiplier,
    offset_additive,
):
    similarity_multiplier = sharpness_multiplier[0]
    logit_bias = offset_additive[0]
    tensor_rank = lax.axis_index("tensor")
    data_rank = lax.axis_index("dp")
    tensor_count = lax.axis_size("tensor")
    data_count = lax.axis_size("dp")
    planes = data_count // 2
    rows, width = picture_averaged_encodings.shape
    cols = picture_mapping_matrix.shape[1]
    share = rows // tensor_count
    out_rows = width // data_count
    half = jnp.bfloat16

    text = jnp.stack(
        [
            matmul(caption_averaged_encodings, caption_mapping_matrix).astype(half),
            matmul(caption_averaged_encodings, caption_weight_perturbation).astype(half),
        ]
    )
    image = jnp.stack(
        [
            matmul(picture_averaged_encodings, picture_mapping_matrix).astype(half),
            matmul(picture_averaged_encodings, picture_weight_perturbation).astype(half),
        ]
    )

    def share_of(value, axis, mask):
        start = (tensor_rank ^ mask) * share
        return lax.dynamic_slice_in_dim(value, start, share, axis)

    parts = [share_of(text, 1, 0)]
    for mask in range(1, tensor_count):
        parts.append(swapped(share_of(text, 1, mask), "tensor", mask))
    text = jnp.concatenate(parts, axis=2)
    slots = [text] + [swapped(text, "dp", 2 * mask) for mask in range(1, planes)]

    image = jnp.concatenate([image, swapped(image, "dp", 1)], axis=1)
    blocks = [image]
    mask = tensor_count // 2
    image_blocks = {0: image}
    while mask >= 1:
        held = sorted(image_blocks)
        sent = jnp.concatenate([image_blocks[k] for k in held], axis=2)
        got = swapped(sent, "tensor", mask)
        for place, k in enumerate(held):
            image_blocks[k ^ mask] = got[:, :, place * cols : (place + 1) * cols]
        mask //= 2
    image = jnp.concatenate([image_blocks[k] for k in range(tensor_count)], axis=2)
    text = jnp.concatenate(slots, axis=1)

    def out_columns(value, rank):
        taken = [
            lax.dynamic_slice_in_dim(value, (rank ^ (2 * mask)) * out_rows, out_rows, 1)
            for mask in range(planes)
        ]
        return jnp.concatenate(taken, axis=1)

    def plane_encodings(value):
        other = swapped(out_columns(value, data_rank ^ 1), "dp", 1)
        return jnp.concatenate([out_columns(value, data_rank), other], axis=0)

    picture_plane = plane_encodings(picture_averaged_encodings)
    ordered = jnp.concatenate(
        [share_of(caption_averaged_encodings, 0, mask) for mask in range(tensor_count)], axis=0
    )
    caption_plane = plane_encodings(ordered)

    image_unit, image_tangent, image_radius, image_rate = unit_parts(image[0], image[1])
    text_unit, text_tangent, text_radius, text_rate = unit_parts(text[0], text[1])
    image_half = image_unit.astype(half)
    image_tangent_half = image_tangent.astype(half)
    text_half = text_unit.astype(half)
    text_tangent_half = text_tangent.astype(half)

    logits = similarity_multiplier * matmul_nt(text_half, image_half) + logit_bias
    logit_rate = similarity_multiplier * (
        matmul_nt(text_half, image_tangent_half) + matmul_nt(text_tangent_half, image_half)
    )
    probability = jax.nn.sigmoid(logits)
    text_ids = lax.broadcasted_iota(jnp.int32, (logits.shape[0], 1), 0)
    image_ids = lax.broadcasted_iota(jnp.int32, (1, logits.shape[1]), 1)
    positive = ((text_ids < share) & (text_ids + tensor_rank * share == image_ids)).astype(
        jnp.float32
    )
    weight = (probability - positive).astype(half)
    weight_rate = (probability * (1.0 - probability) * logit_rate).astype(half)
    text_grad = similarity_multiplier * matmul(weight, image_half)
    text_grad_rate = similarity_multiplier * (
        matmul(weight_rate, image_half) + matmul(weight, image_tangent_half)
    )
    image_grad = similarity_multiplier * matmul_tn(weight, text_half)
    image_grad_rate = similarity_multiplier * (
        matmul_tn(weight_rate, text_half) + matmul_tn(weight, text_tangent_half)
    )

    text_back = unit_backward(
        text_unit, text_tangent, text_radius, text_rate, text_grad, text_grad_rate
    )
    image_back = unit_backward(
        image_unit, image_tangent, image_radius, image_rate, image_grad, image_grad_rate
    )

    total = text_back[:share]
    for mask in range(1, planes):
        sent = text_back[mask * share : (mask + 1) * share].astype(half)
        total = total + swapped(sent, "dp", 2 * mask).astype(jnp.float32)
    text_back = total.astype(half)
    parts = [text_back[:, :cols]]
    for mask in range(1, tensor_count):
        sent = text_back[:, mask * cols : (mask + 1) * cols]
        parts.append(swapped(sent, "tensor", mask))
    text_back = jnp.concatenate(parts, axis=0)
    text_back = jnp.concatenate([text_back, swapped(text_back, "dp", 1)], axis=0)

    image_blocks = {k: image_back[:, k * cols : (k + 1) * cols] for k in range(tensor_count)}
    mask = 1
    while mask < tensor_count:
        kept = [k for k in sorted(image_blocks) if not k & mask]
        sent = jnp.concatenate([image_blocks[k ^ mask] for k in kept], axis=1)
        got = swapped(sent, "tensor", mask).astype(jnp.float32)
        image_blocks = {
            k: image_blocks[k] + got[:, place * cols : (place + 1) * cols]
            for place, k in enumerate(kept)
        }
        mask *= 2
    image_back = image_blocks[0]
    got = swapped(image_back, "dp", 1)
    image_back = (
        image_back + jnp.concatenate([got[rows:], got[:rows]], axis=0)
    ).astype(half)

    def head(encodings, back):
        product = matmul_tn(encodings, back)
        total = product[:out_rows]
        for mask in range(1, planes):
            sent = product[mask * out_rows : (mask + 1) * out_rows].astype(half)
            total = total + swapped(sent, "dp", 2 * mask).astype(jnp.float32)
        return total

    return (head(picture_plane, image_back), head(caption_plane, text_back))


def call(kernel, outs, *args, after=(), scratch=(), fetched=False):
    count = len(args)

    def body(*refs):
        kernel(*refs[:count], *refs[count + len(after) :])

    def place(value):
        if value.ndim == 1:
            return pl.BlockSpec(memory_space=pltpu.SMEM)
        return pl.BlockSpec(memory_space=pltpu.HBM if fetched else pltpu.VMEM)

    return pl.pallas_call(
        body,
        out_shape=[jax.ShapeDtypeStruct(shape, dtype) for shape, dtype in outs],
        in_specs=[place(value) for value in args]
        + [pl.BlockSpec(memory_space=pl.ANY) for _ in after],
        out_specs=[pl.BlockSpec(memory_space=pltpu.VMEM) for _ in outs],
        scratch_shapes=list(scratch),
        compiler_params=pltpu.CompilerParams(
            vmem_limit_bytes=(62 if fetched else 14) * 1024 * 1024
        ),
    )(*args, *after)


def folds(rows, main, tail):
    across = main // tail
    for k in range(rows // 16):
        here = slice(k * 16, (k + 1) * 16)
        at = rows + k // across * 16
        first = k % across * tail
        yield here, slice(at, at + 16), slice(first, first + tail)


def folded_rows(rows, main, tail):
    return rows + -(-rows // 16 // (main // tail)) * 16


def fold(out, first, value, main):
    rows, cols = value.shape
    out[first : first + rows, :] = value[:, :main].astype(out.dtype)
    for here, there, lanes in folds(rows, main, cols - main):
        there = slice(first + there.start, first + there.stop)
        out[there, lanes] = value[here, main:].astype(out.dtype)


def unfold(ref, first, rows, main, tail):
    tails = [
        ref[first + there.start : first + there.stop, lanes]
        for _, there, lanes in folds(rows, main, tail)
    ]
    return jnp.concatenate([ref[first : first + rows, :], jnp.concatenate(tails, axis=0)], axis=1)


def fetch_project_kernel(share, parts, starts, encodings, weight, direction, *refs):
    outs, held, done = refs[:-4], refs[-4:-1], refs[-1]
    copies = []
    for which, (source, target) in enumerate(zip((encodings, weight, direction), held)):
        rows = source.shape[0] // parts
        for part in range(parts):
            here = pl.ds(part * rows, rows)
            copies.append(
                pltpu.make_async_copy(source.at[here, :], target.at[here, :], done.at[which, part])
            )
    for copy in copies:
        copy.start()
    for copy in copies:
        copy.wait()
    project_kernel(share, starts, *held, *outs)


def project_kernel(share, starts, encodings, weight, direction, *outs):
    main = weight.shape[0] // 128 * 128
    left = jnp.concatenate(
        [
            encodings[pl.ds(pl.multiple_of(starts[k], 16), share), :]
            for k in range(starts.shape[0])
        ],
        axis=0,
    )
    tails = jnp.concatenate([weight[main:, :], direction[main:, :]], axis=0)
    for right, first in ((weight[:main, :], 0), (direction[:main, :], main), (tails, 2 * main)):
        product = matmul_nt(left, right).astype(jnp.bfloat16)
        place = 0
        for out in outs:
            rows = out.shape[0]
            out[:, first : first + right.shape[0]] = product[place : place + rows]
            place += rows


def gathered(blocks, main, tail, which):
    first = 2 * main + which * tail
    mains = [block[:, which * main : (which + 1) * main] for block in blocks]
    tails = [block[:, first : first + tail] for block in blocks]
    return jnp.concatenate(mains + tails, axis=1)


def relay_kernel(mine, got, out):
    rows = mine.shape[0]
    out[:rows, :] = mine[...]
    out[rows:, :] = got[rows:, :]


def text_rows_kernel(main, tail, own, far, near, out):
    rows, width = own.shape[0], out.shape[1] // 2
    parts = (own[...], near[:rows, :], far[:rows, :], near[rows:, :])
    blocks = [part.astype(jnp.float32) for part in parts]
    out[:, :width] = gathered(blocks, main, tail, 0).astype(jnp.bfloat16)
    out[:, width:] = gathered(blocks, main, tail, 1).astype(jnp.bfloat16)


def row_factors(values, tangent):
    squares = jnp.sum(values * values, axis=1, keepdims=True)
    cross = jnp.sum(values * tangent, axis=1, keepdims=True)
    inverse = 1.0 / jnp.sqrt(squares + EPS)
    return inverse, cross * inverse


def unit_rows(values, tangent, inverse, rate):
    unit = values * inverse
    return unit, (tangent - unit * rate) * inverse


def back_rows(unit, tangent, inverse, rate, grad, grad_rate):
    inner = jnp.sum(unit * grad, axis=1, keepdims=True)
    inner_rate = jnp.sum(tangent * grad + unit * grad_rate, axis=1, keepdims=True)
    scaled = rate * inverse
    return (
        grad_rate - tangent * inner - grad * scaled + unit * (inner * scaled - inner_rate)
    ) * inverse


STEP = 48


def image_rows_kernel(main, tail, count, near, far, raw_both, half_both, factors):
    rows = raw_both.shape[0] // 4
    for shard in range(2):
        held = [
            (near, far)[k % 2].at[pl.ds((k - k % 2 + shard) * rows, rows), :] for k in range(count)
        ]

        @pl.loop(0, rows // STEP)
        def _(step):
            here = pl.ds(pl.multiple_of(step * STEP, STEP), STEP)
            there = pl.ds(pl.multiple_of(shard * rows + step * STEP, STEP), STEP)
            parts = [block[here, :].astype(jnp.float32) for block in held]
            values = gathered(parts, main, tail, 0)
            rates = gathered(parts, main, tail, 1)
            inverse, rate = row_factors(values, rates)
            one, two = unit_rows(values, rates, inverse, rate)
            below = pl.ds(pl.multiple_of((2 + shard) * rows + step * STEP, STEP), STEP)
            raw_both[there, :] = values.astype(jnp.bfloat16)
            raw_both[below, :] = rates.astype(jnp.bfloat16)
            half_both[there, :] = one.astype(jnp.bfloat16)
            half_both[below, :] = two.astype(jnp.bfloat16)
            factors[0, there, :] = jnp.broadcast_to(inverse, (STEP, 128))
            factors[1, there, :] = jnp.broadcast_to(rate, (STEP, 128))


def text_rows(text):
    width = text.shape[1] // 2
    values, rates = text[:, :width].astype(jnp.float32), text[:, width:].astype(jnp.float32)
    inverse, rate = row_factors(values, rates)
    return unit_rows(values, rates, inverse, rate) + (inverse, rate)


def weight_kernel(slots, first, start, scalars, half_both, *refs):
    texts, refs = refs[: slots - first], refs[slots - first :]
    held, (text_both, weights, weights_turned) = refs[:-3], refs[-3:]
    bf16 = jnp.bfloat16
    share = texts[0].shape[0]
    count, images = slots * share, half_both.shape[0] // 2
    done = first * share
    multiplier, bias = scalars[0], scalars[1]
    if held:
        for part in range(2):
            here = slice(part * done, (part + 1) * done)
            there = slice(part * count, part * count + done)
            text_both[there, :] = held[0][here, :]
            weights_turned[:, there] = held[2][:, here]
        weights[:done, :] = held[1][...]
    units, tangents = [], []
    for text in texts:
        unit, tangent, _, _ = text_rows(text)
        units.append(unit.astype(bf16))
        tangents.append(tangent.astype(bf16))
    units, both = jnp.concatenate(units, axis=0), jnp.concatenate(units + tangents, axis=0)
    fresh = units.shape[0]
    text_both[done:count, :] = units
    text_both[count + done :, :] = both[fresh:]
    products = matmul_nt(both, half_both[:images, :])
    logits = multiplier * products[:fresh] + bias
    logit_rate = multiplier * (matmul_nt(units, half_both[images:, :]) + products[fresh:])
    probability = jax.nn.sigmoid(logits)
    text_ids = lax.broadcasted_iota(jnp.int32, logits.shape, 0) + done
    image_ids = lax.broadcasted_iota(jnp.int32, logits.shape, 1)
    positive = jnp.where((text_ids < share) & (text_ids + start[0] == image_ids), 1.0, 0.0)
    value = probability - positive
    value_rate = probability * (1.0 - probability) * logit_rate
    weights[done:, :images] = value_rate.astype(bf16)
    weights[done:, images:] = value.astype(bf16)
    weights_turned[:, done:count] = value_rate.T.astype(bf16)
    weights_turned[:, count + done :] = value.T.astype(bf16)


def text_block_kernel(slots, scalars, half_both, weights, *refs):
    texts, sums = refs[:slots], refs[slots:]
    share, images = texts[0].shape[0], half_both.shape[0] // 2
    grad = matmul(weights[:, images:], half_both[:images, :])
    grad_rate = matmul(weights[...], half_both[...])
    for slot, text in enumerate(texts):
        here = slice(slot * share, (slot + 1) * share)
        back = scalars[0] * back_rows(*text_rows(text), grad[here], grad_rate[here])
        at = slice(slot // 2 * share, (slot // 2 + 1) * share)
        sums[slot % 2][at, :] = back.astype(sums[slot % 2].dtype)


def forward_kernel(mine, got, total, sent):
    share = total.shape[0]
    total[...] = mine[:share, :] + got[:share, :].astype(jnp.float32)
    sent[...] = (mine[share:, :] + got[share:, :].astype(jnp.float32)).astype(jnp.bfloat16)


def image_block_kernel(main, tail, scalars, raw_both, factors, text_both, weights, kept, sent):
    rows, width = raw_both.shape[0] // 4, raw_both.shape[1]
    count, texts = width // (main + tail), text_both.shape[0] // 2
    grads = matmul(weights[:, texts:], text_both[:texts, :])
    grad_rates = matmul(weights[...], text_both[...])
    for shard in range(2):
        here = slice(shard * rows, (shard + 1) * rows)
        inverse, rate = factors[0, here, :1], factors[1, here, :1]
        below = slice((2 + shard) * rows, (3 + shard) * rows)
        values, rates = raw_both[here, :], raw_both[below, :]
        unit, tangent = unit_rows(
            values.astype(jnp.float32), rates.astype(jnp.float32), inverse, rate
        )
        back = back_rows(unit, tangent, inverse, rate, grads[here], grad_rates[here])
        back = scalars[0] * back
        for k in range(count):
            out = (kept, sent)[k % 2]
            to = slice(k // 2 * rows, (k // 2 + 1) * rows)
            out[to, shard * main : (shard + 1) * main] = back[:, k * main : (k + 1) * main]
            first = 2 * main + shard * tail
            taken = count * main + k * tail
            out[to, first : first + tail] = back[:, taken : taken + tail]


def text_sum_kernel(main, tail, own, *refs):
    count = own.shape[1] // (main + tail)
    got, outs = refs[:-count], refs[-count:]
    total = own[...]
    for ref in got:
        total = total + ref[...].astype(jnp.float32)
    for k, out in enumerate(outs):
        first = count * main + k * tail
        out[:, :main] = total[:, k * main : (k + 1) * main].astype(jnp.bfloat16)
        out[:, main:] = total[:, first : first + tail].astype(jnp.bfloat16)


def stack_kernel(*refs):
    rows = refs[0].shape[0]
    for k, ref in enumerate(refs[:-1]):
        refs[-1][k * rows : (k + 1) * rows, : ref.shape[1]] = ref[...]


def fold_kernel(*refs):
    value = jnp.concatenate([ref[...] for ref in refs[:-1]], axis=0)
    fold(refs[-1], 0, value, refs[-1].shape[1])


def placed(turned, places, side, out, below):
    count = places.shape[0]
    size, rows = turned.shape[0] // count, turned.shape[1]
    fold = count // 4
    for block in range(count):
        taken = turned[block * size : (block + 1) * size, :]
        slot = places[block]
        at = pl.multiple_of(slot % fold * size, 16)
        for half in range(2):

            @pl.when(slot // fold == 2 * side + half)
            def _():
                out[pl.ds(below + at, size), half * rows : (half + 1) * rows] = taken


def turn_other_kernel(places, core, picture, caption, out):
    encodings = jnp.where(core[0] == 0, picture[...], caption[...])
    placed(encodings.T, places, 1, out, 0)


def turn_kernel(places, picture, caption, out):
    for which, encodings in enumerate((picture, caption)):
        placed(encodings[...].T, places, 0, out, which * (out.shape[0] // 2))


def shard_columns(value, main, tail, shard):
    at = 2 * main + shard * tail
    return jnp.concatenate(
        [value[:, shard * main : (shard + 1) * main], value[:, at : at + tail]], axis=1
    )


def image_pair_kernel(main, tail, share, near, kept, got, total, over_x, over_y, over_both):
    rows = total.shape[0]
    ours = kept[:rows, :] + got[:rows, :]
    theirs = kept[rows:, :] + got[rows:, :]
    total[...] = shard_columns(ours, main, tail, 0)
    fold(over_y, 0, shard_columns(ours, main, tail, 1), main)
    fold(over_both, 0, shard_columns(theirs, main, tail, 1), main)
    value = shard_columns(theirs, main, tail, 0)
    rounded = value.astype(jnp.bfloat16)
    fold(over_x, 0, rounded, main)
    left = value - rounded.astype(jnp.float32)
    left = jnp.where(near[0] == 0, left[: 2 * share], left[2 * share : 4 * share])
    fold(over_x, folded_rows(rows, main, tail), left, main)


def image_sum_kernel(main, tail, share, near, total, over_x, over_y, over_both, out):
    rows = total.shape[0]
    value = total[...]
    for source in (over_x, over_y, over_both):
        value = value + unfold(source, 0, rows, main, tail).astype(jnp.float32)
    left = unfold(over_x, folded_rows(rows, main, tail), 2 * share, main, tail)
    left = left.astype(jnp.float32)
    zero = jnp.zeros_like(left)
    far = near[0] == 0
    value = value + jnp.concatenate(
        [jnp.where(far, zero, left), jnp.where(far, left, zero)], axis=0
    )
    fold(out, 0, value.astype(jnp.bfloat16), main)


def head_kernel(main, tail, head, core, starts, mine, near, far, back, back_other, own, *refs):
    sent, (ordered,) = refs[:-1], refs[-1:]
    size, rows = own.shape[0], ordered.shape[1]
    share = rows // starts.shape[0]
    for which, ref in enumerate((back, back_other)):
        value = unfold(ref, 0, rows, main, tail)
        for k in range(starts.shape[0]):
            at = pl.ds(pl.multiple_of(starts[k], 16), share)
            ordered[which, at, :] = value[k * share : (k + 1) * share]
    count = (len(sent) + 1) // 2
    other = jnp.where(core[0] == head, near[...], far[...])
    for half in range(2):
        here = slice(head * count * size, (head + 1) * count * size)
        lanes = slice(half * rows, (half + 1) * rows)
        product = matmul(mine[here, lanes], ordered[0]) + matmul(other[:, lanes], ordered[1])
        for place in range(count):
            part = product[place * size : (place + 1) * size]
            slot = half * count + place
            if slot == 0:
                own[...] = part
            else:
                fold(sent[slot - 1], 0, part, main)


def final_kernel(main, tail, own, *refs):
    got, out = refs[:-1], refs[-1]
    total = own[...]
    for ref in got:
        total = total + unfold(ref, 0, own.shape[0], main, tail).astype(jnp.float32)
    out[...] = total


def final_kernel(main, tail, own, *refs):
    got, out = refs[:-1], refs[-1]
    size = own.shape[0]
    total = own[:, :main]
    for ref in got:
        total = total + ref[:size, :].astype(jnp.float32)
    out[:, :main] = total
    for rows_in, rows_out, lanes_out in folds(size, main, tail):
        total = own[rows_in, main:]
        for ref in got:
            total = total + ref[rows_out, lanes_out].astype(jnp.float32)
        out[rows_in, main:] = total


def packed(
    picture_averaged_encodings,
    caption_averaged_encodings,
    picture_mapping_matrix,
    caption_mapping_matrix,
    picture_weight_perturbation,
    caption_weight_perturbation,
    sharpness_multiplier,
    offset_additive,
):
    tensor_rank = lax.axis_index("tensor")
    data_rank = lax.axis_index("dp")
    count = lax.axis_size("tensor")
    data_count = lax.axis_size("dp")
    planes = data_count // 2
    rows, width = picture_averaged_encodings.shape
    cols = picture_mapping_matrix.shape[1]
    main = cols // 128 * 128
    tail = cols - main
    share = rows // count
    size = width // data_count
    wide = -(-2 * cols // 128) * 128
    f32, bf16 = jnp.float32, jnp.bfloat16
    ranks = jnp.arange(count, dtype=jnp.int32)
    starts = (ranks ^ tensor_rank) * share
    plain = ranks * share

    parts = 3
    blocks = call(
        functools.partial(fetch_project_kernel, share, parts),
        [((share, 2 * cols), bf16)] * 2 + [((2 * share, 2 * cols), bf16)],
        starts,
        caption_averaged_encodings,
        caption_mapping_matrix.T,
        caption_weight_perturbation.T,
        scratch=[
            pltpu.VMEM((rows, width), bf16),
            pltpu.VMEM((cols, width), bf16),
            pltpu.VMEM((cols, width), bf16),
            pltpu.SemaphoreType.DMA((3, parts)),
        ],
        fetched=True,
    )
    text_far = swapped(blocks[2], "tensor", 2)
    (relay,) = call(relay_kernel, [((2 * share, 2 * cols), bf16)], blocks[1], text_far)
    text_near = swapped(relay, "tensor", 1)

    (image,) = call(
        functools.partial(project_kernel, share),
        [((rows, 2 * cols), bf16)],
        plain,
        picture_averaged_encodings,
        picture_mapping_matrix.T,
        picture_weight_perturbation.T,
    )
    image_other = swapped(image, "dp", 1)
    image_far = swapped(image, "tensor", 2)
    image_far_other = swapped(image_other, "tensor", 2)

    (text,) = call(
        functools.partial(text_rows_kernel, main, tail),
        [((share, 2 * width), bf16)],
        blocks[0],
        text_far,
        text_near,
    )
    text_two = swapped(text, "dp", 4)
    text_one = swapped(text, "dp", 2)
    text_three = swapped(text_two, "dp", 2)
    texts = [text, text_one, text_two, text_three]

    block_ids = jnp.arange(data_count, dtype=jnp.int32)
    slots = ((block_ids ^ data_rank) >> 1) + planes * ((block_ids ^ data_rank) & 1)
    core = (tensor_rank & 1).astype(jnp.int32).reshape(1)
    (other,) = call(
        turn_other_kernel,
        [((planes // 2 * size, 2 * rows), bf16)],
        slots,
        core,
        picture_averaged_encodings,
        caption_averaged_encodings,
        after=(image_other,),
    )
    other = swapped(other, "dp", 1)
    others = (other, swapped(other, "tensor", 1))

    (near,) = call(
        stack_kernel,
        [((4 * rows, wide), bf16)],
        image,
        image_other,
        image_far,
        image_far_other,
        after=(text_one, text_two, others[0]),
    )
    far = swapped(near, "tensor", 1)
    raw_both, half_both, factors = call(
        functools.partial(image_rows_kernel, main, tail, count),
        [
            ((4 * rows, width), bf16),
            ((4 * rows, width), bf16),
            ((2, 2 * rows, 128), f32),
        ],
        near,
        far,
    )

    scalars = jnp.concatenate([sharpness_multiplier, offset_additive])
    def block_weights(slots, first, *held, after=()):
        return call(
            functools.partial(weight_kernel, slots, first),
            [
                ((2 * slots * share, width), bf16),
                ((slots * share, 4 * rows), bf16),
                ((2 * rows, 2 * slots * share), bf16),
            ],
            (tensor_rank * share).astype(jnp.int32).reshape(1),
            scalars,
            half_both,
            *texts[first:slots],
            *held,
            after=after,
        )

    held = block_weights(planes - 1, 0, after=(others[1],))
    text_both, weights, weights_turned = block_weights(planes, planes - 1, *held)
    kept, sent = call(
        functools.partial(image_block_kernel, main, tail),
        [((2 * rows, wide), f32)] * 2,
        scalars,
        raw_both,
        factors,
        text_both,
        weights_turned,
    )
    outs = call(
        functools.partial(text_block_kernel, planes),
        [((2 * share, width), f32), ((2 * share, width), bf16)],
        scalars,
        half_both,
        weights,
        *texts,
        after=(kept,),
    )

    near = (tensor_rank // 2).astype(jnp.int32).reshape(1)
    tall = folded_rows(rows, main, tail)
    more = folded_rows(2 * share, main, tail)
    total, to_x, to_y, to_both = call(
        functools.partial(image_pair_kernel, main, tail, share),
        [((rows, cols), f32), ((tall + more, main), bf16)] + [((tall, main), bf16)] * 2,
        near,
        kept,
        swapped(sent, "tensor", 1),
        after=(outs[1],),
    )
    flat = [(source, source ^ (count + 2)) for source in range(data_count * count)]
    (image_back,) = call(
        functools.partial(image_sum_kernel, main, tail, share),
        [((tall, main), bf16)],
        near,
        total,
        swapped(to_x, "tensor", 2),
        swapped(to_y, "dp", 1),
        lax.ppermute(to_both, ("dp", "tensor"), flat),
    )
    image_back_other = swapped(image_back, "dp", 1)

    (mine,) = call(
        turn_kernel,
        [((planes * size, 2 * rows), bf16)],
        slots,
        picture_averaged_encodings,
        caption_averaged_encodings,
        after=(image_back,),
    )

    def head(which, order, back, back_other):
        return call(
            functools.partial(head_kernel, main, tail, which),
            [((size, cols), f32)]
            + [((folded_rows(size, main, tail), main), bf16)] * (planes - 1),
            core,
            order,
            mine,
            *others,
            back,
            back_other,
            scratch=[pltpu.VMEM((2, rows, cols), bf16)],
        )

    def summed(products):
        got = [swapped(products[k], "dp", 2 * k) for k in range(1, planes)]
        return call(
            functools.partial(final_kernel, main, tail), [((size, cols), f32)], products[0], *got
        )[0]

    image_products = head(0, plain, image_back, image_back_other)

    text_total, text_sent = call(
        forward_kernel,
        [((share, width), f32), ((share, width), bf16)],
        outs[0],
        swapped(outs[1], "dp", 2),
    )
    blocks = call(
        functools.partial(text_sum_kernel, main, tail),
        [((share, cols), bf16)] * count,
        text_total,
        swapped(text_sent, "dp", 4),
        after=(image_back, mine),
    )
    got = [blocks[0]] + [swapped(blocks[k], "tensor", k) for k in range(1, count)]
    (text_back,) = call(fold_kernel, [((tall, main), bf16)], *got, after=(image_products[0],))
    text_back_other = swapped(text_back, "dp", 1)

    text_products = head(1, starts, text_back, text_back_other)
    return summed(image_products), summed(text_products)


def fits(mesh):
    return mesh.shape["tensor"] == 4 and mesh.shape["dp"] == 8


def solution(mesh):
    in_specs = (
        P("dp", None),
        P("dp", None),
        P(None, "tensor"),
        P(None, "tensor"),
        P(None, "tensor"),
        P(None, "tensor"),
        P(),
        P(),
    )
    out_specs = (P("dp", "tensor"), P("dp", "tensor"))
    local = packed if fits(mesh) else general
    return jax.shard_map(local, mesh=mesh, in_specs=in_specs, out_specs=out_specs, check_vma=False)
```

```python
import functools

import jax
import jax.numpy as jnp
from jax import lax
from jax.experimental import pallas as pl
from jax.experimental.pallas import tpu as pltpu
from jax.sharding import PartitionSpec as P

EPS = 1e-06


def swapped(value, axis, mask):
    count = lax.axis_size(axis)
    return lax.ppermute(value, axis, [(source, source ^ mask) for source in range(count)])


def matmul(left, right):
    return jnp.dot(left, right, preferred_element_type=jnp.float32)


def matmul_nt(left, right):
    return lax.dot_general(
        left, right, (((1,), (1,)), ((), ())), preferred_element_type=jnp.float32
    )


def matmul_tn(left, right):
    return lax.dot_general(
        left, right, (((0,), (0,)), ((), ())), preferred_element_type=jnp.float32
    )


def unit_parts(raw, raw_rate):
    values = raw.astype(jnp.float32)
    tangent = raw_rate.astype(jnp.float32)
    radius = jnp.sqrt(jnp.sum(values * values, axis=1, keepdims=True) + EPS)
    unit = values / radius
    rate = jnp.sum(unit * tangent, axis=1, keepdims=True)
    unit_tangent = (tangent - unit * rate) / radius
    return (unit, unit_tangent, radius, rate)


def unit_backward(unit, unit_tangent, radius, rate, grad, grad_rate):
    inner = jnp.sum(unit * grad, axis=1, keepdims=True)
    inner_rate = jnp.sum(unit_tangent * grad + unit * grad_rate, axis=1, keepdims=True)
    first = (grad - unit * inner) / radius
    return (grad_rate - unit_tangent * inner - unit * inner_rate - first * rate) / radius


def general(
    picture_averaged_encodings,
    caption_averaged_encodings,
    picture_mapping_matrix,
    caption_mapping_matrix,
    picture_weight_perturbation,
    caption_weight_perturbation,
    sharpness_multiplier,
    offset_additive,
):
    similarity_multiplier = sharpness_multiplier[0]
    logit_bias = offset_additive[0]
    tensor_rank = lax.axis_index("tensor")
    data_rank = lax.axis_index("dp")
    tensor_count = lax.axis_size("tensor")
    data_count = lax.axis_size("dp")
    planes = data_count // 2
    rows, width = picture_averaged_encodings.shape
    cols = picture_mapping_matrix.shape[1]
    share = rows // tensor_count
    out_rows = width // data_count
    half = jnp.bfloat16

    text = jnp.stack(
        [
            matmul(caption_averaged_encodings, caption_mapping_matrix).astype(half),
            matmul(caption_averaged_encodings, caption_weight_perturbation).astype(half),
        ]
    )
    image = jnp.stack(
        [
            matmul(picture_averaged_encodings, picture_mapping_matrix).astype(half),
            matmul(picture_averaged_encodings, picture_weight_perturbation).astype(half),
        ]
    )

    def share_of(value, axis, mask):
        start = (tensor_rank ^ mask) * share
        return lax.dynamic_slice_in_dim(value, start, share, axis)

    parts = [share_of(text, 1, 0)]
    for mask in range(1, tensor_count):
        parts.append(swapped(share_of(text, 1, mask), "tensor", mask))
    text = jnp.concatenate(parts, axis=2)
    slots = [text] + [swapped(text, "dp", 2 * mask) for mask in range(1, planes)]

    image = jnp.concatenate([image, swapped(image, "dp", 1)], axis=1)
    blocks = [image]
    mask = tensor_count // 2
    image_blocks = {0: image}
    while mask >= 1:
        held = sorted(image_blocks)
        sent = jnp.concatenate([image_blocks[k] for k in held], axis=2)
        got = swapped(sent, "tensor", mask)
        for place, k in enumerate(held):
            image_blocks[k ^ mask] = got[:, :, place * cols : (place + 1) * cols]
        mask //= 2
    image = jnp.concatenate([image_blocks[k] for k in range(tensor_count)], axis=2)
    text = jnp.concatenate(slots, axis=1)

    def out_columns(value, rank):
        taken = [
            lax.dynamic_slice_in_dim(value, (rank ^ (2 * mask)) * out_rows, out_rows, 1)
            for mask in range(planes)
        ]
        return jnp.concatenate(taken, axis=1)

    def plane_encodings(value):
        other = swapped(out_columns(value, data_rank ^ 1), "dp", 1)
        return jnp.concatenate([out_columns(value, data_rank), other], axis=0)

    picture_plane = plane_encodings(picture_averaged_encodings)
    ordered = jnp.concatenate(
        [share_of(caption_averaged_encodings, 0, mask) for mask in range(tensor_count)], axis=0
    )
    caption_plane = plane_encodings(ordered)

    image_unit, image_tangent, image_radius, image_rate = unit_parts(image[0], image[1])
    text_unit, text_tangent, text_radius, text_rate = unit_parts(text[0], text[1])
    image_half = image_unit.astype(half)
    image_tangent_half = image_tangent.astype(half)
    text_half = text_unit.astype(half)
    text_tangent_half = text_tangent.astype(half)

    logits = similarity_multiplier * matmul_nt(text_half, image_half) + logit_bias
    logit_rate = similarity_multiplier * (
        matmul_nt(text_half, image_tangent_half) + matmul_nt(text_tangent_half, image_half)
    )
    probability = jax.nn.sigmoid(logits)
    text_ids = lax.broadcasted_iota(jnp.int32, (logits.shape[0], 1), 0)
    image_ids = lax.broadcasted_iota(jnp.int32, (1, logits.shape[1]), 1)
    positive = ((text_ids < share) & (text_ids + tensor_rank * share == image_ids)).astype(
        jnp.float32
    )
    weight = (probability - positive).astype(half)
    weight_rate = (probability * (1.0 - probability) * logit_rate).astype(half)
    text_grad = similarity_multiplier * matmul(weight, image_half)
    text_grad_rate = similarity_multiplier * (
        matmul(weight_rate, image_half) + matmul(weight, image_tangent_half)
    )
    image_grad = similarity_multiplier * matmul_tn(weight, text_half)
    image_grad_rate = similarity_multiplier * (
        matmul_tn(weight_rate, text_half) + matmul_tn(weight, text_tangent_half)
    )

    text_back = unit_backward(
        text_unit, text_tangent, text_radius, text_rate, text_grad, text_grad_rate
    )
    image_back = unit_backward(
        image_unit, image_tangent, image_radius, image_rate, image_grad, image_grad_rate
    )

    total = text_back[:share]
    for mask in range(1, planes):
        sent = text_back[mask * share : (mask + 1) * share].astype(half)
        total = total + swapped(sent, "dp", 2 * mask).astype(jnp.float32)
    text_back = total.astype(half)
    parts = [text_back[:, :cols]]
    for mask in range(1, tensor_count):
        sent = text_back[:, mask * cols : (mask + 1) * cols]
        parts.append(swapped(sent, "tensor", mask))
    text_back = jnp.concatenate(parts, axis=0)
    text_back = jnp.concatenate([text_back, swapped(text_back, "dp", 1)], axis=0)

    image_blocks = {k: image_back[:, k * cols : (k + 1) * cols] for k in range(tensor_count)}
    mask = 1
    while mask < tensor_count:
        kept = [k for k in sorted(image_blocks) if not k & mask]
        sent = jnp.concatenate([image_blocks[k ^ mask] for k in kept], axis=1)
        got = swapped(sent, "tensor", mask).astype(jnp.float32)
        image_blocks = {
            k: image_blocks[k] + got[:, place * cols : (place + 1) * cols]
            for place, k in enumerate(kept)
        }
        mask *= 2
    image_back = image_blocks[0]
    got = swapped(image_back, "dp", 1)
    image_back = (
        image_back + jnp.concatenate([got[rows:], got[:rows]], axis=0)
    ).astype(half)

    def head(encodings, back):
        product = matmul_tn(encodings, back)
        total = product[:out_rows]
        for mask in range(1, planes):
            sent = product[mask * out_rows : (mask + 1) * out_rows].astype(half)
            total = total + swapped(sent, "dp", 2 * mask).astype(jnp.float32)
        return total

    return (head(picture_plane, image_back), head(caption_plane, text_back))


def call(kernel, outs, *args, after=(), scratch=(), fetched=False):
    count = len(args)

    def body(*refs):
        kernel(*refs[:count], *refs[count + len(after) :])

    def place(value):
        if value.ndim == 1:
            return pl.BlockSpec(memory_space=pltpu.SMEM)
        return pl.BlockSpec(memory_space=pltpu.HBM if fetched else pltpu.VMEM)

    return pl.pallas_call(
        body,
        out_shape=[jax.ShapeDtypeStruct(shape, dtype) for shape, dtype in outs],
        in_specs=[place(value) for value in args]
        + [pl.BlockSpec(memory_space=pl.ANY) for _ in after],
        out_specs=[pl.BlockSpec(memory_space=pltpu.VMEM) for _ in outs],
        scratch_shapes=list(scratch),
        compiler_params=pltpu.CompilerParams(
            vmem_limit_bytes=(62 if fetched else 14) * 1024 * 1024
        ),
    )(*args, *after)


def folds(rows, main, tail):
    across = main // tail
    for k in range(rows // 16):
        here = slice(k * 16, (k + 1) * 16)
        at = rows + k // across * 16
        first = k % across * tail
        yield here, slice(at, at + 16), slice(first, first + tail)


def folded_rows(rows, main, tail):
    return rows + -(-rows // 16 // (main // tail)) * 16


def fold(out, first, value, main):
    rows, cols = value.shape
    out[first : first + rows, :] = value[:, :main].astype(out.dtype)
    for here, there, lanes in folds(rows, main, cols - main):
        there = slice(first + there.start, first + there.stop)
        out[there, lanes] = value[here, main:].astype(out.dtype)


def unfold(ref, first, rows, main, tail):
    tails = [
        ref[first + there.start : first + there.stop, lanes]
        for _, there, lanes in folds(rows, main, tail)
    ]
    return jnp.concatenate([ref[first : first + rows, :], jnp.concatenate(tails, axis=0)], axis=1)


def fetch_project_kernel(share, parts, starts, encodings, weight, direction, *refs):
    outs, held, done = refs[:-4], refs[-4:-1], refs[-1]
    copies = []
    for which, (source, target) in enumerate(zip((encodings, weight, direction), held)):
        rows = source.shape[0] // parts
        for part in range(parts):
            here = pl.ds(part * rows, rows)
            copies.append(
                pltpu.make_async_copy(source.at[here, :], target.at[here, :], done.at[which, part])
            )
    for copy in copies:
        copy.start()
    for copy in copies[: 2 * parts]:
        copy.wait()

    def arrived():
        for copy in copies[2 * parts :]:
            copy.wait()

    project_kernel(share, starts, *held, *outs, arrived=arrived)


def project_kernel(share, starts, encodings, weight, direction, *outs, arrived=lambda: None):
    main = weight.shape[0] // 128 * 128
    left = jnp.concatenate(
        [
            encodings[pl.ds(pl.multiple_of(starts[k], 16), share), :]
            for k in range(starts.shape[0])
        ],
        axis=0,
    )
    for first in (0, main, 2 * main):
        if first == main:
            arrived()
        if first < 2 * main:
            right = (weight, direction)[first // main][:main, :]
        else:
            right = jnp.concatenate([weight[main:, :], direction[main:, :]], axis=0)
        product = matmul_nt(left, right).astype(jnp.bfloat16)
        place = 0
        for out in outs:
            rows = out.shape[0]
            out[:, first : first + right.shape[0]] = product[place : place + rows]
            place += rows


def gathered(blocks, main, tail, which):
    first = 2 * main + which * tail
    mains = [block[:, which * main : (which + 1) * main] for block in blocks]
    tails = [block[:, first : first + tail] for block in blocks]
    return jnp.concatenate(mains + tails, axis=1)


def relay_kernel(mine, got, out):
    rows = mine.shape[0]
    out[:rows, :] = mine[...]
    out[rows:, :] = got[rows:, :]


def text_rows_kernel(main, tail, own, far, near, out):
    rows, width = own.shape[0], out.shape[1] // 2
    parts = (own[...], near[:rows, :], far[:rows, :], near[rows:, :])
    blocks = [part.astype(jnp.float32) for part in parts]
    out[:, :width] = gathered(blocks, main, tail, 0).astype(jnp.bfloat16)
    out[:, width:] = gathered(blocks, main, tail, 1).astype(jnp.bfloat16)


def row_factors(values, tangent):
    squares = jnp.sum(values * values, axis=1, keepdims=True)
    cross = jnp.sum(values * tangent, axis=1, keepdims=True)
    inverse = 1.0 / jnp.sqrt(squares + EPS)
    return inverse, cross * inverse


def unit_rows(values, tangent, inverse, rate):
    unit = values * inverse
    return unit, (tangent - unit * rate) * inverse


def back_rows(unit, tangent, inverse, rate, grad, grad_rate):
    inner = jnp.sum(unit * grad, axis=1, keepdims=True)
    inner_rate = jnp.sum(tangent * grad + unit * grad_rate, axis=1, keepdims=True)
    scaled = rate * inverse
    return (
        grad_rate - tangent * inner - grad * scaled + unit * (inner * scaled - inner_rate)
    ) * inverse


STEP = 48


def image_rows_kernel(main, tail, count, near, far, raw_both, half_both, factors):
    rows = raw_both.shape[0] // 4
    for shard in range(2):
        held = [
            (near, far)[k % 2].at[pl.ds((k - k % 2 + shard) * rows, rows), :] for k in range(count)
        ]

        @pl.loop(0, rows // STEP)
        def _(step):
            here = pl.ds(pl.multiple_of(step * STEP, STEP), STEP)
            there = pl.ds(pl.multiple_of(shard * rows + step * STEP, STEP), STEP)
            parts = [block[here, :].astype(jnp.float32) for block in held]
            values = gathered(parts, main, tail, 0)
            rates = gathered(parts, main, tail, 1)
            inverse, rate = row_factors(values, rates)
            one, two = unit_rows(values, rates, inverse, rate)
            below = pl.ds(pl.multiple_of((2 + shard) * rows + step * STEP, STEP), STEP)
            raw_both[there, :] = values.astype(jnp.bfloat16)
            raw_both[below, :] = rates.astype(jnp.bfloat16)
            half_both[there, :] = one.astype(jnp.bfloat16)
            half_both[below, :] = two.astype(jnp.bfloat16)
            factors[0, there, :] = jnp.broadcast_to(inverse, (STEP, 128))
            factors[1, there, :] = jnp.broadcast_to(rate, (STEP, 128))


def text_rows(text):
    width = text.shape[1] // 2
    values, rates = text[:, :width].astype(jnp.float32), text[:, width:].astype(jnp.float32)
    inverse, rate = row_factors(values, rates)
    return unit_rows(values, rates, inverse, rate) + (inverse, rate)


def weight_kernel(slots, first, start, scalars, half_both, *refs):
    texts, refs = refs[: slots - first], refs[slots - first :]
    held, (text_both, weights, weights_turned) = refs[:-3], refs[-3:]
    bf16 = jnp.bfloat16
    share = texts[0].shape[0]
    count, images = slots * share, half_both.shape[0] // 2
    done = first * share
    multiplier, bias = scalars[0], scalars[1]
    if held:
        for part in range(2):
            here = slice(part * done, (part + 1) * done)
            there = slice(part * count, part * count + done)
            text_both[there, :] = held[0][here, :]
            weights_turned[:, there] = held[2][:, here]
        weights[:done, :] = held[1][...]
    units, tangents = [], []
    for text in texts:
        unit, tangent, _, _ = text_rows(text)
        units.append(unit.astype(bf16))
        tangents.append(tangent.astype(bf16))
    units, both = jnp.concatenate(units, axis=0), jnp.concatenate(units + tangents, axis=0)
    fresh = units.shape[0]
    text_both[done:count, :] = units
    text_both[count + done :, :] = both[fresh:]
    products = matmul_nt(both, half_both[:images, :])
    logits = multiplier * products[:fresh] + bias
    logit_rate = multiplier * (matmul_nt(units, half_both[images:, :]) + products[fresh:])
    probability = jax.nn.sigmoid(logits)
    text_ids = lax.broadcasted_iota(jnp.int32, logits.shape, 0) + done
    image_ids = lax.broadcasted_iota(jnp.int32, logits.shape, 1)
    positive = jnp.where((text_ids < share) & (text_ids + start[0] == image_ids), 1.0, 0.0)
    value = probability - positive
    value_rate = probability * (1.0 - probability) * logit_rate
    weights[done:, :images] = value_rate.astype(bf16)
    weights[done:, images:] = value.astype(bf16)
    weights_turned[:, done:count] = value_rate.T.astype(bf16)
    weights_turned[:, count + done :] = value.T.astype(bf16)


def text_block_kernel(slots, scalars, half_both, weights, *refs):
    texts, sums = refs[:slots], refs[slots:]
    share, images = texts[0].shape[0], half_both.shape[0] // 2
    grad = matmul(weights[:, images:], half_both[:images, :])
    grad_rate = matmul(weights[...], half_both[...])
    for slot, text in enumerate(texts):
        here = slice(slot * share, (slot + 1) * share)
        back = scalars[0] * back_rows(*text_rows(text), grad[here], grad_rate[here])
        at = slice(slot // 2 * share, (slot // 2 + 1) * share)
        sums[slot % 2][at, :] = back.astype(sums[slot % 2].dtype)


def forward_kernel(mine, got, total, sent):
    share = total.shape[0]
    total[...] = mine[:share, :] + got[:share, :].astype(jnp.float32)
    sent[...] = (mine[share:, :] + got[share:, :].astype(jnp.float32)).astype(jnp.bfloat16)


def image_block_kernel(main, tail, scalars, raw_both, factors, text_both, weights, kept, sent):
    rows, width = raw_both.shape[0] // 4, raw_both.shape[1]
    count, texts = width // (main + tail), text_both.shape[0] // 2
    grads = matmul(weights[:, texts:], text_both[:texts, :])
    grad_rates = matmul(weights[...], text_both[...])
    for shard in range(2):
        here = slice(shard * rows, (shard + 1) * rows)
        inverse, rate = factors[0, here, :1], factors[1, here, :1]
        below = slice((2 + shard) * rows, (3 + shard) * rows)
        values, rates = raw_both[here, :], raw_both[below, :]
        unit, tangent = unit_rows(
            values.astype(jnp.float32), rates.astype(jnp.float32), inverse, rate
        )
        back = back_rows(unit, tangent, inverse, rate, grads[here], grad_rates[here])
        back = scalars[0] * back
        for k in range(count):
            out = (kept, sent)[k % 2]
            to = slice(k // 2 * rows, (k // 2 + 1) * rows)
            out[to, shard * main : (shard + 1) * main] = back[:, k * main : (k + 1) * main]
            first = 2 * main + shard * tail
            taken = count * main + k * tail
            out[to, first : first + tail] = back[:, taken : taken + tail]


def text_sum_kernel(main, tail, own, *refs):
    count = own.shape[1] // (main + tail)
    got, outs = refs[:-count], refs[-count:]
    total = own[...]
    for ref in got:
        total = total + ref[...].astype(jnp.float32)
    for k, out in enumerate(outs):
        first = count * main + k * tail
        out[:, :main] = total[:, k * main : (k + 1) * main].astype(jnp.bfloat16)
        out[:, main:] = total[:, first : first + tail].astype(jnp.bfloat16)


def stack_kernel(*refs):
    rows = refs[0].shape[0]
    for k, ref in enumerate(refs[:-1]):
        refs[-1][k * rows : (k + 1) * rows, : ref.shape[1]] = ref[...]


def fold_kernel(*refs):
    value = jnp.concatenate([ref[...] for ref in refs[:-1]], axis=0)
    fold(refs[-1], 0, value, refs[-1].shape[1])


def turn_kernel(places, core, picture, caption, mine, other):
    for which, encodings in enumerate((picture, caption)):
        turned = encodings[...].T
        count = places.shape[0]
        size, rows = turned.shape[0] // count, turned.shape[1]
        fold = count // 4
        for block in range(count):
            taken = turned[block * size : (block + 1) * size, :]
            slot = places[block]
            at = pl.multiple_of(slot % fold * size, 16)
            for half in range(2):
                lanes = slice(half * rows, (half + 1) * rows)

                @pl.when(slot // fold == half)
                def _():
                    mine[pl.ds(which * fold * size + at, size), lanes] = taken

                @pl.when((slot // fold == 2 + half) & (core[0] == which))
                def _():
                    other[pl.ds(at, size), lanes] = taken


def shard_columns(value, main, tail, shard):
    at = 2 * main + shard * tail
    return jnp.concatenate(
        [value[:, shard * main : (shard + 1) * main], value[:, at : at + tail]], axis=1
    )


def image_pair_kernel(main, tail, share, near, kept, got, total, over_x, over_y, over_both):
    rows = total.shape[0]
    ours = kept[:rows, :] + got[:rows, :]
    theirs = kept[rows:, :] + got[rows:, :]
    total[...] = shard_columns(ours, main, tail, 0)
    fold(over_y, 0, shard_columns(ours, main, tail, 1), main)
    fold(over_both, 0, shard_columns(theirs, main, tail, 1), main)
    value = shard_columns(theirs, main, tail, 0)
    rounded = value.astype(jnp.bfloat16)
    fold(over_x, 0, rounded, main)
    left = value - rounded.astype(jnp.float32)
    left = jnp.where(near[0] == 0, left[: 2 * share], left[2 * share : 4 * share])
    fold(over_x, folded_rows(rows, main, tail), left, main)


def image_sum_kernel(main, tail, share, near, total, over_x, over_y, over_both, out):
    rows = total.shape[0]
    value = total[...]
    for source in (over_x, over_y, over_both):
        value = value + unfold(source, 0, rows, main, tail).astype(jnp.float32)
    left = unfold(over_x, folded_rows(rows, main, tail), 2 * share, main, tail)
    left = left.astype(jnp.float32)
    zero = jnp.zeros_like(left)
    far = near[0] == 0
    value = value + jnp.concatenate(
        [jnp.where(far, zero, left), jnp.where(far, left, zero)], axis=0
    )
    fold(out, 0, value.astype(jnp.bfloat16), main)


def head_kernel(main, tail, head, core, starts, mine, near, far, back, back_other, own, *refs):
    sent, (ordered,) = refs[:-1], refs[-1:]
    size, rows = own.shape[0], ordered.shape[1]
    share = rows // starts.shape[0]
    for which, ref in enumerate((back, back_other)):
        value = unfold(ref, 0, rows, main, tail)
        for k in range(starts.shape[0]):
            at = pl.ds(pl.multiple_of(starts[k], 16), share)
            ordered[which, at, :] = value[k * share : (k + 1) * share]
    count = (len(sent) + 1) // 2
    other = jnp.where(core[0] == head, near[...], far[...])
    for half in range(2):
        here = slice(head * count * size, (head + 1) * count * size)
        lanes = slice(half * rows, (half + 1) * rows)
        product = matmul(mine[here, lanes], ordered[0]) + matmul(other[:, lanes], ordered[1])
        for place in range(count):
            part = product[place * size : (place + 1) * size]
            slot = half * count + place
            if slot == 0:
                own[...] = part
            else:
                fold(sent[slot - 1], 0, part, main)


def final_kernel(main, tail, own, *refs):
    got, out = refs[:-1], refs[-1]
    total = own[...]
    for ref in got:
        total = total + unfold(ref, 0, own.shape[0], main, tail).astype(jnp.float32)
    out[...] = total


def final_kernel(main, tail, own, *refs):
    got, out = refs[:-1], refs[-1]
    size = own.shape[0]
    total = own[:, :main]
    for ref in got:
        total = total + ref[:size, :].astype(jnp.float32)
    out[:, :main] = total
    for rows_in, rows_out, lanes_out in folds(size, main, tail):
        total = own[rows_in, main:]
        for ref in got:
            total = total + ref[rows_out, lanes_out].astype(jnp.float32)
        out[rows_in, main:] = total


def packed(
    picture_averaged_encodings,
    caption_averaged_encodings,
    picture_mapping_matrix,
    caption_mapping_matrix,
    picture_weight_perturbation,
    caption_weight_perturbation,
    sharpness_multiplier,
    offset_additive,
):
    tensor_rank = lax.axis_index("tensor")
    data_rank = lax.axis_index("dp")
    count = lax.axis_size("tensor")
    data_count = lax.axis_size("dp")
    planes = data_count // 2
    rows, width = picture_averaged_encodings.shape
    cols = picture_mapping_matrix.shape[1]
    main = cols // 128 * 128
    tail = cols - main
    share = rows // count
    size = width // data_count
    wide = -(-2 * cols // 128) * 128
    f32, bf16 = jnp.float32, jnp.bfloat16
    ranks = jnp.arange(count, dtype=jnp.int32)
    starts = (ranks ^ tensor_rank) * share
    plain = ranks * share

    parts = 3
    blocks = call(
        functools.partial(fetch_project_kernel, share, parts),
        [((share, 2 * cols), bf16)] * 2 + [((2 * share, 2 * cols), bf16)],
        starts,
        caption_averaged_encodings,
        caption_mapping_matrix.T,
        caption_weight_perturbation.T,
        scratch=[
            pltpu.VMEM((rows, width), bf16),
            pltpu.VMEM((cols, width), bf16),
            pltpu.VMEM((cols, width), bf16),
            pltpu.SemaphoreType.DMA((3, parts)),
        ],
        fetched=True,
    )
    text_far = swapped(blocks[2], "tensor", 2)
    (relay,) = call(relay_kernel, [((2 * share, 2 * cols), bf16)], blocks[1], text_far)
    text_near = swapped(relay, "tensor", 1)

    (image,) = call(
        functools.partial(project_kernel, share),
        [((rows, 2 * cols), bf16)],
        plain,
        picture_averaged_encodings,
        picture_mapping_matrix.T,
        picture_weight_perturbation.T,
    )
    image_other = swapped(image, "dp", 1)
    image_far = swapped(image, "tensor", 2)
    image_far_other = swapped(image_other, "tensor", 2)

    (text,) = call(
        functools.partial(text_rows_kernel, main, tail),
        [((share, 2 * width), bf16)],
        blocks[0],
        text_far,
        text_near,
    )
    text_two = swapped(text, "dp", 4)
    text_one = swapped(text, "dp", 2)
    text_three = swapped(text_two, "dp", 2)
    texts = [text, text_one, text_two, text_three]

    block_ids = jnp.arange(data_count, dtype=jnp.int32)
    slots = ((block_ids ^ data_rank) >> 1) + planes * ((block_ids ^ data_rank) & 1)
    core = (tensor_rank & 1).astype(jnp.int32).reshape(1)
    mine, other = call(
        turn_kernel,
        [((planes * size, 2 * rows), bf16), ((planes // 2 * size, 2 * rows), bf16)],
        slots,
        core,
        picture_averaged_encodings,
        caption_averaged_encodings,
        after=(image_other,),
    )
    other = swapped(other, "dp", 1)
    others = (other, swapped(other, "tensor", 1))

    (near,) = call(
        stack_kernel,
        [((4 * rows, wide), bf16)],
        image,
        image_other,
        image_far,
        image_far_other,
        after=(text_one, text_two, others[0]),
    )
    far = swapped(near, "tensor", 1)
    raw_both, half_both, factors = call(
        functools.partial(image_rows_kernel, main, tail, count),
        [
            ((4 * rows, width), bf16),
            ((4 * rows, width), bf16),
            ((2, 2 * rows, 128), f32),
        ],
        near,
        far,
    )

    scalars = jnp.concatenate([sharpness_multiplier, offset_additive])
    def block_weights(slots, first, *held, after=()):
        return call(
            functools.partial(weight_kernel, slots, first),
            [
                ((2 * slots * share, width), bf16),
                ((slots * share, 4 * rows), bf16),
                ((2 * rows, 2 * slots * share), bf16),
            ],
            (tensor_rank * share).astype(jnp.int32).reshape(1),
            scalars,
            half_both,
            *texts[first:slots],
            *held,
            after=after,
        )

    held = block_weights(planes - 1, 0, after=(others[1],))
    text_both, weights, weights_turned = block_weights(planes, planes - 1, *held)
    kept, sent = call(
        functools.partial(image_block_kernel, main, tail),
        [((2 * rows, wide), f32)] * 2,
        scalars,
        raw_both,
        factors,
        text_both,
        weights_turned,
    )
    outs = call(
        functools.partial(text_block_kernel, planes),
        [((2 * share, width), f32), ((2 * share, width), bf16)],
        scalars,
        half_both,
        weights,
        *texts,
        after=(kept,),
    )

    near = (tensor_rank // 2).astype(jnp.int32).reshape(1)
    tall = folded_rows(rows, main, tail)
    more = folded_rows(2 * share, main, tail)
    total, to_x, to_y, to_both = call(
        functools.partial(image_pair_kernel, main, tail, share),
        [((rows, cols), f32), ((tall + more, main), bf16)] + [((tall, main), bf16)] * 2,
        near,
        kept,
        swapped(sent, "tensor", 1),
        after=(outs[1],),
    )
    flat = [(source, source ^ (count + 2)) for source in range(data_count * count)]
    (image_back,) = call(
        functools.partial(image_sum_kernel, main, tail, share),
        [((tall, main), bf16)],
        near,
        total,
        swapped(to_x, "tensor", 2),
        swapped(to_y, "dp", 1),
        lax.ppermute(to_both, ("dp", "tensor"), flat),
    )
    image_back_other = swapped(image_back, "dp", 1)

    def head(which, order, back, back_other):
        return call(
            functools.partial(head_kernel, main, tail, which),
            [((size, cols), f32)]
            + [((folded_rows(size, main, tail), main), bf16)] * (planes - 1),
            core,
            order,
            mine,
            *others,
            back,
            back_other,
            scratch=[pltpu.VMEM((2, rows, cols), bf16)],
        )

    def summed(products):
        got = [swapped(products[k], "dp", 2 * k) for k in range(1, planes)]
        return call(
            functools.partial(final_kernel, main, tail), [((size, cols), f32)], products[0], *got
        )[0]

    image_products = head(0, plain, image_back, image_back_other)

    text_total, text_sent = call(
        forward_kernel,
        [((share, width), f32), ((share, width), bf16)],
        outs[0],
        swapped(outs[1], "dp", 2),
    )
    blocks = call(
        functools.partial(text_sum_kernel, main, tail),
        [((share, cols), bf16)] * count,
        text_total,
        swapped(text_sent, "dp", 4),
        after=(image_back,),
    )
    got = [blocks[0]] + [swapped(blocks[k], "tensor", k) for k in range(1, count)]
    (text_back,) = call(fold_kernel, [((tall, main), bf16)], *got, after=(image_products[0],))
    text_back_other = swapped(text_back, "dp", 1)

    text_products = head(1, starts, text_back, text_back_other)
    return summed(image_products), summed(text_products)


def fits(mesh):
    return mesh.shape["tensor"] == 4 and mesh.shape["dp"] == 8


def solution(mesh):
    in_specs = (
        P("dp", None),
        P("dp", None),
        P(None, "tensor"),
        P(None, "tensor"),
        P(None, "tensor"),
        P(None, "tensor"),
        P(),
        P(),
    )
    out_specs = (P("dp", "tensor"), P("dp", "tensor"))
    local = packed if fits(mesh) else general
    return jax.shard_map(local, mesh=mesh, in_specs=in_specs, out_specs=out_specs, check_vma=False)
```
